32 devices in a mesh: groups: 2 (over y), seq: 4 (over z), head: 4 (over x, core).
Axes of the slice: x: 2, y: 2, z: 4, core: 2. Of those that a mesh axis runs over, the one named last changes fastest.
Arguments:
- x_in: bfloat16 [1024, 8192], P(('groups', 'seq'), 'head'), parts along dimension 0, may hold values from -6 to 6
- bc_in: bfloat16 [1024, 8, 256], P(('groups', 'seq'), 'head'), parts along dimension 0, may hold values from -6 to 6
- z_in: bfloat16 [1024, 8192], P(('groups', 'seq'), 'head'), parts along dimension 0, may hold values from -6 to 6
- dt_raw: float32 [1024, 128], P(('groups', 'seq'), 'head'), parts along dimension 0, may hold values from -12 to 0
- conv_x: float32 [4, 8192], P(None, 'head'), may hold values from -3 to 3
- conv_bc: float32 [4, 8, 256], P(None, 'head'), may hold values from -3 to 3
- a_log: float32 [128], P('head'), may hold values from -0.35 to 0.35
- d_skip: float32 [128], P('head'), may hold values from 0.5 to 1.5
- norm_gain: float32 [8192], P('head'), may hold values from 0.25 to 1.75
Outputs:
- out: bfloat16 [1024, 8192], P(('groups', 'seq'), 'head'), parts along dimension 0
The draws below stay inside these ranges and needn't reach their ends.
There are 2 independent parts, one for each index of `groups`. The reference program is written for one: setup_inputs(seed, part) draws one part's arguments, and reference() takes and returns one part's arrays. A program takes and returns all parts, laid end to end along the dimension named above; an argument that names none is the same for every part. Nothing has to cross between parts.
All inputs are finite; a program needn't handle non-finite values.
Results may differ from the reference program's by a relative error of at most 0.0056.
Values may be sent and summed in bfloat16 or wider, within the bound.
No kernel may reach another device: no remote copies, remote signals or barrier semaphores. Data moves between devices by JAX's collectives and lax.ppermute only.
A program may use at most 192 MiB of HBM per device.

```python
import jax
import jax.numpy as jnp
from jax import lax

LOCAL_HEADS = 128
HEAD_DIM = 64
STATE = 128
BC_GROUPS = 8
CONV = 4
BLOCK = 128
WINDOW_TOKENS = 512
INNER = 8192


def draw_dt_raw(key, part):
    random_keys = jax.random.split(key, 6)
    share = 0.5
    slow = jax.random.uniform(random_keys[0], (LOCAL_HEADS,)) < share
    fast_rate = 1.0 / jax.random.uniform(random_keys[1], (LOCAL_HEADS,), minval=30.0, maxval=50.0)
    slow_rate = jax.random.uniform(random_keys[2], (LOCAL_HEADS,), minval=0.25, maxval=0.5) / WINDOW_TOKENS
    baseline_rate = jnp.where(slow, slow_rate, fast_rate)
    noisy_steps = jnp.exp(jax.random.uniform(random_keys[3], (WINDOW_TOKENS, LOCAL_HEADS), minval=-0.5, maxval=0.5))
    spike_positions = jax.random.randint(random_keys[4], (3,), 0, WINDOW_TOKENS)
    spike_draw = jnp.any(jnp.arange(WINDOW_TOKENS)[:, None] == spike_positions[None, :], axis=1)
    spike_height = jax.random.uniform(random_keys[5], (WINDOW_TOKENS, LOCAL_HEADS), minval=0.25, maxval=0.5)
    time_step_values = jnp.where(spike_draw[:, None], spike_height, baseline_rate[None, :] * noisy_steps)
    return jnp.log(jnp.expm1(time_step_values)).astype(jnp.float32)


def block_levels(stream_key, extent, pieces, smallest, largest):
    def one(axis_at, blocks):
        draws = jax.random.uniform(jax.random.fold_in(jax.random.fold_in(stream_key, 6), axis_at), (blocks,), jnp.float32, smallest / len(pieces), largest / len(pieces))
        return jnp.repeat(jnp.exp(draws), extent[axis_at] // blocks).reshape((-1,) + (1,) * (len(extent) - axis_at - 1))

    level = one(*pieces[0])
    for cut in pieces[1:]:
        level = level * one(*cut)
    return level


def bell_draw(rng, shape, spread, most, cuts=(), dtype=jnp.bfloat16):
    drawn = spread * jax.random.normal(rng, shape, jnp.float32)
    if cuts:
        drawn = drawn * block_levels(rng, shape, cuts, -0.22, 0.18)
    return jnp.clip(drawn, -most, most).astype(dtype)


def setup_inputs(seed: int = 0, part: int = 0) -> dict:
    arg_keys = jax.random.split(jax.random.key(seed), 10)
    part_keys = jax.random.split(jax.random.fold_in(arg_keys[9], part), 10)
    x_in = bell_draw(part_keys[0], (WINDOW_TOKENS, INNER), 1.0, 6.0, ((0, 4), (1, 4)))
    bc_in = bell_draw(part_keys[1], (WINDOW_TOKENS, BC_GROUPS, 2 * STATE), 1.0, 6.0, ((0, 4), (1, 4)))
    z_in = bell_draw(part_keys[2], (WINDOW_TOKENS, INNER), 1.0, 6.0, ((0, 4), (1, 4)))
    dt_raw = draw_dt_raw(jax.random.fold_in(jax.random.fold_in(arg_keys[9], part), 71), part)
    conv_x = bell_draw(arg_keys[4], (CONV, INNER), CONV ** -0.5, 3.0, ((1, 4),), jnp.float32)
    conv_bc = bell_draw(arg_keys[5], (CONV, BC_GROUPS, 2 * STATE), CONV ** -0.5, 3.0, ((1, 4),), jnp.float32)
    a_log = jnp.clip(jax.random.uniform(arg_keys[6], (LOCAL_HEADS,), jnp.float32, -0.35, 0.35) * block_levels(arg_keys[6], (LOCAL_HEADS,), ((0, 4),), -0.4, 0.0), -0.35, 0.35)
    d_skip = jnp.clip(0.5 + 1.0 * jax.random.uniform(arg_keys[7], (LOCAL_HEADS,), jnp.float32) ** block_levels(arg_keys[7], (LOCAL_HEADS,), ((0, 4),), -0.2, 0.2), 0.5, 1.5)
    norm_gain = jnp.clip(1.0 + 0.15 * jax.random.normal(arg_keys[8], (INNER,), jnp.float32), 0.25, 1.75)
    return {"x_in": x_in, "bc_in": bc_in, "z_in": z_in, "dt_raw": dt_raw, "conv_x": conv_x, "conv_bc": conv_bc, "a_log": a_log, "d_skip": d_skip, "norm_gain": norm_gain}


EPS = 1e-05

def conv_silu(tail_rows, series, taps):
    length = series.shape[0]
    padded = jnp.concatenate([tail_rows, series.astype(jnp.float32)], axis=0)
    running = jnp.zeros(series.shape, jnp.float32)
    for offset in range(taps.shape[0]):
        running = running + taps[offset] * padded[offset:offset + length]
    return jax.nn.silu(running).astype(jnp.bfloat16)

def block_terms(inputs, b_input, c_output, deltas, rates):
    cum_rate = jnp.cumsum(rates, axis=0)
    cum_moved = jnp.transpose(cum_rate, (1, 2, 0))
    delta_moved = jnp.transpose(deltas, (1, 2, 0))
    places = jnp.arange(cum_rate.shape[0])
    causal = places[:, None] >= places[None, :]
    gaps_all = cum_moved[..., :, None] - cum_moved[..., None, :]
    decays = jnp.where(causal, jnp.exp(jnp.where(causal, gaps_all, 0.0)), 0.0)
    intersection = jnp.einsum('tgn,sgn->gts', c_output.astype(jnp.float32), b_input.astype(jnp.float32))
    weight = (decays * delta_moved[..., None, :] * intersection[:, None]).astype(jnp.bfloat16)
    y_intra = jnp.einsum('ghts,sghp->tghp', weight.astype(jnp.float32), inputs.astype(jnp.float32))
    tail_decay = jnp.exp(cum_rate[-1] - cum_rate) * deltas
    scaled = (tail_decay[..., None] * inputs.astype(jnp.float32)).astype(jnp.bfloat16)
    states = jnp.einsum('sghp,sgn->ghpn', scaled.astype(jnp.float32), b_input.astype(jnp.float32))
    return (y_intra, states, cum_rate, jnp.exp(cum_rate[-1]))

def block_output(y_intra, cum_rate, c_output, inputs, gates, incoming, skip, gain):
    state_half = incoming.astype(jnp.bfloat16)
    from_state = jnp.einsum('tgn,ghpn->tghp', c_output.astype(jnp.float32), state_half.astype(jnp.float32))
    mixed = y_intra + jnp.exp(cum_rate)[..., None] * from_state + skip[..., None] * inputs.astype(jnp.float32)
    gated = mixed * jax.nn.silu(gates.astype(jnp.float32))
    mean_sq = lax.optimization_barrier(jnp.mean(gated * gated, axis=(2, 3), keepdims=True))
    return (gated * lax.rsqrt(mean_sq + EPS) * gain).astype(jnp.bfloat16)

def reference(x_in, bc_in, z_in, dt_raw, conv_x, conv_bc, a_log, d_skip, norm_gain):
    rim = CONV - 1
    x_act = conv_silu(jnp.zeros((rim, INNER), jnp.float32), x_in, conv_x)
    bc_act = conv_silu(jnp.zeros((rim, BC_GROUPS, 2 * STATE), jnp.float32), bc_in, conv_bc)
    deltas = jax.nn.softplus(dt_raw)
    rates = -jnp.exp(a_log)[None, :] * deltas
    per_group = LOCAL_HEADS // BC_GROUPS
    block_count = WINDOW_TOKENS // BLOCK
    inputs = x_act.reshape(block_count, BLOCK, BC_GROUPS, per_group, HEAD_DIM)
    b_input = bc_act[:, :, :STATE].reshape(block_count, BLOCK, BC_GROUPS, STATE)
    c_output = bc_act[:, :, STATE:].reshape(block_count, BLOCK, BC_GROUPS, STATE)
    delta_blocks = deltas.reshape(block_count, BLOCK, BC_GROUPS, per_group)
    rate_blocks = rates.reshape(block_count, BLOCK, BC_GROUPS, per_group)
    gates = z_in.reshape(block_count, BLOCK, BC_GROUPS, per_group, HEAD_DIM)
    skip = d_skip.reshape(BC_GROUPS, per_group)
    gain = norm_gain.reshape(BC_GROUPS, per_group, HEAD_DIM)

    def advance(carry, piece):
        inputs_b, b_part, c_part, delta_part, rate_part, gate_part = piece
        y_intra, states, cum_rate, block_decay = block_terms(inputs_b, b_part, c_part, delta_part, rate_part)
        result = block_output(y_intra, cum_rate, c_part, inputs_b, gate_part, carry, skip, gain)
        return (block_decay[..., None, None] * carry + states, result)
    start = jnp.zeros((BC_GROUPS, per_group, HEAD_DIM, STATE), jnp.float32)
    _, outputs = lax.scan(advance, start, (inputs, b_input, c_output, delta_blocks, rate_blocks, gates))
    return outputs.reshape(WINDOW_TOKENS, INNER)
```

```python
import functools

import jax
import jax.numpy as jnp
from jax import lax
from jax.experimental import pallas as pl
from jax.experimental.pallas import tpu as pltpu
from jax.sharding import PartitionSpec as P

EPS = 1e-05
F32 = jnp.float32
BF16 = jnp.bfloat16
CHAIN_MOST = 4


def silu(u):
    return 0.5 * u * (1.0 + jnp.tanh(0.5 * u))


def softplus(v):
    return jnp.maximum(v, 0.0) + jnp.log1p(jnp.exp(-jnp.abs(v)))


def halves(v, count, axis):
    parts = []
    for _ in range(count - 1):
        part = v.astype(BF16)
        parts.append(part)
        v = v - part.astype(F32)
    parts.append(v.astype(BF16))
    return jnp.concatenate(parts, axis=axis)


def spread(per_head, head_dim, count):
    heads = per_head.shape[0]
    rows = lax.broadcasted_iota(jnp.int32, (heads * count, heads * head_dim), 0)
    cols = lax.broadcasted_iota(jnp.int32, (heads * count, heads * head_dim), 1)
    pick = (rows % heads == cols // head_dim).astype(F32).astype(BF16)
    return lax.dot_general(
        halves(per_head, count, 0), pick, (((0,), (0,)), ((), ())), preferred_element_type=F32
    )


def spread_row(column, head_dim):
    heads = column.shape[0]
    rows = lax.broadcasted_iota(jnp.int32, (heads, heads * head_dim), 0)
    cols = lax.broadcasted_iota(jnp.int32, (heads, heads * head_dim), 1)
    return jnp.sum(jnp.where(rows == cols // head_dim, column, 0.0), axis=0, keepdims=True)


def as_column(row, start, heads):
    every = row.shape[1]
    rows = lax.broadcasted_iota(jnp.int32, (heads, every), 0)
    cols = lax.broadcasted_iota(jnp.int32, (heads, every), 1)
    return jnp.sum(jnp.where(cols == rows + start, row, 0.0), axis=1, keepdims=True)


def conv_act(series, tail, taps):
    count = taps.shape[0]
    above = tail.shape[0]
    padded = jnp.concatenate([tail, series], axis=0)
    total = taps[count - 1 : count] * series
    for back in range(1, count):
        total = total + taps[count - 1 - back : count - back] * pltpu.roll(padded, back, 0)[above:]
    return silu(total).astype(BF16)


def rates(dt_raw, a_log_row, start):
    heads, tokens = dt_raw.shape
    dt = softplus(dt_raw)
    rate = -jnp.exp(as_column(a_log_row, start, heads)) * dt
    earlier = lax.broadcasted_iota(jnp.int32, (tokens, tokens), 0)
    later = lax.broadcasted_iota(jnp.int32, (tokens, tokens), 1)
    upto = (earlier <= later).astype(F32)
    cum = jnp.dot(rate, upto, precision=lax.Precision.HIGHEST, preferred_element_type=F32)
    return dt, cum


def state_kernel(
    group, start, head_dim, x, tail_x, bc, tail_bc, taps_x, taps_bc, dt_raw, a_log,
    x_act, bc_act, state, state_half, decay,
):
    dt, cum = rates(dt_raw[...], a_log[...], start)
    end = cum[:, -1:]
    act = conv_act(x[...].astype(F32), tail_x[...].astype(F32), taps_x[...])
    x_act[...] = act
    bc_here = conv_act(
        bc[...].astype(F32)[:, group], tail_bc[...].astype(F32), taps_bc[...][:, group]
    )
    bc_act[...] = bc_here
    tail_decay = spread(jnp.exp(end - cum) * dt, head_dim, 2)
    scaled = (tail_decay * act.astype(F32)).astype(BF16)
    b = bc_here[:, : bc_here.shape[1] // 2]
    total = lax.dot_general(b, scaled, (((0,), (0,)), ((), ())), preferred_element_type=F32)
    state[...] = total
    state_half[...] = total.astype(BF16)
    decay[...] = spread_row(jnp.exp(end), head_dim)


def intra_kernel(start, head_dim, x_act, bc_act, z, dt_raw, a_log, d_skip, y_part, lead):
    dt, cum = rates(dt_raw[...], a_log[...], start)
    heads, tokens = dt.shape
    state_dim = bc_act.shape[1] // 2
    b, c = bc_act[:, :state_dim], bc_act[:, state_dim:]
    inner = lax.dot_general(c, b, (((1,), (1,)), ((), ())), preferred_element_type=F32)
    t_at = lax.broadcasted_iota(jnp.int32, (tokens, tokens), 0)
    s_at = lax.broadcasted_iota(jnp.int32, (tokens, tokens), 1)
    inner = jnp.where(t_at >= s_at, inner, 0.0)
    cum_t = cum.T
    gate = silu(z[...].astype(F32))
    lead[...] = gate * spread(jnp.exp(cum), head_dim, 2)
    skip = spread_row(as_column(d_skip[...], start, heads), head_dim)
    pair = 2 * head_dim
    for first in range(0, heads, 2):
        cut = slice(first * head_dim, first * head_dim + pair)
        act = x_act[:, cut]
        lane = lax.broadcasted_iota(jnp.int32, act.shape, 1)
        wide = act.astype(F32)
        blocks = jnp.concatenate(
            [jnp.where(lane < head_dim, wide, 0.0), jnp.where(lane < head_dim, 0.0, wide)], axis=0
        ).astype(BF16)
        weights = []
        for h in (first, first + 1):
            gap = jnp.minimum(cum_t[:, h : h + 1] - cum[h : h + 1, :], 0.0)
            weights.append((jnp.exp(gap) * dt[h : h + 1, :] * inner).astype(BF16))
        y = jnp.dot(jnp.concatenate(weights, axis=1), blocks, preferred_element_type=F32)
        y_part[:, cut] = (y + skip[:, cut] * wide) * gate[:, cut]


def output_kernel(seen, c, y_part, lead, gain, *refs):
    arrived, out = refs[:seen], refs[-1]
    state = arrived[0][...]
    for more in arrived[1:]:
        state = state + more[...]
    from_state = jnp.dot(c[...], state, preferred_element_type=F32)
    gated = y_part[...] + lead[...] * from_state
    mean_sq = jnp.mean(gated * gated, axis=1, keepdims=True)
    out[...] = (gated * lax.rsqrt(mean_sq + EPS) * gain[...]).astype(BF16)


def params():
    return pltpu.CompilerParams(vmem_limit_bytes=32 * 1024 * 1024)


def chain(state, to_send, decay, devices):
    arrived = []
    for hop in range(devices - 1):
        came = lax.ppermute(to_send, "seq", [(hop, hop + 1)])
        arrived.append(came)
        to_send = (decay * came.astype(F32) + state).astype(BF16)
    return arrived


def doubling(state, to_send, decay, devices):
    def moved(value, distance):
        return lax.ppermute(value, "seq", [(i, i + distance) for i in range(devices - distance)])

    total, decay = moved(to_send, 1), moved(decay, 1)
    distance = 1
    while distance < devices - 1:
        came = moved(total, distance)
        total = (decay * came.astype(F32) + total.astype(F32)).astype(BF16)
        decay = decay * moved(decay, distance)
        distance *= 2
    return [total]


def shards(x_in, bc_in, z_in, dt_raw, conv_x, conv_bc, a_log, d_skip, norm_gain):
    tokens, width = x_in.shape
    groups = bc_in.shape[1]
    state_dim = bc_in.shape[2] // 2
    heads = dt_raw.shape[1]
    head_dim = width // heads
    taps = conv_x.shape[0]
    cols = width // groups
    per_group = heads // groups
    devices = lax.axis_size("seq")
    rim = 8

    route = [(i, i + 1) for i in range(devices - 1)]
    rows = jnp.concatenate(
        [x_in[tokens - rim :], bc_in[tokens - rim :].reshape(rim, groups * 2 * state_dim)], axis=1
    )
    got = lax.ppermute(rows, "seq", route)
    dt_t = dt_raw.T
    a_row = a_log.reshape(1, heads)
    d_row = d_skip.reshape(1, heads)
    gain = norm_gain.reshape(1, width)

    def whole(array):
        return pl.BlockSpec(array.shape, lambda i: (0,) * array.ndim)

    def column(height, wide, at):
        return pl.BlockSpec((height, wide), lambda i: (0, at))

    states = []
    for g in range(groups):
        states.append(
            pl.pallas_call(
                functools.partial(state_kernel, g, g * per_group, head_dim),
                out_shape=(
                    jax.ShapeDtypeStruct((tokens, cols), BF16),
                    jax.ShapeDtypeStruct((tokens, 2 * state_dim), BF16),
                    jax.ShapeDtypeStruct((state_dim, cols), F32),
                    jax.ShapeDtypeStruct((state_dim, cols), BF16),
                    jax.ShapeDtypeStruct((1, cols), F32),
                ),
                in_specs=[
                    column(tokens, cols, g),
                    column(rim, cols, g),
                    whole(bc_in),
                    column(rim, 2 * state_dim, width // (2 * state_dim) + g),
                    column(taps, cols, g),
                    whole(conv_bc),
                    pl.BlockSpec((per_group, tokens), lambda i, g=g: (g, 0)),
                    whole(a_row),
                ],
                out_specs=(
                    column(tokens, cols, 0),
                    column(tokens, 2 * state_dim, 0),
                    column(state_dim, cols, 0),
                    column(state_dim, cols, 0),
                    column(1, cols, 0),
                ),
                grid=(1,),
                compiler_params=params(),
                name="states",
            )(x_in, got, bc_in, got, conv_x, conv_bc, dt_t, a_row)
        )

    scan = chain if devices <= CHAIN_MOST else doubling
    arrived = [scan(*states[g][2:], devices) for g in range(groups)]

    parts = []
    for g in range(groups):
        act, bc_act, _, _, _ = states[g]
        parts.append(
            pl.pallas_call(
                functools.partial(intra_kernel, g * per_group, head_dim),
                out_shape=(
                    jax.ShapeDtypeStruct((tokens, cols), F32),
                    jax.ShapeDtypeStruct((tokens, cols), F32),
                ),
                in_specs=[
                    whole(act),
                    whole(bc_act),
                    column(tokens, cols, g),
                    pl.BlockSpec((per_group, tokens), lambda i, g=g: (g, 0)),
                    whole(a_row),
                    whole(d_row),
                ],
                out_specs=(column(tokens, cols, 0), column(tokens, cols, 0)),
                grid=(1,),
                compiler_params=params(),
                cost_estimate=pl.CostEstimate(
                    flops=4 * tokens * tokens * cols,
                    bytes_accessed=12 * tokens * cols,
                    transcendentals=tokens * tokens * per_group,
                ),
                name="intra",
            )(act, bc_act, z_in, dt_t, a_row, d_row)
        )

    out = None
    for g in range(groups):
        y_part, lead = parts[g]
        bc_act = states[g][1]
        operands = [bc_act, y_part, lead, gain] + arrived[g]
        specs = [
            column(tokens, state_dim, 1), whole(y_part), whole(lead), column(1, cols, g)
        ] + [whole(v) for v in arrived[g]]
        aliases = {}
        if out is not None:
            aliases = {len(operands): 0}
            operands.append(out)
            specs.append(pl.BlockSpec(memory_space=pl.ANY))
        out = pl.pallas_call(
            functools.partial(output_kernel, len(arrived[g])),
            out_shape=jax.ShapeDtypeStruct((tokens, width), BF16),
            in_specs=specs,
            out_specs=column(tokens, cols, g),
            grid=(1,),
            input_output_aliases=aliases,
            compiler_params=params(),
            name="outputs",
        )(*operands)
    return out


def solution(mesh):
    return jax.shard_map(
        shards,
        mesh=mesh,
        in_specs=(
            P(("groups", "seq"), "head"),
            P(("groups", "seq"), "head", None),
            P(("groups", "seq"), "head"),
            P(("groups", "seq"), "head"),
            P(None, "head"),
            P(None, "head", None),
            P("head"),
            P("head"),
            P("head"),
        ),
        out_specs=P(("groups", "seq"), "head"),
        check_vma=False,
    )
```

```python
import functools

import jax
import jax.numpy as jnp
from jax import lax
from jax.experimental import pallas as pl
from jax.experimental.pallas import tpu as pltpu
from jax.sharding import PartitionSpec as P

EPS = 1e-05
F32 = jnp.float32
BF16 = jnp.bfloat16
CHAIN_MOST = 4
SLICES = 3
CHUNK = 256
LANES = 128


def silu(u):
    return 0.5 * u * (1.0 + jnp.tanh(0.5 * u))


def softplus(v):
    return jnp.maximum(v, 0.0) + jnp.log1p(jnp.exp(-jnp.abs(v)))


def halves(v, count, axis):
    parts = []
    for _ in range(count - 1):
        part = v.astype(BF16)
        parts.append(part)
        v = v - part.astype(F32)
    parts.append(v.astype(BF16))
    return jnp.concatenate(parts, axis=axis)


def spread(per_head, head_dim, count):
    heads = per_head.shape[0]
    rows = lax.broadcasted_iota(jnp.int32, (heads * count, heads * head_dim), 0)
    cols = lax.broadcasted_iota(jnp.int32, (heads * count, heads * head_dim), 1)
    pick = (rows % heads == cols // head_dim).astype(F32).astype(BF16)
    return lax.dot_general(
        halves(per_head, count, 0), pick, (((0,), (0,)), ((), ())), preferred_element_type=F32
    )


def spread_row(column, head_dim):
    heads = column.shape[0]
    rows = lax.broadcasted_iota(jnp.int32, (heads, heads * head_dim), 0)
    cols = lax.broadcasted_iota(jnp.int32, (heads, heads * head_dim), 1)
    return jnp.sum(jnp.where(rows == cols // head_dim, column, 0.0), axis=0, keepdims=True)


def as_column(row, start, heads):
    every = row.shape[1]
    rows = lax.broadcasted_iota(jnp.int32, (heads, every), 0)
    cols = lax.broadcasted_iota(jnp.int32, (heads, every), 1)
    return jnp.sum(jnp.where(cols == rows + start, row, 0.0), axis=1, keepdims=True)


def conv_act(series, tail, taps):
    count = taps.shape[0]
    above = tail.shape[0]
    padded = jnp.concatenate([tail, series], axis=0)
    total = taps[count - 1 : count] * series
    for back in range(1, count):
        total = total + taps[count - 1 - back : count - back] * pltpu.roll(padded, back, 0)[above:]
    return silu(total).astype(BF16)


def rates(dt_raw, a_log_row, start):
    heads, tokens = dt_raw.shape
    dt = softplus(dt_raw)
    rate = -jnp.exp(as_column(a_log_row, start, heads)) * dt
    earlier = lax.broadcasted_iota(jnp.int32, (tokens, tokens), 0)
    later = lax.broadcasted_iota(jnp.int32, (tokens, tokens), 1)
    upto = (earlier <= later).astype(F32)
    cum = jnp.dot(rate, upto, precision=lax.Precision.HIGHEST, preferred_element_type=F32)
    return dt, cum


def started(pairs, sems):
    copies = [pltpu.make_async_copy(src, dst, sems.at[i]) for i, (src, dst) in enumerate(pairs)]
    for copy in copies:
        copy.start()
    return copies


def emit_states(head_dim, x, tail_x, bc, tail_bc, taps_x, taps_bc, dt_raw, a_log, wide, emit):
    dt, cum = rates(dt_raw[...], a_log[...], 0)
    end = cum[:, -1:]
    tail_decay = jnp.exp(end - cum) * dt
    groups = bc.shape[1]
    state_dim = bc.shape[2] // 2
    cols = x.shape[1] // groups
    heads = dt.shape[0] // groups
    for g in range(groups):
        b = conv_act(
            bc[:, :, :state_dim].astype(F32)[:, g],
            tail_bc(g),
            taps_bc[:, :, :state_dim][:, g],
        )
        b_t = b.astype(F32).T.astype(BF16)
        wide[...] = spread(tail_decay[g * heads : (g + 1) * heads], head_dim, 2)
        for at in range(0, cols, CHUNK):
            cut = slice(g * cols + at, g * cols + at + CHUNK)
            act = conv_act(x[:, cut].astype(F32), tail_x(cut), taps_x[:, cut])
            scaled = (wide[:, at : at + CHUNK] * act.astype(F32)).astype(BF16)
            emit(cut, jnp.dot(b_t, scaled, preferred_element_type=F32))
    return end


def first_kernel(head_dim, cuts, *refs):
    active, x_hbm, bc_hbm, taps_x_hbm, taps_bc_hbm, dt_hbm, a_hbm = refs[:7]
    pack, halves_out = refs[7], refs[8 : 8 + len(cuts)]
    x, bc, taps_x, taps_bc, dt_raw, a_log, last_x, last_bc, wide, sems = refs[8 + len(cuts) :]
    tokens, width = x.shape
    rows, groups, both = last_bc.shape
    first = active[0] == 1
    ends = started(
        [
            (x_hbm.at[pl.ds(tokens - rows, rows)], last_x),
            (bc_hbm.at[pl.ds(tokens - rows, rows)], last_bc),
        ],
        sems,
    )
    inner = [(x_hbm, x), (bc_hbm, bc), (taps_x_hbm, taps_x), (taps_bc_hbm, taps_bc),
             (dt_hbm, dt_raw), (a_hbm, a_log)]
    rest = sems.at[pl.ds(2, len(inner))]

    @pl.when(first)
    def _():
        started(inner, rest)

    for copy in ends:
        copy.wait()
    pack[:, :width] = last_x[...]
    wide_bc = last_bc[...].astype(F32)
    for g in range(groups):
        pack[:, width + g * both : width + (g + 1) * both] = wide_bc[:, g].astype(BF16)

    @pl.when(first)
    def _():
        for i, (src, dst) in enumerate(inner):
            pltpu.make_async_copy(src, dst, rest.at[i]).wait()

        def emit(cut, total):
            for (low, high), out in zip(cuts, halves_out):
                begin, stop = max(low, cut.start), min(high, cut.stop)
                if begin < stop:
                    out[:, begin - low : stop - low] = total[
                        :, begin - cut.start : stop - cut.start
                    ].astype(BF16)

        emit_states(
            head_dim, x,
            lambda cut: jnp.zeros((8, cut.stop - cut.start), F32),
            bc, lambda g: jnp.zeros((8, both // 2), F32),
            taps_x, taps_bc, dt_raw, a_log, wide, emit,
        )


def later_kernel(head_dim, *refs):
    active, got, x_hbm, bc_hbm, taps_x_hbm, taps_bc_hbm, dt_hbm, a_hbm = refs[:8]
    state, decay = refs[8:10]
    x, bc, taps_x, taps_bc, dt_raw, a_log, wide, sems = refs[10:]
    width = x.shape[1]
    both = bc.shape[2]
    pairs = [(x_hbm, x), (bc_hbm, bc), (taps_x_hbm, taps_x), (taps_bc_hbm, taps_bc),
             (dt_hbm, dt_raw), (a_hbm, a_log)]

    @pl.when(active[0] == 1)
    def _():
        for copy in started(pairs, sems):
            copy.wait()

        def emit(cut, total):
            state[:, cut] = total

        def tail_bc(g):
            at = width + g * both
            return got[:, at : at + both // 2].astype(F32)[-8:]

        end = emit_states(
            head_dim, x, lambda cut: got[:, cut].astype(F32)[-8:], bc, tail_bc,
            taps_x, taps_bc, dt_raw, a_log, wide, emit,
        )
        decay[...] = spread_row(jnp.exp(end), head_dim)


def intra_kernel(
    head_dim, x, got, bc, z, taps_x, taps_bc, dt_raw, a_log, d_skip, y_part, lead, c_act, wide
):
    dt, cum = rates(dt_raw[...], a_log[...], 0)
    tokens, width = x.shape
    groups, both = bc.shape[1:]
    state_dim = both // 2
    cols = width // groups
    heads = dt.shape[0] // groups
    cum_t = cum.T
    leading = jnp.exp(cum)
    skip = spread_row(as_column(d_skip[...], 0, dt.shape[0]), head_dim)
    t_at = lax.broadcasted_iota(jnp.int32, (tokens, tokens), 0)
    s_at = lax.broadcasted_iota(jnp.int32, (tokens, tokens), 1)
    pair = 2 * head_dim
    for g in range(groups):
        at = width + g * both
        bc_act = conv_act(
            bc[...].astype(F32)[:, g], got[:, at : at + both].astype(F32)[-8:], taps_bc[...][:, g]
        )
        b, c = bc_act[:, :state_dim], bc_act[:, state_dim:]
        c_act[:, g * state_dim : (g + 1) * state_dim] = c
        inner = lax.dot_general(c, b, (((1,), (1,)), ((), ())), preferred_element_type=F32)
        inner = jnp.where(t_at >= s_at, inner, 0.0)
        wide[...] = spread(leading[g * heads : (g + 1) * heads], head_dim, 2)
        for first in range(0, heads, 2):
            here = first * head_dim
            cut = slice(g * cols + here, g * cols + here + pair)
            act = conv_act(x[:, cut].astype(F32), got[:, cut].astype(F32)[-8:], taps_x[:, cut])
            lane = lax.broadcasted_iota(jnp.int32, act.shape, 1)
            full = act.astype(F32)
            blocks = jnp.concatenate(
                [jnp.where(lane < head_dim, full, 0.0), jnp.where(lane < head_dim, 0.0, full)],
                axis=0,
            ).astype(BF16)
            weights = []
            for h in (g * heads + first, g * heads + first + 1):
                gap = jnp.minimum(cum_t[:, h : h + 1] - cum[h : h + 1, :], 0.0)
                weights.append((jnp.exp(gap) * dt[h : h + 1, :] * inner).astype(BF16))
            y = jnp.dot(jnp.concatenate(weights, axis=1), blocks, preferred_element_type=F32)
            gate = silu(z[:, cut].astype(F32))
            y_part[:, cut] = (y + skip[:, cut] * full) * gate
            lead[:, cut] = wide[:, here : here + pair] * gate


def output_kernel(spans, seen, c, y_part, lead, gain, *refs):
    arrived, out = refs[: len(spans) * seen], refs[-1]
    gated = []
    for i, (low, high, at) in enumerate(spans):
        state = arrived[i * seen][:, low:high]
        for more in arrived[i * seen + 1 : (i + 1) * seen]:
            state = state + more[:, low:high]
        from_state = jnp.dot(c[...], state, preferred_element_type=F32)
        cut = slice(at, at + high - low)
        gated.append(y_part[:, cut] + lead[:, cut] * from_state)
    gated = jnp.concatenate(gated, axis=1)
    mean_sq = jnp.mean(gated * gated, axis=1, keepdims=True)
    out[...] = (gated * lax.rsqrt(mean_sq + EPS) * gain[...]).astype(BF16)


def params(mib):
    return pltpu.CompilerParams(vmem_limit_bytes=mib * 1024 * 1024)


def chain(firsts, state, decay, cuts, devices):
    arrived = [[] for _ in cuts]
    to_send = firsts
    for hop in range(devices - 1):
        came = [lax.ppermute(v, "seq", [(hop, hop + 1)]) for v in to_send]
        for seen, v in zip(arrived, came):
            seen.append(v)
        to_send = [
            (decay[:, low:high] * v.astype(F32) + state[:, low:high]).astype(BF16)
            for (low, high), v in zip(cuts, came)
        ]
    return arrived


def doubling(state, decay, devices):
    def moved(value, distance):
        return lax.ppermute(value, "seq", [(i, i + distance) for i in range(devices - distance)])

    total, decay = moved(state.astype(BF16), 1), moved(decay, 1)
    distance = 1
    while distance < devices - 1:
        came = moved(total, distance)
        total = (decay * came.astype(F32) + total.astype(F32)).astype(BF16)
        decay = decay * moved(decay, distance)
        distance *= 2
    return total


def shards(x_in, bc_in, z_in, dt_raw, conv_x, conv_bc, a_log, d_skip, norm_gain):
    tokens, width = x_in.shape
    groups, both = bc_in.shape[1:]
    state_dim = both // 2
    heads = dt_raw.shape[1]
    head_dim = width // heads
    cols = width // groups
    devices = lax.axis_size("seq")
    place = lax.axis_index("seq")
    rows = 16

    tiles = width // LANES
    edges = [LANES * (tiles * i // SLICES) for i in range(SLICES + 1)]
    cuts = list(zip(edges[:-1], edges[1:]))
    chained = devices <= CHAIN_MOST

    dt_t = dt_raw.T
    a_row = a_log.reshape(1, heads)
    d_row = d_skip.reshape(1, heads)
    gain = norm_gain.reshape(1, width)
    is_first = (place == 0).astype(jnp.int32).reshape(1)
    operands = [x_in, bc_in, conv_x, conv_bc, dt_t, a_row]
    landed = [pltpu.VMEM(v.shape, v.dtype) for v in operands]
    scalar = pl.BlockSpec(memory_space=pltpu.SMEM)
    any_space = [pl.BlockSpec(memory_space=pl.ANY)] * len(operands)

    def column(height, wide, at):
        return pl.BlockSpec((height, wide), lambda i: (0, at))

    def whole(array):
        return pl.BlockSpec(array.shape, lambda i: (0,) * len(array.shape))

    last, *firsts = pl.pallas_call(
        functools.partial(first_kernel, head_dim, cuts),
        out_shape=[jax.ShapeDtypeStruct((rows, width + groups * both), BF16)]
        + [jax.ShapeDtypeStruct((state_dim, high - low), BF16) for low, high in cuts],
        in_specs=[scalar] + any_space,
        scratch_shapes=landed
        + [
            pltpu.VMEM((rows, width), BF16),
            pltpu.VMEM((rows, groups, both), BF16),
            pltpu.VMEM((tokens, cols), F32),
            pltpu.SemaphoreType.DMA((2 + len(operands),)),
        ],
        compiler_params=params(56),
        name="first_states",
    )(is_first, *operands)

    got = lax.ppermute(last, "seq", [(i, i + 1) for i in range(devices - 1)])
    runs = 1 - is_first if chained else jnp.ones((1,), jnp.int32)
    state, decay = pl.pallas_call(
        functools.partial(later_kernel, head_dim),
        out_shape=(
            jax.ShapeDtypeStruct((state_dim, width), F32),
            jax.ShapeDtypeStruct((1, width), F32),
        ),
        in_specs=[scalar, pl.BlockSpec(memory_space=pltpu.VMEM)] + any_space,
        scratch_shapes=landed
        + [pltpu.VMEM((tokens, cols), F32), pltpu.SemaphoreType.DMA((len(operands),))],
        compiler_params=params(56),
        name="later_states",
    )(runs, got, *operands)

    if chained:
        arrived = chain(firsts, state, decay, cuts, devices)
    else:
        total = doubling(state, decay, devices)
        arrived = [[total[:, low:high]] for low, high in cuts]

    y_part, lead, c_act = pl.pallas_call(
        functools.partial(intra_kernel, head_dim),
        out_shape=(
            jax.ShapeDtypeStruct((tokens, width), F32),
            jax.ShapeDtypeStruct((tokens, width), F32),
            jax.ShapeDtypeStruct((tokens, groups * state_dim), BF16),
        ),
        scratch_shapes=[pltpu.VMEM((tokens, cols), F32)],
        compiler_params=params(32),
        cost_estimate=pl.CostEstimate(
            flops=4 * tokens * tokens * width,
            bytes_accessed=12 * tokens * width,
            transcendentals=tokens * tokens * heads,
        ),
        name="intra",
    )(x_in, got, bc_in, z_in, conv_x, conv_bc, dt_t, a_row, d_row)

    out = None
    for g in range(groups):
        spans, taken = [], []
        for (low, high), seen in zip(cuts, arrived):
            begin, stop = max(low, g * cols), min(high, (g + 1) * cols)
            if begin < stop:
                spans.append((begin - low, stop - low, begin - g * cols))
                taken += seen
        inputs = [c_act, y_part, lead, gain] + taken
        specs = [
            column(tokens, state_dim, g),
            column(tokens, cols, g),
            column(tokens, cols, g),
            column(1, cols, g),
        ] + [whole(v) for v in taken]
        aliases = {}
        if out is not None:
            aliases = {len(inputs): 0}
            inputs.append(out)
            specs.append(pl.BlockSpec(memory_space=pl.ANY))
        out = pl.pallas_call(
            functools.partial(output_kernel, spans, len(arrived[0])),
            out_shape=jax.ShapeDtypeStruct((tokens, width), BF16),
            in_specs=specs,
            out_specs=column(tokens, cols, g),
            grid=(1,),
            input_output_aliases=aliases,
            compiler_params=params(32),
            name="outputs",
        )(*inputs)
    return out


def solution(mesh):
    return jax.shard_map(
        shards,
        mesh=mesh,
        in_specs=(
            P(("groups", "seq"), "head"),
            P(("groups", "seq"), "head", None),
            P(("groups", "seq"), "head"),
            P(("groups", "seq"), "head"),
            P(None, "head"),
            P(None, "head", None),
            P("head"),
            P("head"),
            P("head"),
        ),
        out_specs=P(("groups", "seq"), "head"),
        check_vma=False,
    )
```

```python
import functools

import jax
import jax.numpy as jnp
from jax import lax
from jax.experimental import pallas as pl
from jax.experimental.pallas import tpu as pltpu
from jax.sharding import PartitionSpec as P

EPS = 1e-05
F32 = jnp.float32
BF16 = jnp.bfloat16
CHAIN_MOST = 4
SLICES = 2
CHUNK = 256


def silu(u):
    return 0.5 * u * (1.0 + jnp.tanh(0.5 * u))


def softplus(v):
    return jnp.maximum(v, 0.0) + jnp.log1p(jnp.exp(-jnp.abs(v)))


def halves(v, count, axis):
    parts = []
    for _ in range(count - 1):
        part = v.astype(BF16)
        parts.append(part)
        v = v - part.astype(F32)
    parts.append(v.astype(BF16))
    return jnp.concatenate(parts, axis=axis)


def spread(per_head, head_dim, count):
    heads = per_head.shape[0]
    rows = lax.broadcasted_iota(jnp.int32, (heads * count, heads * head_dim), 0)
    cols = lax.broadcasted_iota(jnp.int32, (heads * count, heads * head_dim), 1)
    pick = (rows % heads == cols // head_dim).astype(F32).astype(BF16)
    return lax.dot_general(
        halves(per_head, count, 0), pick, (((0,), (0,)), ((), ())), preferred_element_type=F32
    )


def spread_row(column, head_dim):
    heads = column.shape[0]
    rows = lax.broadcasted_iota(jnp.int32, (heads, heads * head_dim), 0)
    cols = lax.broadcasted_iota(jnp.int32, (heads, heads * head_dim), 1)
    return jnp.sum(jnp.where(rows == cols // head_dim, column, 0.0), axis=0, keepdims=True)


def as_column(row, start, heads):
    every = row.shape[1]
    rows = lax.broadcasted_iota(jnp.int32, (heads, every), 0)
    cols = lax.broadcasted_iota(jnp.int32, (heads, every), 1)
    return jnp.sum(jnp.where(cols == rows + start, row, 0.0), axis=1, keepdims=True)


def conv_act(series, tail, taps):
    count = taps.shape[0]
    above = tail.shape[0]
    padded = jnp.concatenate([tail, series], axis=0)
    total = taps[count - 1 : count] * series
    for back in range(1, count):
        total = total + taps[count - 1 - back : count - back] * pltpu.roll(padded, back, 0)[above:]
    return silu(total).astype(BF16)


def rates(dt_raw, a_log_row, start):
    heads, tokens = dt_raw.shape
    dt = softplus(dt_raw)
    rate = -jnp.exp(as_column(a_log_row, start, heads)) * dt
    earlier = lax.broadcasted_iota(jnp.int32, (tokens, tokens), 0)
    later = lax.broadcasted_iota(jnp.int32, (tokens, tokens), 1)
    upto = (earlier <= later).astype(F32)
    cum = jnp.dot(rate, upto, precision=lax.Precision.HIGHEST, preferred_element_type=F32)
    return dt, cum


def started(pairs, sems):
    copies = [pltpu.make_async_copy(src, dst, sems.at[i]) for i, (src, dst) in enumerate(pairs)]
    for copy in copies:
        copy.start()
    return copies


def emit_states(
    head_dim, chunks, x, tail_x, bc, tail_bc, taps_x, taps_bc, dt_raw, a_log, wide, emit
):
    dt, cum = rates(dt_raw[...], a_log[...], 0)
    end = cum[:, -1:]
    tail_decay = jnp.exp(end - cum) * dt
    groups = bc.shape[1]
    state_dim = bc.shape[2] // 2
    heads = dt.shape[0] // groups
    cols = heads * head_dim
    for g in range(groups):
        mine = [c for c in chunks if c.start // cols == g]
        if not mine:
            continue
        b = conv_act(
            bc[:, :, :state_dim].astype(F32)[:, g],
            tail_bc(g),
            taps_bc[:, :, :state_dim][:, g],
        )
        b_t = b.astype(F32).T.astype(BF16)
        wide[...] = spread(tail_decay[g * heads : (g + 1) * heads], head_dim, 2)
        for cut in mine:
            act = conv_act(x[:, cut].astype(F32), tail_x(cut), taps_x[:, cut])
            at = cut.start - g * cols
            scaled = (wide[:, at : at + cut.stop - cut.start] * act.astype(F32)).astype(BF16)
            emit(cut, jnp.dot(b_t, scaled, preferred_element_type=F32))
    return end


def chunks_of(cuts):
    return [slice(at, at + CHUNK) for low, high in cuts for at in range(low, high, CHUNK)]


def owner_of(cut, cuts):
    at = [i for i, (low, high) in enumerate(cuts) if low <= cut.start < high][0]
    return at, slice(cut.start - cuts[at][0], cut.stop - cuts[at][0])


def first_kernel(head_dim, cuts, *refs):
    active, x_hbm, bc_hbm, taps_x_hbm, taps_bc_hbm, dt_hbm, a_hbm = refs[:7]
    outs = refs[7 : 7 + len(cuts)]
    x, bc, taps_x, taps_bc, dt_raw, a_log, wide, sems = refs[7 + len(cuts) :]
    span = pl.ds(cuts[0][0], cuts[-1][1] - cuts[0][0])

    @pl.when(active[0] == 1)
    def _():
        make_first(
            head_dim, cuts, outs,
            started(
                [(x_hbm.at[:, span], x.at[:, span]), (bc_hbm, bc), (taps_x_hbm, taps_x),
                 (taps_bc_hbm, taps_bc), (dt_hbm, dt_raw), (a_hbm, a_log)],
                sems,
            ),
            x, bc, taps_x, taps_bc, dt_raw, a_log, wide,
        )


def make_first(head_dim, cuts, outs, copies, x, bc, *more):
    for copy in copies:
        copy.wait()

    def emit(cut, total):
        at, here = owner_of(cut, cuts)
        outs[at][:, here] = total.astype(BF16)

    emit_states(
        head_dim, chunks_of(cuts), x,
        lambda cut: jnp.zeros((8, cut.stop - cut.start), F32),
        bc, lambda g: jnp.zeros((8, bc.shape[2] // 2), F32),
        *more, emit,
    )


def second_kernel(head_dim, cuts, *refs):
    active, _, x_hbm, bc_hbm, taps_x_hbm, taps_bc_hbm, dt_hbm, a_hbm = refs[:8]
    pack, outs = refs[8], refs[9 : 9 + len(cuts)]
    x, bc, taps_x, taps_bc, dt_raw, a_log, wide, last_x, last_bc, sems = refs[9 + len(cuts) :]
    tokens, width = x.shape
    rows, groups, both = last_bc.shape
    span = pl.ds(cuts[0][0], cuts[-1][1] - cuts[0][0])
    ends = started(
        [
            (x_hbm.at[pl.ds(tokens - rows, rows)], last_x),
            (bc_hbm.at[pl.ds(tokens - rows, rows)], last_bc),
        ],
        sems,
    )
    inner = [(x_hbm.at[:, span], x.at[:, span]), (bc_hbm, bc), (taps_x_hbm, taps_x),
             (taps_bc_hbm, taps_bc), (dt_hbm, dt_raw), (a_hbm, a_log)]
    rest = sems.at[pl.ds(2, len(inner))]

    @pl.when(active[0] == 1)
    def _():
        started(inner, rest)

    for copy in ends:
        copy.wait()
    pack[:, :width] = last_x[...].astype(F32)[-8:].astype(BF16)
    wide_bc = last_bc[...].astype(F32)
    for g in range(groups):
        pack[:, width + g * both : width + (g + 1) * both] = wide_bc[-8:, g].astype(BF16)

    @pl.when(active[0] == 1)
    def _():
        make_first(
            head_dim, cuts, outs,
            [pltpu.make_async_copy(src, dst, rest.at[i]) for i, (src, dst) in enumerate(inner)],
            x, bc, taps_x, taps_bc, dt_raw, a_log, wide,
        )


def later_kernel(head_dim, cuts, *refs):
    active, got, x_hbm, bc_hbm, taps_x_hbm, taps_bc_hbm, dt_hbm, a_hbm = refs[:8]
    states, decays = refs[8 : 8 + len(cuts)], refs[8 + len(cuts) : 8 + 2 * len(cuts)]
    x, bc, taps_x, taps_bc, dt_raw, a_log, wide, sems = refs[8 + 2 * len(cuts) :]
    width = x.shape[1]
    both = bc.shape[2]
    pairs = [(x_hbm, x), (bc_hbm, bc), (taps_x_hbm, taps_x), (taps_bc_hbm, taps_bc),
             (dt_hbm, dt_raw), (a_hbm, a_log)]

    @pl.when(active[0] == 1)
    def _():
        for copy in started(pairs, sems):
            copy.wait()

        def emit(cut, total):
            at, here = owner_of(cut, cuts)
            states[at][:, here] = total

        def tail_bc(g):
            at = width + g * both
            return got[:, at : at + both // 2].astype(F32)

        end = emit_states(
            head_dim, chunks_of(cuts), x, lambda cut: got[:, cut].astype(F32), bc, tail_bc,
            taps_x, taps_bc, dt_raw, a_log, wide, emit,
        )
        row = spread_row(jnp.exp(end), head_dim)
        for decay, (low, high) in zip(decays, cuts):
            decay[...] = row[:, low:high]


def intra_kernel(
    head_dim, x, got, bc, z, taps_x, taps_bc, dt_raw, a_log, d_skip, y_part, lead, c_act, wide
):
    dt, cum = rates(dt_raw[...], a_log[...], 0)
    tokens, width = x.shape
    groups, both = bc.shape[1:]
    state_dim = both // 2
    cols = width // groups
    heads = dt.shape[0] // groups
    cum_t = cum.T
    leading = jnp.exp(cum)
    skip = spread_row(as_column(d_skip[...], 0, dt.shape[0]), head_dim)
    t_at = lax.broadcasted_iota(jnp.int32, (tokens, tokens), 0)
    s_at = lax.broadcasted_iota(jnp.int32, (tokens, tokens), 1)
    pair = 2 * head_dim
    for g in range(groups):
        at = width + g * both
        bc_act = conv_act(
            bc[...].astype(F32)[:, g], got[:, at : at + both].astype(F32), taps_bc[...][:, g]
        )
        b, c = bc_act[:, :state_dim], bc_act[:, state_dim:]
        c_act[:, g * state_dim : (g + 1) * state_dim] = c
        inner = lax.dot_general(c, b, (((1,), (1,)), ((), ())), preferred_element_type=F32)
        inner = jnp.where(t_at >= s_at, inner, 0.0)
        wide[...] = spread(leading[g * heads : (g + 1) * heads], head_dim, 2)
        for first in range(0, heads, 2):
            here = first * head_dim
            cut = slice(g * cols + here, g * cols + here + pair)
            act = conv_act(x[:, cut].astype(F32), got[:, cut].astype(F32), taps_x[:, cut])
            lane = lax.broadcasted_iota(jnp.int32, act.shape, 1)
            full = act.astype(F32)
            blocks = jnp.concatenate(
                [jnp.where(lane < head_dim, full, 0.0), jnp.where(lane < head_dim, 0.0, full)],
                axis=0,
            ).astype(BF16)
            weights = []
            for h in (g * heads + first, g * heads + first + 1):
                gap = jnp.minimum(cum_t[:, h : h + 1] - cum[h : h + 1, :], 0.0)
                weights.append((jnp.exp(gap) * dt[h : h + 1, :] * inner).astype(BF16))
            y = jnp.dot(jnp.concatenate(weights, axis=1), blocks, preferred_element_type=F32)
            gate = silu(z[:, cut].astype(F32))
            y_part[:, cut] = (y + skip[:, cut] * full) * gate
            lead[:, cut] = wide[:, here : here + pair] * gate


def output_kernel(spans, seen, c, y_part, lead, gain, *refs):
    arrived, out = refs[: len(spans) * seen], refs[-1]
    gated = []
    for i, (low, high, at) in enumerate(spans):
        state = arrived[i * seen][:, low:high]
        for more in arrived[i * seen + 1 : (i + 1) * seen]:
            state = state + more[:, low:high]
        from_state = jnp.dot(c[...], state, preferred_element_type=F32)
        cut = slice(at, at + high - low)
        gated.append(y_part[:, cut] + lead[:, cut] * from_state)
    gated = jnp.concatenate(gated, axis=1)
    mean_sq = jnp.mean(gated * gated, axis=1, keepdims=True)
    out[...] = (gated * lax.rsqrt(mean_sq + EPS) * gain[...]).astype(BF16)


def params(mib):
    return pltpu.CompilerParams(vmem_limit_bytes=mib * 1024 * 1024)


def chain(firsts, states, decays, devices):
    arrived = [[] for _ in firsts]
    to_send = firsts
    for hop in range(devices - 1):
        came = [lax.ppermute(v, "seq", [(hop, hop + 1)]) for v in to_send]
        for seen, v in zip(arrived, came):
            seen.append(v)
        to_send = []
        for decay, state, v in zip(decays, states, came):
            if to_send:
                v, _ = lax.optimization_barrier((v, to_send[-1]))
            to_send.append((decay * v.astype(F32) + state).astype(BF16))
    return arrived


def doubling(state, decay, devices):
    def moved(value, distance):
        return lax.ppermute(value, "seq", [(i, i + distance) for i in range(devices - distance)])

    total, decay = moved(state.astype(BF16), 1), moved(decay, 1)
    distance = 1
    while distance < devices - 1:
        came = moved(total, distance)
        total = (decay * came.astype(F32) + total.astype(F32)).astype(BF16)
        decay = decay * moved(decay, distance)
        distance *= 2
    return total


def shards(x_in, bc_in, z_in, dt_raw, conv_x, conv_bc, a_log, d_skip, norm_gain):
    tokens, width = x_in.shape
    groups, both = bc_in.shape[1:]
    state_dim = both // 2
    heads = dt_raw.shape[1]
    head_dim = width // heads
    cols = width // groups
    devices = lax.axis_size("seq")
    place = lax.axis_index("seq")
    rim = 8
    tiles = width // CHUNK
    edges = [CHUNK * -(-tiles * i // SLICES) for i in range(SLICES + 1)]
    cuts = list(zip(edges[:-1], edges[1:]))
    chained = devices <= CHAIN_MOST

    dt_t = dt_raw.T
    a_row = a_log.reshape(1, heads)
    d_row = d_skip.reshape(1, heads)
    gain = norm_gain.reshape(1, width)
    is_first = (place == 0).astype(jnp.int32).reshape(1)
    operands = [x_in, bc_in, conv_x, conv_bc, dt_t, a_row]
    operands = [pltpu.with_memory_space_constraint(v, pltpu.HBM) for v in operands]
    scratch = [pltpu.VMEM(v.shape, v.dtype) for v in operands] + [pltpu.VMEM((tokens, cols), F32)]
    scalar = pl.BlockSpec(memory_space=pltpu.SMEM)
    in_vmem = pl.BlockSpec(memory_space=pltpu.VMEM)
    anywhere = pl.BlockSpec(memory_space=pl.ANY)
    in_hbm = [pl.BlockSpec(memory_space=pltpu.HBM)] * len(operands)

    def column(height, wide, at):
        return pl.BlockSpec((height, wide), lambda i: (0, at))

    def whole(array):
        return pl.BlockSpec(array.shape, lambda i: (0,) * len(array.shape))

    def sent(some):
        return [jax.ShapeDtypeStruct((state_dim, high - low), BF16) for low, high in some]

    (first,) = pl.pallas_call(
        functools.partial(first_kernel, head_dim, cuts[:1]),
        out_shape=sent(cuts[:1]),
        in_specs=[scalar] + in_hbm,
        scratch_shapes=scratch + [pltpu.SemaphoreType.DMA((len(operands),))],
        compiler_params=params(16),
        name="first_states",
    )(is_first, *operands)
    last, *others = pl.pallas_call(
        functools.partial(second_kernel, head_dim, cuts[1:]),
        out_shape=[jax.ShapeDtypeStruct((rim, width + groups * both), BF16)] + sent(cuts[1:]),
        in_specs=[scalar, anywhere] + in_hbm,
        scratch_shapes=scratch
        + [
            pltpu.VMEM((2 * rim, width), BF16),
            pltpu.VMEM((2 * rim, groups, both), BF16),
            pltpu.SemaphoreType.DMA((2 + len(operands),)),
        ],
        compiler_params=params(16),
        name="second_states",
    )(is_first, first, *operands)

    got = lax.ppermute(last, "seq", [(i, i + 1) for i in range(devices - 1)])
    runs = 1 - is_first if chained else jnp.ones((1,), jnp.int32)
    made = pl.pallas_call(
        functools.partial(later_kernel, head_dim, cuts),
        out_shape=[jax.ShapeDtypeStruct((state_dim, high - low), F32) for low, high in cuts]
        + [jax.ShapeDtypeStruct((1, high - low), F32) for low, high in cuts],
        in_specs=[scalar, in_vmem] + in_hbm,
        scratch_shapes=scratch + [pltpu.SemaphoreType.DMA((len(operands),))],
        compiler_params=params(16),
        name="later_states",
    )(runs, got, *operands)
    states, decays = made[: len(cuts)], made[len(cuts) :]

    if chained:
        arrived = chain([first] + others, states, decays, devices)
    else:
        arrived = [[doubling(state, decay, devices)] for state, decay in zip(states, decays)]

    y_part, lead, c_act = pl.pallas_call(
        functools.partial(intra_kernel, head_dim),
        out_shape=(
            jax.ShapeDtypeStruct((tokens, width), F32),
            jax.ShapeDtypeStruct((tokens, width), F32),
            jax.ShapeDtypeStruct((tokens, groups * state_dim), BF16),
        ),
        scratch_shapes=[pltpu.VMEM((tokens, cols), F32)],
        compiler_params=params(32),
        cost_estimate=pl.CostEstimate(
            flops=4 * tokens * tokens * width,
            bytes_accessed=12 * tokens * width,
            transcendentals=tokens * tokens * heads,
        ),
        name="intra",
    )(x_in, got, bc_in, z_in, conv_x, conv_bc, dt_t, a_row, d_row)

    out = None
    for g in range(groups):
        spans, taken = [], []
        for (low, high), seen in zip(cuts, arrived):
            begin, stop = max(low, g * cols), min(high, (g + 1) * cols)
            if begin < stop:
                spans.append((begin - low, stop - low, begin - g * cols))
                taken += seen
        inputs = [c_act, y_part, lead, gain] + taken
        specs = [
            column(tokens, state_dim, g),
            column(tokens, cols, g),
            column(tokens, cols, g),
            column(1, cols, g),
        ] + [whole(v) for v in taken]
        aliases = {}
        if out is not None:
            aliases = {len(inputs): 0}
            inputs.append(out)
            specs.append(pl.BlockSpec(memory_space=pl.ANY))
        out = pl.pallas_call(
            functools.partial(output_kernel, spans, len(arrived[0])),
            out_shape=jax.ShapeDtypeStruct((tokens, width), BF16),
            in_specs=specs,
            out_specs=column(tokens, cols, g),
            grid=(1,),
            input_output_aliases=aliases,
            compiler_params=params(32),
            name="outputs",
        )(*inputs)
    return out


def solution(mesh):
    return jax.shard_map(
        shards,
        mesh=mesh,
        in_specs=(
            P(("groups", "seq"), "head"),
            P(("groups", "seq"), "head", None),
            P(("groups", "seq"), "head"),
            P(("groups", "seq"), "head"),
            P(None, "head"),
            P(None, "head", None),
            P("head"),
            P("head"),
            P("head"),
        ),
        out_specs=P(("groups", "seq"), "head"),
        check_vma=False,
    )
```

```python
import functools

import jax
import jax.numpy as jnp
from jax import lax
from jax.experimental import pallas as pl
from jax.experimental.pallas import tpu as pltpu
from jax.sharding import PartitionSpec as P

EPS = 1e-05
F32 = jnp.float32
BF16 = jnp.bfloat16
CHAIN_MOST = 4
PER_GROUP = 2
CHUNK = 256
RIM = 8


def silu(u):
    return 0.5 * u * (1.0 + jnp.tanh(0.5 * u))


def softplus(v):
    return jnp.maximum(v, 0.0) + jnp.log1p(jnp.exp(-jnp.abs(v)))


def halves(v, count, axis):
    parts = []
    for _ in range(count - 1):
        part = v.astype(BF16)
        parts.append(part)
        v = v - part.astype(F32)
    parts.append(v.astype(BF16))
    return jnp.concatenate(parts, axis=axis)


def spread(per_head, head_dim, count):
    heads = per_head.shape[0]
    rows = lax.broadcasted_iota(jnp.int32, (heads * count, heads * head_dim), 0)
    cols = lax.broadcasted_iota(jnp.int32, (heads * count, heads * head_dim), 1)
    pick = (rows % heads == cols // head_dim).astype(F32).astype(BF16)
    return lax.dot_general(
        halves(per_head, count, 0), pick, (((0,), (0,)), ((), ())), preferred_element_type=F32
    )


def spread_row(column, head_dim):
    heads = column.shape[0]
    rows = lax.broadcasted_iota(jnp.int32, (heads, heads * head_dim), 0)
    cols = lax.broadcasted_iota(jnp.int32, (heads, heads * head_dim), 1)
    return jnp.sum(jnp.where(rows == cols // head_dim, column, 0.0), axis=0, keepdims=True)


def as_column(row, start, heads):
    every = row.shape[1]
    rows = lax.broadcasted_iota(jnp.int32, (heads, every), 0)
    cols = lax.broadcasted_iota(jnp.int32, (heads, every), 1)
    return jnp.sum(jnp.where(cols == rows + start, row, 0.0), axis=1, keepdims=True)


def conv_act(series, tail, taps):
    count = taps.shape[0]
    above = tail.shape[0]
    padded = jnp.concatenate([tail, series], axis=0)
    total = taps[count - 1 : count] * series
    for back in range(1, count):
        total = total + taps[count - 1 - back : count - back] * pltpu.roll(padded, back, 0)[above:]
    return silu(total).astype(BF16)


def rates(dt_raw, a_log_row, start):
    heads, tokens = dt_raw.shape
    dt = softplus(dt_raw)
    rate = -jnp.exp(as_column(a_log_row, start, heads)) * dt
    earlier = lax.broadcasted_iota(jnp.int32, (tokens, tokens), 0)
    later = lax.broadcasted_iota(jnp.int32, (tokens, tokens), 1)
    upto = (earlier <= later).astype(F32)
    cum = jnp.dot(rate, upto, precision=lax.Precision.HIGHEST, preferred_element_type=F32)
    return dt, cum


def emit_states(
    head_dim, group, chunks, x, tail_x, bc, tail_bc, taps_x, taps_bc, dt_raw, a_log, wide, emit
):
    dt, cum = rates(dt_raw[...], a_log[...], 0)
    end = cum[:, -1:]
    tail_decay = jnp.exp(end - cum) * dt
    state_dim = bc.shape[2] // 2
    heads = dt.shape[0] // bc.shape[1]
    mine = slice(group * heads, (group + 1) * heads)
    b = conv_act(
        bc[:, :, :state_dim].astype(F32)[:, group], tail_bc, taps_bc[:, :, :state_dim][:, group]
    )
    b_t = b.astype(F32).T.astype(BF16)
    wide[...] = spread(tail_decay[mine], head_dim, 2)
    decay = spread_row(jnp.exp(end[mine]), head_dim)
    for cut in chunks:
        act = conv_act(x[:, cut].astype(F32), tail_x(cut), taps_x[:, cut])
        at = cut.start - group * heads * head_dim
        here = slice(at, at + cut.stop - cut.start)
        scaled = (wide[:, here] * act.astype(F32)).astype(BF16)
        emit(cut, jnp.dot(b_t, scaled, preferred_element_type=F32), decay[:, here])


def chunks_of(low, high):
    return [slice(at, at + CHUNK) for at in range(low, high, CHUNK)]


def first_kernel(
    head_dim, group, low, high, active, _, x_hbm, bc_hbm, taps_x_hbm, taps_bc_hbm, dt_hbm, a_hbm,
    out, x, bc, taps_x, taps_bc, dt_raw, a_log, wide, sems,
):
    span = pl.ds(low, high - low)

    @pl.when(active[0] == 1)
    def _():
        pairs = [
            (x_hbm.at[:, span], x.at[:, span]), (bc_hbm, bc), (taps_x_hbm, taps_x),
            (taps_bc_hbm, taps_bc), (dt_hbm, dt_raw), (a_hbm, a_log),
        ]
        copies = [pltpu.make_async_copy(*pair, sems.at[i]) for i, pair in enumerate(pairs)]
        for copy in copies:
            copy.start()
        for copy in copies:
            copy.wait()
        both = bc.shape[2]
        state_dim = out.shape[0] - RIM
        tail_bc = bc[...].astype(F32)[-RIM:, group]
        if high - low > both:
            tail_bc = jnp.concatenate(
                [tail_bc, jnp.zeros((RIM, high - low - both), F32)], axis=1
            )
        rows = lax.broadcasted_iota(jnp.int32, (RIM, high - low), 0)
        tail_x = x[:, low:high].astype(F32)[-RIM:]
        keep = taps_x.shape[0] - 1
        tail = jnp.where(rows >= RIM - keep, tail_x, pltpu.roll(tail_bc, RIM - keep, 0))
        out[state_dim:, :] = tail.astype(BF16)

        def emit(cut, total, _):
            out[:state_dim, cut.start - low : cut.stop - low] = total.astype(BF16)

        emit_states(
            head_dim, group, chunks_of(low, high), x,
            lambda cut: jnp.zeros((RIM, cut.stop - cut.start), F32),
            bc, jnp.zeros((RIM, both // 2), F32), taps_x, taps_bc, dt_raw, a_log, wide, emit,
        )


def join_kernel(
    head_dim, group, low, high, active, came, x, bc, taps_x, taps_bc, dt_raw, a_log, out, wide
):
    @pl.when(active[0] == 1)
    def _():
        state_dim = out.shape[0]
        keep = taps_x.shape[0] - 1
        tail = came[...].astype(F32)[state_dim:]
        tail_bc = pltpu.roll(tail[:, : bc.shape[2]], keep, 0)[:, : bc.shape[2] // 2]

        def emit(cut, total, decay):
            here = slice(cut.start - low, cut.stop - low)
            before = came[:state_dim, here].astype(F32)
            out[:, here] = (decay * before + total).astype(BF16)

        emit_states(
            head_dim, group, chunks_of(low, high), x,
            lambda cut: tail[:, cut.start - low : cut.stop - low],
            bc, tail_bc, taps_x, taps_bc, dt_raw, a_log, wide, emit,
        )


def pack_kernel(_, x_hbm, bc_hbm, pack, last_x, last_bc, sems):
    tokens, width = x_hbm.shape
    rows, groups, both = last_bc.shape
    copies = [
        pltpu.make_async_copy(x_hbm.at[pl.ds(tokens - rows, rows)], last_x, sems.at[0]),
        pltpu.make_async_copy(bc_hbm.at[pl.ds(tokens - rows, rows)], last_bc, sems.at[1]),
    ]
    for copy in copies:
        copy.start()
    for copy in copies:
        copy.wait()
    pack[:, :width] = last_x[...].astype(F32)[-RIM:].astype(BF16)
    wide_bc = last_bc[...].astype(F32)
    for g in range(groups):
        pack[:, width + g * both : width + (g + 1) * both] = wide_bc[-RIM:, g].astype(BF16)


def later_kernel(head_dim, cuts, active, got, _, x, bc, taps_x, taps_bc, dt_raw, a_log, *refs):
    states, decays, wide = refs[: len(cuts)], refs[len(cuts) : 2 * len(cuts)], refs[-1]
    width = x.shape[1]
    both = bc.shape[2]

    @pl.when(active[0] == 1)
    def _():
        for state, row, (group, low, high) in zip(states, decays, cuts):

            def emit(cut, total, decay):
                here = slice(cut.start - low, cut.stop - low)
                state[:, here] = total
                row[:, here] = decay

            at = width + group * both
            emit_states(
                head_dim, group, chunks_of(low, high), x, lambda cut: got[:, cut].astype(F32),
                bc, got[:, at : at + both // 2].astype(F32),
                taps_x, taps_bc, dt_raw, a_log, wide, emit,
            )


def intra_kernel(
    head_dim, x, got, bc, z, taps_x, taps_bc, dt_raw, a_log, d_skip, y_part, lead, c_act, wide
):
    dt, cum = rates(dt_raw[...], a_log[...], 0)
    tokens, width = x.shape
    groups, both = bc.shape[1:]
    state_dim = both // 2
    cols = width // groups
    heads = dt.shape[0] // groups
    cum_t = cum.T
    leading = jnp.exp(cum)
    skip = spread_row(as_column(d_skip[...], 0, dt.shape[0]), head_dim)
    t_at = lax.broadcasted_iota(jnp.int32, (tokens, tokens), 0)
    s_at = lax.broadcasted_iota(jnp.int32, (tokens, tokens), 1)
    pair = 2 * head_dim
    for g in range(groups):
        at = width + g * both
        bc_act = conv_act(
            bc[...].astype(F32)[:, g], got[:, at : at + both].astype(F32), taps_bc[...][:, g]
        )
        b, c = bc_act[:, :state_dim], bc_act[:, state_dim:]
        c_act[:, g * state_dim : (g + 1) * state_dim] = c
        inner = lax.dot_general(c, b, (((1,), (1,)), ((), ())), preferred_element_type=F32)
        inner = jnp.where(t_at >= s_at, inner, 0.0)
        wide[...] = spread(leading[g * heads : (g + 1) * heads], head_dim, 2)
        for first in range(0, heads, 2):
            here = first * head_dim
            cut = slice(g * cols + here, g * cols + here + pair)
            act = conv_act(x[:, cut].astype(F32), got[:, cut].astype(F32), taps_x[:, cut])
            lane = lax.broadcasted_iota(jnp.int32, act.shape, 1)
            full = act.astype(F32)
            blocks = jnp.concatenate(
                [jnp.where(lane < head_dim, full, 0.0), jnp.where(lane < head_dim, 0.0, full)],
                axis=0,
            ).astype(BF16)
            weights = []
            for h in (g * heads + first, g * heads + first + 1):
                gap = jnp.minimum(cum_t[:, h : h + 1] - cum[h : h + 1, :], 0.0)
                weights.append((jnp.exp(gap) * dt[h : h + 1, :] * inner).astype(BF16))
            y = jnp.dot(jnp.concatenate(weights, axis=1), blocks, preferred_element_type=F32)
            gate = silu(z[:, cut].astype(F32))
            y_part[:, cut] = (y + skip[:, cut] * full) * gate
            lead[:, cut] = wide[:, here : here + pair] * gate


def gated_slice(c, y_part, lead, arrived):
    state = arrived[0][: c.shape[1]]
    for more in arrived[1:]:
        state = state + more[...]
    return y_part[...] + lead[...] * jnp.dot(c[...], state, preferred_element_type=F32)


def gated_kernel(c, y_part, lead, *refs):
    refs[-1][...] = gated_slice(c, y_part, lead, refs[:-1])


def output_kernel(ready, seen, c, y_part, lead, gain, *refs):
    gated = [v[...] for v in refs[:ready]]
    gated.append(gated_slice(c, y_part, lead, refs[ready : ready + seen]))
    gated = jnp.concatenate(gated, axis=1)
    mean_sq = jnp.mean(gated * gated, axis=1, keepdims=True)
    refs[-1][...] = (gated * lax.rsqrt(mean_sq + EPS) * gain[...]).astype(BF16)


def params(mib):
    return pltpu.CompilerParams(vmem_limit_bytes=mib * 1024 * 1024)


def doubling(state, decay, devices):
    def moved(value, distance):
        return lax.ppermute(value, "seq", [(i, i + distance) for i in range(devices - distance)])

    total, decay = moved(state.astype(BF16), 1), moved(decay, 1)
    distance = 1
    while distance < devices - 1:
        came = moved(total, distance)
        total = (decay * came.astype(F32) + total.astype(F32)).astype(BF16)
        decay = decay * moved(decay, distance)
        distance *= 2
    return total


def seen_last(arrived, cuts, group):
    return [seen for (g, _, _), seen in zip(cuts, arrived) if g == group][-1]


def shards(x_in, bc_in, z_in, dt_raw, conv_x, conv_bc, a_log, d_skip, norm_gain):
    tokens, width = x_in.shape
    groups, both = bc_in.shape[1:]
    state_dim = both // 2
    heads = dt_raw.shape[1]
    head_dim = width // heads
    cols = width // groups
    devices = lax.axis_size("seq")
    place = lax.axis_index("seq")
    step = cols // PER_GROUP
    cuts = [(at // cols, at, at + step) for at in range(0, width, step)]

    dt_t = dt_raw.T
    a_row = a_log.reshape(1, heads)
    d_row = d_skip.reshape(1, heads)
    gain = norm_gain.reshape(1, width)
    operands = [x_in, bc_in, conv_x, conv_bc, dt_t, a_row]
    pinned = [pltpu.with_memory_space_constraint(v, pltpu.HBM) for v in operands]
    wide = pltpu.VMEM((tokens, cols), F32)
    landed = [pltpu.VMEM(v.shape, v.dtype) for v in operands] + [wide]
    scalar = pl.BlockSpec(memory_space=pltpu.SMEM)
    in_vmem = pl.BlockSpec(memory_space=pltpu.VMEM)
    anywhere = pl.BlockSpec(memory_space=pl.ANY)
    in_hbm = [pl.BlockSpec(memory_space=pltpu.HBM)] * len(operands)

    def column(height, wide, at):
        return pl.BlockSpec((height, wide), lambda i: (0, at))

    def whole(array):
        return pl.BlockSpec(array.shape, lambda i: (0,) * len(array.shape))

    def here(condition):
        return condition.astype(jnp.int32).reshape(1)

    def shifted(value, route):
        return lax.ppermute(value, "seq", route)

    def first_states(token, group, low, high):
        return pl.pallas_call(
            functools.partial(first_kernel, head_dim, group, low, high),
            out_shape=jax.ShapeDtypeStruct((state_dim + RIM, high - low), BF16),
            in_specs=[scalar, anywhere] + in_hbm,
            scratch_shapes=landed + [pltpu.SemaphoreType.DMA((len(operands),))],
            compiler_params=params(16),
            name="first_states",
        )(here(place == 0), token, *pinned)

    def joined(came, group, low, high):
        return pl.pallas_call(
            functools.partial(join_kernel, head_dim, group, low, high),
            out_shape=jax.ShapeDtypeStruct((state_dim, high - low), BF16),
            in_specs=[scalar] + [in_vmem] * (1 + len(operands)),
            scratch_shapes=[wide],
            compiler_params=params(16),
            name="joined_states",
        )(here(place == 1), came, *operands)

    def packed(token):
        return pl.pallas_call(
            pack_kernel,
            out_shape=jax.ShapeDtypeStruct((RIM, width + groups * both), BF16),
            in_specs=[anywhere] + in_hbm[:2],
            scratch_shapes=[
                pltpu.VMEM((2 * RIM, width), BF16),
                pltpu.VMEM((2 * RIM, groups, both), BF16),
                pltpu.SemaphoreType.DMA((2,)),
            ],
            compiler_params=params(16),
            name="last_rows",
        )(token, *pinned[:2])

    def later_states(condition, got, token):
        made = pl.pallas_call(
            functools.partial(later_kernel, head_dim, cuts),
            out_shape=[
                jax.ShapeDtypeStruct((state_dim, high - low), F32) for _, low, high in cuts
            ]
            + [jax.ShapeDtypeStruct((1, high - low), F32) for _, low, high in cuts],
            in_specs=[scalar, in_vmem, anywhere] + [in_vmem] * len(operands),
            scratch_shapes=[wide],
            compiler_params=params(16),
            name="later_states",
        )(here(condition), got, token, *operands)
        return made[: len(cuts)], made[len(cuts) :]

    along = [(i, i + 1) for i in range(devices - 1)]
    if devices <= CHAIN_MOST:
        arrived = []
        token = a_row
        for cut in cuts:
            token = first_states(token, *cut)
            arrived.append([shifted(token, along[:1])])
        got = shifted(packed(token), along)
        if devices > 2:
            token = None
            for seen, cut in zip(arrived, cuts):
                if token is not None:
                    seen[0], _ = lax.optimization_barrier((seen[0], token))
                token = joined(seen[0], *cut)
                seen.append(shifted(token, along[1:2]))
        if devices > 3:
            states, decays = later_states(place >= 2, got, token)
        for hop in range(2, devices - 1):
            token = None
            for seen, decay, state in zip(arrived, decays, states):
                if token is not None:
                    seen[-1], _ = lax.optimization_barrier((seen[-1], token))
                token = (decay * seen[-1].astype(F32) + state).astype(BF16)
                seen.append(shifted(token, along[hop : hop + 1]))
    else:
        got = shifted(packed(a_row), along)
        states, decays = later_states(place >= 0, got, a_row)
        arrived = [[doubling(state, decay, devices)] for state, decay in zip(states, decays)]

    y_part, lead, c_act = pl.pallas_call(
        functools.partial(intra_kernel, head_dim),
        out_shape=(
            jax.ShapeDtypeStruct((tokens, width), F32),
            jax.ShapeDtypeStruct((tokens, width), F32),
            jax.ShapeDtypeStruct((tokens, groups * state_dim), BF16),
        ),
        scratch_shapes=[pltpu.VMEM((tokens, cols), F32)],
        compiler_params=params(32),
        cost_estimate=pl.CostEstimate(
            flops=4 * tokens * tokens * width,
            bytes_accessed=12 * tokens * width,
            transcendentals=tokens * tokens * heads,
        ),
        name="intra",
    )(x_in, got, bc_in, z_in, conv_x, conv_bc, dt_t, a_row, d_row)

    out = None
    for g in range(groups):
        ready = []
        for (group, low, high), seen in zip(cuts, arrived):
            if group != g:
                continue
            inputs = [c_act, y_part, lead]
            specs = [column(tokens, state_dim, g)] + [column(tokens, step, low // step)] * 2
            if high < (g + 1) * cols:
                ready.append(
                    pl.pallas_call(
                        gated_kernel,
                        out_shape=jax.ShapeDtypeStruct((tokens, step), F32),
                        in_specs=specs + [whole(v) for v in seen],
                        out_specs=column(tokens, step, 0),
                        grid=(1,),
                        compiler_params=params(16),
                        name="gated",
                    )(*inputs, *seen)
                )
        inputs += [gain] + ready + seen_last(arrived, cuts, g)
        specs += [column(1, cols, g)] + [whole(v) for v in ready + seen_last(arrived, cuts, g)]
        aliases = {}
        if out is not None:
            aliases = {len(inputs): 0}
            inputs.append(out)
            specs.append(pl.BlockSpec(memory_space=pl.ANY))
        out = pl.pallas_call(
            functools.partial(output_kernel, len(ready), len(arrived[0])),
            out_shape=jax.ShapeDtypeStruct((tokens, width), BF16),
            in_specs=specs,
            out_specs=column(tokens, cols, g),
            grid=(1,),
            input_output_aliases=aliases,
            compiler_params=params(32),
            name="outputs",
        )(*inputs)
    return out


def solution(mesh):
    return jax.shard_map(
        shards,
        mesh=mesh,
        in_specs=(
            P(("groups", "seq"), "head"),
            P(("groups", "seq"), "head", None),
            P(("groups", "seq"), "head"),
            P(("groups", "seq"), "head"),
            P(None, "head"),
            P(None, "head", None),
            P("head"),
            P("head"),
            P("head"),
        ),
        out_specs=P(("groups", "seq"), "head"),
        check_vma=False,
    )
```

```python
import functools

import jax
import jax.numpy as jnp
from jax import lax
from jax.experimental import pallas as pl
from jax.experimental.pallas import tpu as pltpu
from jax.sharding import PartitionSpec as P

EPS = 1e-05
F32 = jnp.float32
BF16 = jnp.bfloat16
CHAIN_MOST = 4
PER_GROUP = 2
CHUNK = 256
RIM = 8


def silu(u):
    return 0.5 * u * (1.0 + jnp.tanh(0.5 * u))


def softplus(v):
    return jnp.maximum(v, 0.0) + jnp.log1p(jnp.exp(-jnp.abs(v)))


def halves(v, count, axis):
    parts = []
    for _ in range(count - 1):
        part = v.astype(BF16)
        parts.append(part)
        v = v - part.astype(F32)
    parts.append(v.astype(BF16))
    return jnp.concatenate(parts, axis=axis)


def spread(per_head, head_dim, count):
    heads = per_head.shape[0]
    rows = lax.broadcasted_iota(jnp.int32, (heads * count, heads * head_dim), 0)
    cols = lax.broadcasted_iota(jnp.int32, (heads * count, heads * head_dim), 1)
    pick = (rows % heads == cols // head_dim).astype(F32).astype(BF16)
    return lax.dot_general(
        halves(per_head, count, 0), pick, (((0,), (0,)), ((), ())), preferred_element_type=F32
    )


def spread_row(column, head_dim):
    heads = column.shape[0]
    rows = lax.broadcasted_iota(jnp.int32, (heads, heads * head_dim), 0)
    cols = lax.broadcasted_iota(jnp.int32, (heads, heads * head_dim), 1)
    return jnp.sum(jnp.where(rows == cols // head_dim, column, 0.0), axis=0, keepdims=True)


def as_column(row, start, heads):
    every = row.shape[1]
    rows = lax.broadcasted_iota(jnp.int32, (heads, every), 0)
    cols = lax.broadcasted_iota(jnp.int32, (heads, every), 1)
    return jnp.sum(jnp.where(cols == rows + start, row, 0.0), axis=1, keepdims=True)


def conv_act(series, tail, taps):
    count = taps.shape[0]
    above = tail.shape[0]
    padded = jnp.concatenate([tail, series], axis=0)
    total = taps[count - 1 : count] * series
    for back in range(1, count):
        total = total + taps[count - 1 - back : count - back] * pltpu.roll(padded, back, 0)[above:]
    return silu(total).astype(BF16)


def rates(dt_raw, a_log_row, start):
    heads, tokens = dt_raw.shape
    dt = softplus(dt_raw)
    rate = -jnp.exp(as_column(a_log_row, start, heads)) * dt
    earlier = lax.broadcasted_iota(jnp.int32, (tokens, tokens), 0)
    later = lax.broadcasted_iota(jnp.int32, (tokens, tokens), 1)
    upto = (earlier <= later).astype(F32)
    cum = jnp.dot(rate, upto, precision=lax.Precision.HIGHEST, preferred_element_type=F32)
    return dt, cum


def emit_states(
    head_dim, group, chunks, x, tail_x, bc, tail_bc, taps_x, taps_bc, dt_raw, a_log, wide, emit
):
    dt, cum = rates(dt_raw[...], a_log[...], 0)
    end = cum[:, -1:]
    tail_decay = jnp.exp(end - cum) * dt
    state_dim = bc.shape[2] // 2
    heads = dt.shape[0] // bc.shape[1]
    mine = slice(group * heads, (group + 1) * heads)
    b = conv_act(
        bc[:, :, :state_dim].astype(F32)[:, group], tail_bc, taps_bc[:, :, :state_dim][:, group]
    )
    b_t = b.astype(F32).T.astype(BF16)
    wide[...] = spread(tail_decay[mine], head_dim, 2)
    decay = spread_row(jnp.exp(end[mine]), head_dim)
    for cut in chunks:
        act = conv_act(x[:, cut].astype(F32), tail_x(cut), taps_x[:, cut])
        at = cut.start - group * heads * head_dim
        here = slice(at, at + cut.stop - cut.start)
        scaled = (wide[:, here] * act.astype(F32)).astype(BF16)
        emit(cut, jnp.dot(b_t, scaled, preferred_element_type=F32), decay[:, here])


def chunks_of(low, high):
    return [slice(at, at + CHUNK) for at in range(low, high, CHUNK)]


def head_rows(x, bc, group, low, high, out, taps_x, taps_bc, dt_raw, a_log, wide):
    head_dim = x.shape[1] // dt_raw.shape[0]
    state_dim = bc.shape[2] // 2

    def emit(cut, total, _):
        out[:state_dim, cut.start - low : cut.stop - low] = total.astype(BF16)

    emit_states(
        head_dim, group, chunks_of(low, high), x,
        lambda cut: jnp.zeros((RIM, cut.stop - cut.start), F32),
        bc, jnp.zeros((RIM, state_dim), F32), taps_x, taps_bc, dt_raw, a_log, wide, emit,
    )


def first_kernel(
    group, low, high, active, x_hbm, bc_hbm, taps_x_hbm, taps_bc_hbm, dt_hbm, a_hbm,
    out, x, bc, taps_x, taps_bc, dt_raw, a_log, wide, sems,
):
    tokens, width = x.shape
    groups, both = bc.shape[1:]

    @pl.when(active[0] == 1)
    def _():
        pairs = [
            (x_hbm, x), (bc_hbm, bc), (taps_x_hbm, taps_x),
            (taps_bc_hbm, taps_bc), (dt_hbm, dt_raw), (a_hbm, a_log),
        ]
        copies = [pltpu.make_async_copy(*pair, sems.at[i]) for i, pair in enumerate(pairs)]
        for copy in copies:
            copy.start()
        for copy in copies:
            copy.wait()
        state_dim, step = both // 2, high - low
        keep = taps_x.shape[0] - 1
        extra = out.shape[0] - state_dim
        last_bc = bc[tokens - 2 * RIM :].astype(F32)[-RIM:]
        last = [x[tokens - 2 * RIM :, :].astype(F32)[-RIM:]] + [last_bc[:, g] for g in range(groups)]
        last = jnp.concatenate(last, axis=1)
        at = lax.broadcasted_iota(jnp.int32, (extra, step), 0)
        below = jnp.zeros((extra, step), F32)
        fill = jnp.zeros((extra - RIM, step), F32)
        for k in range(last.shape[1] // step):
            block = jnp.concatenate([last[:, k * step : (k + 1) * step], fill], axis=0)
            block = pltpu.roll(block, (keep * (k + 1) - RIM) % extra, 0)
            below = jnp.where((at >= keep * k) & (at < keep * (k + 1)), block, below)
        out[state_dim:, :] = below.astype(BF16)
        head_rows(x, bc, group, low, high, out, taps_x, taps_bc, dt_raw, a_log, wide)


def next_kernel(
    group, low, high, active, _, x, bc, taps_x, taps_bc, dt_raw, a_log, out, wide
):
    @pl.when(active[0] == 1)
    def _():
        head_rows(x, bc, group, low, high, out, taps_x, taps_bc, dt_raw, a_log, wide)


def pack_kernel(_, x, bc, pack):
    tokens, width = x.shape
    groups, both = bc.shape[1:]
    pack[:, :width] = x[tokens - 2 * RIM :, :].astype(F32)[-RIM:].astype(BF16)
    last_bc = bc[tokens - 2 * RIM :].astype(F32)[-RIM:]
    for g in range(groups):
        pack[:, width + g * both : width + (g + 1) * both] = last_bc[:, g].astype(BF16)


def later_kernel(
    group, low, high, active, rows, _, x, bc, taps_x, taps_bc, dt_raw, a_log, state, decay, wide
):
    width = x.shape[1]
    both = bc.shape[2]
    state_dim = both // 2
    keep = taps_x.shape[0] - 1
    head_dim = width // dt_raw.shape[0]

    def tail(begin, stop):
        if rows.shape[0] == RIM:
            return rows[:, begin:stop].astype(F32)
        step = rows.shape[1]
        below = rows[state_dim:, begin % step : begin % step + stop - begin].astype(F32)
        extra = below.shape[0]
        return pltpu.roll(below, (RIM - keep * (begin // step + 1)) % extra, 0)[:RIM]

    @pl.when(active[0] == 1)
    def _():
        def emit(cut, total, along):
            here = slice(cut.start - low, cut.stop - low)
            state[:, here] = total
            decay[:, here] = along

        at = width + group * both
        emit_states(
            head_dim, group, chunks_of(low, high), x, lambda cut: tail(cut.start, cut.stop),
            bc, tail(at, at + state_dim), taps_x, taps_bc, dt_raw, a_log, wide, emit,
        )


def intra_kernel(
    head_dim, x, got, bc, z, taps_x, taps_bc, dt_raw, a_log, d_skip, y_part, lead, c_act, wide
):
    dt, cum = rates(dt_raw[...], a_log[...], 0)
    tokens, width = x.shape
    groups, both = bc.shape[1:]
    state_dim = both // 2
    cols = width // groups
    heads = dt.shape[0] // groups
    cum_t = cum.T
    leading = jnp.exp(cum)
    skip = spread_row(as_column(d_skip[...], 0, dt.shape[0]), head_dim)
    t_at = lax.broadcasted_iota(jnp.int32, (tokens, tokens), 0)
    s_at = lax.broadcasted_iota(jnp.int32, (tokens, tokens), 1)
    pair = 2 * head_dim
    for g in range(groups):
        at = width + g * both
        bc_act = conv_act(
            bc[...].astype(F32)[:, g], got[:, at : at + both].astype(F32), taps_bc[...][:, g]
        )
        b, c = bc_act[:, :state_dim], bc_act[:, state_dim:]
        c_act[:, g * state_dim : (g + 1) * state_dim] = c
        inner = lax.dot_general(c, b, (((1,), (1,)), ((), ())), preferred_element_type=F32)
        inner = jnp.where(t_at >= s_at, inner, 0.0)
        wide[...] = spread(leading[g * heads : (g + 1) * heads], head_dim, 2)
        for first in range(0, heads, 2):
            here = first * head_dim
            cut = slice(g * cols + here, g * cols + here + pair)
            act = conv_act(x[:, cut].astype(F32), got[:, cut].astype(F32), taps_x[:, cut])
            lane = lax.broadcasted_iota(jnp.int32, act.shape, 1)
            full = act.astype(F32)
            blocks = jnp.concatenate(
                [jnp.where(lane < head_dim, full, 0.0), jnp.where(lane < head_dim, 0.0, full)],
                axis=0,
            ).astype(BF16)
            weights = []
            for h in (g * heads + first, g * heads + first + 1):
                gap = jnp.minimum(cum_t[:, h : h + 1] - cum[h : h + 1, :], 0.0)
                weights.append((jnp.exp(gap) * dt[h : h + 1, :] * inner).astype(BF16))
            y = jnp.dot(jnp.concatenate(weights, axis=1), blocks, preferred_element_type=F32)
            gate = silu(z[:, cut].astype(F32))
            y_part[:, cut] = (y + skip[:, cut] * full) * gate
            lead[:, cut] = wide[:, here : here + pair] * gate


def gated_slice(c, y_part, lead, arrived):
    state = arrived[0][: c.shape[1]]
    for more in arrived[1:]:
        state = state + more[...]
    return y_part[...] + lead[...] * jnp.dot(c[...], state, preferred_element_type=F32)


def gated_kernel(c, y_part, lead, *refs):
    refs[-1][...] = gated_slice(c, y_part, lead, refs[:-1])


def output_kernel(ready, seen, c, y_part, lead, gain, *refs):
    gated = [v[...] for v in refs[:ready]]
    gated.append(gated_slice(c, y_part, lead, refs[ready : ready + seen]))
    gated = jnp.concatenate(gated, axis=1)
    mean_sq = jnp.mean(gated * gated, axis=1, keepdims=True)
    refs[-1][...] = (gated * lax.rsqrt(mean_sq + EPS) * gain[...]).astype(BF16)


def params(mib):
    return pltpu.CompilerParams(vmem_limit_bytes=mib * 1024 * 1024)


def doubling(state, decay, devices):
    def moved(value, distance):
        return lax.ppermute(value, "seq", [(i, i + distance) for i in range(devices - distance)])

    total, decay = moved(state.astype(BF16), 1), moved(decay, 1)
    distance = 1
    while distance < devices - 1:
        came = moved(total, distance)
        total = (decay * came.astype(F32) + total.astype(F32)).astype(BF16)
        decay = decay * moved(decay, distance)
        distance *= 2
    return total


def seen_last(arrived, cuts, group):
    return [seen for (g, _, _), seen in zip(cuts, arrived) if g == group][-1]


def shards(x_in, bc_in, z_in, dt_raw, conv_x, conv_bc, a_log, d_skip, norm_gain):
    tokens, width = x_in.shape
    groups, both = bc_in.shape[1:]
    state_dim = both // 2
    heads = dt_raw.shape[1]
    head_dim = width // heads
    cols = width // groups
    devices = lax.axis_size("seq")
    place = lax.axis_index("seq")
    step = cols // PER_GROUP
    cuts = [(at // cols, at, at + step) for at in range(0, width, step)]

    taps = conv_x.shape[0]
    dt_t = dt_raw.T
    a_row = a_log.reshape(1, heads)
    d_row = d_skip.reshape(1, heads)
    gain = norm_gain.reshape(1, width)
    operands = [x_in, bc_in, conv_x, conv_bc, dt_t, a_row]
    pinned = [pltpu.with_memory_space_constraint(v, pltpu.HBM) for v in operands]
    wide = pltpu.VMEM((tokens, cols), F32)
    landed = [pltpu.VMEM(v.shape, v.dtype) for v in operands] + [wide]
    scalar = pl.BlockSpec(memory_space=pltpu.SMEM)
    in_vmem = pl.BlockSpec(memory_space=pltpu.VMEM)
    anywhere = pl.BlockSpec(memory_space=pl.ANY)
    in_hbm = [pl.BlockSpec(memory_space=pltpu.HBM)] * len(operands)

    def column(height, wide, at):
        return pl.BlockSpec((height, wide), lambda i: (0, at))

    def whole(array):
        return pl.BlockSpec(array.shape, lambda i: (0,) * len(array.shape))

    def here(condition):
        return condition.astype(jnp.int32).reshape(1)

    def shifted(value, route):
        return lax.ppermute(value, "seq", route)

    def first_states(group, low, high):
        blocks = (width + groups * both) // step
        extra = -(-(taps - 1) * blocks // (2 * RIM)) * 2 * RIM
        return pl.pallas_call(
            functools.partial(first_kernel, group, low, high),
            out_shape=jax.ShapeDtypeStruct((state_dim + extra, high - low), BF16),
            in_specs=[scalar] + in_hbm,
            scratch_shapes=landed + [pltpu.SemaphoreType.DMA((len(operands),))],
            compiler_params=params(16),
            name="first_states",
        )(here(place == 0), *pinned)

    def next_states(token, group, low, high):
        return pl.pallas_call(
            functools.partial(next_kernel, group, low, high),
            out_shape=jax.ShapeDtypeStruct((state_dim, high - low), BF16),
            in_specs=[scalar, anywhere] + [in_vmem] * len(operands),
            scratch_shapes=[wide],
            compiler_params=params(16),
            name="next_states",
        )(here(place == 0), token, *operands)

    def packed(token):
        return pl.pallas_call(
            pack_kernel,
            out_shape=jax.ShapeDtypeStruct((RIM, width + groups * both), BF16),
            in_specs=[anywhere] + [in_vmem] * 2,
            compiler_params=params(16),
            name="last_rows",
        )(token, x_in, bc_in)

    def later_states(condition, rows, token, group, low, high):
        return pl.pallas_call(
            functools.partial(later_kernel, group, low, high),
            out_shape=[
                jax.ShapeDtypeStruct((state_dim, high - low), F32),
                jax.ShapeDtypeStruct((1, high - low), F32),
            ],
            in_specs=[scalar, in_vmem, anywhere] + [in_vmem] * len(operands),
            scratch_shapes=[wide],
            compiler_params=params(16),
            name="later_states",
        )(here(condition), rows, token, *operands)

    along = [(i, i + 1) for i in range(devices - 1)]
    if devices <= CHAIN_MOST:
        sent = [first_states(*cuts[0])]
        for cut in cuts[1:]:
            sent.append(next_states(sent[-1], *cut))
        arrived = [[shifted(v, along[:1])] for v in sent]
        last = packed(sent[-1])
        got = shifted(last, along)
        rows, token = arrived[0][0], last
        for hop in range(1, devices - 1):
            condition = place == 1 if hop == 1 else place >= 2
            for seen, cut in zip(arrived, cuts):
                if hop <= 2:
                    made = later_states(condition, rows, token, *cut)
                    states = [made] if seen is arrived[0] else states + [made]
                before, _ = lax.optimization_barrier((seen[-1], token))
                state, decay = states[len(states) - 1 if hop <= 2 else cuts.index(cut)]
                token = (decay * before[:state_dim].astype(F32) + state).astype(BF16)
                seen.append(shifted(token, along[hop : hop + 1]))
            rows = got
    else:
        got = shifted(packed(a_row), along)
        arrived = [
            [doubling(*later_states(place >= 0, got, a_row, *cut), devices)] for cut in cuts
        ]

    y_part, lead, c_act = pl.pallas_call(
        functools.partial(intra_kernel, head_dim),
        out_shape=(
            jax.ShapeDtypeStruct((tokens, width), F32),
            jax.ShapeDtypeStruct((tokens, width), F32),
            jax.ShapeDtypeStruct((tokens, groups * state_dim), BF16),
        ),
        scratch_shapes=[pltpu.VMEM((tokens, cols), F32)],
        compiler_params=params(32),
        cost_estimate=pl.CostEstimate(
            flops=4 * tokens * tokens * width,
            bytes_accessed=12 * tokens * width,
            transcendentals=tokens * tokens * heads,
        ),
        name="intra",
    )(x_in, got, bc_in, z_in, conv_x, conv_bc, dt_t, a_row, d_row)

    out = None
    for g in range(groups):
        ready = []
        for (group, low, high), seen in zip(cuts, arrived):
            if group != g:
                continue
            inputs = [c_act, y_part, lead]
            specs = [column(tokens, state_dim, g)] + [column(tokens, step, low // step)] * 2
            if high < (g + 1) * cols:
                ready.append(
                    pl.pallas_call(
                        gated_kernel,
                        out_shape=jax.ShapeDtypeStruct((tokens, step), F32),
                        in_specs=specs + [whole(v) for v in seen],
                        out_specs=column(tokens, step, 0),
                        grid=(1,),
                        compiler_params=params(16),
                        name="gated",
                    )(*inputs, *seen)
                )
        inputs += [gain] + ready + seen_last(arrived, cuts, g)
        specs += [column(1, cols, g)] + [whole(v) for v in ready + seen_last(arrived, cuts, g)]
        aliases = {}
        if out is not None:
            aliases = {len(inputs): 0}
            inputs.append(out)
            specs.append(pl.BlockSpec(memory_space=pl.ANY))
        out = pl.pallas_call(
            functools.partial(output_kernel, len(ready), len(arrived[0])),
            out_shape=jax.ShapeDtypeStruct((tokens, width), BF16),
            in_specs=specs,
            out_specs=column(tokens, cols, g),
            grid=(1,),
            input_output_aliases=aliases,
            compiler_params=params(32),
            name="outputs",
        )(*inputs)
    return out


def solution(mesh):
    return jax.shard_map(
        shards,
        mesh=mesh,
        in_specs=(
            P(("groups", "seq"), "head"),
            P(("groups", "seq"), "head", None),
            P(("groups", "seq"), "head"),
            P(("groups", "seq"), "head"),
            P(None, "head"),
            P(None, "head", None),
            P("head"),
            P("head"),
            P("head"),
        ),
        out_specs=P(("groups", "seq"), "head"),
        check_vma=False,
    )
```

```python
import functools

import jax
import jax.numpy as jnp
from jax import lax
from jax.experimental import pallas as pl
from jax.experimental.pallas import tpu as pltpu
from jax.sharding import PartitionSpec as P

EPS = 1e-05
F32 = jnp.float32
BF16 = jnp.bfloat16
CHAIN_MOST = 4
FIRST_PARTS = (3, 5)
OTHER_PARTS = (1, 1)
CHUNK = 128
RIM = 8


def silu(u):
    return 0.5 * u * (1.0 + jnp.tanh(0.5 * u))


def softplus(v):
    return jnp.maximum(v, 0.0) + jnp.log1p(jnp.exp(-jnp.abs(v)))


def halves(v, count, axis):
    parts = []
    for _ in range(count - 1):
        part = v.astype(BF16)
        parts.append(part)
        v = v - part.astype(F32)
    parts.append(v.astype(BF16))
    return jnp.concatenate(parts, axis=axis)


def spread(per_head, head_dim, count):
    heads = per_head.shape[0]
    rows = lax.broadcasted_iota(jnp.int32, (heads * count, heads * head_dim), 0)
    cols = lax.broadcasted_iota(jnp.int32, (heads * count, heads * head_dim), 1)
    pick = (rows % heads == cols // head_dim).astype(F32).astype(BF16)
    return lax.dot_general(
        halves(per_head, count, 0), pick, (((0,), (0,)), ((), ())), preferred_element_type=F32
    )


def spread_row(column, head_dim):
    heads = column.shape[0]
    rows = lax.broadcasted_iota(jnp.int32, (heads, heads * head_dim), 0)
    cols = lax.broadcasted_iota(jnp.int32, (heads, heads * head_dim), 1)
    return jnp.sum(jnp.where(rows == cols // head_dim, column, 0.0), axis=0, keepdims=True)


def as_column(row, start, heads):
    every = row.shape[1]
    rows = lax.broadcasted_iota(jnp.int32, (heads, every), 0)
    cols = lax.broadcasted_iota(jnp.int32, (heads, every), 1)
    return jnp.sum(jnp.where(cols == rows + start, row, 0.0), axis=1, keepdims=True)


def conv_act(series, tail, taps):
    count = taps.shape[0]
    above = tail.shape[0]
    padded = jnp.concatenate([tail, series], axis=0)
    total = taps[count - 1 : count] * series
    for back in range(1, count):
        total = total + taps[count - 1 - back : count - back] * pltpu.roll(padded, back, 0)[above:]
    return silu(total).astype(BF16)


def rates(dt_raw, a_log_row, start):
    heads, tokens = dt_raw.shape
    dt = softplus(dt_raw)
    rate = -jnp.exp(as_column(a_log_row, start, heads)) * dt
    earlier = lax.broadcasted_iota(jnp.int32, (tokens, tokens), 0)
    later = lax.broadcasted_iota(jnp.int32, (tokens, tokens), 1)
    upto = (earlier <= later).astype(F32)
    cum = jnp.dot(rate, upto, precision=lax.Precision.HIGHEST, preferred_element_type=F32)
    return dt, cum


def scales(head_dim, dt_raw, a_log, scale):
    dt, cum = rates(dt_raw[...], a_log[...], 0)
    end = cum[:, -1:]
    scale[...] = spread(jnp.exp(end - cum) * dt, head_dim, 2)
    return spread_row(jnp.exp(end), head_dim)


def emit_states(group, low, high, x, tail_x, bc, tail_bc, taps_x, taps_bc, scale, emit):
    state_dim = bc.shape[2] // 2
    b = conv_act(
        bc[:, :, :state_dim].astype(F32)[:, group], tail_bc, taps_bc[:, :, :state_dim][:, group]
    )
    b_t = b.astype(F32).T.astype(BF16)
    for at in range(low, high, CHUNK):
        cut = slice(at, at + CHUNK)
        act = conv_act(x[:, cut].astype(F32), tail_x(cut), taps_x[:, cut])
        scaled = (scale[:, cut] * act.astype(F32)).astype(BF16)
        emit(slice(at - low, at - low + CHUNK), jnp.dot(b_t, scaled, preferred_element_type=F32))


def head_rows(group, low, high, x, bc, taps_x, taps_bc, scale, out):
    state_dim = bc.shape[2] // 2

    def emit(here, total):
        out[:state_dim, here] = total.astype(BF16)

    emit_states(
        group, low, high, x, lambda cut: jnp.zeros((RIM, CHUNK), F32),
        bc, jnp.zeros((RIM, state_dim), F32), taps_x, taps_bc, scale, emit,
    )


def first_kernel(
    group, low, high, active, x_hbm, bc_hbm, taps_x_hbm, taps_bc_hbm, dt_hbm, a_hbm,
    out, scale, x, bc, taps_x, taps_bc, dt_raw, a_log, sems,
):
    tokens, width = x.shape
    groups, both = bc.shape[1:]

    @pl.when(active[0] == 1)
    def _():
        pairs = [
            (dt_hbm, dt_raw), (a_hbm, a_log), (x_hbm, x), (bc_hbm, bc),
            (taps_x_hbm, taps_x), (taps_bc_hbm, taps_bc),
        ]
        copies = [pltpu.make_async_copy(*pair, sems.at[i]) for i, pair in enumerate(pairs)]
        for copy in copies:
            copy.start()
        for copy in copies[:2]:
            copy.wait()
        scales(width // dt_raw.shape[0], dt_raw, a_log, scale)
        for copy in copies[2:]:
            copy.wait()
        state_dim, step = both // 2, high - low
        keep = taps_x.shape[0] - 1
        extra = out.shape[0] - state_dim
        last_bc = bc[tokens - 2 * RIM :].astype(F32)[-RIM:]
        last = [x[tokens - 2 * RIM :, :].astype(F32)[-RIM:]] + [last_bc[:, g] for g in range(groups)]
        length = width + groups * both
        last.append(jnp.zeros((RIM, -length % step + step), F32))
        last = jnp.concatenate(last, axis=1)
        at = lax.broadcasted_iota(jnp.int32, (extra, step), 0)
        below = jnp.zeros((extra, step), F32)
        fill = jnp.zeros((extra - RIM, step), F32)
        for k in range(-(-length // step)):
            block = jnp.concatenate([last[:, k * step : (k + 1) * step], fill], axis=0)
            block = pltpu.roll(block, (keep * (k + 1) - RIM) % extra, 0)
            below = jnp.where((at >= keep * k) & (at < keep * (k + 1)), block, below)
        out[state_dim:, :] = below.astype(BF16)
        head_rows(group, low, high, x, bc, taps_x, taps_bc, scale, out)


def next_kernel(group, low, high, active, _, x, bc, taps_x, taps_bc, scale, out):
    @pl.when(active[0] == 1)
    def _():
        head_rows(group, low, high, x, bc, taps_x, taps_bc, scale, out)


def prepare_kernel(cuts, _, x, bc, dt_raw, a_log, pack, scale, *decays):
    tokens, width = x.shape
    groups, both = bc.shape[1:]
    pack[:, :width] = x[tokens - 2 * RIM :, :].astype(F32)[-RIM:].astype(BF16)
    last_bc = bc[tokens - 2 * RIM :].astype(F32)[-RIM:]
    for g in range(groups):
        pack[:, width + g * both : width + (g + 1) * both] = last_bc[:, g].astype(BF16)
    row = scales(width // dt_raw.shape[0], dt_raw, a_log, scale)
    for decay, (_, low, high) in zip(decays, cuts):
        decay[...] = row[:, low:high]


def later_kernel(group, low, high, active, rows, _, x, bc, taps_x, taps_bc, scale, state):
    width = x.shape[1]
    both = bc.shape[2]
    state_dim = both // 2
    keep = taps_x.shape[0] - 1

    def tail(begin, stop):
        if rows.shape[0] == RIM:
            return rows[:, begin:stop].astype(F32)
        step = rows.shape[1]
        below = rows[state_dim:, begin % step : begin % step + stop - begin].astype(F32)
        extra = below.shape[0]
        return pltpu.roll(below, (RIM - keep * (begin // step + 1)) % extra, 0)[:RIM]

    @pl.when(active[0] == 1)
    def _():
        def emit(here, total):
            state[:, here] = total

        at = width + group * both
        emit_states(
            group, low, high, x, lambda cut: tail(cut.start, cut.stop),
            bc, tail(at, at + state_dim), taps_x, taps_bc, scale, emit,
        )


def intra_kernel(
    head_dim, x, got, bc, z, taps_x, taps_bc, dt_raw, a_log, d_skip, y_part, lead, c_act, wide
):
    dt, cum = rates(dt_raw[...], a_log[...], 0)
    tokens, width = x.shape
    groups, both = bc.shape[1:]
    state_dim = both // 2
    cols = width // groups
    heads = dt.shape[0] // groups
    cum_t = cum.T
    leading = jnp.exp(cum)
    skip = spread_row(as_column(d_skip[...], 0, dt.shape[0]), head_dim)
    t_at = lax.broadcasted_iota(jnp.int32, (tokens, tokens), 0)
    s_at = lax.broadcasted_iota(jnp.int32, (tokens, tokens), 1)
    pair = 2 * head_dim
    for g in range(groups):
        at = width + g * both
        bc_act = conv_act(
            bc[...].astype(F32)[:, g], got[:, at : at + both].astype(F32), taps_bc[...][:, g]
        )
        b, c = bc_act[:, :state_dim], bc_act[:, state_dim:]
        c_act[:, g * state_dim : (g + 1) * state_dim] = c
        inner = lax.dot_general(c, b, (((1,), (1,)), ((), ())), preferred_element_type=F32)
        inner = jnp.where(t_at >= s_at, inner, 0.0)
        wide[...] = spread(leading[g * heads : (g + 1) * heads], head_dim, 2)
        for first in range(0, heads, 2):
            here = first * head_dim
            cut = slice(g * cols + here, g * cols + here + pair)
            act = conv_act(x[:, cut].astype(F32), got[:, cut].astype(F32), taps_x[:, cut])
            lane = lax.broadcasted_iota(jnp.int32, act.shape, 1)
            full = act.astype(F32)
            blocks = jnp.concatenate(
                [jnp.where(lane < head_dim, full, 0.0), jnp.where(lane < head_dim, 0.0, full)],
                axis=0,
            ).astype(BF16)
            weights = []
            for h in (g * heads + first, g * heads + first + 1):
                gap = jnp.minimum(cum_t[:, h : h + 1] - cum[h : h + 1, :], 0.0)
                weights.append((jnp.exp(gap) * dt[h : h + 1, :] * inner).astype(BF16))
            y = jnp.dot(jnp.concatenate(weights, axis=1), blocks, preferred_element_type=F32)
            gate = silu(z[:, cut].astype(F32))
            y_part[:, cut] = (y + skip[:, cut] * full) * gate
            lead[:, cut] = wide[:, here : here + pair] * gate


def gated_slice(c, y_part, lead, arrived):
    state = arrived[0][: c.shape[1]]
    for more in arrived[1:]:
        state = state + more[...]
    return y_part[...] + lead[...] * jnp.dot(c[...], state, preferred_element_type=F32)


def gated_kernel(c, y_part, lead, *refs):
    refs[-1][...] = gated_slice(c, y_part, lead, refs[:-1])


def output_kernel(ready, seen, c, y_part, lead, gain, *refs):
    gated = [v[...] for v in refs[:ready]]
    gated.append(gated_slice(c, y_part, lead, refs[ready : ready + seen]))
    gated = jnp.concatenate(gated, axis=1)
    mean_sq = jnp.mean(gated * gated, axis=1, keepdims=True)
    refs[-1][...] = (gated * lax.rsqrt(mean_sq + EPS) * gain[...]).astype(BF16)


def params(mib):
    return pltpu.CompilerParams(vmem_limit_bytes=mib * 1024 * 1024)


def doubling(state, decay, devices):
    def moved(value, distance):
        return lax.ppermute(value, "seq", [(i, i + distance) for i in range(devices - distance)])

    total, decay = moved(state.astype(BF16), 1), moved(decay, 1)
    distance = 1
    while distance < devices - 1:
        came = moved(total, distance)
        total = (decay * came.astype(F32) + total.astype(F32)).astype(BF16)
        decay = decay * moved(decay, distance)
        distance *= 2
    return total


def seen_last(arrived, cuts, group):
    return [seen for (g, _, _), seen in zip(cuts, arrived) if g == group][-1]


def shards(x_in, bc_in, z_in, dt_raw, conv_x, conv_bc, a_log, d_skip, norm_gain):
    tokens, width = x_in.shape
    groups, both = bc_in.shape[1:]
    state_dim = both // 2
    heads = dt_raw.shape[1]
    head_dim = width // heads
    cols = width // groups
    devices = lax.axis_size("seq")
    place = lax.axis_index("seq")
    cuts = []
    for g in range(groups):
        parts = FIRST_PARTS if g == 0 else OTHER_PARTS
        edges = [g * cols + cols * sum(parts[:i]) // sum(parts) for i in range(len(parts) + 1)]
        cuts += [(g, low, high) for low, high in zip(edges[:-1], edges[1:])]

    taps = conv_x.shape[0]
    dt_t = dt_raw.T
    a_row = a_log.reshape(1, heads)
    d_row = d_skip.reshape(1, heads)
    gain = norm_gain.reshape(1, width)
    sources = [x_in, bc_in, conv_x, conv_bc]
    operands = sources + [dt_t, a_row]
    pinned = [pltpu.with_memory_space_constraint(v, pltpu.HBM) for v in operands]
    landed = [pltpu.VMEM(v.shape, v.dtype) for v in operands]
    scale_shape = jax.ShapeDtypeStruct((tokens, width), F32)
    scalar = pl.BlockSpec(memory_space=pltpu.SMEM)
    in_vmem = pl.BlockSpec(memory_space=pltpu.VMEM)
    anywhere = pl.BlockSpec(memory_space=pl.ANY)
    in_hbm = [pl.BlockSpec(memory_space=pltpu.HBM)] * len(operands)

    def column(height, wide, at):
        return pl.BlockSpec((height, wide), lambda i: (0, at))

    def slab(low, high):
        return pl.BlockSpec((pl.Element(tokens), pl.Element(high - low)), lambda i: (0, low))

    def whole(array):
        return pl.BlockSpec(array.shape, lambda i: (0,) * len(array.shape))

    def here(condition):
        return condition.astype(jnp.int32).reshape(1)

    def shifted(value, route):
        return lax.ppermute(value, "seq", route)

    def first_states(group, low, high):
        blocks = -(-(width + groups * both) // (high - low))
        extra = -(-(taps - 1) * blocks // (2 * RIM)) * 2 * RIM
        return pl.pallas_call(
            functools.partial(first_kernel, group, low, high),
            out_shape=[jax.ShapeDtypeStruct((state_dim + extra, high - low), BF16), scale_shape],
            in_specs=[scalar] + in_hbm,
            scratch_shapes=landed + [pltpu.SemaphoreType.DMA((len(operands),))],
            compiler_params=params(16),
            name="first_states",
        )(here(place == 0), *pinned)

    def next_states(token, scale, group, low, high):
        return pl.pallas_call(
            functools.partial(next_kernel, group, low, high),
            out_shape=jax.ShapeDtypeStruct((state_dim, high - low), BF16),
            in_specs=[scalar, anywhere] + [in_vmem] * (len(sources) + 1),
            compiler_params=params(16),
            name="next_states",
        )(here(place == 0), token, *sources, scale)

    def prepared(token):
        return pl.pallas_call(
            functools.partial(prepare_kernel, cuts),
            out_shape=[jax.ShapeDtypeStruct((RIM, width + groups * both), BF16), scale_shape]
            + [jax.ShapeDtypeStruct((1, high - low), F32) for _, low, high in cuts],
            in_specs=[anywhere] + [in_vmem] * 4,
            compiler_params=params(16),
            name="prepared",
        )(token, x_in, bc_in, dt_t, a_row)

    def later_states(condition, rows, token, scale, group, low, high):
        return pl.pallas_call(
            functools.partial(later_kernel, group, low, high),
            out_shape=jax.ShapeDtypeStruct((state_dim, high - low), F32),
            in_specs=[scalar, in_vmem, anywhere] + [in_vmem] * (len(sources) + 1),
            compiler_params=params(16),
            name="later_states",
        )(here(condition), rows, token, *sources, scale)

    along = [(i, i + 1) for i in range(devices - 1)]
    if devices <= CHAIN_MOST:
        first, scale = first_states(*cuts[0])
        sent = [first]
        for cut in cuts[1:]:
            sent.append(next_states(sent[-1], scale, *cut))
        last, scale, *decays = prepared(sent[-1])
        got = shifted(last, along)
        arrived = [[shifted(v, along[:1])] for v in sent]
        rows, token = arrived[0][0], last
        for hop in range(1, devices - 1):
            condition = place == 1 if hop == 1 else place >= 2
            after = token
            for i, (seen, cut) in enumerate(zip(arrived, cuts)):
                if hop <= 2:
                    made = later_states(condition, rows, after, scale, *cut)
                    states = [made] if i == 0 else states + [made]
                early = arrived[0][-1] if hop > 1 and i == len(cuts) - 1 else token
                before, _, _ = lax.optimization_barrier((seen[-1], token, early))
                joined = decays[i] * before[:state_dim].astype(F32) + states[i]
                token = joined.astype(BF16)
                after = token if hop == 1 and i == 0 else after
                seen.append(shifted(token, along[hop : hop + 1]))
            rows = got
    else:
        last, scale, *decays = prepared(a_row)
        got = shifted(last, along)
        arrived = []
        for decay, cut in zip(decays, cuts):
            state = later_states(place >= 0, got, a_row, scale, *cut)
            arrived.append([doubling(state, decay, devices)])

    y_part, lead, c_act = pl.pallas_call(
        functools.partial(intra_kernel, head_dim),
        out_shape=(
            jax.ShapeDtypeStruct((tokens, width), F32),
            jax.ShapeDtypeStruct((tokens, width), F32),
            jax.ShapeDtypeStruct((tokens, groups * state_dim), BF16),
        ),
        scratch_shapes=[pltpu.VMEM((tokens, cols), F32)],
        compiler_params=params(32),
        cost_estimate=pl.CostEstimate(
            flops=4 * tokens * tokens * width,
            bytes_accessed=12 * tokens * width,
            transcendentals=tokens * tokens * heads,
        ),
        name="intra",
    )(x_in, got, bc_in, z_in, conv_x, conv_bc, dt_t, a_row, d_row)

    out = None
    for g in range(groups):
        ready = []
        for (group, low, high), seen in zip(cuts, arrived):
            if group != g:
                continue
            inputs = [c_act, y_part, lead]
            specs = [column(tokens, state_dim, g)] + [slab(low, high)] * 2
            if high < (g + 1) * cols:
                ready.append(
                    pl.pallas_call(
                        gated_kernel,
                        out_shape=jax.ShapeDtypeStruct((tokens, high - low), F32),
                        in_specs=specs + [whole(v) for v in seen],
                        out_specs=column(tokens, high - low, 0),
                        grid=(1,),
                        compiler_params=params(16),
                        name="gated",
                    )(*inputs, *seen)
                )
        inputs += [gain] + ready + seen_last(arrived, cuts, g)
        specs += [column(1, cols, g)] + [whole(v) for v in ready + seen_last(arrived, cuts, g)]
        aliases = {}
        if out is not None:
            aliases = {len(inputs): 0}
            inputs.append(out)
            specs.append(pl.BlockSpec(memory_space=pl.ANY))
        out = pl.pallas_call(
            functools.partial(output_kernel, len(ready), len(arrived[0])),
            out_shape=jax.ShapeDtypeStruct((tokens, width), BF16),
            in_specs=specs,
            out_specs=column(tokens, cols, g),
            grid=(1,),
            input_output_aliases=aliases,
            compiler_params=params(32),
            name="outputs",
        )(*inputs)
    return out


def solution(mesh):
    return jax.shard_map(
        shards,
        mesh=mesh,
        in_specs=(
            P(("groups", "seq"), "head"),
            P(("groups", "seq"), "head", None),
            P(("groups", "seq"), "head"),
            P(("groups", "seq"), "head"),
            P(None, "head"),
            P(None, "head", None),
            P("head"),
            P("head"),
            P("head"),
        ),
        out_specs=P(("groups", "seq"), "head"),
        check_vma=False,
    )
```

```python
import functools

import jax
import jax.numpy as jnp
from jax import lax
from jax.experimental import pallas as pl
from jax.experimental.pallas import tpu as pltpu
from jax.sharding import PartitionSpec as P

EPS = 1e-05
F32 = jnp.float32
BF16 = jnp.bfloat16
CHAIN_MOST = 4
FIRST_PARTS = (3, 5)
OTHER_PARTS = (1, 1)
CHUNK = 128
RIM = 8


def silu(u):
    return 0.5 * u * (1.0 + jnp.tanh(0.5 * u))


def softplus(v):
    return jnp.maximum(v, 0.0) + jnp.log1p(jnp.exp(-jnp.abs(v)))


def halves(v, count, axis):
    parts = []
    for _ in range(count - 1):
        part = v.astype(BF16)
        parts.append(part)
        v = v - part.astype(F32)
    parts.append(v.astype(BF16))
    return jnp.concatenate(parts, axis=axis)


def spread(per_head, head_dim, count):
    heads = per_head.shape[0]
    rows = lax.broadcasted_iota(jnp.int32, (heads * count, heads * head_dim), 0)
    cols = lax.broadcasted_iota(jnp.int32, (heads * count, heads * head_dim), 1)
    pick = (rows % heads == cols // head_dim).astype(F32).astype(BF16)
    return lax.dot_general(
        halves(per_head, count, 0), pick, (((0,), (0,)), ((), ())), preferred_element_type=F32
    )


def spread_row(column, head_dim):
    heads = column.shape[0]
    rows = lax.broadcasted_iota(jnp.int32, (heads, heads * head_dim), 0)
    cols = lax.broadcasted_iota(jnp.int32, (heads, heads * head_dim), 1)
    return jnp.sum(jnp.where(rows == cols // head_dim, column, 0.0), axis=0, keepdims=True)


def as_column(row, start, heads):
    every = row.shape[1]
    rows = lax.broadcasted_iota(jnp.int32, (heads, every), 0)
    cols = lax.broadcasted_iota(jnp.int32, (heads, every), 1)
    return jnp.sum(jnp.where(cols == rows + start, row, 0.0), axis=1, keepdims=True)


def conv_act(series, tail, taps):
    count = taps.shape[0]
    above = tail.shape[0]
    padded = jnp.concatenate([tail, series], axis=0)
    total = taps[count - 1 : count] * series
    for back in range(1, count):
        total = total + taps[count - 1 - back : count - back] * pltpu.roll(padded, back, 0)[above:]
    return silu(total).astype(BF16)


def rates(dt_raw, a_log_row, start):
    heads, tokens = dt_raw.shape
    dt = softplus(dt_raw)
    rate = -jnp.exp(as_column(a_log_row, start, heads)) * dt
    earlier = lax.broadcasted_iota(jnp.int32, (tokens, tokens), 0)
    later = lax.broadcasted_iota(jnp.int32, (tokens, tokens), 1)
    upto = (earlier <= later).astype(F32)
    cum = jnp.dot(rate, upto, precision=lax.Precision.HIGHEST, preferred_element_type=F32)
    return dt, cum


def scales(head_dim, dt_raw, a_log, scale):
    dt, cum = rates(dt_raw[...], a_log[...], 0)
    end = cum[:, -1:]
    scale[...] = spread(jnp.exp(end - cum) * dt, head_dim, 2)
    return spread_row(jnp.exp(end), head_dim)


def emit_states(group, low, high, x, tail_x, bc, tail_bc, taps_x, taps_bc, scale, emit):
    state_dim = bc.shape[2] // 2
    b = conv_act(
        bc[:, :, :state_dim].astype(F32)[:, group], tail_bc, taps_bc[:, :, :state_dim][:, group]
    )
    b_t = b.astype(F32).T.astype(BF16)
    for at in range(low, high, CHUNK):
        cut = slice(at, at + CHUNK)
        act = conv_act(x[:, cut].astype(F32), tail_x(cut), taps_x[:, cut])
        scaled = (scale[:, cut] * act.astype(F32)).astype(BF16)
        emit(slice(at - low, at - low + CHUNK), jnp.dot(b_t, scaled, preferred_element_type=F32))


def head_rows(group, low, high, x, bc, taps_x, taps_bc, scale, out):
    state_dim = bc.shape[2] // 2

    def emit(here, total):
        out[:state_dim, here] = total.astype(BF16)

    emit_states(
        group, low, high, x, lambda cut: jnp.zeros((RIM, CHUNK), F32),
        bc, jnp.zeros((RIM, state_dim), F32), taps_x, taps_bc, scale, emit,
    )


def first_kernel(
    group, low, high, active, x_hbm, bc_hbm, taps_x_hbm, taps_bc_hbm, dt_hbm, a_hbm,
    out, scale, x, bc, taps_x, taps_bc, dt_raw, a_log, sems,
):
    tokens, width = x.shape
    groups, both = bc.shape[1:]

    @pl.when(active[0] == 1)
    def _():
        pairs = [
            (dt_hbm, dt_raw), (a_hbm, a_log), (x_hbm, x), (bc_hbm, bc),
            (taps_x_hbm, taps_x), (taps_bc_hbm, taps_bc),
        ]
        copies = [pltpu.make_async_copy(*pair, sems.at[i]) for i, pair in enumerate(pairs)]
        for copy in copies:
            copy.start()
        for copy in copies[:2]:
            copy.wait()
        scales(width // dt_raw.shape[0], dt_raw, a_log, scale)
        for copy in copies[2:]:
            copy.wait()
        state_dim, step = both // 2, high - low
        keep = taps_x.shape[0] - 1
        extra = out.shape[0] - state_dim
        last_bc = bc[tokens - 2 * RIM :].astype(F32)[-RIM:]
        last = [x[tokens - 2 * RIM :, :].astype(F32)[-RIM:]] + [last_bc[:, g] for g in range(groups)]
        length = width + groups * both
        last.append(jnp.zeros((RIM, -length % step + step), F32))
        last = jnp.concatenate(last, axis=1)
        at = lax.broadcasted_iota(jnp.int32, (extra, step), 0)
        below = jnp.zeros((extra, step), F32)
        fill = jnp.zeros((extra - RIM, step), F32)
        for k in range(-(-length // step)):
            block = jnp.concatenate([last[:, k * step : (k + 1) * step], fill], axis=0)
            block = pltpu.roll(block, (keep * (k + 1) - RIM) % extra, 0)
            below = jnp.where((at >= keep * k) & (at < keep * (k + 1)), block, below)
        out[state_dim:, :] = below.astype(BF16)
        head_rows(group, low, high, x, bc, taps_x, taps_bc, scale, out)


def next_kernel(group, low, high, active, _, x, bc, taps_x, taps_bc, scale, out):
    @pl.when(active[0] == 1)
    def _():
        head_rows(group, low, high, x, bc, taps_x, taps_bc, scale, out)


def prepare_kernel(cuts, _, x, bc, dt_raw, a_log, pack, scale, *decays):
    tokens, width = x.shape
    groups, both = bc.shape[1:]
    pack[:, :width] = x[tokens - 2 * RIM :, :].astype(F32)[-RIM:].astype(BF16)
    last_bc = bc[tokens - 2 * RIM :].astype(F32)[-RIM:]
    for g in range(groups):
        pack[:, width + g * both : width + (g + 1) * both] = last_bc[:, g].astype(BF16)
    row = scales(width // dt_raw.shape[0], dt_raw, a_log, scale)
    for decay, (_, low, high) in zip(decays, cuts):
        decay[...] = row[:, low:high]


def later_kernel(group, low, high, active, rows, _, x, bc, taps_x, taps_bc, scale, state):
    width = x.shape[1]
    both = bc.shape[2]
    state_dim = both // 2
    keep = taps_x.shape[0] - 1

    def tail(begin, stop):
        if rows.shape[0] == RIM:
            return rows[:, begin:stop].astype(F32)
        step = rows.shape[1]
        below = rows[state_dim:, begin % step : begin % step + stop - begin].astype(F32)
        extra = below.shape[0]
        return pltpu.roll(below, (RIM - keep * (begin // step + 1)) % extra, 0)[:RIM]

    @pl.when(active[0] == 1)
    def _():
        def emit(here, total):
            state[:, here] = total

        at = width + group * both
        emit_states(
            group, low, high, x, lambda cut: tail(cut.start, cut.stop),
            bc, tail(at, at + state_dim), taps_x, taps_bc, scale, emit,
        )


def intra_kernel(
    head_dim, x, got_soon, got_late, bc, z, taps_x, taps_bc, dt_raw, a_log, d_skip,
    y_part, lead, c_act, wide
):
    dt, cum = rates(dt_raw[...], a_log[...], 0)
    got = got_soon[...].astype(F32) + got_late[...].astype(F32)
    tokens, width = x.shape
    groups, both = bc.shape[1:]
    state_dim = both // 2
    cols = width // groups
    heads = dt.shape[0] // groups
    cum_t = cum.T
    leading = jnp.exp(cum)
    skip = spread_row(as_column(d_skip[...], 0, dt.shape[0]), head_dim)
    t_at = lax.broadcasted_iota(jnp.int32, (tokens, tokens), 0)
    s_at = lax.broadcasted_iota(jnp.int32, (tokens, tokens), 1)
    pair = 2 * head_dim
    for g in range(groups):
        at = width + g * both
        bc_act = conv_act(
            bc[...].astype(F32)[:, g], got[:, at : at + both], taps_bc[...][:, g]
        )
        b, c = bc_act[:, :state_dim], bc_act[:, state_dim:]
        c_act[:, g * state_dim : (g + 1) * state_dim] = c
        inner = lax.dot_general(c, b, (((1,), (1,)), ((), ())), preferred_element_type=F32)
        inner = jnp.where(t_at >= s_at, inner, 0.0)
        wide[...] = spread(leading[g * heads : (g + 1) * heads], head_dim, 2)
        for first in range(0, heads, 2):
            here = first * head_dim
            cut = slice(g * cols + here, g * cols + here + pair)
            act = conv_act(x[:, cut].astype(F32), got[:, cut], taps_x[:, cut])
            lane = lax.broadcasted_iota(jnp.int32, act.shape, 1)
            full = act.astype(F32)
            blocks = jnp.concatenate(
                [jnp.where(lane < head_dim, full, 0.0), jnp.where(lane < head_dim, 0.0, full)],
                axis=0,
            ).astype(BF16)
            weights = []
            for h in (g * heads + first, g * heads + first + 1):
                gap = jnp.minimum(cum_t[:, h : h + 1] - cum[h : h + 1, :], 0.0)
                weights.append((jnp.exp(gap) * dt[h : h + 1, :] * inner).astype(BF16))
            y = jnp.dot(jnp.concatenate(weights, axis=1), blocks, preferred_element_type=F32)
            gate = silu(z[:, cut].astype(F32))
            y_part[:, cut] = (y + skip[:, cut] * full) * gate
            lead[:, cut] = wide[:, here : here + pair] * gate


def gated_slice(c, y_part, lead, arrived):
    state = arrived[0][: c.shape[1]]
    for more in arrived[1:]:
        state = state + more[...]
    return y_part[...] + lead[...] * jnp.dot(c[...], state, preferred_element_type=F32)


def gated_kernel(c, y_part, lead, *refs):
    refs[-1][...] = gated_slice(c, y_part, lead, refs[:-1])


def output_kernel(ready, seen, c, y_part, lead, gain, *refs):
    gated = [v[...] for v in refs[:ready]]
    gated.append(gated_slice(c, y_part, lead, refs[ready : ready + seen]))
    gated = jnp.concatenate(gated, axis=1)
    mean_sq = jnp.mean(gated * gated, axis=1, keepdims=True)
    refs[-1][...] = (gated * lax.rsqrt(mean_sq + EPS) * gain[...]).astype(BF16)


def params(mib):
    return pltpu.CompilerParams(vmem_limit_bytes=mib * 1024 * 1024)


def doubling(state, decay, devices):
    def moved(value, distance):
        return lax.ppermute(value, "seq", [(i, i + distance) for i in range(devices - distance)])

    total, decay = moved(state.astype(BF16), 1), moved(decay, 1)
    distance = 1
    while distance < devices - 1:
        came = moved(total, distance)
        total = (decay * came.astype(F32) + total.astype(F32)).astype(BF16)
        decay = decay * moved(decay, distance)
        distance *= 2
    return total


def seen_last(arrived, cuts, group):
    return [seen for (g, _, _), seen in zip(cuts, arrived) if g == group][-1]


def shards(x_in, bc_in, z_in, dt_raw, conv_x, conv_bc, a_log, d_skip, norm_gain):
    tokens, width = x_in.shape
    groups, both = bc_in.shape[1:]
    state_dim = both // 2
    heads = dt_raw.shape[1]
    head_dim = width // heads
    cols = width // groups
    devices = lax.axis_size("seq")
    place = lax.axis_index("seq")
    cuts = []
    for g in range(groups):
        parts = FIRST_PARTS if g == 0 else OTHER_PARTS
        edges = [g * cols + cols * sum(parts[:i]) // sum(parts) for i in range(len(parts) + 1)]
        cuts += [(g, low, high) for low, high in zip(edges[:-1], edges[1:])]

    taps = conv_x.shape[0]
    dt_t = dt_raw.T
    a_row = a_log.reshape(1, heads)
    d_row = d_skip.reshape(1, heads)
    gain = norm_gain.reshape(1, width)
    sources = [x_in, bc_in, conv_x, conv_bc]
    operands = sources + [dt_t, a_row]
    pinned = [pltpu.with_memory_space_constraint(v, pltpu.HBM) for v in operands]
    landed = [pltpu.VMEM(v.shape, v.dtype) for v in operands]
    scale_shape = jax.ShapeDtypeStruct((tokens, width), F32)
    scalar = pl.BlockSpec(memory_space=pltpu.SMEM)
    in_vmem = pl.BlockSpec(memory_space=pltpu.VMEM)
    anywhere = pl.BlockSpec(memory_space=pl.ANY)
    in_hbm = [pl.BlockSpec(memory_space=pltpu.HBM)] * len(operands)

    def column(height, wide, at):
        return pl.BlockSpec((height, wide), lambda i: (0, at))

    def slab(low, high):
        return pl.BlockSpec((pl.Element(tokens), pl.Element(high - low)), lambda i: (0, low))

    def whole(array):
        return pl.BlockSpec(array.shape, lambda i: (0,) * len(array.shape))

    def here(condition):
        return condition.astype(jnp.int32).reshape(1)

    def shifted(value, route):
        return lax.ppermute(value, "seq", route)

    def first_states(group, low, high):
        blocks = -(-(width + groups * both) // (high - low))
        extra = -(-(taps - 1) * blocks // (2 * RIM)) * 2 * RIM
        return pl.pallas_call(
            functools.partial(first_kernel, group, low, high),
            out_shape=[jax.ShapeDtypeStruct((state_dim + extra, high - low), BF16), scale_shape],
            in_specs=[scalar] + in_hbm,
            scratch_shapes=landed + [pltpu.SemaphoreType.DMA((len(operands),))],
            compiler_params=params(16),
            name="first_states",
        )(here(place == 0), *pinned)

    def next_states(token, scale, group, low, high):
        return pl.pallas_call(
            functools.partial(next_kernel, group, low, high),
            out_shape=jax.ShapeDtypeStruct((state_dim, high - low), BF16),
            in_specs=[scalar, anywhere] + [in_vmem] * (len(sources) + 1),
            compiler_params=params(16),
            name="next_states",
        )(here(place == 0), token, *sources, scale)

    def prepared(token):
        return pl.pallas_call(
            functools.partial(prepare_kernel, cuts),
            out_shape=[jax.ShapeDtypeStruct((RIM, width + groups * both), BF16), scale_shape]
            + [jax.ShapeDtypeStruct((1, high - low), F32) for _, low, high in cuts],
            in_specs=[anywhere] + [in_vmem] * 4,
            compiler_params=params(16),
            name="prepared",
        )(token, x_in, bc_in, dt_t, a_row)

    def later_states(condition, rows, token, scale, group, low, high):
        return pl.pallas_call(
            functools.partial(later_kernel, group, low, high),
            out_shape=jax.ShapeDtypeStruct((state_dim, high - low), F32),
            in_specs=[scalar, in_vmem, anywhere] + [in_vmem] * (len(sources) + 1),
            compiler_params=params(16),
            name="later_states",
        )(here(condition), rows, token, *sources, scale)

    along = [(i, i + 1) for i in range(devices - 1)]
    if devices <= CHAIN_MOST:
        first, scale = first_states(*cuts[0])
        sent = [first]
        for cut in cuts[1:]:
            sent.append(next_states(sent[-1], scale, *cut))
        last, scale, *decays = prepared(sent[-1])
        soon = along[1 : max(devices - 2, 1)]
        got = shifted(last, soon) if soon else jnp.zeros_like(last)
        arrived = [[shifted(v, along[:1])] for v in sent]
        rows, token, late = arrived[0][0], last, None
        for hop in range(1, devices - 1):
            condition = place == 1 if hop == 1 else place >= 2
            after = token
            for i, (seen, cut) in enumerate(zip(arrived, cuts)):
                if hop <= 2:
                    made = later_states(condition, rows, after, scale, *cut)
                    states = [made] if i == 0 else states + [made]
                early = (arrived[0][-1], late) if hop > 1 and i == len(cuts) - 1 else ()
                before, *_ = lax.optimization_barrier((seen[-1], token) + early)
                joined = decays[i] * before[:state_dim].astype(F32) + states[i]
                token = joined.astype(BF16)
                if hop == devices - 2 and i == 0:
                    last, _ = lax.optimization_barrier((last, token))
                    late = shifted(last, [pair for pair in along if pair not in soon])
                after = token if hop == 1 and i == 0 else after
                seen.append(shifted(token, along[hop : hop + 1]))
            rows = got
        if late is None:
            late = shifted(last, along)
        got = [got, late]
    else:
        last, scale, *decays = prepared(a_row)
        got = shifted(last, along)
        arrived = []
        for decay, cut in zip(decays, cuts):
            state = later_states(place >= 0, got, a_row, scale, *cut)
            arrived.append([doubling(state, decay, devices)])
        got = [got, jnp.zeros_like(got)]

    y_part, lead, c_act = pl.pallas_call(
        functools.partial(intra_kernel, head_dim),
        out_shape=(
            jax.ShapeDtypeStruct((tokens, width), F32),
            jax.ShapeDtypeStruct((tokens, width), F32),
            jax.ShapeDtypeStruct((tokens, groups * state_dim), BF16),
        ),
        scratch_shapes=[pltpu.VMEM((tokens, cols), F32)],
        compiler_params=params(32),
        cost_estimate=pl.CostEstimate(
            flops=4 * tokens * tokens * width,
            bytes_accessed=12 * tokens * width,
            transcendentals=tokens * tokens * heads,
        ),
        name="intra",
    )(x_in, *got, bc_in, z_in, conv_x, conv_bc, dt_t, a_row, d_row)

    out = None
    for g in range(groups):
        ready = []
        for (group, low, high), seen in zip(cuts, arrived):
            if group != g:
                continue
            inputs = [c_act, y_part, lead]
            specs = [column(tokens, state_dim, g)] + [slab(low, high)] * 2
            if high < (g + 1) * cols:
                ready.append(
                    pl.pallas_call(
                        gated_kernel,
                        out_shape=jax.ShapeDtypeStruct((tokens, high - low), F32),
                        in_specs=specs + [whole(v) for v in seen],
                        out_specs=column(tokens, high - low, 0),
                        grid=(1,),
                        compiler_params=params(16),
                        name="gated",
                    )(*inputs, *seen)
                )
        inputs += [gain] + ready + seen_last(arrived, cuts, g)
        specs += [column(1, cols, g)] + [whole(v) for v in ready + seen_last(arrived, cuts, g)]
        aliases = {}
        if out is not None:
            aliases = {len(inputs): 0}
            inputs.append(out)
            specs.append(pl.BlockSpec(memory_space=pl.ANY))
        out = pl.pallas_call(
            functools.partial(output_kernel, len(ready), len(arrived[0])),
            out_shape=jax.ShapeDtypeStruct((tokens, width), BF16),
            in_specs=specs,
            out_specs=column(tokens, cols, g),
            grid=(1,),
            input_output_aliases=aliases,
            compiler_params=params(32),
            name="outputs",
        )(*inputs)
    return out


def solution(mesh):
    return jax.shard_map(
        shards,
        mesh=mesh,
        in_specs=(
            P(("groups", "seq"), "head"),
            P(("groups", "seq"), "head", None),
            P(("groups", "seq"), "head"),
            P(("groups", "seq"), "head"),
            P(None, "head"),
            P(None, "head", None),
            P("head"),
            P("head"),
            P("head"),
        ),
        out_specs=P(("groups", "seq"), "head"),
        check_vma=False,
    )
```

```python
import functools

import jax
import jax.numpy as jnp
from jax import lax
from jax.experimental import pallas as pl
from jax.experimental.pallas import tpu as pltpu
from jax.sharding import PartitionSpec as P

EPS = 1e-05
F32 = jnp.float32
BF16 = jnp.bfloat16
CHAIN_MOST = 4
FIRST_PARTS = (1, 1)
OTHER_PARTS = (1, 1)
CHUNK = 128
RIM = 8


def silu(u):
    return 0.5 * u * (1.0 + jnp.tanh(0.5 * u))


def softplus(v):
    return jnp.maximum(v, 0.0) + jnp.log1p(jnp.exp(-jnp.abs(v)))


def halves(v, count, axis):
    parts = []
    for _ in range(count - 1):
        part = v.astype(BF16)
        parts.append(part)
        v = v - part.astype(F32)
    parts.append(v.astype(BF16))
    return jnp.concatenate(parts, axis=axis)


def spread(per_head, head_dim, count):
    heads = per_head.shape[0]
    rows = lax.broadcasted_iota(jnp.int32, (heads * count, heads * head_dim), 0)
    cols = lax.broadcasted_iota(jnp.int32, (heads * count, heads * head_dim), 1)
    pick = (rows % heads == cols // head_dim).astype(F32).astype(BF16)
    return lax.dot_general(
        halves(per_head, count, 0), pick, (((0,), (0,)), ((), ())), preferred_element_type=F32
    )


def spread_row(column, head_dim):
    heads = column.shape[0]
    rows = lax.broadcasted_iota(jnp.int32, (heads, heads * head_dim), 0)
    cols = lax.broadcasted_iota(jnp.int32, (heads, heads * head_dim), 1)
    return jnp.sum(jnp.where(rows == cols // head_dim, column, 0.0), axis=0, keepdims=True)


def as_column(row, start, heads):
    every = row.shape[1]
    rows = lax.broadcasted_iota(jnp.int32, (heads, every), 0)
    cols = lax.broadcasted_iota(jnp.int32, (heads, every), 1)
    return jnp.sum(jnp.where(cols == rows + start, row, 0.0), axis=1, keepdims=True)


def conv_act(series, tail, taps):
    count = taps.shape[0]
    above = tail.shape[0]
    padded = jnp.concatenate([tail, series], axis=0)
    total = taps[count - 1 : count] * series
    for back in range(1, count):
        total = total + taps[count - 1 - back : count - back] * pltpu.roll(padded, back, 0)[above:]
    return silu(total).astype(BF16)


def rates(dt_raw, a_log_row, start):
    heads, tokens = dt_raw.shape
    dt = softplus(dt_raw)
    rate = -jnp.exp(as_column(a_log_row, start, heads)) * dt
    earlier = lax.broadcasted_iota(jnp.int32, (tokens, tokens), 0)
    later = lax.broadcasted_iota(jnp.int32, (tokens, tokens), 1)
    upto = (earlier <= later).astype(F32)
    cum = jnp.dot(rate, upto, precision=lax.Precision.HIGHEST, preferred_element_type=F32)
    return dt, cum


def scales(head_dim, dt_raw, a_log, scale):
    dt, cum = rates(dt_raw[...], a_log[...], 0)
    end = cum[:, -1:]
    scale[...] = spread(jnp.exp(end - cum) * dt, head_dim, 2)
    return spread_row(jnp.exp(end), head_dim)


def emit_states(group, low, high, x, tail_x, bc, tail_bc, taps_x, taps_bc, scale, emit):
    state_dim = bc.shape[2] // 2
    b = conv_act(
        bc[:, :, :state_dim].astype(F32)[:, group], tail_bc, taps_bc[:, :, :state_dim][:, group]
    )
    b_t = b.astype(F32).T.astype(BF16)
    for at in range(low, high, CHUNK):
        cut = slice(at, at + CHUNK)
        act = conv_act(x[:, cut].astype(F32), tail_x(cut), taps_x[:, cut])
        scaled = (scale[:, cut] * act.astype(F32)).astype(BF16)
        emit(slice(at - low, at - low + CHUNK), jnp.dot(b_t, scaled, preferred_element_type=F32))


def head_rows(group, low, high, x, bc, taps_x, taps_bc, scale, out):
    state_dim = bc.shape[2] // 2

    def emit(here, total):
        out[:state_dim, here] = total.astype(BF16)

    emit_states(
        group, low, high, x, lambda cut: jnp.zeros((RIM, CHUNK), F32),
        bc, jnp.zeros((RIM, state_dim), F32), taps_x, taps_bc, scale, emit,
    )


def first_kernel(
    group, low, high, active, x_hbm, bc_hbm, taps_x_hbm, taps_bc_hbm, dt_hbm, a_hbm,
    out, scale, x, bc, taps_x, taps_bc, dt_raw, a_log, sems,
):
    tokens, width = x.shape
    groups, both = bc.shape[1:]

    @pl.when(active[0] == 1)
    def _():
        pairs = [
            (dt_hbm, dt_raw), (a_hbm, a_log), (x_hbm, x), (bc_hbm, bc),
            (taps_x_hbm, taps_x), (taps_bc_hbm, taps_bc),
        ]
        copies = [pltpu.make_async_copy(*pair, sems.at[i]) for i, pair in enumerate(pairs)]
        for copy in copies:
            copy.start()
        for copy in copies[:2]:
            copy.wait()
        scales(width // dt_raw.shape[0], dt_raw, a_log, scale)
        for copy in copies[2:]:
            copy.wait()
        state_dim, step = both // 2, high - low
        keep = taps_x.shape[0] - 1
        extra = out.shape[0] - state_dim
        last_bc = bc[tokens - 2 * RIM :].astype(F32)[-RIM:]
        last = [x[tokens - 2 * RIM :, :].astype(F32)[-RIM:]] + [last_bc[:, g] for g in range(groups)]
        length = width + groups * both
        last.append(jnp.zeros((RIM, -length % step + step), F32))
        last = jnp.concatenate(last, axis=1)
        at = lax.broadcasted_iota(jnp.int32, (extra, step), 0)
        below = jnp.zeros((extra, step), F32)
        fill = jnp.zeros((extra - RIM, step), F32)
        for k in range(-(-length // step)):
            block = jnp.concatenate([last[:, k * step : (k + 1) * step], fill], axis=0)
            block = pltpu.roll(block, (keep * (k + 1) - RIM) % extra, 0)
            below = jnp.where((at >= keep * k) & (at < keep * (k + 1)), block, below)
        out[state_dim:, :] = below.astype(BF16)
        head_rows(group, low, high, x, bc, taps_x, taps_bc, scale, out)


def next_kernel(group, low, high, active, _, x, bc, taps_x, taps_bc, scale, out):
    @pl.when(active[0] == 1)
    def _():
        head_rows(group, low, high, x, bc, taps_x, taps_bc, scale, out)


def prepare_kernel(cuts, _, x, bc, dt_raw, a_log, gain, pack, gain_out, scale, *decays):
    tokens, width = x.shape
    groups, both = bc.shape[1:]
    pack[:, :width] = x[tokens - 2 * RIM :, :].astype(F32)[-RIM:].astype(BF16)
    last_bc = bc[tokens - 2 * RIM :].astype(F32)[-RIM:]
    for g in range(groups):
        pack[:, width + g * both : width + (g + 1) * both] = last_bc[:, g].astype(BF16)
    gain_out[...] = gain[...]
    row = scales(width // dt_raw.shape[0], dt_raw, a_log, scale)
    for decay, (_, low, high) in zip(decays, cuts):
        decay[...] = row[:, low:high]


def rows_before(rows, begin, stop, keep, state_dim):
    if rows.shape[0] == RIM:
        return rows[:, begin:stop].astype(F32)
    step = rows.shape[1]
    below = rows[state_dim:, begin % step : begin % step + stop - begin].astype(F32)
    return pltpu.roll(below, (RIM - keep * (begin // step + 1)) % below.shape[0], 0)[:RIM]


def later_kernel(group, low, high, active, rows, _, x, bc, taps_x, taps_bc, scale, state):
    both = bc.shape[2]
    state_dim = both // 2
    keep = taps_x.shape[0] - 1

    @pl.when(active[0] == 1)
    def _():
        def emit(here, total):
            state[:, here] = total

        at = x.shape[1] + group * both
        emit_states(
            group, low, high, x,
            lambda cut: rows_before(rows, cut.start, cut.stop, keep, state_dim),
            bc, rows_before(rows, at, at + state_dim, keep, state_dim),
            taps_x, taps_bc, scale, emit,
        )


def intra_kernel(group, count, _, *refs):
    sources, refs = refs[:count], refs[count:]
    x, bc, z, taps_x, taps_bc, dt_raw, a_log, d_skip, y_part, lead, c_act, wide = refs
    tokens, cols = z.shape
    both = bc.shape[2]
    state_dim = both // 2
    keep = taps_x.shape[0] - 1
    heads = dt_raw.shape[0]
    head_dim = cols // heads
    dt, cum = rates(dt_raw[...], a_log[...], group * heads)
    cum_t = cum.T
    wide[...] = spread(jnp.exp(cum), head_dim, 2)
    skip = spread_row(as_column(d_skip[...], group * heads, heads), head_dim)

    def before(begin, stop):
        found = [rows_before(rows, begin, stop, keep, state_dim) for rows in sources]
        return sum(found[1:], found[0])

    at = x.shape[1] + group * both
    tail_bc = jnp.concatenate(
        [before(at, at + state_dim), before(at + state_dim, at + both)], axis=1
    )
    bc_act = conv_act(bc[...].astype(F32)[:, group], tail_bc, taps_bc[...][:, group])
    b, c = bc_act[:, :state_dim], bc_act[:, state_dim:]
    c_act[...] = c
    inner = lax.dot_general(c, b, (((1,), (1,)), ((), ())), preferred_element_type=F32)
    t_at = lax.broadcasted_iota(jnp.int32, (tokens, tokens), 0)
    s_at = lax.broadcasted_iota(jnp.int32, (tokens, tokens), 1)
    inner = jnp.where(t_at >= s_at, inner, 0.0)
    pair = 2 * head_dim
    for first in range(0, heads, 2):
        here = slice(first * head_dim, first * head_dim + pair)
        cut = slice(group * cols + here.start, group * cols + here.stop)
        act = conv_act(x[:, cut].astype(F32), before(cut.start, cut.stop), taps_x[:, cut])
        lane = lax.broadcasted_iota(jnp.int32, act.shape, 1)
        full = act.astype(F32)
        blocks = jnp.concatenate(
            [jnp.where(lane < head_dim, full, 0.0), jnp.where(lane < head_dim, 0.0, full)],
            axis=0,
        ).astype(BF16)
        weights = []
        for h in (first, first + 1):
            gap = jnp.minimum(cum_t[:, h : h + 1] - cum[h : h + 1, :], 0.0)
            weights.append((jnp.exp(gap) * dt[h : h + 1, :] * inner).astype(BF16))
        y = jnp.dot(jnp.concatenate(weights, axis=1), blocks, preferred_element_type=F32)
        gate = silu(z[:, here].astype(F32))
        y_part[:, here] = (y + skip[:, here] * full) * gate
        lead[:, here] = wide[:, here] * gate


def gated_slice(which, c, y_part, lead, arrived):
    state = jnp.zeros((c.shape[1], y_part.shape[1]), BF16)
    for i, came in enumerate(arrived):
        state = jnp.where(which[0] == i, came[...][: c.shape[1]], state)
    return y_part[...] + lead[...] * jnp.dot(c[...], state, preferred_element_type=F32)


def gated_kernel(which, c, y_part, lead, *refs):
    refs[-1][...] = gated_slice(which, c, y_part, lead, refs[:-1])


def output_kernel(ready, seen, which, c, y_part, lead, gain, *refs):
    gated = [v[...] for v in refs[:ready]]
    gated.append(gated_slice(which, c, y_part, lead, refs[ready : ready + seen]))
    gated = jnp.concatenate(gated, axis=1)
    mean_sq = jnp.mean(gated * gated, axis=1, keepdims=True)
    refs[-1][...] = (gated * lax.rsqrt(mean_sq + EPS) * gain[...]).astype(BF16)


def params(mib):
    return pltpu.CompilerParams(vmem_limit_bytes=mib * 1024 * 1024)


def doubling(state, decay, devices):
    def moved(value, distance):
        return lax.ppermute(value, "seq", [(i, i + distance) for i in range(devices - distance)])

    total, decay = moved(state.astype(BF16), 1), moved(decay, 1)
    distance = 1
    while distance < devices - 1:
        came = moved(total, distance)
        total = (decay * came.astype(F32) + total.astype(F32)).astype(BF16)
        decay = decay * moved(decay, distance)
        distance *= 2
    return total


def seen_last(arrived, cuts, group):
    return [seen for (g, _, _), seen in zip(cuts, arrived) if g == group][-1]


def shards(x_in, bc_in, z_in, dt_raw, conv_x, conv_bc, a_log, d_skip, norm_gain):
    tokens, width = x_in.shape
    groups, both = bc_in.shape[1:]
    state_dim = both // 2
    heads = dt_raw.shape[1]
    head_dim = width // heads
    cols = width // groups
    devices = lax.axis_size("seq")
    place = lax.axis_index("seq")
    cuts = []
    for g in range(groups):
        parts = FIRST_PARTS if g == 0 else OTHER_PARTS
        edges = [g * cols + cols * sum(parts[:i]) // sum(parts) for i in range(len(parts) + 1)]
        cuts += [(g, low, high) for low, high in zip(edges[:-1], edges[1:])]

    taps = conv_x.shape[0]
    dt_t = dt_raw.T
    a_row = a_log.reshape(1, heads)
    d_row = d_skip.reshape(1, heads)
    gain = norm_gain.reshape(1, width)
    sources = [x_in, bc_in, conv_x, conv_bc]
    operands = sources + [dt_t, a_row]
    pinned = [pltpu.with_memory_space_constraint(v, pltpu.HBM) for v in operands]
    landed = [pltpu.VMEM(v.shape, v.dtype) for v in operands]
    scale_shape = jax.ShapeDtypeStruct((tokens, width), F32)
    scalar = pl.BlockSpec(memory_space=pltpu.SMEM)
    in_vmem = pl.BlockSpec(memory_space=pltpu.VMEM)
    anywhere = pl.BlockSpec(memory_space=pl.ANY)
    in_hbm = [pl.BlockSpec(memory_space=pltpu.HBM)] * len(operands)

    def column(height, wide, at):
        return pl.BlockSpec((height, wide), lambda i: (0, at))

    def slab(low, high):
        return pl.BlockSpec((pl.Element(tokens), pl.Element(high - low)), lambda i: (0, low))

    def whole(array):
        return pl.BlockSpec(array.shape, lambda i: (0,) * len(array.shape))

    def here(condition):
        return condition.astype(jnp.int32).reshape(1)

    def shifted(value, route):
        return lax.ppermute(value, "seq", route)

    def first_states(group, low, high):
        blocks = -(-(width + groups * both) // (high - low))
        extra = -(-(taps - 1) * blocks // (2 * RIM)) * 2 * RIM
        return pl.pallas_call(
            functools.partial(first_kernel, group, low, high),
            out_shape=[jax.ShapeDtypeStruct((state_dim + extra, high - low), BF16), scale_shape],
            in_specs=[scalar] + in_hbm,
            scratch_shapes=landed + [pltpu.SemaphoreType.DMA((len(operands),))],
            compiler_params=params(16),
            name="first_states",
        )(here(place == 0), *pinned)

    def next_states(token, scale, spare, group, low, high):
        return pl.pallas_call(
            functools.partial(next_kernel, group, low, high),
            out_shape=jax.ShapeDtypeStruct((state_dim + spare, high - low), BF16),
            in_specs=[scalar, anywhere] + [in_vmem] * (len(sources) + 1),
            compiler_params=params(16),
            name="next_states",
        )(here(place == 0), token, *sources, scale)

    def prepared(token):
        return pl.pallas_call(
            functools.partial(prepare_kernel, cuts),
            out_shape=[
                jax.ShapeDtypeStruct((RIM, width + groups * both), BF16),
                jax.ShapeDtypeStruct((1, width), F32),
                scale_shape,
            ]
            + [jax.ShapeDtypeStruct((1, high - low), F32) for _, low, high in cuts],
            in_specs=[anywhere] + [in_vmem] * 5,
            compiler_params=params(16),
            name="prepared",
        )(token, x_in, bc_in, dt_t, a_row, gain)

    def later_states(condition, rows, token, scale, group, low, high):
        return pl.pallas_call(
            functools.partial(later_kernel, group, low, high),
            out_shape=jax.ShapeDtypeStruct((state_dim, high - low), F32),
            in_specs=[scalar, in_vmem, anywhere] + [in_vmem] * (len(sources) + 1),
            compiler_params=params(16),
            name="later_states",
        )(here(condition), rows, token, *sources, scale)

    along = [(i, i + 1) for i in range(devices - 1)]
    def intra(token, befores, group):
        return pl.pallas_call(
            functools.partial(intra_kernel, group, len(befores)),
            out_shape=[
                jax.ShapeDtypeStruct((tokens, cols), F32),
                jax.ShapeDtypeStruct((tokens, cols), F32),
                jax.ShapeDtypeStruct((tokens, state_dim), BF16),
            ],
            in_specs=[anywhere]
            + [whole(v) for v in befores]
            + [
                whole(x_in), whole(bc_in), column(tokens, cols, group),
                whole(conv_x), whole(conv_bc),
                pl.BlockSpec((heads // groups, tokens), lambda i: (group, 0)),
                whole(a_row), whole(d_row),
            ],
            out_specs=[column(tokens, cols, 0)] * 2 + [column(tokens, state_dim, 0)],
            grid=(1,),
            scratch_shapes=[pltpu.VMEM((tokens, cols), F32)],
            compiler_params=params(24),
            cost_estimate=pl.CostEstimate(
                flops=4 * tokens * tokens * cols,
                bytes_accessed=12 * tokens * cols,
                transcendentals=tokens * tokens * heads // groups,
            ),
            name="intra",
        )(token, *befores, x_in, bc_in, z_in, conv_x, conv_bc, dt_t, a_row, d_row)

    if devices <= CHAIN_MOST:
        first, scale = first_states(*cuts[0])
        spare = first.shape[0] - state_dim + RIM
        sent = [first]
        for i, cut in enumerate(cuts[1:], 1):
            if i == len(cuts) - 2:
                last, gain, scale_own, *decays = prepared(sent[-1])
                sent.append(next_states(last, scale, 0, *cut))
            else:
                sent.append(next_states(sent[-1], scale, spare if i == 1 else 0, *cut))
        soon = along[1 : max(devices - 2, 1)]
        late = along[max(devices - 2, 1) :]
        befores = [shifted(last, soon)] if soon else []
        arrived = [[shifted(v, along[:1])] for v in sent[:-1]] + [[]]
        waiting = sent[-1]
        befores.append(arrived[0][0])
        rows, token = arrived[0][0], last
        for hop in range(1, devices - 1):
            runs = place == 1 if hop == 1 else (place >= 2) & (place < devices - 1)
            after = token if hop == 1 else settled
            for i, cut in enumerate(cuts):
                if hop <= 2:
                    made = later_states(runs, rows, after, scale_own, *cut)
                    states = [made] if i == 0 else states + [made]
                early = ()
                if hop == devices - 2 and hop > 1 and i == len(cuts) - 1:
                    early = (befores[-1],)
                before, *_ = lax.optimization_barrier((arrived[i][-1], token) + early)
                joined = decays[i] * before[:state_dim].astype(F32) + states[i]
                token = joined.astype(BF16)
                if hop == 1 and i == 0:
                    after = token
                if hop == 1 and i == 1:
                    settled = token
                if i == 0:
                    both_ways = jnp.where(place == hop - 1, waiting, token)
                    came = shifted(both_ways, along[hop - 1 : hop + 1])
                    arrived[-1].append(came)
                    arrived[0].append(came)
                elif i < len(cuts) - 1:
                    arrived[i].append(shifted(token, along[hop : hop + 1]))
            waiting = token
            if hop == 1 and late:
                moved, _ = lax.optimization_barrier((last, token))
                befores.append(shifted(moved, late))
            rows = befores[0]
        arrived[-1].append(shifted(waiting, along[devices - 2 :]))
        which = place - 1
    else:
        last, gain, scale, *decays = prepared(a_row)
        befores = [shifted(last, along)]
        arrived = []
        for decay, cut in zip(decays, cuts):
            state = later_states(place >= 0, befores[0], a_row, scale, *cut)
            arrived.append([doubling(state, decay, devices)])
        which = jnp.zeros_like(place)
    which = which.astype(jnp.int32).reshape(1)
    parts = [intra(a_row, befores, g) for g in range(groups)]

    out = None
    for g in range(groups):
        ready = []
        for (group, low, high), seen in zip(cuts, arrived):
            if group != g:
                continue
            y_part, lead, c_act = parts[g]
            inputs = [which, c_act, y_part, lead]
            specs = [scalar, whole(c_act)] + [slab(low - g * cols, high - g * cols)] * 2
            if high < (g + 1) * cols:
                ready.append(
                    pl.pallas_call(
                        gated_kernel,
                        out_shape=jax.ShapeDtypeStruct((tokens, high - low), F32),
                        in_specs=specs + [whole(v) for v in seen],
                        out_specs=column(tokens, high - low, 0),
                        grid=(1,),
                        compiler_params=params(16),
                        name="gated",
                    )(*inputs, *seen)
                )
        inputs += [gain] + ready + seen_last(arrived, cuts, g)
        specs += [column(1, cols, g)] + [whole(v) for v in ready + seen_last(arrived, cuts, g)]
        aliases = {}
        if out is not None:
            aliases = {len(inputs): 0}
            inputs.append(out)
            specs.append(pl.BlockSpec(memory_space=pl.ANY))
        out = pl.pallas_call(
            functools.partial(output_kernel, len(ready), len(arrived[0])),
            out_shape=jax.ShapeDtypeStruct((tokens, width), BF16),
            in_specs=specs,
            out_specs=column(tokens, cols, g),
            grid=(1,),
            input_output_aliases=aliases,
            compiler_params=params(32),
            name="outputs",
        )(*inputs)
    return out


def solution(mesh):
    return jax.shard_map(
        shards,
        mesh=mesh,
        in_specs=(
            P(("groups", "seq"), "head"),
            P(("groups", "seq"), "head", None),
            P(("groups", "seq"), "head"),
            P(("groups", "seq"), "head"),
            P(None, "head"),
            P(None, "head", None),
            P("head"),
            P("head"),
            P("head"),
        ),
        out_specs=P(("groups", "seq"), "head"),
        check_vma=False,
    )
```

```python
import functools

import jax
import jax.numpy as jnp
from jax import lax
from jax.experimental import pallas as pl
from jax.experimental.pallas import tpu as pltpu
from jax.sharding import PartitionSpec as P

EPS = 1e-05
F32 = jnp.float32
BF16 = jnp.bfloat16
CHAIN_MOST = 4
FIRST_PARTS = (3, 5)
OTHER_PARTS = (1, 1)
CHUNK = 128
RIM = 8


def silu(u):
    return 0.5 * u * (1.0 + jnp.tanh(0.5 * u))


def softplus(v):
    return jnp.maximum(v, 0.0) + jnp.log1p(jnp.exp(-jnp.abs(v)))


def halves(v, count, axis):
    parts = []
    for _ in range(count - 1):
        part = v.astype(BF16)
        parts.append(part)
        v = v - part.astype(F32)
    parts.append(v.astype(BF16))
    return jnp.concatenate(parts, axis=axis)


def spread(per_head, head_dim, count):
    heads = per_head.shape[0]
    rows = lax.broadcasted_iota(jnp.int32, (heads * count, heads * head_dim), 0)
    cols = lax.broadcasted_iota(jnp.int32, (heads * count, heads * head_dim), 1)
    pick = (rows % heads == cols // head_dim).astype(F32).astype(BF16)
    return lax.dot_general(
        halves(per_head, count, 0), pick, (((0,), (0,)), ((), ())), preferred_element_type=F32
    )


def spread_row(column, head_dim):
    heads = column.shape[0]
    rows = lax.broadcasted_iota(jnp.int32, (heads, heads * head_dim), 0)
    cols = lax.broadcasted_iota(jnp.int32, (heads, heads * head_dim), 1)
    return jnp.sum(jnp.where(rows == cols // head_dim, column, 0.0), axis=0, keepdims=True)


def as_column(row, start, heads):
    every = row.shape[1]
    rows = lax.broadcasted_iota(jnp.int32, (heads, every), 0)
    cols = lax.broadcasted_iota(jnp.int32, (heads, every), 1)
    return jnp.sum(jnp.where(cols == rows + start, row, 0.0), axis=1, keepdims=True)


def conv_act(series, tail, taps):
    count = taps.shape[0]
    above = tail.shape[0]
    padded = jnp.concatenate([tail, series], axis=0)
    total = taps[count - 1 : count] * series
    for back in range(1, count):
        total = total + taps[count - 1 - back : count - back] * pltpu.roll(padded, back, 0)[above:]
    return silu(total).astype(BF16)


def rates(dt_raw, a_log_row, start):
    heads, tokens = dt_raw.shape
    dt = softplus(dt_raw)
    rate = -jnp.exp(as_column(a_log_row, start, heads)) * dt
    earlier = lax.broadcasted_iota(jnp.int32, (tokens, tokens), 0)
    later = lax.broadcasted_iota(jnp.int32, (tokens, tokens), 1)
    upto = (earlier <= later).astype(F32)
    cum = jnp.dot(rate, upto, precision=lax.Precision.HIGHEST, preferred_element_type=F32)
    return dt, cum


def scales(head_dim, dt_raw, a_log, scale):
    dt, cum = rates(dt_raw[...], a_log[...], 0)
    end = cum[:, -1:]
    scale[...] = spread(jnp.exp(end - cum) * dt, head_dim, 2)
    return spread_row(jnp.exp(end), head_dim)


def emit_states(group, low, high, x, tail_x, bc, tail_bc, taps_x, taps_bc, scale, emit):
    state_dim = bc.shape[2] // 2
    b = conv_act(
        bc[:, :, :state_dim].astype(F32)[:, group], tail_bc, taps_bc[:, :, :state_dim][:, group]
    )
    b_t = b.astype(F32).T.astype(BF16)
    for at in range(low, high, CHUNK):
        cut = slice(at, at + CHUNK)
        act = conv_act(x[:, cut].astype(F32), tail_x(cut), taps_x[:, cut])
        scaled = (scale[:, cut] * act.astype(F32)).astype(BF16)
        emit(slice(at - low, at - low + CHUNK), jnp.dot(b_t, scaled, preferred_element_type=F32))


def head_rows(group, low, high, x, bc, taps_x, taps_bc, scale, out):
    state_dim = bc.shape[2] // 2

    def emit(here, total):
        out[:state_dim, here] = total.astype(BF16)

    emit_states(
        group, low, high, x, lambda cut: jnp.zeros((RIM, CHUNK), F32),
        bc, jnp.zeros((RIM, state_dim), F32), taps_x, taps_bc, scale, emit,
    )


def first_kernel(
    group, low, high, active, x_hbm, bc_hbm, taps_x_hbm, taps_bc_hbm, dt_hbm, a_hbm,
    out, scale, x, bc, taps_x, taps_bc, dt_raw, a_log, sems,
):
    tokens, width = x.shape
    groups, both = bc.shape[1:]

    @pl.when(active[0] == 1)
    def _():
        pairs = [
            (dt_hbm, dt_raw), (a_hbm, a_log), (x_hbm, x), (bc_hbm, bc),
            (taps_x_hbm, taps_x), (taps_bc_hbm, taps_bc),
        ]
        copies = [pltpu.make_async_copy(*pair, sems.at[i]) for i, pair in enumerate(pairs)]
        for copy in copies:
            copy.start()
        for copy in copies[:2]:
            copy.wait()
        scales(width // dt_raw.shape[0], dt_raw, a_log, scale)
        for copy in copies[2:]:
            copy.wait()
        state_dim, step = both // 2, high - low
        keep = taps_x.shape[0] - 1
        extra = out.shape[0] - state_dim
        last_bc = bc[tokens - 2 * RIM :].astype(F32)[-RIM:]
        last = [x[tokens - 2 * RIM :, :].astype(F32)[-RIM:]] + [last_bc[:, g] for g in range(groups)]
        length = width + groups * both
        last.append(jnp.zeros((RIM, -length % step + step), F32))
        last = jnp.concatenate(last, axis=1)
        at = lax.broadcasted_iota(jnp.int32, (extra, step), 0)
        below = jnp.zeros((extra, step), F32)
        fill = jnp.zeros((extra - RIM, step), F32)
        for k in range(-(-length // step)):
            block = jnp.concatenate([last[:, k * step : (k + 1) * step], fill], axis=0)
            block = pltpu.roll(block, (keep * (k + 1) - RIM) % extra, 0)
            below = jnp.where((at >= keep * k) & (at < keep * (k + 1)), block, below)
        out[state_dim:, :] = below.astype(BF16)
        head_rows(group, low, high, x, bc, taps_x, taps_bc, scale, out)


def next_kernel(group, low, high, active, _, x, bc, taps_x, taps_bc, scale, out):
    @pl.when(active[0] == 1)
    def _():
        head_rows(group, low, high, x, bc, taps_x, taps_bc, scale, out)


def prepare_kernel(cuts, _, x, bc, dt_raw, a_log, gain, pack, gain_out, scale, *decays):
    tokens, width = x.shape
    groups, both = bc.shape[1:]
    pack[:, :width] = x[tokens - 2 * RIM :, :].astype(F32)[-RIM:].astype(BF16)
    last_bc = bc[tokens - 2 * RIM :].astype(F32)[-RIM:]
    for g in range(groups):
        pack[:, width + g * both : width + (g + 1) * both] = last_bc[:, g].astype(BF16)
    gain_out[...] = gain[...]
    row = scales(width // dt_raw.shape[0], dt_raw, a_log, scale)
    for decay, (_, low, high) in zip(decays, cuts):
        decay[...] = row[:, low:high]


def rows_before(rows, begin, stop, keep, state_dim):
    if rows.shape[0] == RIM:
        return rows[:, begin:stop].astype(F32)
    step = rows.shape[1]
    below = rows[state_dim:, begin % step : begin % step + stop - begin].astype(F32)
    return pltpu.roll(below, (RIM - keep * (begin // step + 1)) % below.shape[0], 0)[:RIM]


def later_kernel(group, low, high, active, rows, _, x, bc, taps_x, taps_bc, scale, state):
    both = bc.shape[2]
    state_dim = both // 2
    keep = taps_x.shape[0] - 1

    @pl.when(active[0] == 1)
    def _():
        def emit(here, total):
            state[:, here] = total

        at = x.shape[1] + group * both
        emit_states(
            group, low, high, x,
            lambda cut: rows_before(rows, cut.start, cut.stop, keep, state_dim),
            bc, rows_before(rows, at, at + state_dim, keep, state_dim),
            taps_x, taps_bc, scale, emit,
        )


def intra_kernel(count, _, *refs):
    sources, refs = refs[:count], refs[count:]
    x, bc, z, taps_x, taps_bc, dt_raw, a_log, d_skip, y_part, lead, c_act, wide = refs
    tokens, width = x.shape
    groups, both = bc.shape[1:]
    state_dim = both // 2
    keep = taps_x.shape[0] - 1
    cols = width // groups
    heads = dt_raw.shape[0] // groups
    head_dim = cols // heads
    dt, cum = rates(dt_raw[...], a_log[...], 0)
    cum_t = cum.T
    leading = jnp.exp(cum)
    skip = spread_row(as_column(d_skip[...], 0, groups * heads), head_dim)
    t_at = lax.broadcasted_iota(jnp.int32, (tokens, tokens), 0)
    s_at = lax.broadcasted_iota(jnp.int32, (tokens, tokens), 1)
    pair = 2 * head_dim

    def before(begin, stop):
        found = [rows_before(rows, begin, stop, keep, state_dim) for rows in sources]
        return sum(found[1:], found[0])

    for g in range(groups):
        at = width + g * both
        tail_bc = jnp.concatenate(
            [before(at, at + state_dim), before(at + state_dim, at + both)], axis=1
        )
        bc_act = conv_act(bc[...].astype(F32)[:, g], tail_bc, taps_bc[...][:, g])
        b, c = bc_act[:, :state_dim], bc_act[:, state_dim:]
        c_act[:, g * state_dim : (g + 1) * state_dim] = c
        inner = lax.dot_general(c, b, (((1,), (1,)), ((), ())), preferred_element_type=F32)
        inner = jnp.where(t_at >= s_at, inner, 0.0)
        wide[...] = spread(leading[g * heads : (g + 1) * heads], head_dim, 2)
        for first in range(0, heads, 2):
            here = slice(first * head_dim, first * head_dim + pair)
            cut = slice(g * cols + here.start, g * cols + here.stop)
            act = conv_act(x[:, cut].astype(F32), before(cut.start, cut.stop), taps_x[:, cut])
            lane = lax.broadcasted_iota(jnp.int32, act.shape, 1)
            full = act.astype(F32)
            blocks = jnp.concatenate(
                [jnp.where(lane < head_dim, full, 0.0), jnp.where(lane < head_dim, 0.0, full)],
                axis=0,
            ).astype(BF16)
            weights = []
            for h in (g * heads + first, g * heads + first + 1):
                gap = jnp.minimum(cum_t[:, h : h + 1] - cum[h : h + 1, :], 0.0)
                weights.append((jnp.exp(gap) * dt[h : h + 1, :] * inner).astype(BF16))
            y = jnp.dot(jnp.concatenate(weights, axis=1), blocks, preferred_element_type=F32)
            gate = silu(z[:, cut].astype(F32))
            y_part[:, cut] = (y + skip[:, cut] * full) * gate
            lead[:, cut] = wide[:, here] * gate


def gated_slice(c, y_part, lead, arrived):
    state = arrived[0][: c.shape[1]]
    for more in arrived[1:]:
        state = state + more[...]
    return y_part[...] + lead[...] * jnp.dot(c[...], state, preferred_element_type=F32)


def gated_kernel(c, y_part, lead, *refs):
    refs[-1][...] = gated_slice(c, y_part, lead, refs[:-1])


def output_kernel(ready, seen, c, y_part, lead, gain, *refs):
    gated = [v[...] for v in refs[:ready]]
    gated.append(gated_slice(c, y_part, lead, refs[ready : ready + seen]))
    gated = jnp.concatenate(gated, axis=1)
    mean_sq = jnp.mean(gated * gated, axis=1, keepdims=True)
    refs[-1][...] = (gated * lax.rsqrt(mean_sq + EPS) * gain[...]).astype(BF16)


def params(mib):
    return pltpu.CompilerParams(vmem_limit_bytes=mib * 1024 * 1024)


def doubling(state, decay, devices):
    def moved(value, distance):
        return lax.ppermute(value, "seq", [(i, i + distance) for i in range(devices - distance)])

    total, decay = moved(state.astype(BF16), 1), moved(decay, 1)
    distance = 1
    while distance < devices - 1:
        came = moved(total, distance)
        total = (decay * came.astype(F32) + total.astype(F32)).astype(BF16)
        decay = decay * moved(decay, distance)
        distance *= 2
    return total


def seen_last(arrived, cuts, group):
    return [seen for (g, _, _), seen in zip(cuts, arrived) if g == group][-1]


def shards(x_in, bc_in, z_in, dt_raw, conv_x, conv_bc, a_log, d_skip, norm_gain):
    tokens, width = x_in.shape
    groups, both = bc_in.shape[1:]
    state_dim = both // 2
    heads = dt_raw.shape[1]
    head_dim = width // heads
    cols = width // groups
    devices = lax.axis_size("seq")
    place = lax.axis_index("seq")
    cuts = []
    for g in range(groups):
        parts = FIRST_PARTS if g == 0 else OTHER_PARTS
        edges = [g * cols + cols * sum(parts[:i]) // sum(parts) for i in range(len(parts) + 1)]
        cuts += [(g, low, high) for low, high in zip(edges[:-1], edges[1:])]

    taps = conv_x.shape[0]
    dt_t = dt_raw.T
    a_row = a_log.reshape(1, heads)
    d_row = d_skip.reshape(1, heads)
    gain = norm_gain.reshape(1, width)
    sources = [x_in, bc_in, conv_x, conv_bc]
    operands = sources + [dt_t, a_row]
    pinned = [pltpu.with_memory_space_constraint(v, pltpu.HBM) for v in operands]
    landed = [pltpu.VMEM(v.shape, v.dtype) for v in operands]
    scale_shape = jax.ShapeDtypeStruct((tokens, width), F32)
    scalar = pl.BlockSpec(memory_space=pltpu.SMEM)
    in_vmem = pl.BlockSpec(memory_space=pltpu.VMEM)
    anywhere = pl.BlockSpec(memory_space=pl.ANY)
    in_hbm = [pl.BlockSpec(memory_space=pltpu.HBM)] * len(operands)

    def column(height, wide, at):
        return pl.BlockSpec((height, wide), lambda i: (0, at))

    def slab(low, high):
        return pl.BlockSpec((pl.Element(tokens), pl.Element(high - low)), lambda i: (0, low))

    def whole(array):
        return pl.BlockSpec(array.shape, lambda i: (0,) * len(array.shape))

    def here(condition):
        return condition.astype(jnp.int32).reshape(1)

    def shifted(value, route):
        return lax.ppermute(value, "seq", route)

    def first_states(group, low, high):
        blocks = -(-(width + groups * both) // (high - low))
        extra = -(-(taps - 1) * blocks // (2 * RIM)) * 2 * RIM
        return pl.pallas_call(
            functools.partial(first_kernel, group, low, high),
            out_shape=[jax.ShapeDtypeStruct((state_dim + extra, high - low), BF16), scale_shape],
            in_specs=[scalar] + in_hbm,
            scratch_shapes=landed + [pltpu.SemaphoreType.DMA((len(operands),))],
            compiler_params=params(16),
            name="first_states",
        )(here(place == 0), *pinned)

    def next_states(token, scale, group, low, high):
        return pl.pallas_call(
            functools.partial(next_kernel, group, low, high),
            out_shape=jax.ShapeDtypeStruct((state_dim, high - low), BF16),
            in_specs=[scalar, anywhere] + [in_vmem] * (len(sources) + 1),
            compiler_params=params(16),
            name="next_states",
        )(here(place == 0), token, *sources, scale)

    def prepared(token):
        return pl.pallas_call(
            functools.partial(prepare_kernel, cuts),
            out_shape=[
                jax.ShapeDtypeStruct((RIM, width + groups * both), BF16),
                jax.ShapeDtypeStruct((1, width), F32),
                scale_shape,
            ]
            + [jax.ShapeDtypeStruct((1, high - low), F32) for _, low, high in cuts],
            in_specs=[anywhere] + [in_vmem] * 5,
            compiler_params=params(16),
            name="prepared",
        )(token, x_in, bc_in, dt_t, a_row, gain)

    def later_states(condition, rows, token, scale, group, low, high):
        return pl.pallas_call(
            functools.partial(later_kernel, group, low, high),
            out_shape=jax.ShapeDtypeStruct((state_dim, high - low), F32),
            in_specs=[scalar, in_vmem, anywhere] + [in_vmem] * (len(sources) + 1),
            compiler_params=params(16),
            name="later_states",
        )(here(condition), rows, token, *sources, scale)

    along = [(i, i + 1) for i in range(devices - 1)]
    def intra(token, befores):
        return pl.pallas_call(
            functools.partial(intra_kernel, len(befores)),
            out_shape=[
                scale_shape, scale_shape, jax.ShapeDtypeStruct((tokens, groups * state_dim), BF16)
            ],
            in_specs=[anywhere] + [in_vmem] * (len(befores) + 8),
            scratch_shapes=[pltpu.VMEM((tokens, cols), F32)],
            compiler_params=params(24),
            cost_estimate=pl.CostEstimate(
                flops=4 * tokens * tokens * width,
                bytes_accessed=12 * tokens * width,
                transcendentals=tokens * tokens * heads,
            ),
            name="intra",
        )(token, *befores, x_in, bc_in, z_in, conv_x, conv_bc, dt_t, a_row, d_row)

    part = None
    if devices <= CHAIN_MOST:
        first, scale = first_states(*cuts[0])
        sent = [first, next_states(first, scale, *cuts[1])]
        last, gain, scale_own, *decays = prepared(sent[-1])
        token = last
        for cut in cuts[2:]:
            sent.append(next_states(token, scale, *cut))
            token = sent[-1]
        soon = along[1 : max(devices - 2, 1)]
        late = along[max(devices - 2, 1) :]
        befores = [shifted(last, soon)] if soon else []
        arrived = [[shifted(v, along[:1])] for v in sent]
        befores.append(arrived[0][0])
        rows, token = arrived[0][0], last
        for hop in range(1, devices - 1):
            runs = place == 1 if hop == 1 else (place >= 2) & (place < devices - 1)
            after = token
            for i, cut in enumerate(cuts):
                if hop <= 2:
                    made = later_states(runs, rows, after, scale_own, *cut)
                    states = [made] if i == 0 else states + [made]
                early = ()
                if hop == devices - 2 and hop > 1 and i == 1:
                    part = intra(token, befores)
                    early = (part[0],)
                if hop == devices - 2 and hop > 1 and i == len(cuts) - 1:
                    early = (arrived[0][-1],)
                before, *_ = lax.optimization_barrier((arrived[i][-1], token) + early)
                joined = decays[i] * before[:state_dim].astype(F32) + states[i]
                token = joined.astype(BF16)
                after = token if hop == 1 else after
                arrived[i].append(shifted(token, along[hop : hop + 1]))
            if hop == 1 and late:
                moved, _ = lax.optimization_barrier((last, token))
                befores.append(shifted(moved, late))
            rows = befores[0]
    else:
        last, gain, scale, *decays = prepared(a_row)
        befores = [shifted(last, along)]
        arrived = []
        for decay, cut in zip(decays, cuts):
            state = later_states(place >= 0, befores[0], a_row, scale, *cut)
            arrived.append([doubling(state, decay, devices)])
    y_part, lead, c_act = part or intra(a_row, befores)

    out = None
    for g in range(groups):
        ready = []
        for (group, low, high), seen in zip(cuts, arrived):
            if group != g:
                continue
            inputs = [c_act, y_part, lead]
            specs = [column(tokens, state_dim, g)] + [slab(low, high)] * 2
            if high < (g + 1) * cols:
                ready.append(
                    pl.pallas_call(
                        gated_kernel,
                        out_shape=jax.ShapeDtypeStruct((tokens, high - low), F32),
                        in_specs=specs + [whole(v) for v in seen],
                        out_specs=column(tokens, high - low, 0),
                        grid=(1,),
                        compiler_params=params(16),
                        name="gated",
                    )(*inputs, *seen)
                )
        inputs += [gain] + ready + seen_last(arrived, cuts, g)
        specs += [column(1, cols, g)] + [whole(v) for v in ready + seen_last(arrived, cuts, g)]
        aliases = {}
        if out is not None:
            aliases = {len(inputs): 0}
            inputs.append(out)
            specs.append(pl.BlockSpec(memory_space=pl.ANY))
        out = pl.pallas_call(
            functools.partial(output_kernel, len(ready), len(arrived[0])),
            out_shape=jax.ShapeDtypeStruct((tokens, width), BF16),
            in_specs=specs,
            out_specs=column(tokens, cols, g),
            grid=(1,),
            input_output_aliases=aliases,
            compiler_params=params(32),
            name="outputs",
        )(*inputs)
    return out


def solution(mesh):
    return jax.shard_map(
        shards,
        mesh=mesh,
        in_specs=(
            P(("groups", "seq"), "head"),
            P(("groups", "seq"), "head", None),
            P(("groups", "seq"), "head"),
            P(("groups", "seq"), "head"),
            P(None, "head"),
            P(None, "head", None),
            P("head"),
            P("head"),
            P("head"),
        ),
        out_specs=P(("groups", "seq"), "head"),
        check_vma=False,
    )
```

```python
import functools

import jax
import jax.numpy as jnp
from jax import lax
from jax.experimental import pallas as pl
from jax.experimental.pallas import tpu as pltpu
from jax.sharding import PartitionSpec as P

EPS = 1e-05
F32 = jnp.float32
BF16 = jnp.bfloat16
CHAIN_MOST = 4
FIRST_PARTS = (3, 5)
OTHER_PARTS = (1, 1)
CHUNK = 128
RIM = 8


def silu(u):
    return 0.5 * u * (1.0 + jnp.tanh(0.5 * u))


def softplus(v):
    return jnp.maximum(v, 0.0) + jnp.log1p(jnp.exp(-jnp.abs(v)))


def halves(v, count, axis):
    parts = []
    for _ in range(count - 1):
        part = v.astype(BF16)
        parts.append(part)
        v = v - part.astype(F32)
    parts.append(v.astype(BF16))
    return jnp.concatenate(parts, axis=axis)


def spread(per_head, head_dim, count):
    heads = per_head.shape[0]
    rows = lax.broadcasted_iota(jnp.int32, (heads * count, heads * head_dim), 0)
    cols = lax.broadcasted_iota(jnp.int32, (heads * count, heads * head_dim), 1)
    pick = (rows % heads == cols // head_dim).astype(F32).astype(BF16)
    return lax.dot_general(
        halves(per_head, count, 0), pick, (((0,), (0,)), ((), ())), preferred_element_type=F32
    )


def spread_row(column, head_dim):
    heads = column.shape[0]
    rows = lax.broadcasted_iota(jnp.int32, (heads, heads * head_dim), 0)
    cols = lax.broadcasted_iota(jnp.int32, (heads, heads * head_dim), 1)
    return jnp.sum(jnp.where(rows == cols // head_dim, column, 0.0), axis=0, keepdims=True)


def as_column(row, start, heads):
    every = row.shape[1]
    rows = lax.broadcasted_iota(jnp.int32, (heads, every), 0)
    cols = lax.broadcasted_iota(jnp.int32, (heads, every), 1)
    return jnp.sum(jnp.where(cols == rows + start, row, 0.0), axis=1, keepdims=True)


def conv_act(series, tail, taps):
    count = taps.shape[0]
    above = tail.shape[0]
    padded = jnp.concatenate([tail, series], axis=0)
    total = taps[count - 1 : count] * series
    for back in range(1, count):
        total = total + taps[count - 1 - back : count - back] * pltpu.roll(padded, back, 0)[above:]
    return silu(total).astype(BF16)


def rates(dt_raw, a_log_row, start):
    heads, tokens = dt_raw.shape
    dt = softplus(dt_raw)
    rate = -jnp.exp(as_column(a_log_row, start, heads)) * dt
    earlier = lax.broadcasted_iota(jnp.int32, (tokens, tokens), 0)
    later = lax.broadcasted_iota(jnp.int32, (tokens, tokens), 1)
    upto = (earlier <= later).astype(F32)
    cum = jnp.dot(rate, upto, precision=lax.Precision.HIGHEST, preferred_element_type=F32)
    return dt, cum


def scales(head_dim, dt_raw, a_log, scale):
    dt, cum = rates(dt_raw[...], a_log[...], 0)
    end = cum[:, -1:]
    scale[...] = spread(jnp.exp(end - cum) * dt, head_dim, 2)
    return spread_row(jnp.exp(end), head_dim)


def emit_states(group, low, high, x, tail_x, bc, tail_bc, taps_x, taps_bc, scale, emit):
    state_dim = bc.shape[2] // 2
    b = conv_act(
        bc[:, :, :state_dim].astype(F32)[:, group], tail_bc, taps_bc[:, :, :state_dim][:, group]
    )
    b_t = b.astype(F32).T.astype(BF16)
    for at in range(low, high, CHUNK):
        cut = slice(at, at + CHUNK)
        act = conv_act(x[:, cut].astype(F32), tail_x(cut), taps_x[:, cut])
        scaled = (scale[:, cut] * act.astype(F32)).astype(BF16)
        emit(slice(at - low, at - low + CHUNK), jnp.dot(b_t, scaled, preferred_element_type=F32))


def head_rows(group, low, high, x, bc, taps_x, taps_bc, scale, out):
    state_dim = bc.shape[2] // 2

    def emit(here, total):
        out[:state_dim, here] = total.astype(BF16)

    emit_states(
        group, low, high, x, lambda cut: jnp.zeros((RIM, CHUNK), F32),
        bc, jnp.zeros((RIM, state_dim), F32), taps_x, taps_bc, scale, emit,
    )


def first_kernel(
    group, low, high, active, x_hbm, bc_hbm, taps_x_hbm, taps_bc_hbm, dt_hbm, a_hbm,
    out, scale, x, bc, taps_x, taps_bc, dt_raw, a_log, sems,
):
    tokens, width = x.shape
    groups, both = bc.shape[1:]

    @pl.when(active[0] == 1)
    def _():
        pairs = [
            (dt_hbm, dt_raw), (a_hbm, a_log), (x_hbm, x), (bc_hbm, bc),
            (taps_x_hbm, taps_x), (taps_bc_hbm, taps_bc),
        ]
        copies = [pltpu.make_async_copy(*pair, sems.at[i]) for i, pair in enumerate(pairs)]
        for copy in copies:
            copy.start()
        for copy in copies[:2]:
            copy.wait()
        scales(width // dt_raw.shape[0], dt_raw, a_log, scale)
        for copy in copies[2:]:
            copy.wait()
        state_dim, step = both // 2, high - low
        keep = taps_x.shape[0] - 1
        extra = out.shape[0] - state_dim
        last_bc = bc[tokens - 2 * RIM :].astype(F32)[-RIM:]
        last = [x[tokens - 2 * RIM :, :].astype(F32)[-RIM:]] + [last_bc[:, g] for g in range(groups)]
        length = width + groups * both
        last.append(jnp.zeros((RIM, -length % step + step), F32))
        last = jnp.concatenate(last, axis=1)
        at = lax.broadcasted_iota(jnp.int32, (extra, step), 0)
        below = jnp.zeros((extra, step), F32)
        fill = jnp.zeros((extra - RIM, step), F32)
        for k in range(-(-length // step)):
            block = jnp.concatenate([last[:, k * step : (k + 1) * step], fill], axis=0)
            block = pltpu.roll(block, (keep * (k + 1) - RIM) % extra, 0)
            below = jnp.where((at >= keep * k) & (at < keep * (k + 1)), block, below)
        out[state_dim:, :] = below.astype(BF16)
        head_rows(group, low, high, x, bc, taps_x, taps_bc, scale, out)


def next_kernel(group, low, high, active, _, x, bc, taps_x, taps_bc, scale, out):
    @pl.when(active[0] == 1)
    def _():
        head_rows(group, low, high, x, bc, taps_x, taps_bc, scale, out)


def prepare_kernel(cuts, _, x, bc, dt_raw, a_log, gain, pack, gain_out, scale, *decays):
    tokens, width = x.shape
    groups, both = bc.shape[1:]
    pack[:, :width] = x[tokens - 2 * RIM :, :].astype(F32)[-RIM:].astype(BF16)
    last_bc = bc[tokens - 2 * RIM :].astype(F32)[-RIM:]
    for g in range(groups):
        pack[:, width + g * both : width + (g + 1) * both] = last_bc[:, g].astype(BF16)
    gain_out[...] = gain[...]
    row = scales(width // dt_raw.shape[0], dt_raw, a_log, scale)
    for decay, (_, low, high) in zip(decays, cuts):
        decay[...] = row[:, low:high]


def rows_before(rows, begin, stop, keep, state_dim):
    if rows.shape[0] == RIM:
        return rows[:, begin:stop].astype(F32)
    step = rows.shape[1]
    below = rows[state_dim:, begin % step : begin % step + stop - begin].astype(F32)
    return pltpu.roll(below, (RIM - keep * (begin // step + 1)) % below.shape[0], 0)[:RIM]


def later_kernel(group, low, high, active, rows, _, x, bc, taps_x, taps_bc, scale, state):
    both = bc.shape[2]
    state_dim = both // 2
    keep = taps_x.shape[0] - 1

    @pl.when(active[0] == 1)
    def _():
        def emit(here, total):
            state[:, here] = total

        at = x.shape[1] + group * both
        emit_states(
            group, low, high, x,
            lambda cut: rows_before(rows, cut.start, cut.stop, keep, state_dim),
            bc, rows_before(rows, at, at + state_dim, keep, state_dim),
            taps_x, taps_bc, scale, emit,
        )


def intra_kernel(count, _, *refs):
    sources, refs = refs[:count], refs[count:]
    x, bc, z, taps_x, taps_bc, dt_raw, a_log, d_skip, y_part, lead, c_act, wide = refs
    tokens, width = x.shape
    groups, both = bc.shape[1:]
    state_dim = both // 2
    keep = taps_x.shape[0] - 1
    cols = width // groups
    heads = dt_raw.shape[0] // groups
    head_dim = cols // heads
    dt, cum = rates(dt_raw[...], a_log[...], 0)
    cum_t = cum.T
    leading = jnp.exp(cum)
    skip = spread_row(as_column(d_skip[...], 0, groups * heads), head_dim)
    t_at = lax.broadcasted_iota(jnp.int32, (tokens, tokens), 0)
    s_at = lax.broadcasted_iota(jnp.int32, (tokens, tokens), 1)
    pair = 2 * head_dim

    def before(begin, stop):
        found = [rows_before(rows, begin, stop, keep, state_dim) for rows in sources]
        return sum(found[1:], found[0])

    for g in range(groups):
        at = width + g * both
        tail_bc = jnp.concatenate(
            [before(at, at + state_dim), before(at + state_dim, at + both)], axis=1
        )
        bc_act = conv_act(bc[...].astype(F32)[:, g], tail_bc, taps_bc[...][:, g])
        b, c = bc_act[:, :state_dim], bc_act[:, state_dim:]
        c_act[:, g * state_dim : (g + 1) * state_dim] = c
        inner = lax.dot_general(c, b, (((1,), (1,)), ((), ())), preferred_element_type=F32)
        inner = jnp.where(t_at >= s_at, inner, 0.0)
        wide[...] = spread(leading[g * heads : (g + 1) * heads], head_dim, 2)
        for first in range(0, heads, 2):
            here = slice(first * head_dim, first * head_dim + pair)
            cut = slice(g * cols + here.start, g * cols + here.stop)
            act = conv_act(x[:, cut].astype(F32), before(cut.start, cut.stop), taps_x[:, cut])
            lane = lax.broadcasted_iota(jnp.int32, act.shape, 1)
            full = act.astype(F32)
            blocks = jnp.concatenate(
                [jnp.where(lane < head_dim, full, 0.0), jnp.where(lane < head_dim, 0.0, full)],
                axis=0,
            ).astype(BF16)
            weights = []
            for h in (g * heads + first, g * heads + first + 1):
                gap = jnp.minimum(cum_t[:, h : h + 1] - cum[h : h + 1, :], 0.0)
                weights.append((jnp.exp(gap) * dt[h : h + 1, :] * inner).astype(BF16))
            y = jnp.dot(jnp.concatenate(weights, axis=1), blocks, preferred_element_type=F32)
            gate = silu(z[:, cut].astype(F32))
            y_part[:, cut] = (y + skip[:, cut] * full) * gate
            lead[:, cut] = wide[:, here] * gate


def gated_slice(c, y_part, lead, arrived):
    state = arrived[0][: c.shape[1]]
    for more in arrived[1:]:
        state = state + more[...]
    return y_part[...] + lead[...] * jnp.dot(c[...], state, preferred_element_type=F32)


def gated_kernel(c, y_part, lead, *refs):
    refs[-1][...] = gated_slice(c, y_part, lead, refs[:-1])


def output_kernel(ready, seen, c, y_part, lead, gain, *refs):
    gated = [v[...] for v in refs[:ready]]
    gated.append(gated_slice(c, y_part, lead, refs[ready : ready + seen]))
    gated = jnp.concatenate(gated, axis=1)
    mean_sq = jnp.mean(gated * gated, axis=1, keepdims=True)
    refs[-1][...] = (gated * lax.rsqrt(mean_sq + EPS) * gain[...]).astype(BF16)


def params(mib):
    return pltpu.CompilerParams(vmem_limit_bytes=mib * 1024 * 1024)


def doubling(state, decay, devices):
    def moved(value, distance):
        return lax.ppermute(value, "seq", [(i, i + distance) for i in range(devices - distance)])

    total, decay = moved(state.astype(BF16), 1), moved(decay, 1)
    distance = 1
    while distance < devices - 1:
        came = moved(total, distance)
        total = (decay * came.astype(F32) + total.astype(F32)).astype(BF16)
        decay = decay * moved(decay, distance)
        distance *= 2
    return total


def seen_last(arrived, cuts, group):
    return [seen for (g, _, _), seen in zip(cuts, arrived) if g == group][-1]


def shards(x_in, bc_in, z_in, dt_raw, conv_x, conv_bc, a_log, d_skip, norm_gain):
    tokens, width = x_in.shape
    groups, both = bc_in.shape[1:]
    state_dim = both // 2
    heads = dt_raw.shape[1]
    head_dim = width // heads
    cols = width // groups
    devices = lax.axis_size("seq")
    place = lax.axis_index("seq")
    cuts = []
    for g in range(groups):
        parts = FIRST_PARTS if g == 0 else OTHER_PARTS
        edges = [g * cols + cols * sum(parts[:i]) // sum(parts) for i in range(len(parts) + 1)]
        cuts += [(g, low, high) for low, high in zip(edges[:-1], edges[1:])]

    taps = conv_x.shape[0]
    dt_t = dt_raw.T
    a_row = a_log.reshape(1, heads)
    d_row = d_skip.reshape(1, heads)
    gain = norm_gain.reshape(1, width)
    sources = [x_in, bc_in, conv_x, conv_bc]
    operands = sources + [dt_t, a_row]
    pinned = [pltpu.with_memory_space_constraint(v, pltpu.HBM) for v in operands]
    landed = [pltpu.VMEM(v.shape, v.dtype) for v in operands]
    scale_shape = jax.ShapeDtypeStruct((tokens, width), F32)
    scalar = pl.BlockSpec(memory_space=pltpu.SMEM)
    in_vmem = pl.BlockSpec(memory_space=pltpu.VMEM)
    anywhere = pl.BlockSpec(memory_space=pl.ANY)
    in_hbm = [pl.BlockSpec(memory_space=pltpu.HBM)] * len(operands)

    def column(height, wide, at):
        return pl.BlockSpec((height, wide), lambda i: (0, at))

    def slab(low, high):
        return pl.BlockSpec((pl.Element(tokens), pl.Element(high - low)), lambda i: (0, low))

    def whole(array):
        return pl.BlockSpec(array.shape, lambda i: (0,) * len(array.shape))

    def here(condition):
        return condition.astype(jnp.int32).reshape(1)

    def shifted(value, route):
        return lax.ppermute(value, "seq", route)

    def first_states(group, low, high):
        blocks = -(-(width + groups * both) // (high - low))
        extra = -(-(taps - 1) * blocks // (2 * RIM)) * 2 * RIM
        return pl.pallas_call(
            functools.partial(first_kernel, group, low, high),
            out_shape=[jax.ShapeDtypeStruct((state_dim + extra, high - low), BF16), scale_shape],
            in_specs=[scalar] + in_hbm,
            scratch_shapes=landed + [pltpu.SemaphoreType.DMA((len(operands),))],
            compiler_params=params(16),
            name="first_states",
        )(here(place == 0), *pinned)

    def next_states(token, scale, group, low, high):
        return pl.pallas_call(
            functools.partial(next_kernel, group, low, high),
            out_shape=jax.ShapeDtypeStruct((state_dim, high - low), BF16),
            in_specs=[scalar, anywhere] + [in_vmem] * (len(sources) + 1),
            compiler_params=params(16),
            name="next_states",
        )(here(place == 0), token, *sources, scale)

    def prepared(token):
        return pl.pallas_call(
            functools.partial(prepare_kernel, cuts),
            out_shape=[
                jax.ShapeDtypeStruct((RIM, width + groups * both), BF16),
                jax.ShapeDtypeStruct((1, width), F32),
                scale_shape,
            ]
            + [jax.ShapeDtypeStruct((1, high - low), F32) for _, low, high in cuts],
            in_specs=[anywhere] + [in_vmem] * 5,
            compiler_params=params(16),
            name="prepared",
        )(token, x_in, bc_in, dt_t, a_row, gain)

    def later_states(condition, rows, token, scale, group, low, high):
        return pl.pallas_call(
            functools.partial(later_kernel, group, low, high),
            out_shape=jax.ShapeDtypeStruct((state_dim, high - low), F32),
            in_specs=[scalar, in_vmem, anywhere] + [in_vmem] * (len(sources) + 1),
            compiler_params=params(16),
            name="later_states",
        )(here(condition), rows, token, *sources, scale)

    along = [(i, i + 1) for i in range(devices - 1)]
    def intra(token, befores):
        return pl.pallas_call(
            functools.partial(intra_kernel, len(befores)),
            out_shape=[
                scale_shape, scale_shape, jax.ShapeDtypeStruct((tokens, groups * state_dim), BF16)
            ],
            in_specs=[anywhere] + [in_vmem] * (len(befores) + 8),
            scratch_shapes=[pltpu.VMEM((tokens, cols), F32)],
            compiler_params=params(24),
            cost_estimate=pl.CostEstimate(
                flops=4 * tokens * tokens * width,
                bytes_accessed=12 * tokens * width,
                transcendentals=tokens * tokens * heads,
            ),
            name="intra",
        )(token, *befores, x_in, bc_in, z_in, conv_x, conv_bc, dt_t, a_row, d_row)

    if devices <= CHAIN_MOST:
        first, scale = first_states(*cuts[0])
        sent = [first, next_states(first, scale, *cuts[1])]
        last, gain, scale_own, *decays = prepared(sent[-1])
        token = last
        for cut in cuts[2:]:
            sent.append(next_states(token, scale, *cut))
            token = sent[-1]
        soon = along[1 : max(devices - 2, 1)]
        late = along[max(devices - 2, 1) :]
        befores = [shifted(last, soon)] if soon else []
        arrived = [[shifted(v, along[:1])] for v in sent]
        befores.append(arrived[0][0])
        rows, token = arrived[0][0], last
        for hop in range(1, devices - 1):
            runs = place == 1 if hop == 1 else (place >= 2) & (place < devices - 1)
            after = token
            for i, cut in enumerate(cuts):
                if hop <= 2:
                    made = later_states(runs, rows, after, scale_own, *cut)
                    states = [made] if i == 0 else states + [made]
                early = ()
                if hop == devices - 2 and hop > 1 and i == len(cuts) - 1:
                    early = (arrived[0][-1], befores[-1])
                before, *_ = lax.optimization_barrier((arrived[i][-1], token) + early)
                joined = decays[i] * before[:state_dim].astype(F32) + states[i]
                token = joined.astype(BF16)
                after = token if hop == 1 else after
                arrived[i].append(shifted(token, along[hop : hop + 1]))
            if hop == 1 and late:
                moved, _ = lax.optimization_barrier((last, token))
                befores.append(shifted(moved, late))
            rows = befores[0]
    else:
        last, gain, scale, *decays = prepared(a_row)
        befores = [shifted(last, along)]
        arrived = []
        for decay, cut in zip(decays, cuts):
            state = later_states(place >= 0, befores[0], a_row, scale, *cut)
            arrived.append([doubling(state, decay, devices)])
    y_part, lead, c_act = intra(a_row, befores)

    out = None
    for g in range(groups):
        ready = []
        for (group, low, high), seen in zip(cuts, arrived):
            if group != g:
                continue
            inputs = [c_act, y_part, lead]
            specs = [column(tokens, state_dim, g)] + [slab(low, high)] * 2
            if high < (g + 1) * cols:
                ready.append(
                    pl.pallas_call(
                        gated_kernel,
                        out_shape=jax.ShapeDtypeStruct((tokens, high - low), F32),
                        in_specs=specs + [whole(v) for v in seen],
                        out_specs=column(tokens, high - low, 0),
                        grid=(1,),
                        compiler_params=params(16),
                        name="gated",
                    )(*inputs, *seen)
                )
        inputs += [gain] + ready + seen_last(arrived, cuts, g)
        specs += [column(1, cols, g)] + [whole(v) for v in ready + seen_last(arrived, cuts, g)]
        aliases = {}
        if out is not None:
            aliases = {len(inputs): 0}
            inputs.append(out)
            specs.append(pl.BlockSpec(memory_space=pl.ANY))
        out = pl.pallas_call(
            functools.partial(output_kernel, len(ready), len(arrived[0])),
            out_shape=jax.ShapeDtypeStruct((tokens, width), BF16),
            in_specs=specs,
            out_specs=column(tokens, cols, g),
            grid=(1,),
            input_output_aliases=aliases,
            compiler_params=params(32),
            name="outputs",
        )(*inputs)
    return out


def solution(mesh):
    return jax.shard_map(
        shards,
        mesh=mesh,
        in_specs=(
            P(("groups", "seq"), "head"),
            P(("groups", "seq"), "head", None),
            P(("groups", "seq"), "head"),
            P(("groups", "seq"), "head"),
            P(None, "head"),
            P(None, "head", None),
            P("head"),
            P("head"),
            P("head"),
        ),
        out_specs=P(("groups", "seq"), "head"),
        check_vma=False,
    )
```

```python
import functools

import jax
import jax.numpy as jnp
from jax import lax
from jax.experimental import pallas as pl
from jax.experimental.pallas import tpu as pltpu
from jax.sharding import PartitionSpec as P

EPS = 1e-05
F32 = jnp.float32
BF16 = jnp.bfloat16
CHAIN_MOST = 4
PARTS = (3, 5, 4, 4)
CHUNK = 128
RIM = 8


def silu(u):
    return 0.5 * u * (1.0 + jnp.tanh(0.5 * u))


def softplus(v):
    return jnp.maximum(v, 0.0) + jnp.log1p(jnp.exp(-jnp.abs(v)))


def halves(v, count, axis):
    parts = []
    for _ in range(count - 1):
        part = v.astype(BF16)
        parts.append(part)
        v = v - part.astype(F32)
    parts.append(v.astype(BF16))
    return jnp.concatenate(parts, axis=axis)


def spread(per_head, head_dim, count):
    heads = per_head.shape[0]
    rows = lax.broadcasted_iota(jnp.int32, (heads * count, heads * head_dim), 0)
    cols = lax.broadcasted_iota(jnp.int32, (heads * count, heads * head_dim), 1)
    pick = (rows % heads == cols // head_dim).astype(F32).astype(BF16)
    return lax.dot_general(
        halves(per_head, count, 0), pick, (((0,), (0,)), ((), ())), preferred_element_type=F32
    )


def spread_row(column, head_dim):
    heads = column.shape[0]
    rows = lax.broadcasted_iota(jnp.int32, (heads, heads * head_dim), 0)
    cols = lax.broadcasted_iota(jnp.int32, (heads, heads * head_dim), 1)
    return jnp.sum(jnp.where(rows == cols // head_dim, column, 0.0), axis=0, keepdims=True)


def as_column(row, start, heads):
    every = row.shape[1]
    rows = lax.broadcasted_iota(jnp.int32, (heads, every), 0)
    cols = lax.broadcasted_iota(jnp.int32, (heads, every), 1)
    return jnp.sum(jnp.where(cols == rows + start, row, 0.0), axis=1, keepdims=True)


def conv_act(series, tail, taps):
    count = taps.shape[0]
    above = tail.shape[0]
    padded = jnp.concatenate([tail, series], axis=0)
    total = taps[count - 1 : count] * series
    for back in range(1, count):
        total = total + taps[count - 1 - back : count - back] * pltpu.roll(padded, back, 0)[above:]
    return silu(total).astype(BF16)


def rates(dt_raw, a_log_row, start):
    heads, tokens = dt_raw.shape
    dt = softplus(dt_raw)
    rate = -jnp.exp(as_column(a_log_row, start, heads)) * dt
    earlier = lax.broadcasted_iota(jnp.int32, (tokens, tokens), 0)
    later = lax.broadcasted_iota(jnp.int32, (tokens, tokens), 1)
    upto = (earlier <= later).astype(F32).astype(BF16)
    cum = jnp.dot(
        halves(rate, 3, 1), jnp.concatenate([upto] * 3, axis=0), preferred_element_type=F32
    )
    return dt, cum


def scales(groups, head_dim, dt_raw, a_log, scale):
    dt, cum = rates(dt_raw[...], a_log[...], 0)
    end = cum[:, -1:]
    tail_decay = jnp.exp(end - cum) * dt
    heads = dt.shape[0] // groups
    for g in range(groups):
        scale[:, g * heads * head_dim : (g + 1) * heads * head_dim] = spread(
            tail_decay[g * heads : (g + 1) * heads], head_dim, 2
        )
    return spread_row(jnp.exp(end), head_dim)


def by_group(low, high, cols):
    found = []
    while low < high:
        stop = min(high, (low // cols + 1) * cols)
        found.append((low // cols, low, stop))
        low = stop
    return found


def emit_states(low, high, x, tail_x, bc, tail_bc, taps_x, taps_bc, scale, emit):
    groups, both = bc.shape[1:]
    state_dim = both // 2
    for group, begin, stop in by_group(low, high, x.shape[1] // groups):
        b = conv_act(
            bc[:, :, :state_dim].astype(F32)[:, group],
            tail_bc(group),
            taps_bc[:, :, :state_dim][:, group],
        )
        b_t = b.astype(F32).T.astype(BF16)
        for at in range(begin, stop, CHUNK):
            cut = slice(at, at + CHUNK)
            act = conv_act(x[:, cut].astype(F32), tail_x(cut), taps_x[:, cut])
            scaled = (scale[:, cut] * act.astype(F32)).astype(BF16)
            here = slice(at - low, at - low + CHUNK)
            emit(here, jnp.dot(b_t, scaled, preferred_element_type=F32))


def head_rows(low, high, x, bc, taps_x, taps_bc, scale, out):
    state_dim = bc.shape[2] // 2

    def emit(here, total):
        out[:state_dim, here] = total.astype(BF16)

    emit_states(
        low, high, x, lambda cut: jnp.zeros((RIM, CHUNK), F32),
        bc, lambda group: jnp.zeros((RIM, state_dim), F32), taps_x, taps_bc, scale, emit,
    )


def first_kernel(
    low, high, active, x_hbm, bc_hbm, taps_x_hbm, taps_bc_hbm, dt_hbm, a_hbm,
    out, scale, x, bc, taps_x, taps_bc, dt_raw, a_log, sems,
):
    tokens, width = x.shape
    groups, both = bc.shape[1:]

    @pl.when(active[0] == 1)
    def _():
        pairs = [
            (dt_hbm, dt_raw), (a_hbm, a_log), (x_hbm, x), (bc_hbm, bc),
            (taps_x_hbm, taps_x), (taps_bc_hbm, taps_bc),
        ]
        copies = [pltpu.make_async_copy(*pair, sems.at[i]) for i, pair in enumerate(pairs)]
        for copy in copies:
            copy.start()
        for copy in copies[:2]:
            copy.wait()
        scales(groups, width // dt_raw.shape[0], dt_raw, a_log, scale)
        for copy in copies[2:]:
            copy.wait()
        state_dim, step = both // 2, high - low
        keep = taps_x.shape[0] - 1
        extra = out.shape[0] - state_dim
        last_bc = bc[tokens - 2 * RIM :].astype(F32)[-RIM:]
        last = [x[tokens - 2 * RIM :, :].astype(F32)[-RIM:]] + [last_bc[:, g] for g in range(groups)]
        length = width + groups * both
        last.append(jnp.zeros((RIM, -length % step + step), F32))
        last = jnp.concatenate(last, axis=1)
        at = lax.broadcasted_iota(jnp.int32, (extra, step), 0)
        below = jnp.zeros((extra, step), F32)
        fill = jnp.zeros((extra - RIM, step), F32)
        for k in range(-(-length // step)):
            block = jnp.concatenate([last[:, k * step : (k + 1) * step], fill], axis=0)
            block = pltpu.roll(block, (keep * (k + 1) - RIM) % extra, 0)
            below = jnp.where((at >= keep * k) & (at < keep * (k + 1)), block, below)
        out[state_dim:, :] = below.astype(BF16)
        head_rows(low, high, x, bc, taps_x, taps_bc, scale, out)


def next_kernel(low, high, active, _, x, bc, taps_x, taps_bc, scale, out):
    @pl.when(active[0] == 1)
    def _():
        head_rows(low, high, x, bc, taps_x, taps_bc, scale, out)


def prepare_kernel(cuts, _, x, bc, dt_raw, a_log, gain, pack, gain_out, scale, *decays):
    tokens, width = x.shape
    groups, both = bc.shape[1:]
    pack[:, :width] = x[tokens - 2 * RIM :, :].astype(F32)[-RIM:].astype(BF16)
    last_bc = bc[tokens - 2 * RIM :].astype(F32)[-RIM:]
    for g in range(groups):
        pack[:, width + g * both : width + (g + 1) * both] = last_bc[:, g].astype(BF16)
    gain_out[...] = gain[...]
    row = scales(groups, width // dt_raw.shape[0], dt_raw, a_log, scale)
    for decay, (low, high) in zip(decays, cuts):
        decay[...] = row[:, low:high]


def rows_before(rows, begin, stop, keep, state_dim):
    if rows.shape[0] == RIM:
        return rows[:, begin:stop].astype(F32)
    step = rows.shape[1]
    below = rows[state_dim:, begin % step : begin % step + stop - begin].astype(F32)
    return pltpu.roll(below, (RIM - keep * (begin // step + 1)) % below.shape[0], 0)[:RIM]


def later_kernel(low, high, active, rows, _, x, bc, taps_x, taps_bc, scale, state):
    both = bc.shape[2]
    state_dim = both // 2
    keep = taps_x.shape[0] - 1

    def before(begin, stop):
        return rows_before(rows, begin, stop, keep, state_dim)

    def tail_bc(group):
        at = x.shape[1] + group * both
        return before(at, at + state_dim)

    @pl.when(active[0] == 1)
    def _():
        def emit(here, total):
            state[:, here] = total

        emit_states(
            low, high, x, lambda cut: before(cut.start, cut.stop), bc, tail_bc,
            taps_x, taps_bc, scale, emit,
        )


def intra_kernel(count, _, *refs):
    sources, refs = refs[:count], refs[count:]
    x, bc, z, taps_x, taps_bc, dt_raw, a_log, d_skip, y_part, lead, c_act, wide = refs
    tokens, width = x.shape
    groups, both = bc.shape[1:]
    state_dim = both // 2
    keep = taps_x.shape[0] - 1
    cols = width // groups
    heads = dt_raw.shape[0] // groups
    head_dim = cols // heads
    dt, cum = rates(dt_raw[...], a_log[...], 0)
    cum_t = cum.T
    leading = jnp.exp(cum)
    skip = spread_row(as_column(d_skip[...], 0, groups * heads), head_dim)
    t_at = lax.broadcasted_iota(jnp.int32, (tokens, tokens), 0)
    s_at = lax.broadcasted_iota(jnp.int32, (tokens, tokens), 1)
    pair = 2 * head_dim

    def before(begin, stop):
        found = [rows_before(rows, begin, stop, keep, state_dim) for rows in sources]
        return sum(found[1:], found[0])

    for g in range(groups):
        at = width + g * both
        tail_bc = jnp.concatenate(
            [before(at, at + state_dim), before(at + state_dim, at + both)], axis=1
        )
        bc_act = conv_act(bc[...].astype(F32)[:, g], tail_bc, taps_bc[...][:, g])
        b, c = bc_act[:, :state_dim], bc_act[:, state_dim:]
        c_act[:, g * state_dim : (g + 1) * state_dim] = c
        inner = lax.dot_general(c, b, (((1,), (1,)), ((), ())), preferred_element_type=F32)
        inner = jnp.where(t_at >= s_at, inner, 0.0)
        wide[...] = spread(leading[g * heads : (g + 1) * heads], head_dim, 2)
        for first in range(0, heads, 2):
            here = slice(first * head_dim, first * head_dim + pair)
            cut = slice(g * cols + here.start, g * cols + here.stop)
            act = conv_act(x[:, cut].astype(F32), before(cut.start, cut.stop), taps_x[:, cut])
            lane = lax.broadcasted_iota(jnp.int32, act.shape, 1)
            full = act.astype(F32)
            blocks = jnp.concatenate(
                [jnp.where(lane < head_dim, full, 0.0), jnp.where(lane < head_dim, 0.0, full)],
                axis=0,
            ).astype(BF16)
            weights = []
            for h in (g * heads + first, g * heads + first + 1):
                gap = jnp.minimum(cum_t[:, h : h + 1] - cum[h : h + 1, :], 0.0)
                weights.append((jnp.exp(gap) * dt[h : h + 1, :] * inner).astype(BF16))
            y = jnp.dot(jnp.concatenate(weights, axis=1), blocks, preferred_element_type=F32)
            gate = silu(z[:, cut].astype(F32))
            y_part[:, cut] = (y + skip[:, cut] * full) * gate
            lead[:, cut] = wide[:, here] * gate


def gated_slice(low, which, c, y_part, lead, arrived):
    tokens, width = y_part.shape
    state_dim = arrived[-1].shape[0]
    size = arrived[-1].shape[1]
    state = jnp.zeros((state_dim, size), BF16)
    for i, came in enumerate(arrived):
        state = jnp.where(which[0] == i, came[...][:state_dim], state)
    pieces = []
    for group, begin, stop in by_group(low, low + size, width * state_dim // c.shape[1]):
        from_state = jnp.dot(
            c[:, group * state_dim : (group + 1) * state_dim],
            state[:, begin - low : stop - low],
            preferred_element_type=F32,
        )
        pieces.append(y_part[:, begin:stop] + lead[:, begin:stop] * from_state)
    return pieces


def gated_kernel(low, which, c, y_part, lead, *refs):
    at = 0
    for piece in gated_slice(low, which, c, y_part, lead, refs[:-1]):
        refs[-1][:, at : at + piece.shape[1]] = piece
        at += piece.shape[1]


def output_kernel(begin, ready, low, which, c, y_part, lead, gain, *refs):
    out, made, sems = refs[-3:]
    tokens, cols = made.shape
    pieces = [refs[i][:, a:b] for i, (a, b) in enumerate(ready)]
    if low is not None:
        arrived = refs[len(ready) : len(refs) - 3]
        if begin > 0:
            arrived = arrived[:-1]
        pieces += gated_slice(low, which, c, y_part, lead, arrived)
    total = jnp.zeros((tokens, 1), F32)
    for piece in pieces:
        total = total + jnp.sum(piece * piece, axis=1, keepdims=True)
    factor = lax.rsqrt(total / cols + EPS)
    copies = []
    at = 0
    for i, piece in enumerate(pieces):
        span = slice(at, at + piece.shape[1])
        made[:, span] = (piece * factor * gain[:, begin + at : begin + span.stop]).astype(BF16)
        copies.append(
            pltpu.make_async_copy(
                made.at[:, span], out.at[:, pl.ds(begin + at, piece.shape[1])], sems.at[i]
            )
        )
        copies[-1].start()
        at = span.stop
    for copy in copies:
        copy.wait()


def params(mib):
    return pltpu.CompilerParams(vmem_limit_bytes=mib * 1024 * 1024)


def doubling(state, decay, devices):
    def moved(value, distance):
        return lax.ppermute(value, "seq", [(i, i + distance) for i in range(devices - distance)])

    total, decay = moved(state.astype(BF16), 1), moved(decay, 1)
    distance = 1
    while distance < devices - 1:
        came = moved(total, distance)
        total = (decay * came.astype(F32) + total.astype(F32)).astype(BF16)
        decay = decay * moved(decay, distance)
        distance *= 2
    return total


def shards(x_in, bc_in, z_in, dt_raw, conv_x, conv_bc, a_log, d_skip, norm_gain):
    tokens, width = x_in.shape
    groups, both = bc_in.shape[1:]
    state_dim = both // 2
    heads = dt_raw.shape[1]
    head_dim = width // heads
    cols = width // groups
    devices = lax.axis_size("seq")
    place = lax.axis_index("seq")
    edges = [width * sum(PARTS[:i]) // sum(PARTS) for i in range(len(PARTS) + 1)]
    cuts = list(zip(edges[:-1], edges[1:]))

    taps = conv_x.shape[0]
    dt_t = dt_raw.T
    a_row = a_log.reshape(1, heads)
    d_row = d_skip.reshape(1, heads)
    gain = norm_gain.reshape(1, width)
    sources = [x_in, bc_in, conv_x, conv_bc]
    operands = sources + [dt_t, a_row]
    pinned = [pltpu.with_memory_space_constraint(v, pltpu.HBM) for v in operands]
    landed = [pltpu.VMEM(v.shape, v.dtype) for v in operands]
    scale_shape = jax.ShapeDtypeStruct((tokens, width), F32)
    scalar = pl.BlockSpec(memory_space=pltpu.SMEM)
    in_vmem = pl.BlockSpec(memory_space=pltpu.VMEM)
    anywhere = pl.BlockSpec(memory_space=pl.ANY)
    in_hbm = [pl.BlockSpec(memory_space=pltpu.HBM)] * len(operands)

    def here(condition):
        return condition.astype(jnp.int32).reshape(1)

    def shifted(value, route):
        return lax.ppermute(value, "seq", route)

    def first_states(low, high):
        blocks = -(-(width + groups * both) // (high - low))
        extra = -(-(taps - 1) * blocks // (2 * RIM)) * 2 * RIM
        return pl.pallas_call(
            functools.partial(first_kernel, low, high),
            out_shape=[jax.ShapeDtypeStruct((state_dim + extra, high - low), BF16), scale_shape],
            in_specs=[scalar] + in_hbm,
            scratch_shapes=landed + [pltpu.SemaphoreType.DMA((len(operands),))],
            compiler_params=params(16),
            name="first_states",
        )(here(place == 0), *pinned)

    def next_states(token, scale, low, high):
        return pl.pallas_call(
            functools.partial(next_kernel, low, high),
            out_shape=jax.ShapeDtypeStruct((state_dim, high - low), BF16),
            in_specs=[scalar, anywhere] + [in_vmem] * (len(sources) + 1),
            compiler_params=params(16),
            name="next_states",
        )(here(place == 0), token, *sources, scale)

    def prepared(token):
        return pl.pallas_call(
            functools.partial(prepare_kernel, cuts),
            out_shape=[
                jax.ShapeDtypeStruct((RIM, width + groups * both), BF16),
                jax.ShapeDtypeStruct((1, width), F32),
                scale_shape,
            ]
            + [jax.ShapeDtypeStruct((1, high - low), F32) for low, high in cuts],
            in_specs=[anywhere] + [in_vmem] * 5,
            compiler_params=params(16),
            name="prepared",
        )(token, x_in, bc_in, dt_t, a_row, gain)

    def later_states(condition, rows, token, scale, low, high):
        return pl.pallas_call(
            functools.partial(later_kernel, low, high),
            out_shape=jax.ShapeDtypeStruct((state_dim, high - low), F32),
            in_specs=[scalar, in_vmem, anywhere] + [in_vmem] * (len(sources) + 1),
            compiler_params=params(16),
            name="later_states",
        )(here(condition), rows, token, *sources, scale)

    along = [(i, i + 1) for i in range(devices - 1)]
    def intra(token, befores):
        return pl.pallas_call(
            functools.partial(intra_kernel, len(befores)),
            out_shape=[
                scale_shape, scale_shape, jax.ShapeDtypeStruct((tokens, groups * state_dim), BF16)
            ],
            in_specs=[anywhere] + [in_vmem] * (len(befores) + 8),
            scratch_shapes=[pltpu.VMEM((tokens, cols), F32)],
            compiler_params=params(24),
            cost_estimate=pl.CostEstimate(
                flops=4 * tokens * tokens * width,
                bytes_accessed=12 * tokens * width,
                transcendentals=tokens * tokens * heads,
            ),
            name="intra",
        )(token, *befores, x_in, bc_in, z_in, conv_x, conv_bc, dt_t, a_row, d_row)

    if devices <= CHAIN_MOST:
        first, scale = first_states(*cuts[0])
        sent = [first, next_states(first, scale, *cuts[1])]
        last, gain, scale_own, *decays = prepared(sent[-1])
        token = last
        for cut in cuts[2:]:
            sent.append(next_states(token, scale, *cut))
            token = sent[-1]
        soon = along[1 : max(devices - 2, 1)]
        late = along[max(devices - 2, 1) :]
        befores = [shifted(last, soon)] if soon else []
        arrived = [[shifted(v, along[:1])] for v in sent]
        befores.append(arrived[0][0])
        rows, token = arrived[0][0], last
        for hop in range(1, devices - 1):
            runs = place == 1 if hop == 1 else (place >= 2) & (place < devices - 1)
            after = token
            for i, cut in enumerate(cuts):
                if hop <= 2:
                    made = later_states(runs, rows, after, scale_own, *cut)
                    states = [made] if i == 0 else states + [made]
                early = ()
                if hop == devices - 2 and hop > 1 and i == len(cuts) - 1:
                    early = (arrived[0][-1], befores[-1])
                before, *_ = lax.optimization_barrier((arrived[i][-1], token) + early)
                joined = decays[i] * before[:state_dim].astype(F32) + states[i]
                token = joined.astype(BF16)
                after = token if hop == 1 else after
                arrived[i].append(shifted(token, along[hop : hop + 1]))
            if hop == 1 and late:
                moved, _ = lax.optimization_barrier((last, token))
                befores.append(shifted(moved, late))
            rows = befores[0]
        which = place - 1
    else:
        last, gain, scale, *decays = prepared(a_row)
        befores = [shifted(last, along)]
        arrived = []
        for decay, cut in zip(decays, cuts):
            state = later_states(place >= 0, befores[0], a_row, scale, *cut)
            arrived.append([doubling(state, decay, devices)])
        which = jnp.zeros_like(place)
    which = which.astype(jnp.int32).reshape(1)
    y_part, lead, c_act = intra(a_row, befores)

    common = [which, c_act, y_part, lead]
    common_specs = [scalar] + [in_vmem] * 3
    last_low, last_high = cuts[-1]
    ready = []
    for (low, high), seen in zip(cuts[:-1], arrived):
        ready.append(
            pl.pallas_call(
                functools.partial(gated_kernel, low),
                out_shape=jax.ShapeDtypeStruct((tokens, high - low), F32),
                in_specs=common_specs + [in_vmem] * len(seen),
                compiler_params=params(16),
                name="gated",
            )(*common, *seen)
        )
    out = None
    for g in range(groups):
        begin, stop = g * cols, (g + 1) * cols
        taken, spans = [], []
        for (low, high), v in zip(cuts[:-1], ready):
            if low < stop and high > begin:
                taken.append(v)
                spans.append((max(low, begin) - low, min(high, stop) - low))
        inputs = taken
        unready = None
        if last_low < stop:
            unready = last_low
            inputs = taken + arrived[-1]
        aliases = {}
        specs = common_specs + [in_vmem] * (1 + len(inputs))
        if out is not None:
            aliases = {len(common) + 1 + len(inputs): 0}
            inputs = inputs + [out]
            specs = specs + [anywhere]
        out = pl.pallas_call(
            functools.partial(output_kernel, begin, spans, unready),
            out_shape=jax.ShapeDtypeStruct((tokens, width), BF16),
            in_specs=specs,
            out_specs=anywhere,
            scratch_shapes=[
                pltpu.VMEM((tokens, cols), BF16),
                pltpu.SemaphoreType.DMA((len(cuts) + groups,)),
            ],
            input_output_aliases=aliases,
            compiler_params=params(16),
            name="outputs",
        )(*common, gain, *inputs)
    return out


def solution(mesh):
    return jax.shard_map(
        shards,
        mesh=mesh,
        in_specs=(
            P(("groups", "seq"), "head"),
            P(("groups", "seq"), "head", None),
            P(("groups", "seq"), "head"),
            P(("groups", "seq"), "head"),
            P(None, "head"),
            P(None, "head", None),
            P("head"),
            P("head"),
            P("head"),
        ),
        out_specs=P(("groups", "seq"), "head"),
        check_vma=False,
    )
```

```python
import functools

import jax
import jax.numpy as jnp
from jax import lax
from jax.experimental import pallas as pl
from jax.experimental.pallas import tpu as pltpu
from jax.sharding import PartitionSpec as P

EPS = 1e-05
F32 = jnp.float32
BF16 = jnp.bfloat16
CHAIN_MOST = 4
PARTS = (3, 5, 4, 4)
CHUNK = 128
RIM = 8


def silu(u):
    return 0.5 * u * (1.0 + jnp.tanh(0.5 * u))


def softplus(v):
    return jnp.maximum(v, 0.0) + jnp.log1p(jnp.exp(-jnp.abs(v)))


def halves(v, count, axis):
    parts = []
    for _ in range(count - 1):
        part = v.astype(BF16)
        parts.append(part)
        v = v - part.astype(F32)
    parts.append(v.astype(BF16))
    return jnp.concatenate(parts, axis=axis)


def spread(per_head, head_dim, count):
    heads = per_head.shape[0]
    rows = lax.broadcasted_iota(jnp.int32, (heads * count, heads * head_dim), 0)
    cols = lax.broadcasted_iota(jnp.int32, (heads * count, heads * head_dim), 1)
    pick = (rows % heads == cols // head_dim).astype(F32).astype(BF16)
    return lax.dot_general(
        halves(per_head, count, 0), pick, (((0,), (0,)), ((), ())), preferred_element_type=F32
    )


def spread_row(column, head_dim):
    heads = column.shape[0]
    rows = lax.broadcasted_iota(jnp.int32, (heads, heads * head_dim), 0)
    cols = lax.broadcasted_iota(jnp.int32, (heads, heads * head_dim), 1)
    return jnp.sum(jnp.where(rows == cols // head_dim, column, 0.0), axis=0, keepdims=True)


def as_column(row, start, heads):
    every = row.shape[1]
    rows = lax.broadcasted_iota(jnp.int32, (heads, every), 0)
    cols = lax.broadcasted_iota(jnp.int32, (heads, every), 1)
    return jnp.sum(jnp.where(cols == rows + start, row, 0.0), axis=1, keepdims=True)


def conv_act(series, tail, taps):
    count = taps.shape[0]
    above = tail.shape[0]
    padded = jnp.concatenate([tail, series], axis=0)
    total = taps[count - 1 : count] * series
    for back in range(1, count):
        total = total + taps[count - 1 - back : count - back] * pltpu.roll(padded, back, 0)[above:]
    return silu(total).astype(BF16)


def rates(dt_raw, a_log_row, start):
    heads, tokens = dt_raw.shape
    dt = softplus(dt_raw)
    rate = -jnp.exp(as_column(a_log_row, start, heads)) * dt
    earlier = lax.broadcasted_iota(jnp.int32, (tokens, tokens), 0)
    later = lax.broadcasted_iota(jnp.int32, (tokens, tokens), 1)
    upto = (earlier <= later).astype(F32).astype(BF16)
    cum = jnp.dot(
        halves(rate, 3, 1), jnp.concatenate([upto] * 3, axis=0), preferred_element_type=F32
    )
    return dt, cum


def scales(groups, head_dim, dt_raw, a_log, scale):
    dt, cum = rates(dt_raw[...], a_log[...], 0)
    end = cum[:, -1:]
    tail_decay = jnp.exp(end - cum) * dt
    heads = dt.shape[0] // groups
    for g in range(groups):
        scale[:, g * heads * head_dim : (g + 1) * heads * head_dim] = spread(
            tail_decay[g * heads : (g + 1) * heads], head_dim, 2
        )
    return spread_row(jnp.exp(end), head_dim)


def by_group(low, high, cols):
    found = []
    while low < high:
        stop = min(high, (low // cols + 1) * cols)
        found.append((low // cols, low, stop))
        low = stop
    return found


def emit_states(low, high, x, tail_x, bc, tail_bc, taps_x, taps_bc, scale, emit):
    groups, both = bc.shape[1:]
    state_dim = both // 2
    for group, begin, stop in by_group(low, high, x.shape[1] // groups):
        b = conv_act(
            bc[:, :, :state_dim].astype(F32)[:, group],
            tail_bc(group),
            taps_bc[:, :, :state_dim][:, group],
        )
        b_t = b.astype(F32).T.astype(BF16)
        for at in range(begin, stop, CHUNK):
            cut = slice(at, at + CHUNK)
            act = conv_act(x[:, cut].astype(F32), tail_x(cut), taps_x[:, cut])
            scaled = (scale[:, cut] * act.astype(F32)).astype(BF16)
            here = slice(at - low, at - low + CHUNK)
            emit(here, jnp.dot(b_t, scaled, preferred_element_type=F32))


def head_rows(low, high, x, bc, taps_x, taps_bc, scale, out):
    state_dim = bc.shape[2] // 2

    def emit(here, total):
        out[:state_dim, here] = total.astype(BF16)

    emit_states(
        low, high, x, lambda cut: jnp.zeros((RIM, CHUNK), F32),
        bc, lambda group: jnp.zeros((RIM, state_dim), F32), taps_x, taps_bc, scale, emit,
    )


def first_kernel(
    low, high, active, x_hbm, bc_hbm, taps_x_hbm, taps_bc_hbm, dt_hbm, a_hbm,
    out, scale, x, bc, taps_x, taps_bc, dt_raw, a_log, sems,
):
    tokens, width = x.shape
    groups, both = bc.shape[1:]

    @pl.when(active[0] == 1)
    def _():
        pairs = [
            (dt_hbm, dt_raw), (a_hbm, a_log), (x_hbm, x), (bc_hbm, bc),
            (taps_x_hbm, taps_x), (taps_bc_hbm, taps_bc),
        ]
        copies = [pltpu.make_async_copy(*pair, sems.at[i]) for i, pair in enumerate(pairs)]
        for copy in copies:
            copy.start()
        for copy in copies[:2]:
            copy.wait()
        scales(groups, width // dt_raw.shape[0], dt_raw, a_log, scale)
        for copy in copies[2:]:
            copy.wait()
        state_dim, step = both // 2, high - low
        keep = taps_x.shape[0] - 1
        extra = out.shape[0] - state_dim
        last_bc = bc[tokens - 2 * RIM :].astype(F32)[-RIM:]
        last = [x[tokens - 2 * RIM :, :].astype(F32)[-RIM:]] + [last_bc[:, g] for g in range(groups)]
        length = width + groups * both
        last.append(jnp.zeros((RIM, -length % step + step), F32))
        last = jnp.concatenate(last, axis=1)
        at = lax.broadcasted_iota(jnp.int32, (extra, step), 0)
        below = jnp.zeros((extra, step), F32)
        fill = jnp.zeros((extra - RIM, step), F32)
        for k in range(-(-length // step)):
            block = jnp.concatenate([last[:, k * step : (k + 1) * step], fill], axis=0)
            block = pltpu.roll(block, (keep * (k + 1) - RIM) % extra, 0)
            below = jnp.where((at >= keep * k) & (at < keep * (k + 1)), block, below)
        out[state_dim:, :] = below.astype(BF16)
        head_rows(low, high, x, bc, taps_x, taps_bc, scale, out)


def next_kernel(low, high, active, _, x, bc, taps_x, taps_bc, scale, out):
    @pl.when(active[0] == 1)
    def _():
        head_rows(low, high, x, bc, taps_x, taps_bc, scale, out)


def prepare_kernel(cuts, _, x, bc, dt_raw, a_log, gain, pack, gain_out, scale, *decays):
    tokens, width = x.shape
    groups, both = bc.shape[1:]
    pack[:, :width] = x[tokens - 2 * RIM :, :].astype(F32)[-RIM:].astype(BF16)
    last_bc = bc[tokens - 2 * RIM :].astype(F32)[-RIM:]
    for g in range(groups):
        pack[:, width + g * both : width + (g + 1) * both] = last_bc[:, g].astype(BF16)
    gain_out[...] = gain[...]
    row = scales(groups, width // dt_raw.shape[0], dt_raw, a_log, scale)
    for decay, (low, high) in zip(decays, cuts):
        decay[...] = row[:, low:high]


def rows_before(rows, begin, stop, keep, state_dim):
    if rows.shape[0] == RIM:
        return rows[:, begin:stop].astype(F32)
    step = rows.shape[1]
    below = rows[state_dim:, begin % step : begin % step + stop - begin].astype(F32)
    return pltpu.roll(below, (RIM - keep * (begin // step + 1)) % below.shape[0], 0)[:RIM]


def later_kernel(low, high, active, rows, _, x, bc, taps_x, taps_bc, scale, state):
    both = bc.shape[2]
    state_dim = both // 2
    keep = taps_x.shape[0] - 1

    def before(begin, stop):
        return rows_before(rows, begin, stop, keep, state_dim)

    def tail_bc(group):
        at = x.shape[1] + group * both
        return before(at, at + state_dim)

    @pl.when(active[0] == 1)
    def _():
        def emit(here, total):
            state[:, here] = total

        emit_states(
            low, high, x, lambda cut: before(cut.start, cut.stop), bc, tail_bc,
            taps_x, taps_bc, scale, emit,
        )


def gate_kernel(groups, _, z_hbm, dt_raw, a_log, gate, lead, dt_out, cum_out, z, sem):
    copy = pltpu.make_async_copy(z_hbm, z, sem)
    copy.start()
    dt, cum = rates(dt_raw[...], a_log[...], 0)
    dt_out[...] = dt
    cum_out[...] = cum
    leading = jnp.exp(cum)
    heads = dt.shape[0] // groups
    cols = z.shape[1] // groups
    for g in range(groups):
        lead[:, g * cols : (g + 1) * cols] = spread(
            leading[g * heads : (g + 1) * heads], cols // heads, 2
        )
    copy.wait()
    for at in range(0, z.shape[1], CHUNK):
        cut = slice(at, at + CHUNK)
        here = silu(z[:, cut].astype(F32))
        gate[:, cut] = here
        lead[:, cut] = lead[:, cut] * here


def intra_kernel(count, *refs):
    sources, refs = refs[:count], refs[count:]
    x, bc, gate, taps_x, taps_bc, dt, cum, d_skip, y_part, c_act = refs
    tokens, width = x.shape
    groups, both = bc.shape[1:]
    state_dim = both // 2
    keep = taps_x.shape[0] - 1
    cols = width // groups
    heads = dt.shape[0] // groups
    head_dim = cols // heads
    cum_t = cum[...].T
    skip = spread_row(as_column(d_skip[...], 0, groups * heads), head_dim)
    t_at = lax.broadcasted_iota(jnp.int32, (tokens, tokens), 0)
    s_at = lax.broadcasted_iota(jnp.int32, (tokens, tokens), 1)
    pair = 2 * head_dim

    def before(begin, stop):
        found = [rows_before(rows, begin, stop, keep, state_dim) for rows in sources]
        return sum(found[1:], found[0])

    for g in range(groups):
        at = width + g * both
        tail_bc = jnp.concatenate(
            [before(at, at + state_dim), before(at + state_dim, at + both)], axis=1
        )
        bc_act = conv_act(bc[...].astype(F32)[:, g], tail_bc, taps_bc[...][:, g])
        b, c = bc_act[:, :state_dim], bc_act[:, state_dim:]
        c_act[:, g * state_dim : (g + 1) * state_dim] = c
        inner = lax.dot_general(c, b, (((1,), (1,)), ((), ())), preferred_element_type=F32)
        inner = jnp.where(t_at >= s_at, inner, 0.0)
        for first in range(0, heads, 2):
            here = first * head_dim
            cut = slice(g * cols + here, g * cols + here + pair)
            act = conv_act(x[:, cut].astype(F32), before(cut.start, cut.stop), taps_x[:, cut])
            lane = lax.broadcasted_iota(jnp.int32, act.shape, 1)
            full = act.astype(F32)
            blocks = jnp.concatenate(
                [jnp.where(lane < head_dim, full, 0.0), jnp.where(lane < head_dim, 0.0, full)],
                axis=0,
            ).astype(BF16)
            weights = []
            for h in (g * heads + first, g * heads + first + 1):
                gap = jnp.minimum(cum_t[:, h : h + 1] - cum[h : h + 1, :], 0.0)
                weights.append((jnp.exp(gap) * dt[h : h + 1, :] * inner).astype(BF16))
            y = jnp.dot(jnp.concatenate(weights, axis=1), blocks, preferred_element_type=F32)
            y_part[:, cut] = (y + skip[:, cut] * full) * gate[:, cut]


def gated_slice(low, which, c, y_part, lead, arrived):
    tokens, width = y_part.shape
    state_dim = arrived[-1].shape[0]
    size = arrived[-1].shape[1]
    state = jnp.zeros((state_dim, size), BF16)
    for i, came in enumerate(arrived):
        state = jnp.where(which[0] == i, came[...][:state_dim], state)
    pieces = []
    for group, begin, stop in by_group(low, low + size, width * state_dim // c.shape[1]):
        from_state = jnp.dot(
            c[:, group * state_dim : (group + 1) * state_dim],
            state[:, begin - low : stop - low],
            preferred_element_type=F32,
        )
        pieces.append(y_part[:, begin:stop] + lead[:, begin:stop] * from_state)
    return pieces


def gated_kernel(low, which, c, y_part, lead, *refs):
    at = 0
    for piece in gated_slice(low, which, c, y_part, lead, refs[:-1]):
        refs[-1][:, at : at + piece.shape[1]] = piece
        at += piece.shape[1]


def output_kernel(begin, ready, low, which, c, y_part, lead, gain, *refs):
    out, made, sems = refs[-3:]
    tokens, cols = made.shape
    pieces = [refs[i][:, a:b] for i, (a, b) in enumerate(ready)]
    if low is not None:
        arrived = refs[len(ready) : len(refs) - 3]
        if begin > 0:
            arrived = arrived[:-1]
        pieces += gated_slice(low, which, c, y_part, lead, arrived)
    total = jnp.zeros((tokens, 1), F32)
    for piece in pieces:
        total = total + jnp.sum(piece * piece, axis=1, keepdims=True)
    factor = lax.rsqrt(total / cols + EPS)
    copies = []
    at = 0
    for i, piece in enumerate(pieces):
        span = slice(at, at + piece.shape[1])
        made[:, span] = (piece * factor * gain[:, begin + at : begin + span.stop]).astype(BF16)
        copies.append(
            pltpu.make_async_copy(
                made.at[:, span], out.at[:, pl.ds(begin + at, piece.shape[1])], sems.at[i]
            )
        )
        copies[-1].start()
        at = span.stop
    for copy in copies:
        copy.wait()


def params(mib):
    return pltpu.CompilerParams(vmem_limit_bytes=mib * 1024 * 1024)


def doubling(state, decay, devices):
    def moved(value, distance):
        return lax.ppermute(value, "seq", [(i, i + distance) for i in range(devices - distance)])

    total, decay = moved(state.astype(BF16), 1), moved(decay, 1)
    distance = 1
    while distance < devices - 1:
        came = moved(total, distance)
        total = (decay * came.astype(F32) + total.astype(F32)).astype(BF16)
        decay = decay * moved(decay, distance)
        distance *= 2
    return total


def shards(x_in, bc_in, z_in, dt_raw, conv_x, conv_bc, a_log, d_skip, norm_gain):
    tokens, width = x_in.shape
    groups, both = bc_in.shape[1:]
    state_dim = both // 2
    heads = dt_raw.shape[1]
    head_dim = width // heads
    cols = width // groups
    devices = lax.axis_size("seq")
    place = lax.axis_index("seq")
    edges = [width * sum(PARTS[:i]) // sum(PARTS) for i in range(len(PARTS) + 1)]
    cuts = list(zip(edges[:-1], edges[1:]))

    taps = conv_x.shape[0]
    dt_t = dt_raw.T
    a_row = a_log.reshape(1, heads)
    d_row = d_skip.reshape(1, heads)
    gain = norm_gain.reshape(1, width)
    sources = [x_in, bc_in, conv_x, conv_bc]
    operands = sources + [dt_t, a_row]
    pinned = [pltpu.with_memory_space_constraint(v, pltpu.HBM) for v in operands]
    landed = [pltpu.VMEM(v.shape, v.dtype) for v in operands]
    scale_shape = jax.ShapeDtypeStruct((tokens, width), F32)
    scalar = pl.BlockSpec(memory_space=pltpu.SMEM)
    in_vmem = pl.BlockSpec(memory_space=pltpu.VMEM)
    anywhere = pl.BlockSpec(memory_space=pl.ANY)
    in_hbm = [pl.BlockSpec(memory_space=pltpu.HBM)] * len(operands)

    def here(condition):
        return condition.astype(jnp.int32).reshape(1)

    def shifted(value, route):
        return lax.ppermute(value, "seq", route)

    def first_states(low, high):
        blocks = -(-(width + groups * both) // (high - low))
        extra = -(-(taps - 1) * blocks // (2 * RIM)) * 2 * RIM
        return pl.pallas_call(
            functools.partial(first_kernel, low, high),
            out_shape=[jax.ShapeDtypeStruct((state_dim + extra, high - low), BF16), scale_shape],
            in_specs=[scalar] + in_hbm,
            scratch_shapes=landed + [pltpu.SemaphoreType.DMA((len(operands),))],
            compiler_params=params(16),
            name="first_states",
        )(here(place == 0), *pinned)

    def next_states(token, scale, low, high):
        return pl.pallas_call(
            functools.partial(next_kernel, low, high),
            out_shape=jax.ShapeDtypeStruct((state_dim, high - low), BF16),
            in_specs=[scalar, anywhere] + [in_vmem] * (len(sources) + 1),
            compiler_params=params(16),
            name="next_states",
        )(here(place == 0), token, *sources, scale)

    def prepared(token):
        return pl.pallas_call(
            functools.partial(prepare_kernel, cuts),
            out_shape=[
                jax.ShapeDtypeStruct((RIM, width + groups * both), BF16),
                jax.ShapeDtypeStruct((1, width), F32),
                scale_shape,
            ]
            + [jax.ShapeDtypeStruct((1, high - low), F32) for low, high in cuts],
            in_specs=[anywhere] + [in_vmem] * 5,
            compiler_params=params(16),
            name="prepared",
        )(token, x_in, bc_in, dt_t, a_row, gain)

    def later_states(condition, rows, token, scale, low, high):
        return pl.pallas_call(
            functools.partial(later_kernel, low, high),
            out_shape=jax.ShapeDtypeStruct((state_dim, high - low), F32),
            in_specs=[scalar, in_vmem, anywhere] + [in_vmem] * (len(sources) + 1),
            compiler_params=params(16),
            name="later_states",
        )(here(condition), rows, token, *sources, scale)

    along = [(i, i + 1) for i in range(devices - 1)]
    def gates(token):
        per_head = jax.ShapeDtypeStruct((heads, tokens), F32)
        return pl.pallas_call(
            functools.partial(gate_kernel, groups),
            out_shape=[scale_shape, scale_shape, per_head, per_head],
            in_specs=[anywhere, pl.BlockSpec(memory_space=pltpu.HBM)] + [in_vmem] * 2,
            scratch_shapes=[pltpu.VMEM(z_in.shape, z_in.dtype), pltpu.SemaphoreType.DMA],
            compiler_params=params(16),
            name="gates",
        )(token, pltpu.with_memory_space_constraint(z_in, pltpu.HBM), dt_t, a_row)

    def intra(befores, gate, dt, cum):
        return pl.pallas_call(
            functools.partial(intra_kernel, len(befores)),
            out_shape=[
                scale_shape, jax.ShapeDtypeStruct((tokens, groups * state_dim), BF16)
            ],
            in_specs=[in_vmem] * (len(befores) + 8),
            compiler_params=params(24),
            cost_estimate=pl.CostEstimate(
                flops=4 * tokens * tokens * width,
                bytes_accessed=12 * tokens * width,
                transcendentals=tokens * tokens * heads,
            ),
            name="intra",
        )(*befores, x_in, bc_in, gate, conv_x, conv_bc, dt, cum, d_row)

    gate_parts = None
    if devices <= CHAIN_MOST:
        first, scale = first_states(*cuts[0])
        sent = [first, next_states(first, scale, *cuts[1])]
        last, gain, scale_own, *decays = prepared(sent[-1])
        token = last
        for cut in cuts[2:]:
            sent.append(next_states(token, scale, *cut))
            token = sent[-1]
        soon = along[1 : max(devices - 2, 1)]
        late = along[max(devices - 2, 1) :]
        befores = [shifted(last, soon)] if soon else []
        arrived = [[shifted(v, along[:1])] for v in sent]
        befores.append(arrived[0][0])
        rows, token = arrived[0][0], last
        for hop in range(1, devices - 1):
            runs = place == 1 if hop == 1 else (place >= 2) & (place < devices - 1)
            for i, cut in enumerate(cuts):
                if hop == 1:
                    after = last if i == 0 else made_at[1 if i == len(cuts) - 1 else 0]
                if hop <= 2:
                    made = later_states(runs, rows, after, scale_own, *cut)
                    states = [made] if i == 0 else states + [made]
                early = ()
                if hop == devices - 2 and hop > 1 and i == 1:
                    gate_parts = gates(token)
                    early = (gate_parts[0],)
                if hop == devices - 2 and hop > 1 and i == len(cuts) - 1:
                    early = (arrived[0][-1], befores[-1])
                before, *_ = lax.optimization_barrier((arrived[i][-1], token) + early)
                joined = decays[i] * before[:state_dim].astype(F32) + states[i]
                token = joined.astype(BF16)
                made_at = [token] if i == 0 else made_at + [token]
                if hop == 1 and i == 1 and late:
                    moved, _ = lax.optimization_barrier((last, token))
                    befores.append(shifted(moved, late))
                arrived[i].append(shifted(token, along[hop : hop + 1]))
            rows, after = befores[0], token
        which = place - 1
    else:
        last, gain, scale, *decays = prepared(a_row)
        befores = [shifted(last, along)]
        arrived = []
        for decay, cut in zip(decays, cuts):
            state = later_states(place >= 0, befores[0], a_row, scale, *cut)
            arrived.append([doubling(state, decay, devices)])
        which = jnp.zeros_like(place)
    which = which.astype(jnp.int32).reshape(1)
    gate, lead, dt, cum = gate_parts or gates(a_row)
    y_part, c_act = intra(befores, gate, dt, cum)

    common = [which, c_act, y_part, lead]
    common_specs = [scalar] + [in_vmem] * 3
    last_low, last_high = cuts[-1]
    ready = []
    for (low, high), seen in zip(cuts[:-1], arrived):
        ready.append(
            pl.pallas_call(
                functools.partial(gated_kernel, low),
                out_shape=jax.ShapeDtypeStruct((tokens, high - low), F32),
                in_specs=common_specs + [in_vmem] * len(seen),
                compiler_params=params(16),
                name="gated",
            )(*common, *seen)
        )
    out = None
    for g in range(groups):
        begin, stop = g * cols, (g + 1) * cols
        taken, spans = [], []
        for (low, high), v in zip(cuts[:-1], ready):
            if low < stop and high > begin:
                taken.append(v)
                spans.append((max(low, begin) - low, min(high, stop) - low))
        inputs = taken
        unready = None
        if last_low < stop:
            unready = last_low
            inputs = taken + arrived[-1]
        aliases = {}
        specs = common_specs + [in_vmem] * (1 + len(inputs))
        if out is not None:
            aliases = {len(common) + 1 + len(inputs): 0}
            inputs = inputs + [out]
            specs = specs + [anywhere]
        out = pl.pallas_call(
            functools.partial(output_kernel, begin, spans, unready),
            out_shape=jax.ShapeDtypeStruct((tokens, width), BF16),
            in_specs=specs,
            out_specs=anywhere,
            scratch_shapes=[
                pltpu.VMEM((tokens, cols), BF16),
                pltpu.SemaphoreType.DMA((len(cuts) + groups,)),
            ],
            input_output_aliases=aliases,
            compiler_params=params(16),
            name="outputs",
        )(*common, gain, *inputs)
    return out


def solution(mesh):
    return jax.shard_map(
        shards,
        mesh=mesh,
        in_specs=(
            P(("groups", "seq"), "head"),
            P(("groups", "seq"), "head", None),
            P(("groups", "seq"), "head"),
            P(("groups", "seq"), "head"),
            P(None, "head"),
            P(None, "head", None),
            P("head"),
            P("head"),
            P("head"),
        ),
        out_specs=P(("groups", "seq"), "head"),
        check_vma=False,
    )
```

```python
import functools

import jax
import jax.numpy as jnp
from jax import lax
from jax.experimental import pallas as pl
from jax.experimental.pallas import tpu as pltpu
from jax.sharding import PartitionSpec as P

EPS = 1e-05
F32 = jnp.float32
BF16 = jnp.bfloat16
CHAIN_MOST = 4
PARTS = (3, 5, 4, 4)
CHUNK = 128
RIM = 8


def silu(u):
    return 0.5 * u * (1.0 + jnp.tanh(0.5 * u))


def softplus(v):
    return jnp.maximum(v, 0.0) + jnp.log1p(jnp.exp(-jnp.abs(v)))


def halves(v, count, axis):
    parts = []
    for _ in range(count - 1):
        part = v.astype(BF16)
        parts.append(part)
        v = v - part.astype(F32)
    parts.append(v.astype(BF16))
    return jnp.concatenate(parts, axis=axis)


def spread(per_head, head_dim, count):
    heads = per_head.shape[0]
    rows = lax.broadcasted_iota(jnp.int32, (heads * count, heads * head_dim), 0)
    cols = lax.broadcasted_iota(jnp.int32, (heads * count, heads * head_dim), 1)
    pick = (rows % heads == cols // head_dim).astype(F32).astype(BF16)
    return lax.dot_general(
        halves(per_head, count, 0), pick, (((0,), (0,)), ((), ())), preferred_element_type=F32
    )


def spread_row(column, head_dim):
    heads = column.shape[0]
    rows = lax.broadcasted_iota(jnp.int32, (heads, heads * head_dim), 0)
    cols = lax.broadcasted_iota(jnp.int32, (heads, heads * head_dim), 1)
    return jnp.sum(jnp.where(rows == cols // head_dim, column, 0.0), axis=0, keepdims=True)


def as_column(row, start, heads):
    every = row.shape[1]
    rows = lax.broadcasted_iota(jnp.int32, (heads, every), 0)
    cols = lax.broadcasted_iota(jnp.int32, (heads, every), 1)
    return jnp.sum(jnp.where(cols == rows + start, row, 0.0), axis=1, keepdims=True)


def conv_act(series, tail, taps):
    count = taps.shape[0]
    above = tail.shape[0]
    padded = jnp.concatenate([tail, series], axis=0)
    total = taps[count - 1 : count] * series
    for back in range(1, count):
        total = total + taps[count - 1 - back : count - back] * pltpu.roll(padded, back, 0)[above:]
    return silu(total).astype(BF16)


def rates(dt_raw, a_log_row, start):
    heads, tokens = dt_raw.shape
    dt = softplus(dt_raw)
    rate = -jnp.exp(as_column(a_log_row, start, heads)) * dt
    earlier = lax.broadcasted_iota(jnp.int32, (tokens, tokens), 0)
    later = lax.broadcasted_iota(jnp.int32, (tokens, tokens), 1)
    upto = (earlier <= later).astype(F32).astype(BF16)
    cum = jnp.dot(
        halves(rate, 3, 1), jnp.concatenate([upto] * 3, axis=0), preferred_element_type=F32
    )
    return dt, cum


def scales(groups, head_dim, dt_raw, a_log, scale):
    dt, cum = rates(dt_raw[...], a_log[...], 0)
    end = cum[:, -1:]
    tail_decay = jnp.exp(end - cum) * dt
    heads = dt.shape[0] // groups
    for g in range(groups):
        scale[:, g * heads * head_dim : (g + 1) * heads * head_dim] = spread(
            tail_decay[g * heads : (g + 1) * heads], head_dim, 2
        )
    return spread_row(jnp.exp(end), head_dim)


def by_group(low, high, cols):
    found = []
    while low < high:
        stop = min(high, (low // cols + 1) * cols)
        found.append((low // cols, low, stop))
        low = stop
    return found


def emit_states(low, high, x, tail_x, bc, tail_bc, taps_x, taps_bc, scale, emit):
    groups, both = bc.shape[1:]
    state_dim = both // 2
    for group, begin, stop in by_group(low, high, x.shape[1] // groups):
        b = conv_act(
            bc[:, :, :state_dim].astype(F32)[:, group],
            tail_bc(group),
            taps_bc[:, :, :state_dim][:, group],
        )
        b_t = b.astype(F32).T.astype(BF16)
        for at in range(begin, stop, CHUNK):
            cut = slice(at, at + CHUNK)
            act = conv_act(x[:, cut].astype(F32), tail_x(cut), taps_x[:, cut])
            scaled = (scale[:, cut] * act.astype(F32)).astype(BF16)
            here = slice(at - low, at - low + CHUNK)
            emit(here, jnp.dot(b_t, scaled, preferred_element_type=F32))


def head_rows(low, high, x, bc, taps_x, taps_bc, scale, out):
    state_dim = bc.shape[2] // 2

    def emit(here, total):
        out[:state_dim, here] = total.astype(BF16)

    emit_states(
        low, high, x, lambda cut: jnp.zeros((RIM, CHUNK), F32),
        bc, lambda group: jnp.zeros((RIM, state_dim), F32), taps_x, taps_bc, scale, emit,
    )


def first_kernel(
    low, high, active, x_hbm, bc_hbm, taps_x_hbm, taps_bc_hbm, dt_hbm, a_hbm,
    out, scale, x, bc, taps_x, taps_bc, dt_raw, a_log, sems,
):
    tokens, width = x.shape
    groups, both = bc.shape[1:]

    @pl.when(active[0] == 1)
    def _():
        pairs = [
            (dt_hbm, dt_raw), (a_hbm, a_log), (x_hbm, x), (bc_hbm, bc),
            (taps_x_hbm, taps_x), (taps_bc_hbm, taps_bc),
        ]
        copies = [pltpu.make_async_copy(*pair, sems.at[i]) for i, pair in enumerate(pairs)]
        for copy in copies:
            copy.start()
        for copy in copies[:2]:
            copy.wait()
        scales(groups, width // dt_raw.shape[0], dt_raw, a_log, scale)
        for copy in copies[2:]:
            copy.wait()
        state_dim, step = both // 2, high - low
        keep = taps_x.shape[0] - 1
        extra = out.shape[0] - state_dim
        last_bc = bc[tokens - 2 * RIM :].astype(F32)[-RIM:]
        last = [x[tokens - 2 * RIM :, :].astype(F32)[-RIM:]] + [last_bc[:, g] for g in range(groups)]
        length = width + groups * both
        last.append(jnp.zeros((RIM, -length % step + step), F32))
        last = jnp.concatenate(last, axis=1)
        at = lax.broadcasted_iota(jnp.int32, (extra, step), 0)
        below = jnp.zeros((extra, step), F32)
        fill = jnp.zeros((extra - RIM, step), F32)
        for k in range(-(-length // step)):
            block = jnp.concatenate([last[:, k * step : (k + 1) * step], fill], axis=0)
            block = pltpu.roll(block, (keep * (k + 1) - RIM) % extra, 0)
            below = jnp.where((at >= keep * k) & (at < keep * (k + 1)), block, below)
        out[state_dim:, :] = below.astype(BF16)
        head_rows(low, high, x, bc, taps_x, taps_bc, scale, out)


def next_kernel(low, high, active, _, x, bc, taps_x, taps_bc, scale, out):
    @pl.when(active[0] == 1)
    def _():
        head_rows(low, high, x, bc, taps_x, taps_bc, scale, out)


def prepare_kernel(
    cuts, _, x, bc, dt_raw, a_log, gain, skip, pack, gain_out, skip_out, scale, *decays
):
    tokens, width = x.shape
    groups, both = bc.shape[1:]
    pack[:, :width] = x[tokens - 2 * RIM :, :].astype(F32)[-RIM:].astype(BF16)
    last_bc = bc[tokens - 2 * RIM :].astype(F32)[-RIM:]
    for g in range(groups):
        pack[:, width + g * both : width + (g + 1) * both] = last_bc[:, g].astype(BF16)
    gain_out[...] = gain[...]
    skip_out[...] = skip[...]
    row = scales(groups, width // dt_raw.shape[0], dt_raw, a_log, scale)
    for decay, (low, high) in zip(decays, cuts):
        decay[...] = row[:, low:high]


def rows_before(rows, begin, stop, keep, state_dim):
    if rows.shape[0] == RIM:
        return rows[:, begin:stop].astype(F32)
    step = rows.shape[1]
    below = rows[state_dim:, begin % step : begin % step + stop - begin].astype(F32)
    return pltpu.roll(below, (RIM - keep * (begin // step + 1)) % below.shape[0], 0)[:RIM]


def later_kernel(low, high, active, rows, _, x, bc, taps_x, taps_bc, scale, state):
    both = bc.shape[2]
    state_dim = both // 2
    keep = taps_x.shape[0] - 1

    def before(begin, stop):
        return rows_before(rows, begin, stop, keep, state_dim)

    def tail_bc(group):
        at = x.shape[1] + group * both
        return before(at, at + state_dim)

    @pl.when(active[0] == 1)
    def _():
        def emit(here, total):
            state[:, here] = total

        emit_states(
            low, high, x, lambda cut: before(cut.start, cut.stop), bc, tail_bc,
            taps_x, taps_bc, scale, emit,
        )


def gate_kernel(groups, _, z_hbm, dt_raw, a_log, gate, lead, dt_out, cum_out, z, sem):
    copy = pltpu.make_async_copy(z_hbm, z, sem)
    copy.start()
    dt, cum = rates(dt_raw[...], a_log[...], 0)
    dt_out[...] = dt
    cum_out[...] = cum
    leading = jnp.exp(cum)
    heads = dt.shape[0] // groups
    cols = z.shape[1] // groups
    for g in range(groups):
        lead[:, g * cols : (g + 1) * cols] = spread(
            leading[g * heads : (g + 1) * heads], cols // heads, 2
        )
    copy.wait()
    for at in range(0, z.shape[1], CHUNK):
        cut = slice(at, at + CHUNK)
        here = silu(z[:, cut].astype(F32))
        gate[:, cut] = here
        lead[:, cut] = lead[:, cut] * here


def intra_kernel(count, *refs):
    sources, refs = refs[:count], refs[count:]
    x, bc, gate, taps_x, taps_bc, dt, cum, d_skip, y_part, c_act = refs
    tokens, width = x.shape
    groups, both = bc.shape[1:]
    state_dim = both // 2
    keep = taps_x.shape[0] - 1
    cols = width // groups
    heads = dt.shape[0] // groups
    head_dim = cols // heads
    cum_t = cum[...].T
    skip = spread_row(as_column(d_skip[...], 0, groups * heads), head_dim)
    t_at = lax.broadcasted_iota(jnp.int32, (tokens, tokens), 0)
    s_at = lax.broadcasted_iota(jnp.int32, (tokens, tokens), 1)
    pair = 2 * head_dim

    def before(begin, stop):
        found = [rows_before(rows, begin, stop, keep, state_dim) for rows in sources]
        return sum(found[1:], found[0])

    for g in range(groups):
        at = width + g * both
        tail_bc = jnp.concatenate(
            [before(at, at + state_dim), before(at + state_dim, at + both)], axis=1
        )
        bc_act = conv_act(bc[...].astype(F32)[:, g], tail_bc, taps_bc[...][:, g])
        b, c = bc_act[:, :state_dim], bc_act[:, state_dim:]
        c_act[:, g * state_dim : (g + 1) * state_dim] = c
        inner = lax.dot_general(c, b, (((1,), (1,)), ((), ())), preferred_element_type=F32)
        inner = jnp.where(t_at >= s_at, inner, 0.0)
        for first in range(0, heads, 2):
            here = first * head_dim
            cut = slice(g * cols + here, g * cols + here + pair)
            act = conv_act(x[:, cut].astype(F32), before(cut.start, cut.stop), taps_x[:, cut])
            lane = lax.broadcasted_iota(jnp.int32, act.shape, 1)
            full = act.astype(F32)
            blocks = jnp.concatenate(
                [jnp.where(lane < head_dim, full, 0.0), jnp.where(lane < head_dim, 0.0, full)],
                axis=0,
            ).astype(BF16)
            weights = []
            for h in (g * heads + first, g * heads + first + 1):
                gap = jnp.minimum(cum_t[:, h : h + 1] - cum[h : h + 1, :], 0.0)
                weights.append((jnp.exp(gap) * dt[h : h + 1, :] * inner).astype(BF16))
            y = jnp.dot(jnp.concatenate(weights, axis=1), blocks, preferred_element_type=F32)
            y_part[:, cut] = (y + skip[:, cut] * full) * gate[:, cut]


def gated_slice(low, which, c, y_part, lead, arrived):
    tokens, width = y_part.shape
    state_dim = arrived[-1].shape[0]
    size = arrived[-1].shape[1]
    state = jnp.zeros((state_dim, size), BF16)
    for i, came in enumerate(arrived):
        state = jnp.where(which[0] == i, came[...][:state_dim], state)
    pieces = []
    for group, begin, stop in by_group(low, low + size, width * state_dim // c.shape[1]):
        from_state = jnp.dot(
            c[:, group * state_dim : (group + 1) * state_dim],
            state[:, begin - low : stop - low],
            preferred_element_type=F32,
        )
        pieces.append(y_part[:, begin:stop] + lead[:, begin:stop] * from_state)
    return pieces


def gated_kernel(low, which, c, y_part, lead, *refs):
    at = 0
    for piece in gated_slice(low, which, c, y_part, lead, refs[:-1]):
        refs[-1][:, at : at + piece.shape[1]] = piece
        at += piece.shape[1]


def output_kernel(begin, ready, low, which, c, y_part, lead, gain, *refs):
    out, made, sems = refs[-3:]
    tokens, cols = made.shape
    pieces = [refs[i][:, a:b] for i, (a, b) in enumerate(ready)]
    if low is not None:
        arrived = refs[len(ready) : len(refs) - 3]
        if begin > 0:
            arrived = arrived[:-1]
        pieces += gated_slice(low, which, c, y_part, lead, arrived)
    total = jnp.zeros((tokens, 1), F32)
    for piece in pieces:
        total = total + jnp.sum(piece * piece, axis=1, keepdims=True)
    factor = lax.rsqrt(total / cols + EPS)
    copies = []
    at = 0
    for i, piece in enumerate(pieces):
        span = slice(at, at + piece.shape[1])
        made[:, span] = (piece * factor * gain[:, begin + at : begin + span.stop]).astype(BF16)
        copies.append(
            pltpu.make_async_copy(
                made.at[:, span], out.at[:, pl.ds(begin + at, piece.shape[1])], sems.at[i]
            )
        )
        copies[-1].start()
        at = span.stop
    for copy in copies:
        copy.wait()


def params(mib):
    return pltpu.CompilerParams(vmem_limit_bytes=mib * 1024 * 1024)


def doubling(state, decay, devices):
    def moved(value, distance):
        return lax.ppermute(value, "seq", [(i, i + distance) for i in range(devices - distance)])

    total, decay = moved(state.astype(BF16), 1), moved(decay, 1)
    distance = 1
    while distance < devices - 1:
        came = moved(total, distance)
        total = (decay * came.astype(F32) + total.astype(F32)).astype(BF16)
        decay = decay * moved(decay, distance)
        distance *= 2
    return total


def shards(x_in, bc_in, z_in, dt_raw, conv_x, conv_bc, a_log, d_skip, norm_gain):
    tokens, width = x_in.shape
    groups, both = bc_in.shape[1:]
    state_dim = both // 2
    heads = dt_raw.shape[1]
    head_dim = width // heads
    cols = width // groups
    devices = lax.axis_size("seq")
    place = lax.axis_index("seq")
    edges = [width * sum(PARTS[:i]) // sum(PARTS) for i in range(len(PARTS) + 1)]
    cuts = list(zip(edges[:-1], edges[1:]))

    taps = conv_x.shape[0]
    dt_t = dt_raw.T
    a_row = a_log.reshape(1, heads)
    d_row = d_skip.reshape(1, heads)
    gain = norm_gain.reshape(1, width)
    sources = [x_in, bc_in, conv_x, conv_bc]
    operands = sources + [dt_t, a_row]
    pinned = [pltpu.with_memory_space_constraint(v, pltpu.HBM) for v in operands]
    landed = [pltpu.VMEM(v.shape, v.dtype) for v in operands]
    scale_shape = jax.ShapeDtypeStruct((tokens, width), F32)
    scalar = pl.BlockSpec(memory_space=pltpu.SMEM)
    in_vmem = pl.BlockSpec(memory_space=pltpu.VMEM)
    anywhere = pl.BlockSpec(memory_space=pl.ANY)
    in_hbm = [pl.BlockSpec(memory_space=pltpu.HBM)] * len(operands)

    def here(condition):
        return condition.astype(jnp.int32).reshape(1)

    def shifted(value, route):
        return lax.ppermute(value, "seq", route)

    def first_states(low, high):
        blocks = -(-(width + groups * both) // (high - low))
        extra = -(-(taps - 1) * blocks // (2 * RIM)) * 2 * RIM
        return pl.pallas_call(
            functools.partial(first_kernel, low, high),
            out_shape=[jax.ShapeDtypeStruct((state_dim + extra, high - low), BF16), scale_shape],
            in_specs=[scalar] + in_hbm,
            scratch_shapes=landed + [pltpu.SemaphoreType.DMA((len(operands),))],
            compiler_params=params(6),
            name="first_states",
        )(here(place == 0), *pinned)

    def next_states(token, scale, low, high):
        return pl.pallas_call(
            functools.partial(next_kernel, low, high),
            out_shape=jax.ShapeDtypeStruct((state_dim, high - low), BF16),
            in_specs=[scalar, anywhere] + [in_vmem] * (len(sources) + 1),
            compiler_params=params(6),
            name="next_states",
        )(here(place == 0), token, *sources, scale)

    def prepared(token):
        return pl.pallas_call(
            functools.partial(prepare_kernel, cuts),
            out_shape=[
                jax.ShapeDtypeStruct((RIM, width + groups * both), BF16),
                jax.ShapeDtypeStruct((1, width), F32),
                jax.ShapeDtypeStruct((1, heads), F32),
                scale_shape,
            ]
            + [jax.ShapeDtypeStruct((1, high - low), F32) for low, high in cuts],
            in_specs=[anywhere] + [in_vmem] * 6,
            compiler_params=params(6),
            name="prepared",
        )(token, x_in, bc_in, dt_t, a_row, gain, d_row)

    def later_states(condition, rows, token, scale, low, high):
        return pl.pallas_call(
            functools.partial(later_kernel, low, high),
            out_shape=jax.ShapeDtypeStruct((state_dim, high - low), F32),
            in_specs=[scalar, in_vmem, anywhere] + [in_vmem] * (len(sources) + 1),
            compiler_params=params(6),
            name="later_states",
        )(here(condition), rows, token, *sources, scale)

    along = [(i, i + 1) for i in range(devices - 1)]
    def gates(token):
        per_head = jax.ShapeDtypeStruct((heads, tokens), F32)
        return pl.pallas_call(
            functools.partial(gate_kernel, groups),
            out_shape=[scale_shape, scale_shape, per_head, per_head],
            in_specs=[anywhere, pl.BlockSpec(memory_space=pltpu.HBM)] + [in_vmem] * 2,
            scratch_shapes=[pltpu.VMEM(z_in.shape, z_in.dtype), pltpu.SemaphoreType.DMA],
            compiler_params=params(6),
            name="gates",
        )(token, pltpu.with_memory_space_constraint(z_in, pltpu.HBM), dt_t, a_row)

    def intra(befores, gate, dt, cum, skip):
        return pl.pallas_call(
            functools.partial(intra_kernel, len(befores)),
            out_shape=[
                scale_shape, jax.ShapeDtypeStruct((tokens, groups * state_dim), BF16)
            ],
            in_specs=[in_vmem] * (len(befores) + 8),
            compiler_params=params(10),
            cost_estimate=pl.CostEstimate(
                flops=4 * tokens * tokens * width,
                bytes_accessed=12 * tokens * width,
                transcendentals=tokens * tokens * heads,
            ),
            name="intra",
        )(*befores, x_in, bc_in, gate, conv_x, conv_bc, dt, cum, skip)

    gate_parts = None
    if devices <= CHAIN_MOST:
        first, scale = first_states(*cuts[0])
        sent = [first, next_states(first, scale, *cuts[1])]
        last, gain, d_row, scale_own, *decays = prepared(sent[-1])
        token = last
        for cut in cuts[2:]:
            sent.append(next_states(token, scale, *cut))
            token = sent[-1]
        soon = along[1 : max(devices - 2, 1)]
        late = along[max(devices - 2, 1) :]
        befores = [shifted(last, soon)] if soon else []
        arrived = [[shifted(v, along[:1])] for v in sent]
        befores.append(arrived[0][0])
        rows, token = arrived[0][0], last
        for hop in range(1, devices - 1):
            runs = place == 1 if hop == 1 else (place >= 2) & (place < devices - 1)
            for i, cut in enumerate(cuts):
                if hop == 1:
                    after = last if i == 0 else made_at[1 if i == len(cuts) - 1 else 0]
                if hop <= 2:
                    made = later_states(runs, rows, after, scale_own, *cut)
                    states = [made] if i == 0 else states + [made]
                early = ()
                if hop == devices - 2 and hop > 1 and i == 1:
                    gate_parts = gates(token)
                    early = (gate_parts[0],)
                if hop == devices - 2 and hop > 1 and i == len(cuts) - 1:
                    early = (arrived[0][-1], befores[-1])
                before, *_ = lax.optimization_barrier((arrived[i][-1], token) + early)
                joined = decays[i] * before[:state_dim].astype(F32) + states[i]
                token = joined.astype(BF16)
                made_at = [token] if i == 0 else made_at + [token]
                if hop == 1 and i == 1 and late:
                    moved, _ = lax.optimization_barrier((last, token))
                    befores.append(shifted(moved, late))
                arrived[i].append(shifted(token, along[hop : hop + 1]))
            rows, after = befores[0], token
        which = place - 1
    else:
        last, gain, d_row, scale, *decays = prepared(a_row)
        befores = [shifted(last, along)]
        arrived = []
        for decay, cut in zip(decays, cuts):
            state = later_states(place >= 0, befores[0], a_row, scale, *cut)
            arrived.append([doubling(state, decay, devices)])
        which = jnp.zeros_like(place)
    which = which.astype(jnp.int32).reshape(1)
    gate, lead, dt, cum = gate_parts or gates(a_row)
    y_part, c_act = intra(befores, gate, dt, cum, d_row)

    common = [which, c_act, y_part, lead]
    common_specs = [scalar] + [in_vmem] * 3
    last_low, last_high = cuts[-1]
    ready = []
    for (low, high), seen in zip(cuts[:-1], arrived):
        ready.append(
            pl.pallas_call(
                functools.partial(gated_kernel, low),
                out_shape=jax.ShapeDtypeStruct((tokens, high - low), F32),
                in_specs=common_specs + [in_vmem] * len(seen),
                compiler_params=params(6),
                name="gated",
            )(*common, *seen)
        )
    out = None
    for g in range(groups):
        begin, stop = g * cols, (g + 1) * cols
        taken, spans = [], []
        for (low, high), v in zip(cuts[:-1], ready):
            if low < stop and high > begin:
                taken.append(v)
                spans.append((max(low, begin) - low, min(high, stop) - low))
        inputs = taken
        unready = None
        if last_low < stop:
            unready = last_low
            inputs = taken + arrived[-1]
        aliases = {}
        specs = common_specs + [in_vmem] * (1 + len(inputs))
        if out is not None:
            aliases = {len(common) + 1 + len(inputs): 0}
            inputs = inputs + [out]
            specs = specs + [anywhere]
        out = pl.pallas_call(
            functools.partial(output_kernel, begin, spans, unready),
            out_shape=jax.ShapeDtypeStruct((tokens, width), BF16),
            in_specs=specs,
            out_specs=anywhere,
            scratch_shapes=[
                pltpu.VMEM((tokens, cols), BF16),
                pltpu.SemaphoreType.DMA((len(cuts) + groups,)),
            ],
            input_output_aliases=aliases,
            compiler_params=params(6),
            name="outputs",
        )(*common, gain, *inputs)
    return out


def solution(mesh):
    return jax.shard_map(
        shards,
        mesh=mesh,
        in_specs=(
            P(("groups", "seq"), "head"),
            P(("groups", "seq"), "head", None),
            P(("groups", "seq"), "head"),
            P(("groups", "seq"), "head"),
            P(None, "head"),
            P(None, "head", None),
            P("head"),
            P("head"),
            P("head"),
        ),
        out_specs=P(("groups", "seq"), "head"),
        check_vma=False,
    )
```

```python
import functools

import jax
import jax.numpy as jnp
from jax import lax
from jax.experimental import pallas as pl
from jax.experimental.pallas import tpu as pltpu
from jax.sharding import PartitionSpec as P

EPS = 1e-05
F32 = jnp.float32
BF16 = jnp.bfloat16
CHAIN_MOST = 4
PARTS = (3, 5, 4, 4)
CHUNK = 128
RIM = 8


def silu(u):
    return 0.5 * u * (1.0 + jnp.tanh(0.5 * u))


def softplus(v):
    return jnp.maximum(v, 0.0) + jnp.log1p(jnp.exp(-jnp.abs(v)))


def halves(v, count, axis):
    parts = []
    for _ in range(count - 1):
        part = v.astype(BF16)
        parts.append(part)
        v = v - part.astype(F32)
    parts.append(v.astype(BF16))
    return jnp.concatenate(parts, axis=axis)


def spread(per_head, head_dim, count):
    heads = per_head.shape[0]
    rows = lax.broadcasted_iota(jnp.int32, (heads * count, heads * head_dim), 0)
    cols = lax.broadcasted_iota(jnp.int32, (heads * count, heads * head_dim), 1)
    pick = (rows % heads == cols // head_dim).astype(F32).astype(BF16)
    return lax.dot_general(
        halves(per_head, count, 0), pick, (((0,), (0,)), ((), ())), preferred_element_type=F32
    )


def spread_row(column, head_dim):
    heads = column.shape[0]
    rows = lax.broadcasted_iota(jnp.int32, (heads, heads * head_dim), 0)
    cols = lax.broadcasted_iota(jnp.int32, (heads, heads * head_dim), 1)
    return jnp.sum(jnp.where(rows == cols // head_dim, column, 0.0), axis=0, keepdims=True)


def as_column(row, start, heads):
    every = row.shape[1]
    rows = lax.broadcasted_iota(jnp.int32, (heads, every), 0)
    cols = lax.broadcasted_iota(jnp.int32, (heads, every), 1)
    return jnp.sum(jnp.where(cols == rows + start, row, 0.0), axis=1, keepdims=True)


def conv_act(series, tail, taps):
    count = taps.shape[0]
    above = tail.shape[0]
    padded = jnp.concatenate([tail, series], axis=0)
    total = taps[count - 1 : count] * series
    for back in range(1, count):
        total = total + taps[count - 1 - back : count - back] * pltpu.roll(padded, back, 0)[above:]
    return silu(total).astype(BF16)


def rates(dt_raw, a_log_row, start):
    heads, tokens = dt_raw.shape
    dt = softplus(dt_raw)
    rate = -jnp.exp(as_column(a_log_row, start, heads)) * dt
    earlier = lax.broadcasted_iota(jnp.int32, (tokens, tokens), 0)
    later = lax.broadcasted_iota(jnp.int32, (tokens, tokens), 1)
    upto = (earlier <= later).astype(F32).astype(BF16)
    cum = jnp.dot(
        halves(rate, 3, 1), jnp.concatenate([upto] * 3, axis=0), preferred_element_type=F32
    )
    return dt, cum


def scales(groups, head_dim, dt_raw, a_log, scale):
    dt, cum = rates(dt_raw[...], a_log[...], 0)
    end = cum[:, -1:]
    tail_decay = jnp.exp(end - cum) * dt
    heads = dt.shape[0] // groups
    for g in range(groups):
        scale[:, g * heads * head_dim : (g + 1) * heads * head_dim] = spread(
            tail_decay[g * heads : (g + 1) * heads], head_dim, 2
        )
    return spread_row(jnp.exp(end), head_dim)


def by_group(low, high, cols):
    found = []
    while low < high:
        stop = min(high, (low // cols + 1) * cols)
        found.append((low // cols, low, stop))
        low = stop
    return found


def emit_states(low, high, x, tail_x, bc, tail_bc, taps_x, taps_bc, scale, emit):
    groups, both = bc.shape[1:]
    state_dim = both // 2
    for group, begin, stop in by_group(low, high, x.shape[1] // groups):
        b = conv_act(
            bc[:, :, :state_dim].astype(F32)[:, group],
            tail_bc(group),
            taps_bc[:, :, :state_dim][:, group],
        )
        b_t = b.astype(F32).T.astype(BF16)
        for at in range(begin, stop, CHUNK):
            cut = slice(at, at + CHUNK)
            act = conv_act(x[:, cut].astype(F32), tail_x(cut), taps_x[:, cut])
            scaled = (scale[:, cut] * act.astype(F32)).astype(BF16)
            here = slice(at - low, at - low + CHUNK)
            emit(here, jnp.dot(b_t, scaled, preferred_element_type=F32))


def head_rows(low, high, x, bc, taps_x, taps_bc, scale, out):
    state_dim = bc.shape[2] // 2

    def emit(here, total):
        out[:state_dim, here] = total.astype(BF16)

    emit_states(
        low, high, x, lambda cut: jnp.zeros((RIM, CHUNK), F32),
        bc, lambda group: jnp.zeros((RIM, state_dim), F32), taps_x, taps_bc, scale, emit,
    )


def first_kernel(
    low, high, active, x_hbm, bc_hbm, taps_x_hbm, taps_bc_hbm, dt_hbm, a_hbm,
    out, scale, x, bc, taps_x, taps_bc, dt_raw, a_log, sems,
):
    tokens, width = x.shape
    groups, both = bc.shape[1:]

    @pl.when(active[0] == 1)
    def _():
        pairs = [
            (dt_hbm, dt_raw), (a_hbm, a_log), (x_hbm, x), (bc_hbm, bc),
            (taps_x_hbm, taps_x), (taps_bc_hbm, taps_bc),
        ]
        copies = [pltpu.make_async_copy(*pair, sems.at[i]) for i, pair in enumerate(pairs)]
        for copy in copies:
            copy.start()
        for copy in copies[:2]:
            copy.wait()
        scales(groups, width // dt_raw.shape[0], dt_raw, a_log, scale)
        for copy in copies[2:]:
            copy.wait()
        state_dim, step = both // 2, high - low
        keep = taps_x.shape[0] - 1
        extra = out.shape[0] - state_dim
        last_bc = bc[tokens - 2 * RIM :].astype(F32)[-RIM:]
        last = [x[tokens - 2 * RIM :, :].astype(F32)[-RIM:]] + [last_bc[:, g] for g in range(groups)]
        length = width + groups * both
        last.append(jnp.zeros((RIM, -length % step + step), F32))
        last = jnp.concatenate(last, axis=1)
        at = lax.broadcasted_iota(jnp.int32, (extra, step), 0)
        below = jnp.zeros((extra, step), F32)
        fill = jnp.zeros((extra - RIM, step), F32)
        for k in range(-(-length // step)):
            block = jnp.concatenate([last[:, k * step : (k + 1) * step], fill], axis=0)
            block = pltpu.roll(block, (keep * (k + 1) - RIM) % extra, 0)
            below = jnp.where((at >= keep * k) & (at < keep * (k + 1)), block, below)
        out[state_dim:, :] = below.astype(BF16)
        head_rows(low, high, x, bc, taps_x, taps_bc, scale, out)


def next_kernel(low, high, active, _, x, bc, taps_x, taps_bc, scale, out):
    @pl.when(active[0] == 1)
    def _():
        head_rows(low, high, x, bc, taps_x, taps_bc, scale, out)


def prepare_kernel(
    cuts, _, x, bc, dt_raw, a_log, gain, skip, pack, gain_out, skip_out, scale, *decays
):
    tokens, width = x.shape
    groups, both = bc.shape[1:]
    pack[:, :width] = x[tokens - 2 * RIM :, :].astype(F32)[-RIM:].astype(BF16)
    last_bc = bc[tokens - 2 * RIM :].astype(F32)[-RIM:]
    for g in range(groups):
        pack[:, width + g * both : width + (g + 1) * both] = last_bc[:, g].astype(BF16)
    gain_out[...] = gain[...]
    skip_out[...] = skip[...]
    row = scales(groups, width // dt_raw.shape[0], dt_raw, a_log, scale)
    for decay, (low, high) in zip(decays, cuts):
        decay[...] = row[:, low:high]


def rows_before(rows, begin, stop, keep, state_dim):
    if rows.shape[0] == RIM:
        return rows[:, begin:stop].astype(F32)
    step = rows.shape[1]
    below = rows[state_dim:, begin % step : begin % step + stop - begin].astype(F32)
    return pltpu.roll(below, (RIM - keep * (begin // step + 1)) % below.shape[0], 0)[:RIM]


def later_kernel(low, high, active, rows, _, x, bc, taps_x, taps_bc, scale, state):
    both = bc.shape[2]
    state_dim = both // 2
    keep = taps_x.shape[0] - 1

    def before(begin, stop):
        return rows_before(rows, begin, stop, keep, state_dim)

    def tail_bc(group):
        at = x.shape[1] + group * both
        return before(at, at + state_dim)

    @pl.when(active[0] == 1)
    def _():
        def emit(here, total):
            state[:, here] = total

        emit_states(
            low, high, x, lambda cut: before(cut.start, cut.stop), bc, tail_bc,
            taps_x, taps_bc, scale, emit,
        )


def gate_kernel(groups, _, z_hbm, dt_raw, a_log, gate, lead, dt_out, cum_out, z, sem):
    copy = pltpu.make_async_copy(z_hbm, z, sem)
    copy.start()
    dt, cum = rates(dt_raw[...], a_log[...], 0)
    dt_out[...] = dt
    cum_out[...] = cum
    leading = jnp.exp(cum)
    heads = dt.shape[0] // groups
    cols = z.shape[1] // groups
    for g in range(groups):
        lead[:, g * cols : (g + 1) * cols] = spread(
            leading[g * heads : (g + 1) * heads], cols // heads, 2
        )
    copy.wait()
    for at in range(0, z.shape[1], CHUNK):
        cut = slice(at, at + CHUNK)
        here = silu(z[:, cut].astype(F32))
        gate[:, cut] = here
        lead[:, cut] = lead[:, cut] * here


def intra_kernel(count, *refs):
    sources, refs = refs[:count], refs[count:]
    x, bc, gate, taps_x, taps_bc, dt, cum, d_skip, y_part, c_act = refs
    tokens, width = x.shape
    groups, both = bc.shape[1:]
    state_dim = both // 2
    keep = taps_x.shape[0] - 1
    cols = width // groups
    heads = dt.shape[0] // groups
    head_dim = cols // heads
    cum_t = cum[...].T
    skip = spread_row(as_column(d_skip[...], 0, groups * heads), head_dim)
    t_at = lax.broadcasted_iota(jnp.int32, (tokens, tokens), 0)
    s_at = lax.broadcasted_iota(jnp.int32, (tokens, tokens), 1)
    pair = 2 * head_dim

    def before(begin, stop):
        found = [rows_before(rows, begin, stop, keep, state_dim) for rows in sources]
        return sum(found[1:], found[0])

    for g in range(groups):
        at = width + g * both
        tail_bc = jnp.concatenate(
            [before(at, at + state_dim), before(at + state_dim, at + both)], axis=1
        )
        bc_act = conv_act(bc[...].astype(F32)[:, g], tail_bc, taps_bc[...][:, g])
        b, c = bc_act[:, :state_dim], bc_act[:, state_dim:]
        c_act[:, g * state_dim : (g + 1) * state_dim] = c
        inner = lax.dot_general(c, b, (((1,), (1,)), ((), ())), preferred_element_type=F32)
        inner = jnp.where(t_at >= s_at, inner, 0.0)
        for first in range(0, heads, 2):
            here = first * head_dim
            cut = slice(g * cols + here, g * cols + here + pair)
            act = conv_act(x[:, cut].astype(F32), before(cut.start, cut.stop), taps_x[:, cut])
            lane = lax.broadcasted_iota(jnp.int32, act.shape, 1)
            full = act.astype(F32)
            blocks = jnp.concatenate(
                [jnp.where(lane < head_dim, full, 0.0), jnp.where(lane < head_dim, 0.0, full)],
                axis=0,
            ).astype(BF16)
            weights = []
            for h in (g * heads + first, g * heads + first + 1):
                gap = jnp.minimum(cum_t[:, h : h + 1] - cum[h : h + 1, :], 0.0)
                weights.append((jnp.exp(gap) * dt[h : h + 1, :] * inner).astype(BF16))
            y = jnp.dot(jnp.concatenate(weights, axis=1), blocks, preferred_element_type=F32)
            y_part[:, cut] = (y + skip[:, cut] * full) * gate[:, cut]


def gated_slice(low, which, c, y_part, lead, arrived):
    tokens, width = y_part.shape
    state_dim = arrived[-1].shape[0]
    size = arrived[-1].shape[1]
    state = jnp.zeros((state_dim, size), BF16)
    for i, came in enumerate(arrived):
        state = jnp.where(which[0] == i, came[...][:state_dim], state)
    pieces = []
    for group, begin, stop in by_group(low, low + size, width * state_dim // c.shape[1]):
        from_state = jnp.dot(
            c[:, group * state_dim : (group + 1) * state_dim],
            state[:, begin - low : stop - low],
            preferred_element_type=F32,
        )
        pieces.append(y_part[:, begin:stop] + lead[:, begin:stop] * from_state)
    return pieces


def gated_kernel(low, which, c, y_part, lead, *refs):
    at = 0
    for piece in gated_slice(low, which, c, y_part, lead, refs[:-1]):
        refs[-1][:, at : at + piece.shape[1]] = piece
        at += piece.shape[1]


def output_kernel(begin, ready, low, which, c, y_part, lead, gain, *refs):
    out, made, sems = refs[-3:]
    tokens, cols = made.shape
    pieces = [refs[i][:, a:b] for i, (a, b) in enumerate(ready)]
    if low is not None:
        arrived = refs[len(ready) : len(refs) - 3]
        if begin > 0:
            arrived = arrived[:-1]
        pieces += gated_slice(low, which, c, y_part, lead, arrived)
    total = jnp.zeros((tokens, 1), F32)
    for piece in pieces:
        total = total + jnp.sum(piece * piece, axis=1, keepdims=True)
    factor = lax.rsqrt(total / cols + EPS)
    copies = []
    at = 0
    for i, piece in enumerate(pieces):
        span = slice(at, at + piece.shape[1])
        made[:, span] = (piece * factor * gain[:, begin + at : begin + span.stop]).astype(BF16)
        copies.append(
            pltpu.make_async_copy(
                made.at[:, span], out.at[:, pl.ds(begin + at, piece.shape[1])], sems.at[i]
            )
        )
        copies[-1].start()
        at = span.stop
    for copy in copies:
        copy.wait()


def params(mib):
    return pltpu.CompilerParams(vmem_limit_bytes=mib * 1024 * 1024)


def doubling(state, decay, devices):
    def moved(value, distance):
        return lax.ppermute(value, "seq", [(i, i + distance) for i in range(devices - distance)])

    total, decay = moved(state.astype(BF16), 1), moved(decay, 1)
    distance = 1
    while distance < devices - 1:
        came = moved(total, distance)
        total = (decay * came.astype(F32) + total.astype(F32)).astype(BF16)
        decay = decay * moved(decay, distance)
        distance *= 2
    return total


def shards(x_in, bc_in, z_in, dt_raw, conv_x, conv_bc, a_log, d_skip, norm_gain):
    tokens, width = x_in.shape
    groups, both = bc_in.shape[1:]
    state_dim = both // 2
    heads = dt_raw.shape[1]
    head_dim = width // heads
    cols = width // groups
    devices = lax.axis_size("seq")
    place = lax.axis_index("seq")
    edges = [width * sum(PARTS[:i]) // sum(PARTS) for i in range(len(PARTS) + 1)]
    cuts = list(zip(edges[:-1], edges[1:]))

    taps = conv_x.shape[0]
    dt_t = dt_raw.T
    a_row = a_log.reshape(1, heads)
    d_row = d_skip.reshape(1, heads)
    gain = norm_gain.reshape(1, width)
    sources = [x_in, bc_in, conv_x, conv_bc]
    operands = sources + [dt_t, a_row]
    pinned = [pltpu.with_memory_space_constraint(v, pltpu.HBM) for v in operands]
    landed = [pltpu.VMEM(v.shape, v.dtype) for v in operands]
    scale_shape = jax.ShapeDtypeStruct((tokens, width), F32)
    scalar = pl.BlockSpec(memory_space=pltpu.SMEM)
    in_vmem = pl.BlockSpec(memory_space=pltpu.VMEM)
    anywhere = pl.BlockSpec(memory_space=pl.ANY)
    in_hbm = [pl.BlockSpec(memory_space=pltpu.HBM)] * len(operands)

    def here(condition):
        return condition.astype(jnp.int32).reshape(1)

    def shifted(value, route):
        return lax.ppermute(value, "seq", route)

    def first_states(low, high):
        blocks = -(-(width + groups * both) // (high - low))
        extra = -(-(taps - 1) * blocks // (2 * RIM)) * 2 * RIM
        return pl.pallas_call(
            functools.partial(first_kernel, low, high),
            out_shape=[jax.ShapeDtypeStruct((state_dim + extra, high - low), BF16), scale_shape],
            in_specs=[scalar] + in_hbm,
            scratch_shapes=landed + [pltpu.SemaphoreType.DMA((len(operands),))],
            compiler_params=params(8),
            name="first_states",
        )(here(place == 0), *pinned)

    def next_states(token, scale, low, high):
        return pl.pallas_call(
            functools.partial(next_kernel, low, high),
            out_shape=jax.ShapeDtypeStruct((state_dim, high - low), BF16),
            in_specs=[scalar, anywhere] + [in_vmem] * (len(sources) + 1),
            compiler_params=params(8),
            name="next_states",
        )(here(place == 0), token, *sources, scale)

    def prepared(token):
        return pl.pallas_call(
            functools.partial(prepare_kernel, cuts),
            out_shape=[
                jax.ShapeDtypeStruct((RIM, width + groups * both), BF16),
                jax.ShapeDtypeStruct((1, width), F32),
                jax.ShapeDtypeStruct((1, heads), F32),
                scale_shape,
            ]
            + [jax.ShapeDtypeStruct((1, high - low), F32) for low, high in cuts],
            in_specs=[anywhere] + [in_vmem] * 6,
            compiler_params=params(8),
            name="prepared",
        )(token, x_in, bc_in, dt_t, a_row, gain, d_row)

    def later_states(condition, rows, token, scale, low, high):
        return pl.pallas_call(
            functools.partial(later_kernel, low, high),
            out_shape=jax.ShapeDtypeStruct((state_dim, high - low), F32),
            in_specs=[scalar, in_vmem, anywhere] + [in_vmem] * (len(sources) + 1),
            compiler_params=params(8),
            name="later_states",
        )(here(condition), rows, token, *sources, scale)

    along = [(i, i + 1) for i in range(devices - 1)]
    def gates(token):
        per_head = jax.ShapeDtypeStruct((heads, tokens), F32)
        return pl.pallas_call(
            functools.partial(gate_kernel, groups),
            out_shape=[scale_shape, scale_shape, per_head, per_head],
            in_specs=[anywhere, anywhere] + [in_vmem] * 2,
            scratch_shapes=[pltpu.VMEM(z_in.shape, z_in.dtype), pltpu.SemaphoreType.DMA],
            compiler_params=params(8),
            name="gates",
        )(token, z_in, dt_t, a_row)

    def intra(befores, gate, dt, cum, skip):
        return pl.pallas_call(
            functools.partial(intra_kernel, len(befores)),
            out_shape=[
                scale_shape, jax.ShapeDtypeStruct((tokens, groups * state_dim), BF16)
            ],
            in_specs=[in_vmem] * (len(befores) + 8),
            compiler_params=params(16),
            cost_estimate=pl.CostEstimate(
                flops=4 * tokens * tokens * width,
                bytes_accessed=12 * tokens * width,
                transcendentals=tokens * tokens * heads,
            ),
            name="intra",
        )(*befores, x_in, bc_in, gate, conv_x, conv_bc, dt, cum, skip)

    gate_parts = None
    if devices <= CHAIN_MOST:
        first, scale = first_states(*cuts[0])
        sent = [first, next_states(first, scale, *cuts[1])]
        last, gain, d_row, scale_own, *decays = prepared(sent[-1])
        token = last
        for cut in cuts[2:]:
            sent.append(next_states(token, scale, *cut))
            token = sent[-1]
        soon = along[1 : max(devices - 2, 1)]
        late = along[max(devices - 2, 1) :]
        befores = [shifted(last, soon)] if soon else []
        arrived = [[shifted(v, along[:1])] for v in sent]
        befores.append(arrived[0][0])
        rows, token = arrived[0][0], last
        for hop in range(1, devices - 1):
            runs = place == 1 if hop == 1 else (place >= 2) & (place < devices - 1)
            for i, cut in enumerate(cuts):
                if hop == 1:
                    after = last if i == 0 else made_at[1 if i == len(cuts) - 1 else 0]
                if hop <= 2:
                    made = later_states(runs, rows, after, scale_own, *cut)
                    states = [made] if i == 0 else states + [made]
                early = ()
                if hop == devices - 2 and hop > 1 and i == 1:
                    gate_parts = gates(token)
                    early = (gate_parts[0],)
                if hop == devices - 2 and hop > 1 and i == len(cuts) - 1:
                    early = (arrived[0][-1], befores[-1])
                before, *_ = lax.optimization_barrier((arrived[i][-1], token) + early)
                joined = decays[i] * before[:state_dim].astype(F32) + states[i]
                token = joined.astype(BF16)
                made_at = [token] if i == 0 else made_at + [token]
                if hop == 1 and i == 1 and late:
                    moved, _ = lax.optimization_barrier((last, token))
                    befores.append(shifted(moved, late))
                arrived[i].append(shifted(token, along[hop : hop + 1]))
            rows, after = befores[0], token
        which = place - 1
    else:
        last, gain, d_row, scale, *decays = prepared(a_row)
        befores = [shifted(last, along)]
        arrived = []
        for decay, cut in zip(decays, cuts):
            state = later_states(place >= 0, befores[0], a_row, scale, *cut)
            arrived.append([doubling(state, decay, devices)])
        which = jnp.zeros_like(place)
    which = which.astype(jnp.int32).reshape(1)
    gate, lead, dt, cum = gate_parts or gates(a_row)
    y_part, c_act = intra(befores, gate, dt, cum, d_row)

    common = [which, c_act, y_part, lead]
    common_specs = [scalar] + [in_vmem] * 3
    last_low, last_high = cuts[-1]
    ready = []
    for (low, high), seen in zip(cuts[:-1], arrived):
        ready.append(
            pl.pallas_call(
                functools.partial(gated_kernel, low),
                out_shape=jax.ShapeDtypeStruct((tokens, high - low), F32),
                in_specs=common_specs + [in_vmem] * len(seen),
                compiler_params=params(8),
                name="gated",
            )(*common, *seen)
        )
    out = None
    for g in range(groups):
        begin, stop = g * cols, (g + 1) * cols
        taken, spans = [], []
        for (low, high), v in zip(cuts[:-1], ready):
            if low < stop and high > begin:
                taken.append(v)
                spans.append((max(low, begin) - low, min(high, stop) - low))
        inputs = taken
        unready = None
        if last_low < stop:
            unready = last_low
            inputs = taken + arrived[-1]
        aliases = {}
        specs = common_specs + [in_vmem] * (1 + len(inputs))
        if out is not None:
            aliases = {len(common) + 1 + len(inputs): 0}
            inputs = inputs + [out]
            specs = specs + [anywhere]
        out = pl.pallas_call(
            functools.partial(output_kernel, begin, spans, unready),
            out_shape=jax.ShapeDtypeStruct((tokens, width), BF16),
            in_specs=specs,
            out_specs=anywhere,
            scratch_shapes=[
                pltpu.VMEM((tokens, cols), BF16),
                pltpu.SemaphoreType.DMA((len(cuts) + groups,)),
            ],
            input_output_aliases=aliases,
            compiler_params=params(8),
            name="outputs",
        )(*common, gain, *inputs)
    return out


def solution(mesh):
    return jax.shard_map(
        shards,
        mesh=mesh,
        in_specs=(
            P(("groups", "seq"), "head"),
            P(("groups", "seq"), "head", None),
            P(("groups", "seq"), "head"),
            P(("groups", "seq"), "head"),
            P(None, "head"),
            P(None, "head", None),
            P("head"),
            P("head"),
            P("head"),
        ),
        out_specs=P(("groups", "seq"), "head"),
        check_vma=False,
    )
```

```python
import functools

import jax
import jax.numpy as jnp
from jax import lax
from jax.experimental import pallas as pl
from jax.experimental.pallas import tpu as pltpu
from jax.sharding import PartitionSpec as P

EPS = 1e-05
F32 = jnp.float32
BF16 = jnp.bfloat16
CHAIN_MOST = 4
PARTS = (3, 5, 4, 4)
CHUNK = 128
RIM = 8


def silu(u):
    return 0.5 * u * (1.0 + jnp.tanh(0.5 * u))


def softplus(v):
    return jnp.maximum(v, 0.0) + jnp.log1p(jnp.exp(-jnp.abs(v)))


def halves(v, count, axis):
    parts = []
    for _ in range(count - 1):
        part = v.astype(BF16)
        parts.append(part)
        v = v - part.astype(F32)
    parts.append(v.astype(BF16))
    return jnp.concatenate(parts, axis=axis)


def spread(per_head, head_dim, count):
    heads = per_head.shape[0]
    rows = lax.broadcasted_iota(jnp.int32, (heads * count, heads * head_dim), 0)
    cols = lax.broadcasted_iota(jnp.int32, (heads * count, heads * head_dim), 1)
    pick = (rows % heads == cols // head_dim).astype(F32).astype(BF16)
    return lax.dot_general(
        halves(per_head, count, 0), pick, (((0,), (0,)), ((), ())), preferred_element_type=F32
    )


def spread_row(column, head_dim):
    heads = column.shape[0]
    rows = lax.broadcasted_iota(jnp.int32, (heads, heads * head_dim), 0)
    cols = lax.broadcasted_iota(jnp.int32, (heads, heads * head_dim), 1)
    return jnp.sum(jnp.where(rows == cols // head_dim, column, 0.0), axis=0, keepdims=True)


def as_column(row, start, heads):
    every = row.shape[1]
    rows = lax.broadcasted_iota(jnp.int32, (heads, every), 0)
    cols = lax.broadcasted_iota(jnp.int32, (heads, every), 1)
    return jnp.sum(jnp.where(cols == rows + start, row, 0.0), axis=1, keepdims=True)


def conv_act(series, tail, taps):
    count = taps.shape[0]
    above = tail.shape[0]
    padded = jnp.concatenate([tail, series], axis=0)
    total = taps[count - 1 : count] * series
    for back in range(1, count):
        total = total + taps[count - 1 - back : count - back] * pltpu.roll(padded, back, 0)[above:]
    return silu(total).astype(BF16)


def rates(dt_raw, a_log_row, start):
    heads, tokens = dt_raw.shape
    dt = softplus(dt_raw)
    rate = -jnp.exp(as_column(a_log_row, start, heads)) * dt
    earlier = lax.broadcasted_iota(jnp.int32, (tokens, tokens), 0)
    later = lax.broadcasted_iota(jnp.int32, (tokens, tokens), 1)
    upto = (earlier <= later).astype(F32).astype(BF16)
    cum = jnp.dot(
        halves(rate, 3, 1), jnp.concatenate([upto] * 3, axis=0), preferred_element_type=F32
    )
    return dt, cum


def scales(groups, head_dim, dt_raw, a_log, scale):
    dt, cum = rates(dt_raw[...], a_log[...], 0)
    end = cum[:, -1:]
    tail_decay = jnp.exp(end - cum) * dt
    heads = dt.shape[0] // groups
    for g in range(groups):
        scale[:, g * heads * head_dim : (g + 1) * heads * head_dim] = spread(
            tail_decay[g * heads : (g + 1) * heads], head_dim, 2
        )
    return spread_row(jnp.exp(end), head_dim)


def by_group(low, high, cols):
    found = []
    while low < high:
        stop = min(high, (low // cols + 1) * cols)
        found.append((low // cols, low, stop))
        low = stop
    return found


def emit_states(low, high, x, tail_x, bc, tail_bc, taps_x, taps_bc, scale, emit):
    groups, both = bc.shape[1:]
    state_dim = both // 2
    for group, begin, stop in by_group(low, high, x.shape[1] // groups):
        b = conv_act(
            bc[:, :, :state_dim].astype(F32)[:, group],
            tail_bc(group),
            taps_bc[:, :, :state_dim][:, group],
        )
        b_t = b.astype(F32).T.astype(BF16)
        for at in range(begin, stop, CHUNK):
            cut = slice(at, at + CHUNK)
            act = conv_act(x[:, cut].astype(F32), tail_x(cut), taps_x[:, cut])
            scaled = (scale[:, cut] * act.astype(F32)).astype(BF16)
            here = slice(at - low, at - low + CHUNK)
            emit(here, jnp.dot(b_t, scaled, preferred_element_type=F32))


def head_rows(low, high, x, bc, taps_x, taps_bc, scale, out):
    state_dim = bc.shape[2] // 2

    def emit(here, total):
        out[:state_dim, here] = total.astype(BF16)

    emit_states(
        low, high, x, lambda cut: jnp.zeros((RIM, CHUNK), F32),
        bc, lambda group: jnp.zeros((RIM, state_dim), F32), taps_x, taps_bc, scale, emit,
    )


def first_kernel(
    low, high, active, x_hbm, bc_hbm, taps_x_hbm, taps_bc_hbm, dt_hbm, a_hbm,
    out, scale, x, bc, taps_x, taps_bc, dt_raw, a_log, sems,
):
    tokens, width = x.shape
    groups, both = bc.shape[1:]

    @pl.when(active[0] == 1)
    def _():
        pairs = [
            (dt_hbm, dt_raw), (a_hbm, a_log), (x_hbm, x), (bc_hbm, bc),
            (taps_x_hbm, taps_x), (taps_bc_hbm, taps_bc),
        ]
        copies = [pltpu.make_async_copy(*pair, sems.at[i]) for i, pair in enumerate(pairs)]
        for copy in copies:
            copy.start()
        for copy in copies[:2]:
            copy.wait()
        scales(groups, width // dt_raw.shape[0], dt_raw, a_log, scale)
        for copy in copies[2:]:
            copy.wait()
        state_dim, step = both // 2, high - low
        keep = taps_x.shape[0] - 1
        extra = out.shape[0] - state_dim
        last_bc = bc[tokens - 2 * RIM :].astype(F32)[-RIM:]
        last = [x[tokens - 2 * RIM :, :].astype(F32)[-RIM:]] + [last_bc[:, g] for g in range(groups)]
        length = width + groups * both
        last.append(jnp.zeros((RIM, -length % step + step), F32))
        last = jnp.concatenate(last, axis=1)
        at = lax.broadcasted_iota(jnp.int32, (extra, step), 0)
        below = jnp.zeros((extra, step), F32)
        fill = jnp.zeros((extra - RIM, step), F32)
        for k in range(-(-length // step)):
            block = jnp.concatenate([last[:, k * step : (k + 1) * step], fill], axis=0)
            block = pltpu.roll(block, (keep * (k + 1) - RIM) % extra, 0)
            below = jnp.where((at >= keep * k) & (at < keep * (k + 1)), block, below)
        out[state_dim:, :] = below.astype(BF16)
        head_rows(low, high, x, bc, taps_x, taps_bc, scale, out)


def next_kernel(low, high, active, _, x, bc, taps_x, taps_bc, scale, out):
    @pl.when(active[0] == 1)
    def _():
        head_rows(low, high, x, bc, taps_x, taps_bc, scale, out)


def prepare_kernel(
    cuts, _, x, bc, dt_raw, a_log, gain, skip, pack, gain_out, skip_out, scale, *decays
):
    tokens, width = x.shape
    groups, both = bc.shape[1:]
    pack[:, :width] = x[tokens - 2 * RIM :, :].astype(F32)[-RIM:].astype(BF16)
    last_bc = bc[tokens - 2 * RIM :].astype(F32)[-RIM:]
    for g in range(groups):
        pack[:, width + g * both : width + (g + 1) * both] = last_bc[:, g].astype(BF16)
    gain_out[...] = gain[...]
    skip_out[...] = skip[...]
    row = scales(groups, width // dt_raw.shape[0], dt_raw, a_log, scale)
    for decay, (low, high) in zip(decays, cuts):
        decay[...] = row[:, low:high]


def rows_before(rows, begin, stop, keep, state_dim):
    if rows.shape[0] == RIM:
        return rows[:, begin:stop].astype(F32)
    step = rows.shape[1]
    below = rows[state_dim:, begin % step : begin % step + stop - begin].astype(F32)
    return pltpu.roll(below, (RIM - keep * (begin // step + 1)) % below.shape[0], 0)[:RIM]


def later_kernel(low, high, active, rows, _, x, bc, taps_x, taps_bc, scale, state):
    both = bc.shape[2]
    state_dim = both // 2
    keep = taps_x.shape[0] - 1

    def before(begin, stop):
        return rows_before(rows, begin, stop, keep, state_dim)

    def tail_bc(group):
        at = x.shape[1] + group * both
        return before(at, at + state_dim)

    @pl.when(active[0] == 1)
    def _():
        def emit(here, total):
            state[:, here] = total

        emit_states(
            low, high, x, lambda cut: before(cut.start, cut.stop), bc, tail_bc,
            taps_x, taps_bc, scale, emit,
        )


def intra_kernel(count, _, *refs):
    sources, refs = refs[:count], refs[count:]
    x, bc, z, taps_x, taps_bc, dt_raw, a_log, d_skip, y_part, lead, c_act, wide = refs
    tokens, width = x.shape
    groups, both = bc.shape[1:]
    state_dim = both // 2
    keep = taps_x.shape[0] - 1
    cols = width // groups
    heads = dt_raw.shape[0] // groups
    head_dim = cols // heads
    dt, cum = rates(dt_raw[...], a_log[...], 0)
    cum_t = cum.T
    leading = jnp.exp(cum)
    skip = spread_row(as_column(d_skip[...], 0, groups * heads), head_dim)
    t_at = lax.broadcasted_iota(jnp.int32, (tokens, tokens), 0)
    s_at = lax.broadcasted_iota(jnp.int32, (tokens, tokens), 1)
    pair = 2 * head_dim

    def before(begin, stop):
        found = [rows_before(rows, begin, stop, keep, state_dim) for rows in sources]
        return sum(found[1:], found[0])

    for g in range(groups):
        at = width + g * both
        tail_bc = jnp.concatenate(
            [before(at, at + state_dim), before(at + state_dim, at + both)], axis=1
        )
        bc_act = conv_act(bc[...].astype(F32)[:, g], tail_bc, taps_bc[...][:, g])
        b, c = bc_act[:, :state_dim], bc_act[:, state_dim:]
        c_act[:, g * state_dim : (g + 1) * state_dim] = c
        inner = lax.dot_general(c, b, (((1,), (1,)), ((), ())), preferred_element_type=F32)
        inner = jnp.where(t_at >= s_at, inner, 0.0)
        wide[...] = spread(leading[g * heads : (g + 1) * heads], head_dim, 2)
        for first in range(0, heads, 2):
            here = slice(first * head_dim, first * head_dim + pair)
            cut = slice(g * cols + here.start, g * cols + here.stop)
            act = conv_act(x[:, cut].astype(F32), before(cut.start, cut.stop), taps_x[:, cut])
            lane = lax.broadcasted_iota(jnp.int32, act.shape, 1)
            full = act.astype(F32)
            blocks = jnp.concatenate(
                [jnp.where(lane < head_dim, full, 0.0), jnp.where(lane < head_dim, 0.0, full)],
                axis=0,
            ).astype(BF16)
            weights = []
            for h in (g * heads + first, g * heads + first + 1):
                gap = jnp.minimum(cum_t[:, h : h + 1] - cum[h : h + 1, :], 0.0)
                weights.append((jnp.exp(gap) * dt[h : h + 1, :] * inner).astype(BF16))
            y = jnp.dot(jnp.concatenate(weights, axis=1), blocks, preferred_element_type=F32)
            gate = silu(z[:, cut].astype(F32))
            y_part[:, cut] = (y + skip[:, cut] * full) * gate
            lead[:, cut] = wide[:, here] * gate


def gated_slice(low, which, c, y_part, lead, arrived):
    tokens, width = y_part.shape
    state_dim = arrived[-1].shape[0]
    size = arrived[-1].shape[1]
    state = jnp.zeros((state_dim, size), BF16)
    for i, came in enumerate(arrived):
        state = jnp.where(which[0] == i, came[...][:state_dim], state)
    pieces = []
    for group, begin, stop in by_group(low, low + size, width * state_dim // c.shape[1]):
        from_state = jnp.dot(
            c[:, group * state_dim : (group + 1) * state_dim],
            state[:, begin - low : stop - low],
            preferred_element_type=F32,
        )
        pieces.append(y_part[:, begin:stop] + lead[:, begin:stop] * from_state)
    return pieces


def gated_kernel(low, which, c, y_part, lead, *refs):
    at = 0
    for piece in gated_slice(low, which, c, y_part, lead, refs[:-1]):
        refs[-1][:, at : at + piece.shape[1]] = piece
        at += piece.shape[1]


def output_kernel(begin, ready, low, which, c, y_part, lead, gain, *refs):
    out, made, sems = refs[-3:]
    tokens, cols = made.shape
    pieces = [refs[i][:, a:b] for i, (a, b) in enumerate(ready)]
    if low is not None:
        arrived = refs[len(ready) : len(refs) - 3]
        if begin > 0:
            arrived = arrived[:-1]
        pieces += gated_slice(low, which, c, y_part, lead, arrived)
    total = jnp.zeros((tokens, 1), F32)
    for piece in pieces:
        total = total + jnp.sum(piece * piece, axis=1, keepdims=True)
    factor = lax.rsqrt(total / cols + EPS)
    copies = []
    at = 0
    for i, piece in enumerate(pieces):
        span = slice(at, at + piece.shape[1])
        made[:, span] = (piece * factor * gain[:, begin + at : begin + span.stop]).astype(BF16)
        copies.append(
            pltpu.make_async_copy(
                made.at[:, span], out.at[:, pl.ds(begin + at, piece.shape[1])], sems.at[i]
            )
        )
        copies[-1].start()
        at = span.stop
    for copy in copies:
        copy.wait()


def params(mib):
    return pltpu.CompilerParams(vmem_limit_bytes=mib * 1024 * 1024)


def doubling(state, decay, devices):
    def moved(value, distance):
        return lax.ppermute(value, "seq", [(i, i + distance) for i in range(devices - distance)])

    total, decay = moved(state.astype(BF16), 1), moved(decay, 1)
    distance = 1
    while distance < devices - 1:
        came = moved(total, distance)
        total = (decay * came.astype(F32) + total.astype(F32)).astype(BF16)
        decay = decay * moved(decay, distance)
        distance *= 2
    return total


def shards(x_in, bc_in, z_in, dt_raw, conv_x, conv_bc, a_log, d_skip, norm_gain):
    tokens, width = x_in.shape
    groups, both = bc_in.shape[1:]
    state_dim = both // 2
    heads = dt_raw.shape[1]
    head_dim = width // heads
    cols = width // groups
    devices = lax.axis_size("seq")
    place = lax.axis_index("seq")
    edges = [width * sum(PARTS[:i]) // sum(PARTS) for i in range(len(PARTS) + 1)]
    cuts = list(zip(edges[:-1], edges[1:]))

    taps = conv_x.shape[0]
    dt_t = dt_raw.T
    a_row = a_log.reshape(1, heads)
    d_row = d_skip.reshape(1, heads)
    gain = norm_gain.reshape(1, width)
    sources = [x_in, bc_in, conv_x, conv_bc]
    operands = sources + [dt_t, a_row]
    pinned = [pltpu.with_memory_space_constraint(v, pltpu.HBM) for v in operands]
    landed = [pltpu.VMEM(v.shape, v.dtype) for v in operands]
    scale_shape = jax.ShapeDtypeStruct((tokens, width), F32)
    scalar = pl.BlockSpec(memory_space=pltpu.SMEM)
    in_vmem = pl.BlockSpec(memory_space=pltpu.VMEM)
    anywhere = pl.BlockSpec(memory_space=pl.ANY)
    in_hbm = [pl.BlockSpec(memory_space=pltpu.HBM)] * len(operands)

    def here(condition):
        return condition.astype(jnp.int32).reshape(1)

    def shifted(value, route):
        return lax.ppermute(value, "seq", route)

    def first_states(low, high):
        blocks = -(-(width + groups * both) // (high - low))
        extra = -(-(taps - 1) * blocks // (2 * RIM)) * 2 * RIM
        return pl.pallas_call(
            functools.partial(first_kernel, low, high),
            out_shape=[jax.ShapeDtypeStruct((state_dim + extra, high - low), BF16), scale_shape],
            in_specs=[scalar] + in_hbm,
            scratch_shapes=landed + [pltpu.SemaphoreType.DMA((len(operands),))],
            compiler_params=params(16),
            name="first_states",
        )(here(place == 0), *pinned)

    def next_states(token, scale, low, high):
        return pl.pallas_call(
            functools.partial(next_kernel, low, high),
            out_shape=jax.ShapeDtypeStruct((state_dim, high - low), BF16),
            in_specs=[scalar, anywhere] + [in_vmem] * (len(sources) + 1),
            compiler_params=params(16),
            name="next_states",
        )(here(place == 0), token, *sources, scale)

    def prepared(token):
        return pl.pallas_call(
            functools.partial(prepare_kernel, cuts),
            out_shape=[
                jax.ShapeDtypeStruct((RIM, width + groups * both), BF16),
                jax.ShapeDtypeStruct((1, width), F32),
                jax.ShapeDtypeStruct((1, heads), F32),
                scale_shape,
            ]
            + [jax.ShapeDtypeStruct((1, high - low), F32) for low, high in cuts],
            in_specs=[anywhere] + [in_vmem] * 6,
            compiler_params=params(16),
            name="prepared",
        )(token, x_in, bc_in, dt_t, a_row, gain, d_row)

    def later_states(condition, rows, token, scale, low, high):
        return pl.pallas_call(
            functools.partial(later_kernel, low, high),
            out_shape=jax.ShapeDtypeStruct((state_dim, high - low), F32),
            in_specs=[scalar, in_vmem, anywhere] + [in_vmem] * (len(sources) + 1),
            compiler_params=params(16),
            name="later_states",
        )(here(condition), rows, token, *sources, scale)

    along = [(i, i + 1) for i in range(devices - 1)]
    def intra(token, befores, skip):
        return pl.pallas_call(
            functools.partial(intra_kernel, len(befores)),
            out_shape=[
                scale_shape, scale_shape, jax.ShapeDtypeStruct((tokens, groups * state_dim), BF16)
            ],
            in_specs=[anywhere] + [in_vmem] * (len(befores) + 8),
            scratch_shapes=[pltpu.VMEM((tokens, cols), F32)],
            compiler_params=params(24),
            cost_estimate=pl.CostEstimate(
                flops=4 * tokens * tokens * width,
                bytes_accessed=12 * tokens * width,
                transcendentals=tokens * tokens * heads,
            ),
            name="intra",
        )(token, *befores, x_in, bc_in, z_in, conv_x, conv_bc, dt_t, a_row, skip)

    if devices <= CHAIN_MOST:
        first, scale = first_states(*cuts[0])
        sent = [first, next_states(first, scale, *cuts[1])]
        last, gain, d_row, scale_own, *decays = prepared(sent[-1])
        token = last
        for cut in cuts[2:]:
            sent.append(next_states(token, scale, *cut))
            token = sent[-1]
        soon = along[1 : max(devices - 2, 1)]
        late = along[max(devices - 2, 1) :]
        befores = [shifted(last, soon)] if soon else []
        arrived = [[shifted(v, along[:1])] for v in sent]
        befores.append(arrived[0][0])
        rows, token = arrived[0][0], last
        for hop in range(1, devices - 1):
            runs = place == 1 if hop == 1 else (place >= 2) & (place < devices - 1)
            for i, cut in enumerate(cuts):
                if hop == 1:
                    after = last if i == 0 else made_at[1 if i == len(cuts) - 1 else 0]
                if hop <= 2:
                    made = later_states(runs, rows, after, scale_own, *cut)
                    states = [made] if i == 0 else states + [made]
                early = ()
                if hop == devices - 2 and hop > 1 and i == len(cuts) - 1:
                    early = (arrived[0][-1], befores[-1])
                before, *_ = lax.optimization_barrier((arrived[i][-1], token) + early)
                joined = decays[i] * before[:state_dim].astype(F32) + states[i]
                token = joined.astype(BF16)
                made_at = [token] if i == 0 else made_at + [token]
                if hop == 1 and i == 1 and late:
                    moved, _ = lax.optimization_barrier((last, token))
                    befores.append(shifted(moved, late))
                arrived[i].append(shifted(token, along[hop : hop + 1]))
            rows, after = befores[0], token
        which = place - 1
    else:
        last, gain, d_row, scale, *decays = prepared(a_row)
        befores = [shifted(last, along)]
        arrived = []
        for decay, cut in zip(decays, cuts):
            state = later_states(place >= 0, befores[0], a_row, scale, *cut)
            arrived.append([doubling(state, decay, devices)])
        which = jnp.zeros_like(place)
    which = which.astype(jnp.int32).reshape(1)
    y_part, lead, c_act = intra(a_row, befores, d_row)

    common = [which, c_act, y_part, lead]
    common_specs = [scalar] + [in_vmem] * 3
    last_low, last_high = cuts[-1]
    ready = []
    for (low, high), seen in zip(cuts[:-1], arrived):
        ready.append(
            pl.pallas_call(
                functools.partial(gated_kernel, low),
                out_shape=jax.ShapeDtypeStruct((tokens, high - low), F32),
                in_specs=common_specs + [in_vmem] * len(seen),
                compiler_params=params(16),
                name="gated",
            )(*common, *seen)
        )
    out = None
    for g in range(groups):
        begin, stop = g * cols, (g + 1) * cols
        taken, spans = [], []
        for (low, high), v in zip(cuts[:-1], ready):
            if low < stop and high > begin:
                taken.append(v)
                spans.append((max(low, begin) - low, min(high, stop) - low))
        inputs = taken
        unready = None
        if last_low < stop:
            unready = last_low
            inputs = taken + arrived[-1]
        aliases = {}
        specs = common_specs + [in_vmem] * (1 + len(inputs))
        if out is not None:
            aliases = {len(common) + 1 + len(inputs): 0}
            inputs = inputs + [out]
            specs = specs + [anywhere]
        out = pl.pallas_call(
            functools.partial(output_kernel, begin, spans, unready),
            out_shape=jax.ShapeDtypeStruct((tokens, width), BF16),
            in_specs=specs,
            out_specs=anywhere,
            scratch_shapes=[
                pltpu.VMEM((tokens, cols), BF16),
                pltpu.SemaphoreType.DMA((len(cuts) + groups,)),
            ],
            input_output_aliases=aliases,
            compiler_params=params(16),
            name="outputs",
        )(*common, gain, *inputs)
    return out


def solution(mesh):
    return jax.shard_map(
        shards,
        mesh=mesh,
        in_specs=(
            P(("groups", "seq"), "head"),
            P(("groups", "seq"), "head", None),
            P(("groups", "seq"), "head"),
            P(("groups", "seq"), "head"),
            P(None, "head"),
            P(None, "head", None),
            P("head"),
            P("head"),
            P("head"),
        ),
        out_specs=P(("groups", "seq"), "head"),
        check_vma=False,
    )
```

```python
import functools

import jax
import jax.numpy as jnp
from jax import lax
from jax.experimental import pallas as pl
from jax.experimental.pallas import tpu as pltpu
from jax.sharding import PartitionSpec as P

EPS = 1e-05
F32 = jnp.float32
BF16 = jnp.bfloat16
CHAIN_MOST = 4
PARTS = (1, 1, 1, 1)
CHUNK = 128
RIM = 8


def silu(u):
    return 0.5 * u * (1.0 + jnp.tanh(0.5 * u))


def softplus(v):
    return jnp.maximum(v, 0.0) + jnp.log1p(jnp.exp(-jnp.abs(v)))


def halves(v, count, axis):
    parts = []
    for _ in range(count - 1):
        part = v.astype(BF16)
        parts.append(part)
        v = v - part.astype(F32)
    parts.append(v.astype(BF16))
    return jnp.concatenate(parts, axis=axis)


def spread(per_head, head_dim, count):
    heads = per_head.shape[0]
    rows = lax.broadcasted_iota(jnp.int32, (heads * count, heads * head_dim), 0)
    cols = lax.broadcasted_iota(jnp.int32, (heads * count, heads * head_dim), 1)
    pick = (rows % heads == cols // head_dim).astype(F32).astype(BF16)
    return lax.dot_general(
        halves(per_head, count, 0), pick, (((0,), (0,)), ((), ())), preferred_element_type=F32
    )


def spread_row(column, head_dim):
    heads = column.shape[0]
    rows = lax.broadcasted_iota(jnp.int32, (heads, heads * head_dim), 0)
    cols = lax.broadcasted_iota(jnp.int32, (heads, heads * head_dim), 1)
    return jnp.sum(jnp.where(rows == cols // head_dim, column, 0.0), axis=0, keepdims=True)


def as_column(row, start, heads):
    every = row.shape[1]
    rows = lax.broadcasted_iota(jnp.int32, (heads, every), 0)
    cols = lax.broadcasted_iota(jnp.int32, (heads, every), 1)
    return jnp.sum(jnp.where(cols == rows + start, row, 0.0), axis=1, keepdims=True)


def conv_act(series, tail, taps):
    count = taps.shape[0]
    above = tail.shape[0]
    padded = jnp.concatenate([tail, series], axis=0)
    total = taps[count - 1 : count] * series
    for back in range(1, count):
        total = total + taps[count - 1 - back : count - back] * pltpu.roll(padded, back, 0)[above:]
    return silu(total).astype(BF16)


def rates(dt_raw, a_log_row, start):
    heads, tokens = dt_raw.shape
    dt = softplus(dt_raw)
    rate = -jnp.exp(as_column(a_log_row, start, heads)) * dt
    earlier = lax.broadcasted_iota(jnp.int32, (tokens, tokens), 0)
    later = lax.broadcasted_iota(jnp.int32, (tokens, tokens), 1)
    upto = (earlier <= later).astype(F32).astype(BF16)
    cum = jnp.dot(
        halves(rate, 3, 1), jnp.concatenate([upto] * 3, axis=0), preferred_element_type=F32
    )
    return dt, cum


def scales(groups, head_dim, dt_raw, a_log, scale):
    dt, cum = rates(dt_raw[...], a_log[...], 0)
    end = cum[:, -1:]
    tail_decay = jnp.exp(end - cum) * dt
    heads = dt.shape[0] // groups
    for g in range(groups):
        scale[:, g * heads * head_dim : (g + 1) * heads * head_dim] = spread(
            tail_decay[g * heads : (g + 1) * heads], head_dim, 2
        )
    return spread_row(jnp.exp(end), head_dim)


def by_group(low, high, cols):
    found = []
    while low < high:
        stop = min(high, (low // cols + 1) * cols)
        found.append((low // cols, low, stop))
        low = stop
    return found


def emit_states(low, high, x, tail_x, bc, tail_bc, taps_x, taps_bc, scale, emit):
    groups, both = bc.shape[1:]
    state_dim = both // 2
    for group, begin, stop in by_group(low, high, x.shape[1] // groups):
        b = conv_act(
            bc[:, :, :state_dim].astype(F32)[:, group],
            tail_bc(group),
            taps_bc[:, :, :state_dim][:, group],
        )
        b_t = b.astype(F32).T.astype(BF16)
        for at in range(begin, stop, CHUNK):
            cut = slice(at, at + CHUNK)
            act = conv_act(x[:, cut].astype(F32), tail_x(cut), taps_x[:, cut])
            scaled = (scale[:, cut] * act.astype(F32)).astype(BF16)
            here = slice(at - low, at - low + CHUNK)
            emit(here, jnp.dot(b_t, scaled, preferred_element_type=F32))


def head_rows(low, high, x, bc, taps_x, taps_bc, scale, out):
    state_dim = bc.shape[2] // 2

    def emit(here, total):
        out[:state_dim, here] = total.astype(BF16)

    emit_states(
        low, high, x, lambda cut: jnp.zeros((RIM, CHUNK), F32),
        bc, lambda group: jnp.zeros((RIM, state_dim), F32), taps_x, taps_bc, scale, emit,
    )


def first_kernel(
    low, high, active, x_hbm, bc_hbm, taps_x_hbm, taps_bc_hbm, dt_hbm, a_hbm,
    out, scale, x, bc, taps_x, taps_bc, dt_raw, a_log, sems,
):
    tokens, width = x.shape
    groups, both = bc.shape[1:]

    @pl.when(active[0] == 1)
    def _():
        pairs = [
            (dt_hbm, dt_raw), (a_hbm, a_log), (x_hbm, x), (bc_hbm, bc),
            (taps_x_hbm, taps_x), (taps_bc_hbm, taps_bc),
        ]
        copies = [pltpu.make_async_copy(*pair, sems.at[i]) for i, pair in enumerate(pairs)]
        for copy in copies:
            copy.start()
        for copy in copies[:2]:
            copy.wait()
        scales(groups, width // dt_raw.shape[0], dt_raw, a_log, scale)
        for copy in copies[2:]:
            copy.wait()
        state_dim, step = both // 2, high - low
        keep = taps_x.shape[0] - 1
        extra = out.shape[0] - state_dim
        last_bc = bc[tokens - 2 * RIM :].astype(F32)[-RIM:]
        last = [x[tokens - 2 * RIM :, :].astype(F32)[-RIM:]] + [last_bc[:, g] for g in range(groups)]
        length = width + groups * both
        last.append(jnp.zeros((RIM, -length % step + step), F32))
        last = jnp.concatenate(last, axis=1)
        at = lax.broadcasted_iota(jnp.int32, (extra, step), 0)
        below = jnp.zeros((extra, step), F32)
        fill = jnp.zeros((extra - RIM, step), F32)
        for k in range(-(-length // step)):
            block = jnp.concatenate([last[:, k * step : (k + 1) * step], fill], axis=0)
            block = pltpu.roll(block, (keep * (k + 1) - RIM) % extra, 0)
            below = jnp.where((at >= keep * k) & (at < keep * (k + 1)), block, below)
        out[state_dim:, :] = below.astype(BF16)
        head_rows(low, high, x, bc, taps_x, taps_bc, scale, out)


def next_kernel(low, high, active, _, x, bc, taps_x, taps_bc, scale, out):
    @pl.when(active[0] == 1)
    def _():
        head_rows(low, high, x, bc, taps_x, taps_bc, scale, out)


def prepare_kernel(cuts, _, x, bc, dt_raw, a_log, gain, pack, gain_out, scale, *decays):
    tokens, width = x.shape
    groups, both = bc.shape[1:]
    pack[:, :width] = x[tokens - 2 * RIM :, :].astype(F32)[-RIM:].astype(BF16)
    last_bc = bc[tokens - 2 * RIM :].astype(F32)[-RIM:]
    for g in range(groups):
        pack[:, width + g * both : width + (g + 1) * both] = last_bc[:, g].astype(BF16)
    gain_out[...] = gain[...]
    row = scales(groups, width // dt_raw.shape[0], dt_raw, a_log, scale)
    for decay, (low, high) in zip(decays, cuts):
        decay[...] = row[:, low:high]


def rows_before(rows, begin, stop, keep, state_dim):
    if rows.shape[0] == RIM:
        return rows[:, begin:stop].astype(F32)
    step = rows.shape[1]
    below = rows[state_dim:, begin % step : begin % step + stop - begin].astype(F32)
    return pltpu.roll(below, (RIM - keep * (begin // step + 1)) % below.shape[0], 0)[:RIM]


def later_kernel(low, high, active, rows, _, x, bc, taps_x, taps_bc, scale, state):
    both = bc.shape[2]
    state_dim = both // 2
    keep = taps_x.shape[0] - 1

    def before(begin, stop):
        return rows_before(rows, begin, stop, keep, state_dim)

    def tail_bc(group):
        at = x.shape[1] + group * both
        return before(at, at + state_dim)

    @pl.when(active[0] == 1)
    def _():
        def emit(here, total):
            state[:, here] = total

        emit_states(
            low, high, x, lambda cut: before(cut.start, cut.stop), bc, tail_bc,
            taps_x, taps_bc, scale, emit,
        )


def intra_kernel(count, _, *refs):
    sources, refs = refs[:count], refs[count:]
    x, bc, z, taps_x, taps_bc, dt_raw, a_log, d_skip, y_part, lead, c_act, wide = refs
    tokens, width = x.shape
    groups, both = bc.shape[1:]
    state_dim = both // 2
    keep = taps_x.shape[0] - 1
    cols = width // groups
    heads = dt_raw.shape[0] // groups
    head_dim = cols // heads
    dt, cum = rates(dt_raw[...], a_log[...], 0)
    cum_t = cum.T
    leading = jnp.exp(cum)
    skip = spread_row(as_column(d_skip[...], 0, groups * heads), head_dim)
    t_at = lax.broadcasted_iota(jnp.int32, (tokens, tokens), 0)
    s_at = lax.broadcasted_iota(jnp.int32, (tokens, tokens), 1)
    pair = 2 * head_dim

    def before(begin, stop):
        found = [rows_before(rows, begin, stop, keep, state_dim) for rows in sources]
        return sum(found[1:], found[0])

    for g in range(groups):
        at = width + g * both
        tail_bc = jnp.concatenate(
            [before(at, at + state_dim), before(at + state_dim, at + both)], axis=1
        )
        bc_act = conv_act(bc[...].astype(F32)[:, g], tail_bc, taps_bc[...][:, g])
        b, c = bc_act[:, :state_dim], bc_act[:, state_dim:]
        c_act[:, g * state_dim : (g + 1) * state_dim] = c
        inner = lax.dot_general(c, b, (((1,), (1,)), ((), ())), preferred_element_type=F32)
        inner = jnp.where(t_at >= s_at, inner, 0.0)
        wide[...] = spread(leading[g * heads : (g + 1) * heads], head_dim, 2)
        for first in range(0, heads, 2):
            here = slice(first * head_dim, first * head_dim + pair)
            cut = slice(g * cols + here.start, g * cols + here.stop)
            act = conv_act(x[:, cut].astype(F32), before(cut.start, cut.stop), taps_x[:, cut])
            lane = lax.broadcasted_iota(jnp.int32, act.shape, 1)
            full = act.astype(F32)
            blocks = jnp.concatenate(
                [jnp.where(lane < head_dim, full, 0.0), jnp.where(lane < head_dim, 0.0, full)],
                axis=0,
            ).astype(BF16)
            weights = []
            for h in (g * heads + first, g * heads + first + 1):
                gap = jnp.minimum(cum_t[:, h : h + 1] - cum[h : h + 1, :], 0.0)
                weights.append((jnp.exp(gap) * dt[h : h + 1, :] * inner).astype(BF16))
            y = jnp.dot(jnp.concatenate(weights, axis=1), blocks, preferred_element_type=F32)
            gate = silu(z[:, cut].astype(F32))
            y_part[:, cut] = (y + skip[:, cut] * full) * gate
            lead[:, cut] = wide[:, here] * gate


def gated_slice(low, which, c, y_part, lead, arrived):
    tokens, width = y_part.shape
    state_dim = arrived[-1].shape[0]
    size = arrived[-1].shape[1]
    state = jnp.zeros((state_dim, size), BF16)
    for i, came in enumerate(arrived):
        state = jnp.where(which[0] == i, came[...][:state_dim], state)
    pieces = []
    for group, begin, stop in by_group(low, low + size, width * state_dim // c.shape[1]):
        from_state = jnp.dot(
            c[:, group * state_dim : (group + 1) * state_dim],
            state[:, begin - low : stop - low],
            preferred_element_type=F32,
        )
        pieces.append(y_part[:, begin:stop] + lead[:, begin:stop] * from_state)
    return pieces


def gated_kernel(low, which, c, y_part, lead, *refs):
    at = 0
    for piece in gated_slice(low, which, c, y_part, lead, refs[:-1]):
        refs[-1][:, at : at + piece.shape[1]] = piece
        at += piece.shape[1]


def output_kernel(begin, ready, low, which, c, y_part, lead, gain, *refs):
    out, made, sems = refs[-3:]
    tokens, cols = made.shape
    pieces = [refs[i][:, a:b] for i, (a, b) in enumerate(ready)]
    if low is not None:
        arrived = refs[len(ready) : len(refs) - 3]
        if begin > 0:
            arrived = arrived[:-1]
        pieces += gated_slice(low, which, c, y_part, lead, arrived)
    total = jnp.zeros((tokens, 1), F32)
    for piece in pieces:
        total = total + jnp.sum(piece * piece, axis=1, keepdims=True)
    factor = lax.rsqrt(total / cols + EPS)
    copies = []
    at = 0
    for i, piece in enumerate(pieces):
        span = slice(at, at + piece.shape[1])
        made[:, span] = (piece * factor * gain[:, begin + at : begin + span.stop]).astype(BF16)
        copies.append(
            pltpu.make_async_copy(
                made.at[:, span], out.at[:, pl.ds(begin + at, piece.shape[1])], sems.at[i]
            )
        )
        copies[-1].start()
        at = span.stop
    for copy in copies:
        copy.wait()


def params(mib):
    return pltpu.CompilerParams(vmem_limit_bytes=mib * 1024 * 1024)


def doubling(state, decay, devices):
    def moved(value, distance):
        return lax.ppermute(value, "seq", [(i, i + distance) for i in range(devices - distance)])

    total, decay = moved(state.astype(BF16), 1), moved(decay, 1)
    distance = 1
    while distance < devices - 1:
        came = moved(total, distance)
        total = (decay * came.astype(F32) + total.astype(F32)).astype(BF16)
        decay = decay * moved(decay, distance)
        distance *= 2
    return total


def shards(x_in, bc_in, z_in, dt_raw, conv_x, conv_bc, a_log, d_skip, norm_gain):
    tokens, width = x_in.shape
    groups, both = bc_in.shape[1:]
    state_dim = both // 2
    heads = dt_raw.shape[1]
    head_dim = width // heads
    cols = width // groups
    devices = lax.axis_size("seq")
    place = lax.axis_index("seq")
    edges = [width * sum(PARTS[:i]) // sum(PARTS) for i in range(len(PARTS) + 1)]
    cuts = list(zip(edges[:-1], edges[1:]))

    taps = conv_x.shape[0]
    dt_t = dt_raw.T
    a_row = a_log.reshape(1, heads)
    d_row = d_skip.reshape(1, heads)
    gain = norm_gain.reshape(1, width)
    sources = [x_in, bc_in, conv_x, conv_bc]
    operands = sources + [dt_t, a_row]
    pinned = [pltpu.with_memory_space_constraint(v, pltpu.HBM) for v in operands]
    landed = [pltpu.VMEM(v.shape, v.dtype) for v in operands]
    scale_shape = jax.ShapeDtypeStruct((tokens, width), F32)
    scalar = pl.BlockSpec(memory_space=pltpu.SMEM)
    in_vmem = pl.BlockSpec(memory_space=pltpu.VMEM)
    anywhere = pl.BlockSpec(memory_space=pl.ANY)
    in_hbm = [pl.BlockSpec(memory_space=pltpu.HBM)] * len(operands)

    def here(condition):
        return condition.astype(jnp.int32).reshape(1)

    def shifted(value, route):
        return lax.ppermute(value, "seq", route)

    def first_states(low, high):
        blocks = -(-(width + groups * both) // (high - low))
        extra = -(-(taps - 1) * blocks // (2 * RIM)) * 2 * RIM
        return pl.pallas_call(
            functools.partial(first_kernel, low, high),
            out_shape=[jax.ShapeDtypeStruct((state_dim + extra, high - low), BF16), scale_shape],
            in_specs=[scalar] + in_hbm,
            scratch_shapes=landed + [pltpu.SemaphoreType.DMA((len(operands),))],
            compiler_params=params(16),
            name="first_states",
        )(here(place == 0), *pinned)

    def next_states(token, scale, low, high):
        return pl.pallas_call(
            functools.partial(next_kernel, low, high),
            out_shape=jax.ShapeDtypeStruct((state_dim, high - low), BF16),
            in_specs=[scalar, anywhere] + [in_vmem] * (len(sources) + 1),
            compiler_params=params(16),
            name="next_states",
        )(here(place == 0), token, *sources, scale)

    def prepared(token):
        return pl.pallas_call(
            functools.partial(prepare_kernel, cuts),
            out_shape=[
                jax.ShapeDtypeStruct((RIM, width + groups * both), BF16),
                jax.ShapeDtypeStruct((1, width), F32),
                scale_shape,
            ]
            + [jax.ShapeDtypeStruct((1, high - low), F32) for low, high in cuts],
            in_specs=[anywhere] + [in_vmem] * 5,
            compiler_params=params(16),
            name="prepared",
        )(token, x_in, bc_in, dt_t, a_row, gain)

    def later_states(condition, rows, token, scale, low, high):
        return pl.pallas_call(
            functools.partial(later_kernel, low, high),
            out_shape=jax.ShapeDtypeStruct((state_dim, high - low), F32),
            in_specs=[scalar, in_vmem, anywhere] + [in_vmem] * (len(sources) + 1),
            compiler_params=params(16),
            name="later_states",
        )(here(condition), rows, token, *sources, scale)

    along = [(i, i + 1) for i in range(devices - 1)]
    def intra(token, befores):
        return pl.pallas_call(
            functools.partial(intra_kernel, len(befores)),
            out_shape=[
                scale_shape, scale_shape, jax.ShapeDtypeStruct((tokens, groups * state_dim), BF16)
            ],
            in_specs=[anywhere] + [in_vmem] * (len(befores) + 8),
            scratch_shapes=[pltpu.VMEM((tokens, cols), F32)],
            compiler_params=params(24),
            cost_estimate=pl.CostEstimate(
                flops=4 * tokens * tokens * width,
                bytes_accessed=12 * tokens * width,
                transcendentals=tokens * tokens * heads,
            ),
            name="intra",
        )(token, *befores, x_in, bc_in, z_in, conv_x, conv_bc, dt_t, a_row, d_row)

    if devices <= CHAIN_MOST:
        first, scale = first_states(*cuts[0])
        sent = [first, next_states(first, scale, *cuts[1])]
        last, gain, scale_own, *decays = prepared(sent[-1])
        token = last
        for cut in cuts[2:]:
            sent.append(next_states(token, scale, *cut))
            token = sent[-1]
        soon = along[1 : max(devices - 2, 1)]
        late = along[max(devices - 2, 1) :]
        befores = [shifted(last, soon)] if soon else []
        arrived = [[shifted(v, along[:1])] for v in sent]
        befores.append(arrived[0][0])
        rows, token = arrived[0][0], last
        for hop in range(1, devices - 1):
            runs = place == 1 if hop == 1 else (place >= 2) & (place < devices - 1)
            after = token
            for i, cut in enumerate(cuts):
                if hop <= 2:
                    made = later_states(runs, rows, after, scale_own, *cut)
                    states = [made] if i == 0 else states + [made]
                early = ()
                if hop == devices - 2 and hop > 1 and i == len(cuts) - 1:
                    early = (befores[-1],)
                before, *_ = lax.optimization_barrier((arrived[i][-1], token) + early)
                joined = decays[i] * before[:state_dim].astype(F32) + states[i]
                token = joined.astype(BF16)
                after = token if hop == 1 else after
                arrived[i].append(shifted(token, along[hop : hop + 1]))
            if hop == 1 and late:
                moved, _ = lax.optimization_barrier((last, token))
                befores.append(shifted(moved, late))
            rows = befores[0]
        which = place - 1
    else:
        last, gain, scale, *decays = prepared(a_row)
        befores = [shifted(last, along)]
        arrived = []
        for decay, cut in zip(decays, cuts):
            state = later_states(place >= 0, befores[0], a_row, scale, *cut)
            arrived.append([doubling(state, decay, devices)])
        which = jnp.zeros_like(place)
    which = which.astype(jnp.int32).reshape(1)
    y_part, lead, c_act = intra(a_row, befores)

    common = [which, c_act, y_part, lead]
    common_specs = [scalar] + [in_vmem] * 3
    last_low, last_high = cuts[-1]
    ready = []
    for (low, high), seen in zip(cuts[:-1], arrived):
        ready.append(
            pl.pallas_call(
                functools.partial(gated_kernel, low),
                out_shape=jax.ShapeDtypeStruct((tokens, high - low), F32),
                in_specs=common_specs + [in_vmem] * len(seen),
                compiler_params=params(16),
                name="gated",
            )(*common, *seen)
        )
    out = None
    for g in range(groups):
        begin, stop = g * cols, (g + 1) * cols
        taken, spans = [], []
        for (low, high), v in zip(cuts[:-1], ready):
            if low < stop and high > begin:
                taken.append(v)
                spans.append((max(low, begin) - low, min(high, stop) - low))
        inputs = taken
        unready = None
        if last_low < stop:
            unready = last_low
            inputs = taken + arrived[-1]
        aliases = {}
        specs = common_specs + [in_vmem] * (1 + len(inputs))
        if out is not None:
            aliases = {len(common) + 1 + len(inputs): 0}
            inputs = inputs + [out]
            specs = specs + [anywhere]
        out = pl.pallas_call(
            functools.partial(output_kernel, begin, spans, unready),
            out_shape=jax.ShapeDtypeStruct((tokens, width), BF16),
            in_specs=specs,
            out_specs=anywhere,
            scratch_shapes=[
                pltpu.VMEM((tokens, cols), BF16),
                pltpu.SemaphoreType.DMA((len(cuts) + groups,)),
            ],
            input_output_aliases=aliases,
            compiler_params=params(16),
            name="outputs",
        )(*common, gain, *inputs)
    return out


def solution(mesh):
    return jax.shard_map(
        shards,
        mesh=mesh,
        in_specs=(
            P(("groups", "seq"), "head"),
            P(("groups", "seq"), "head", None),
            P(("groups", "seq"), "head"),
            P(("groups", "seq"), "head"),
            P(None, "head"),
            P(None, "head", None),
            P("head"),
            P("head"),
            P("head"),
        ),
        out_specs=P(("groups", "seq"), "head"),
        check_vma=False,
    )
```

```python
import functools

import jax
import jax.numpy as jnp
from jax import lax
from jax.experimental import pallas as pl
from jax.experimental.pallas import tpu as pltpu
from jax.sharding import PartitionSpec as P

EPS = 1e-05
F32 = jnp.float32
BF16 = jnp.bfloat16
CHAIN_MOST = 4
PARTS = (1, 1, 1, 1)
CHUNK = 128
RIM = 8


def silu(u):
    return 0.5 * u * (1.0 + jnp.tanh(0.5 * u))


def softplus(v):
    return jnp.maximum(v, 0.0) + jnp.log1p(jnp.exp(-jnp.abs(v)))


def halves(v, count, axis):
    parts = []
    for _ in range(count - 1):
        part = v.astype(BF16)
        parts.append(part)
        v = v - part.astype(F32)
    parts.append(v.astype(BF16))
    return jnp.concatenate(parts, axis=axis)


def spread(per_head, head_dim, count):
    heads = per_head.shape[0]
    rows = lax.broadcasted_iota(jnp.int32, (heads * count, heads * head_dim), 0)
    cols = lax.broadcasted_iota(jnp.int32, (heads * count, heads * head_dim), 1)
    pick = (rows % heads == cols // head_dim).astype(F32).astype(BF16)
    return lax.dot_general(
        halves(per_head, count, 0), pick, (((0,), (0,)), ((), ())), preferred_element_type=F32
    )


def spread_row(column, head_dim):
    heads = column.shape[0]
    rows = lax.broadcasted_iota(jnp.int32, (heads, heads * head_dim), 0)
    cols = lax.broadcasted_iota(jnp.int32, (heads, heads * head_dim), 1)
    return jnp.sum(jnp.where(rows == cols // head_dim, column, 0.0), axis=0, keepdims=True)


def as_column(row, start, heads):
    every = row.shape[1]
    rows = lax.broadcasted_iota(jnp.int32, (heads, every), 0)
    cols = lax.broadcasted_iota(jnp.int32, (heads, every), 1)
    return jnp.sum(jnp.where(cols == rows + start, row, 0.0), axis=1, keepdims=True)


def conv_act(series, tail, taps):
    count = taps.shape[0]
    above = tail.shape[0]
    padded = jnp.concatenate([tail, series], axis=0)
    total = taps[count - 1 : count] * series
    for back in range(1, count):
        total = total + taps[count - 1 - back : count - back] * pltpu.roll(padded, back, 0)[above:]
    return silu(total).astype(BF16)


def rates(dt_raw, a_log_row, start):
    heads, tokens = dt_raw.shape
    dt = softplus(dt_raw)
    rate = -jnp.exp(as_column(a_log_row, start, heads)) * dt
    earlier = lax.broadcasted_iota(jnp.int32, (tokens, tokens), 0)
    later = lax.broadcasted_iota(jnp.int32, (tokens, tokens), 1)
    upto = (earlier <= later).astype(F32).astype(BF16)
    cum = jnp.dot(
        halves(rate, 3, 1), jnp.concatenate([upto] * 3, axis=0), preferred_element_type=F32
    )
    return dt, cum


def scales(groups, head_dim, dt_raw, a_log, scale):
    dt, cum = rates(dt_raw[...], a_log[...], 0)
    end = cum[:, -1:]
    tail_decay = jnp.exp(end - cum) * dt
    heads = dt.shape[0] // groups
    for g in range(groups):
        scale[:, g * heads * head_dim : (g + 1) * heads * head_dim] = spread(
            tail_decay[g * heads : (g + 1) * heads], head_dim, 2
        )
    return spread_row(jnp.exp(end), head_dim)


def by_group(low, high, cols):
    found = []
    while low < high:
        stop = min(high, (low // cols + 1) * cols)
        found.append((low // cols, low, stop))
        low = stop
    return found


def emit_states(low, high, x, tail_x, bc, tail_bc, taps_x, taps_bc, scale, emit):
    groups, both = bc.shape[1:]
    state_dim = both // 2
    for group, begin, stop in by_group(low, high, x.shape[1] // groups):
        b = conv_act(
            bc[:, :, :state_dim].astype(F32)[:, group],
            tail_bc(group),
            taps_bc[:, :, :state_dim][:, group],
        )
        b_t = b.astype(F32).T.astype(BF16)
        for at in range(begin, stop, CHUNK):
            cut = slice(at, at + CHUNK)
            act = conv_act(x[:, cut].astype(F32), tail_x(cut), taps_x[:, cut])
            scaled = (scale[:, cut] * act.astype(F32)).astype(BF16)
            here = slice(at - low, at - low + CHUNK)
            emit(here, jnp.dot(b_t, scaled, preferred_element_type=F32))


def head_rows(low, high, x, bc, taps_x, taps_bc, scale, out):
    state_dim = bc.shape[2] // 2

    def emit(here, total):
        out[:state_dim, here] = total.astype(BF16)

    emit_states(
        low, high, x, lambda cut: jnp.zeros((RIM, CHUNK), F32),
        bc, lambda group: jnp.zeros((RIM, state_dim), F32), taps_x, taps_bc, scale, emit,
    )


def first_kernel(
    low, high, active, x_hbm, bc_hbm, taps_x_hbm, taps_bc_hbm, dt_hbm, a_hbm,
    out, scale, x, bc, taps_x, taps_bc, dt_raw, a_log, sems,
):
    tokens, width = x.shape
    groups, both = bc.shape[1:]

    @pl.when(active[0] == 1)
    def _():
        pairs = [
            (dt_hbm, dt_raw), (a_hbm, a_log), (x_hbm, x), (bc_hbm, bc),
            (taps_x_hbm, taps_x), (taps_bc_hbm, taps_bc),
        ]
        copies = [pltpu.make_async_copy(*pair, sems.at[i]) for i, pair in enumerate(pairs)]
        for copy in copies:
            copy.start()
        for copy in copies[:2]:
            copy.wait()
        scales(groups, width // dt_raw.shape[0], dt_raw, a_log, scale)
        for copy in copies[2:]:
            copy.wait()
        state_dim, step = both // 2, high - low
        keep = taps_x.shape[0] - 1
        extra = out.shape[0] - state_dim
        last_bc = bc[tokens - 2 * RIM :].astype(F32)[-RIM:]
        last = [x[tokens - 2 * RIM :, :].astype(F32)[-RIM:]] + [last_bc[:, g] for g in range(groups)]
        length = width + groups * both
        last.append(jnp.zeros((RIM, -length % step + step), F32))
        last = jnp.concatenate(last, axis=1)
        at = lax.broadcasted_iota(jnp.int32, (extra, step), 0)
        below = jnp.zeros((extra, step), F32)
        fill = jnp.zeros((extra - RIM, step), F32)
        for k in range(-(-length // step)):
            block = jnp.concatenate([last[:, k * step : (k + 1) * step], fill], axis=0)
            block = pltpu.roll(block, (keep * (k + 1) - RIM) % extra, 0)
            below = jnp.where((at >= keep * k) & (at < keep * (k + 1)), block, below)
        out[state_dim:, :] = below.astype(BF16)
        head_rows(low, high, x, bc, taps_x, taps_bc, scale, out)


def next_kernel(low, high, active, _, x, bc, taps_x, taps_bc, scale, out):
    @pl.when(active[0] == 1)
    def _():
        head_rows(low, high, x, bc, taps_x, taps_bc, scale, out)


def prepare_kernel(
    cuts, _, x, bc, dt_raw, a_log, gain, skip_hbm, pack, gain_out, skip_out, scale, *refs
):
    decays, sem = refs[:-1], refs[-1]
    skip_copy = pltpu.make_async_copy(skip_hbm, skip_out, sem.at[0])
    skip_copy.start()
    tokens, width = x.shape
    groups, both = bc.shape[1:]
    pack[:, :width] = x[tokens - 2 * RIM :, :].astype(F32)[-RIM:].astype(BF16)
    last_bc = bc[tokens - 2 * RIM :].astype(F32)[-RIM:]
    for g in range(groups):
        pack[:, width + g * both : width + (g + 1) * both] = last_bc[:, g].astype(BF16)
    gain_out[...] = gain[...]
    row = scales(groups, width // dt_raw.shape[0], dt_raw, a_log, scale)
    for decay, (low, high) in zip(decays, cuts):
        decay[...] = row[:, low:high]
    skip_copy.wait()


def rows_before(rows, begin, stop, keep, state_dim):
    if rows.shape[0] == RIM:
        return rows[:, begin:stop].astype(F32)
    step = rows.shape[1]
    below = rows[state_dim:, begin % step : begin % step + stop - begin].astype(F32)
    return pltpu.roll(below, (RIM - keep * (begin // step + 1)) % below.shape[0], 0)[:RIM]


def later_kernel(low, high, active, rows, _, x, bc, taps_x, taps_bc, scale, state):
    both = bc.shape[2]
    state_dim = both // 2
    keep = taps_x.shape[0] - 1

    def before(begin, stop):
        return rows_before(rows, begin, stop, keep, state_dim)

    def tail_bc(group):
        at = x.shape[1] + group * both
        return before(at, at + state_dim)

    @pl.when(active[0] == 1)
    def _():
        def emit(here, total):
            state[:, here] = total

        emit_states(
            low, high, x, lambda cut: before(cut.start, cut.stop), bc, tail_bc,
            taps_x, taps_bc, scale, emit,
        )


def intra_kernel(count, _, *refs):
    sources, refs = refs[:count], refs[count:]
    x, bc, z, taps_x, taps_bc, dt_raw, a_log, d_skip, y_part, lead, c_act, wide = refs
    tokens, width = x.shape
    groups, both = bc.shape[1:]
    state_dim = both // 2
    keep = taps_x.shape[0] - 1
    cols = width // groups
    heads = dt_raw.shape[0] // groups
    head_dim = cols // heads
    dt, cum = rates(dt_raw[...], a_log[...], 0)
    cum_t = cum.T
    leading = jnp.exp(cum)
    skip = spread_row(as_column(d_skip[...], 0, groups * heads), head_dim)
    t_at = lax.broadcasted_iota(jnp.int32, (tokens, tokens), 0)
    s_at = lax.broadcasted_iota(jnp.int32, (tokens, tokens), 1)
    pair = 2 * head_dim

    def before(begin, stop):
        found = [rows_before(rows, begin, stop, keep, state_dim) for rows in sources]
        return sum(found[1:], found[0])

    for g in range(groups):
        at = width + g * both
        tail_bc = jnp.concatenate(
            [before(at, at + state_dim), before(at + state_dim, at + both)], axis=1
        )
        bc_act = conv_act(bc[...].astype(F32)[:, g], tail_bc, taps_bc[...][:, g])
        b, c = bc_act[:, :state_dim], bc_act[:, state_dim:]
        c_act[:, g * state_dim : (g + 1) * state_dim] = c
        inner = lax.dot_general(c, b, (((1,), (1,)), ((), ())), preferred_element_type=F32)
        inner = jnp.where(t_at >= s_at, inner, 0.0)
        wide[...] = spread(leading[g * heads : (g + 1) * heads], head_dim, 2)
        for first in range(0, heads, 2):
            here = slice(first * head_dim, first * head_dim + pair)
            cut = slice(g * cols + here.start, g * cols + here.stop)
            act = conv_act(x[:, cut].astype(F32), before(cut.start, cut.stop), taps_x[:, cut])
            lane = lax.broadcasted_iota(jnp.int32, act.shape, 1)
            full = act.astype(F32)
            blocks = jnp.concatenate(
                [jnp.where(lane < head_dim, full, 0.0), jnp.where(lane < head_dim, 0.0, full)],
                axis=0,
            ).astype(BF16)
            weights = []
            for h in (g * heads + first, g * heads + first + 1):
                gap = jnp.minimum(cum_t[:, h : h + 1] - cum[h : h + 1, :], 0.0)
                weights.append((jnp.exp(gap) * dt[h : h + 1, :] * inner).astype(BF16))
            y = jnp.dot(jnp.concatenate(weights, axis=1), blocks, preferred_element_type=F32)
            gate = silu(z[:, cut].astype(F32))
            y_part[:, cut] = (y + skip[:, cut] * full) * gate
            lead[:, cut] = wide[:, here] * gate


def gated_slice(low, which, c, y_part, lead, arrived):
    tokens, width = y_part.shape
    state_dim = arrived[-1].shape[0]
    size = arrived[-1].shape[1]
    state = jnp.zeros((state_dim, size), BF16)
    for i, came in enumerate(arrived):
        state = jnp.where(which[0] == i, came[...][:state_dim], state)
    pieces = []
    for group, begin, stop in by_group(low, low + size, width * state_dim // c.shape[1]):
        from_state = jnp.dot(
            c[:, group * state_dim : (group + 1) * state_dim],
            state[:, begin - low : stop - low],
            preferred_element_type=F32,
        )
        pieces.append(y_part[:, begin:stop] + lead[:, begin:stop] * from_state)
    return pieces


def gated_kernel(low, which, c, y_part, lead, *refs):
    at = 0
    for piece in gated_slice(low, which, c, y_part, lead, refs[:-1]):
        refs[-1][:, at : at + piece.shape[1]] = piece
        at += piece.shape[1]


def output_kernel(begin, ready, low, which, c, y_part, lead, gain, *refs):
    out, made, sems = refs[-3:]
    tokens, cols = made.shape
    pieces = [refs[i][:, a:b] for i, (a, b) in enumerate(ready)]
    if low is not None:
        arrived = refs[len(ready) : len(refs) - 3]
        if begin > 0:
            arrived = arrived[:-1]
        pieces += gated_slice(low, which, c, y_part, lead, arrived)
    total = jnp.zeros((tokens, 1), F32)
    for piece in pieces:
        total = total + jnp.sum(piece * piece, axis=1, keepdims=True)
    factor = lax.rsqrt(total / cols + EPS)
    copies = []
    at = 0
    for i, piece in enumerate(pieces):
        span = slice(at, at + piece.shape[1])
        made[:, span] = (piece * factor * gain[:, begin + at : begin + span.stop]).astype(BF16)
        copies.append(
            pltpu.make_async_copy(
                made.at[:, span], out.at[:, pl.ds(begin + at, piece.shape[1])], sems.at[i]
            )
        )
        copies[-1].start()
        at = span.stop
    for copy in copies:
        copy.wait()


def params(mib):
    return pltpu.CompilerParams(vmem_limit_bytes=mib * 1024 * 1024)


def doubling(state, decay, devices):
    def moved(value, distance):
        return lax.ppermute(value, "seq", [(i, i + distance) for i in range(devices - distance)])

    total, decay = moved(state.astype(BF16), 1), moved(decay, 1)
    distance = 1
    while distance < devices - 1:
        came = moved(total, distance)
        total = (decay * came.astype(F32) + total.astype(F32)).astype(BF16)
        decay = decay * moved(decay, distance)
        distance *= 2
    return total


def shards(x_in, bc_in, z_in, dt_raw, conv_x, conv_bc, a_log, d_skip, norm_gain):
    tokens, width = x_in.shape
    groups, both = bc_in.shape[1:]
    state_dim = both // 2
    heads = dt_raw.shape[1]
    head_dim = width // heads
    cols = width // groups
    devices = lax.axis_size("seq")
    place = lax.axis_index("seq")
    edges = [width * sum(PARTS[:i]) // sum(PARTS) for i in range(len(PARTS) + 1)]
    cuts = list(zip(edges[:-1], edges[1:]))

    taps = conv_x.shape[0]
    dt_t = dt_raw.T
    a_row = a_log.reshape(1, heads)
    d_row = d_skip.reshape(1, heads)
    gain = norm_gain.reshape(1, width)
    sources = [x_in, bc_in, conv_x, conv_bc]
    operands = sources + [dt_t, a_row]
    pinned = [pltpu.with_memory_space_constraint(v, pltpu.HBM) for v in operands]
    landed = [pltpu.VMEM(v.shape, v.dtype) for v in operands]
    scale_shape = jax.ShapeDtypeStruct((tokens, width), F32)
    scalar = pl.BlockSpec(memory_space=pltpu.SMEM)
    in_vmem = pl.BlockSpec(memory_space=pltpu.VMEM)
    anywhere = pl.BlockSpec(memory_space=pl.ANY)
    in_hbm = [pl.BlockSpec(memory_space=pltpu.HBM)] * len(operands)

    def here(condition):
        return condition.astype(jnp.int32).reshape(1)

    def shifted(value, route):
        return lax.ppermute(value, "seq", route)

    def first_states(low, high):
        blocks = -(-(width + groups * both) // (high - low))
        extra = -(-(taps - 1) * blocks // (2 * RIM)) * 2 * RIM
        return pl.pallas_call(
            functools.partial(first_kernel, low, high),
            out_shape=[jax.ShapeDtypeStruct((state_dim + extra, high - low), BF16), scale_shape],
            in_specs=[scalar] + in_hbm,
            scratch_shapes=landed + [pltpu.SemaphoreType.DMA((len(operands),))],
            compiler_params=params(8),
            name="first_states",
        )(here(place == 0), *pinned)

    def next_states(token, scale, low, high):
        return pl.pallas_call(
            functools.partial(next_kernel, low, high),
            out_shape=jax.ShapeDtypeStruct((state_dim, high - low), BF16),
            in_specs=[scalar, anywhere] + [in_vmem] * (len(sources) + 1),
            compiler_params=params(8),
            name="next_states",
        )(here(place == 0), token, *sources, scale)

    def prepared(token):
        return pl.pallas_call(
            functools.partial(prepare_kernel, cuts),
            out_shape=[
                jax.ShapeDtypeStruct((RIM, width + groups * both), BF16),
                jax.ShapeDtypeStruct((1, width), F32),
                jax.ShapeDtypeStruct((1, heads), F32),
                scale_shape,
            ]
            + [jax.ShapeDtypeStruct((1, high - low), F32) for low, high in cuts],
            in_specs=[anywhere] + [in_vmem] * 5 + [pl.BlockSpec(memory_space=pltpu.HBM)],
            scratch_shapes=[pltpu.SemaphoreType.DMA((1,))],
            compiler_params=params(8),
            name="prepared",
        )(
            token, x_in, bc_in, dt_t, a_row, gain,
            pltpu.with_memory_space_constraint(d_row, pltpu.HBM),
        )

    def later_states(condition, rows, token, scale, low, high):
        return pl.pallas_call(
            functools.partial(later_kernel, low, high),
            out_shape=jax.ShapeDtypeStruct((state_dim, high - low), F32),
            in_specs=[scalar, in_vmem, anywhere] + [in_vmem] * (len(sources) + 1),
            compiler_params=params(8),
            name="later_states",
        )(here(condition), rows, token, *sources, scale)

    along = [(i, i + 1) for i in range(devices - 1)]
    def intra(token, befores, skip):
        return pl.pallas_call(
            functools.partial(intra_kernel, len(befores)),
            out_shape=[
                scale_shape, scale_shape, jax.ShapeDtypeStruct((tokens, groups * state_dim), BF16)
            ],
            in_specs=[anywhere] + [in_vmem] * (len(befores) + 8),
            scratch_shapes=[pltpu.VMEM((tokens, cols), F32)],
            compiler_params=params(12),
            cost_estimate=pl.CostEstimate(
                flops=4 * tokens * tokens * width,
                bytes_accessed=12 * tokens * width,
                transcendentals=tokens * tokens * heads,
            ),
            name="intra",
        )(token, *befores, x_in, bc_in, z_in, conv_x, conv_bc, dt_t, a_row, skip)

    if devices <= CHAIN_MOST:
        first, scale = first_states(*cuts[0])
        sent = [first, next_states(first, scale, *cuts[1])]
        last, gain, d_row, scale_own, *decays = prepared(sent[-1])
        token = last
        for cut in cuts[2:]:
            sent.append(next_states(token, scale, *cut))
            token = sent[-1]
        soon = along[1 : max(devices - 2, 1)]
        late = along[max(devices - 2, 1) :]
        befores = [shifted(last, soon)] if soon else []
        arrived = [[shifted(v, along[:1])] for v in sent]
        befores.append(arrived[0][0])
        rows, token = arrived[0][0], last
        for hop in range(1, devices - 1):
            runs = place == 1 if hop == 1 else (place >= 2) & (place < devices - 1)
            after = token
            for i, cut in enumerate(cuts):
                if hop <= 2:
                    made = later_states(runs, rows, after, scale_own, *cut)
                    states = [made] if i == 0 else states + [made]
                early = ()
                if hop == devices - 2 and hop > 1 and i == len(cuts) - 1:
                    early = (befores[-1],)
                before, *_ = lax.optimization_barrier((arrived[i][-1], token) + early)
                joined = decays[i] * before[:state_dim].astype(F32) + states[i]
                token = joined.astype(BF16)
                after = token if hop == 1 else after
                arrived[i].append(shifted(token, along[hop : hop + 1]))
            if hop == 1 and late:
                moved, _ = lax.optimization_barrier((last, token))
                befores.append(shifted(moved, late))
            rows = befores[0]
        which = place - 1
    else:
        last, gain, d_row, scale, *decays = prepared(a_row)
        befores = [shifted(last, along)]
        arrived = []
        for decay, cut in zip(decays, cuts):
            state = later_states(place >= 0, befores[0], a_row, scale, *cut)
            arrived.append([doubling(state, decay, devices)])
        which = jnp.zeros_like(place)
    which = which.astype(jnp.int32).reshape(1)
    y_part, lead, c_act = intra(a_row, befores, d_row)

    common = [which, c_act, y_part, lead]
    common_specs = [scalar] + [in_vmem] * 3
    last_low, last_high = cuts[-1]
    ready = []
    for (low, high), seen in zip(cuts[:-1], arrived):
        ready.append(
            pl.pallas_call(
                functools.partial(gated_kernel, low),
                out_shape=jax.ShapeDtypeStruct((tokens, high - low), F32),
                in_specs=common_specs + [in_vmem] * len(seen),
                compiler_params=params(8),
                name="gated",
            )(*common, *seen)
        )
    out = None
    for g in range(groups):
        begin, stop = g * cols, (g + 1) * cols
        taken, spans = [], []
        for (low, high), v in zip(cuts[:-1], ready):
            if low < stop and high > begin:
                taken.append(v)
                spans.append((max(low, begin) - low, min(high, stop) - low))
        inputs = taken
        unready = None
        if last_low < stop:
            unready = last_low
            inputs = taken + arrived[-1]
        aliases = {}
        specs = common_specs + [in_vmem] * (1 + len(inputs))
        if out is not None:
            aliases = {len(common) + 1 + len(inputs): 0}
            inputs = inputs + [out]
            specs = specs + [anywhere]
        out = pl.pallas_call(
            functools.partial(output_kernel, begin, spans, unready),
            out_shape=jax.ShapeDtypeStruct((tokens, width), BF16),
            in_specs=specs,
            out_specs=anywhere,
            scratch_shapes=[
                pltpu.VMEM((tokens, cols), BF16),
                pltpu.SemaphoreType.DMA((len(cuts) + groups,)),
            ],
            input_output_aliases=aliases,
            compiler_params=params(8),
            name="outputs",
        )(*common, gain, *inputs)
    return out


def solution(mesh):
    return jax.shard_map(
        shards,
        mesh=mesh,
        in_specs=(
            P(("groups", "seq"), "head"),
            P(("groups", "seq"), "head", None),
            P(("groups", "seq"), "head"),
            P(("groups", "seq"), "head"),
            P(None, "head"),
            P(None, "head", None),
            P("head"),
            P("head"),
            P("head"),
        ),
        out_specs=P(("groups", "seq"), "head"),
        check_vma=False,
    )
```

```python
import functools

import jax
import jax.numpy as jnp
from jax import lax
from jax.experimental import pallas as pl
from jax.experimental.pallas import tpu as pltpu
from jax.sharding import PartitionSpec as P

EPS = 1e-05
F32 = jnp.float32
BF16 = jnp.bfloat16
CHAIN_MOST = 4
PARTS = (1, 1, 1, 1)
CHUNK = 128
RIM = 8


def silu(u):
    return 0.5 * u * (1.0 + jnp.tanh(0.5 * u))


def softplus(v):
    return jnp.maximum(v, 0.0) + jnp.log1p(jnp.exp(-jnp.abs(v)))


def halves(v, count, axis):
    parts = []
    for _ in range(count - 1):
        part = v.astype(BF16)
        parts.append(part)
        v = v - part.astype(F32)
    parts.append(v.astype(BF16))
    return jnp.concatenate(parts, axis=axis)


def spread(per_head, head_dim, count):
    heads = per_head.shape[0]
    rows = lax.broadcasted_iota(jnp.int32, (heads * count, heads * head_dim), 0)
    cols = lax.broadcasted_iota(jnp.int32, (heads * count, heads * head_dim), 1)
    pick = (rows % heads == cols // head_dim).astype(F32).astype(BF16)
    return lax.dot_general(
        halves(per_head, count, 0), pick, (((0,), (0,)), ((), ())), preferred_element_type=F32
    )


def spread_row(column, head_dim):
    heads = column.shape[0]
    rows = lax.broadcasted_iota(jnp.int32, (heads, heads * head_dim), 0)
    cols = lax.broadcasted_iota(jnp.int32, (heads, heads * head_dim), 1)
    return jnp.sum(jnp.where(rows == cols // head_dim, column, 0.0), axis=0, keepdims=True)


def as_column(row, start, heads):
    every = row.shape[1]
    rows = lax.broadcasted_iota(jnp.int32, (heads, every), 0)
    cols = lax.broadcasted_iota(jnp.int32, (heads, every), 1)
    return jnp.sum(jnp.where(cols == rows + start, row, 0.0), axis=1, keepdims=True)


def conv_act(series, tail, taps):
    count = taps.shape[0]
    above = tail.shape[0]
    padded = jnp.concatenate([tail, series], axis=0)
    total = taps[count - 1 : count] * series
    for back in range(1, count):
        total = total + taps[count - 1 - back : count - back] * pltpu.roll(padded, back, 0)[above:]
    return silu(total).astype(BF16)


def rates(dt_raw, a_log_row, start):
    heads, tokens = dt_raw.shape
    dt = softplus(dt_raw)
    rate = -jnp.exp(as_column(a_log_row, start, heads)) * dt
    earlier = lax.broadcasted_iota(jnp.int32, (tokens, tokens), 0)
    later = lax.broadcasted_iota(jnp.int32, (tokens, tokens), 1)
    upto = (earlier <= later).astype(F32).astype(BF16)
    cum = jnp.dot(
        halves(rate, 3, 1), jnp.concatenate([upto] * 3, axis=0), preferred_element_type=F32
    )
    return dt, cum


def scales(groups, head_dim, dt_raw, a_log, scale):
    dt, cum = rates(dt_raw[...], a_log[...], 0)
    end = cum[:, -1:]
    tail_decay = jnp.exp(end - cum) * dt
    heads = dt.shape[0] // groups
    for g in range(groups):
        scale[:, g * heads * head_dim : (g + 1) * heads * head_dim] = spread(
            tail_decay[g * heads : (g + 1) * heads], head_dim, 2
        )
    return spread_row(jnp.exp(end), head_dim)


def by_group(low, high, cols):
    found = []
    while low < high:
        stop = min(high, (low // cols + 1) * cols)
        found.append((low // cols, low, stop))
        low = stop
    return found


def emit_states(low, high, x, tail_x, bc, tail_bc, taps_x, taps_bc, scale, emit):
    groups, both = bc.shape[1:]
    state_dim = both // 2
    for group, begin, stop in by_group(low, high, x.shape[1] // groups):
        b = conv_act(
            bc[:, :, :state_dim].astype(F32)[:, group],
            tail_bc(group),
            taps_bc[:, :, :state_dim][:, group],
        )
        b_t = b.astype(F32).T.astype(BF16)
        for at in range(begin, stop, CHUNK):
            cut = slice(at, at + CHUNK)
            act = conv_act(x[:, cut].astype(F32), tail_x(cut), taps_x[:, cut])
            scaled = (scale[:, cut] * act.astype(F32)).astype(BF16)
            here = slice(at - low, at - low + CHUNK)
            emit(here, jnp.dot(b_t, scaled, preferred_element_type=F32))


def head_rows(low, high, x, bc, taps_x, taps_bc, scale, out):
    state_dim = bc.shape[2] // 2

    def emit(here, total):
        out[:state_dim, here] = total.astype(BF16)

    emit_states(
        low, high, x, lambda cut: jnp.zeros((RIM, CHUNK), F32),
        bc, lambda group: jnp.zeros((RIM, state_dim), F32), taps_x, taps_bc, scale, emit,
    )


def first_kernel(
    low, high, active, x_hbm, bc_hbm, taps_x_hbm, taps_bc_hbm, dt_hbm, a_hbm,
    out, scale, x, bc, taps_x, taps_bc, dt_raw, a_log, sems,
):
    tokens, width = x.shape
    groups, both = bc.shape[1:]

    @pl.when(active[0] == 1)
    def _():
        pairs = [
            (dt_hbm, dt_raw), (a_hbm, a_log), (x_hbm, x), (bc_hbm, bc),
            (taps_x_hbm, taps_x), (taps_bc_hbm, taps_bc),
        ]
        copies = [pltpu.make_async_copy(*pair, sems.at[i]) for i, pair in enumerate(pairs)]
        for copy in copies:
            copy.start()
        for copy in copies[:2]:
            copy.wait()
        scales(groups, width // dt_raw.shape[0], dt_raw, a_log, scale)
        for copy in copies[2:]:
            copy.wait()
        state_dim, step = both // 2, high - low
        keep = taps_x.shape[0] - 1
        extra = out.shape[0] - state_dim
        last_bc = bc[tokens - 2 * RIM :].astype(F32)[-RIM:]
        last = [x[tokens - 2 * RIM :, :].astype(F32)[-RIM:]] + [last_bc[:, g] for g in range(groups)]
        length = width + groups * both
        last.append(jnp.zeros((RIM, -length % step + step), F32))
        last = jnp.concatenate(last, axis=1)
        at = lax.broadcasted_iota(jnp.int32, (extra, step), 0)
        below = jnp.zeros((extra, step), F32)
        fill = jnp.zeros((extra - RIM, step), F32)
        for k in range(-(-length // step)):
            block = jnp.concatenate([last[:, k * step : (k + 1) * step], fill], axis=0)
            block = pltpu.roll(block, (keep * (k + 1) - RIM) % extra, 0)
            below = jnp.where((at >= keep * k) & (at < keep * (k + 1)), block, below)
        out[state_dim:, :] = below.astype(BF16)
        head_rows(low, high, x, bc, taps_x, taps_bc, scale, out)


def next_kernel(low, high, active, _, x, bc, taps_x, taps_bc, scale, out):
    @pl.when(active[0] == 1)
    def _():
        head_rows(low, high, x, bc, taps_x, taps_bc, scale, out)


def prepare_kernel(cuts, _, x, bc, dt_raw, a_log, gain, pack, gain_out, scale, *decays):
    tokens, width = x.shape
    groups, both = bc.shape[1:]
    pack[:, :width] = x[tokens - 2 * RIM :, :].astype(F32)[-RIM:].astype(BF16)
    last_bc = bc[tokens - 2 * RIM :].astype(F32)[-RIM:]
    for g in range(groups):
        pack[:, width + g * both : width + (g + 1) * both] = last_bc[:, g].astype(BF16)
    gain_out[...] = gain[...]
    row = scales(groups, width // dt_raw.shape[0], dt_raw, a_log, scale)
    for decay, (low, high) in zip(decays, cuts):
        decay[...] = row[:, low:high]


def rows_before(rows, begin, stop, keep, state_dim):
    if rows.shape[0] == RIM:
        return rows[:, begin:stop].astype(F32)
    step = rows.shape[1]
    below = rows[state_dim:, begin % step : begin % step + stop - begin].astype(F32)
    return pltpu.roll(below, (RIM - keep * (begin // step + 1)) % below.shape[0], 0)[:RIM]


def later_kernel(low, high, active, rows, _, x, bc, taps_x, taps_bc, scale, *refs):
    state = refs[-1]
    both = bc.shape[2]
    state_dim = both // 2
    keep = taps_x.shape[0] - 1

    def before(begin, stop):
        return rows_before(rows, begin, stop, keep, state_dim)

    def tail_bc(group):
        at = x.shape[1] + group * both
        return before(at, at + state_dim)

    @pl.when(active[0] == 1)
    def _():
        def emit(here, total):
            state[:, here] = total

        emit_states(
            low, high, x, lambda cut: before(cut.start, cut.stop), bc, tail_bc,
            taps_x, taps_bc, scale, emit,
        )


def intra_kernel(count, _, *refs):
    sources, refs = refs[:count], refs[count:]
    x, bc, z, taps_x, taps_bc, dt_raw, a_log, d_skip, y_part, lead, c_act, wide = refs
    tokens, width = x.shape
    groups, both = bc.shape[1:]
    state_dim = both // 2
    keep = taps_x.shape[0] - 1
    cols = width // groups
    heads = dt_raw.shape[0] // groups
    head_dim = cols // heads
    dt, cum = rates(dt_raw[...], a_log[...], 0)
    cum_t = cum.T
    leading = jnp.exp(cum)
    skip = spread_row(as_column(d_skip[...], 0, groups * heads), head_dim)
    t_at = lax.broadcasted_iota(jnp.int32, (tokens, tokens), 0)
    s_at = lax.broadcasted_iota(jnp.int32, (tokens, tokens), 1)
    pair = 2 * head_dim

    def before(begin, stop):
        found = [rows_before(rows, begin, stop, keep, state_dim) for rows in sources]
        return sum(found[1:], found[0])

    for g in range(groups):
        at = width + g * both
        tail_bc = jnp.concatenate(
            [before(at, at + state_dim), before(at + state_dim, at + both)], axis=1
        )
        bc_act = conv_act(bc[...].astype(F32)[:, g], tail_bc, taps_bc[...][:, g])
        b, c = bc_act[:, :state_dim], bc_act[:, state_dim:]
        c_act[:, g * state_dim : (g + 1) * state_dim] = c
        inner = lax.dot_general(c, b, (((1,), (1,)), ((), ())), preferred_element_type=F32)
        inner = jnp.where(t_at >= s_at, inner, 0.0)
        wide[...] = spread(leading[g * heads : (g + 1) * heads], head_dim, 2)
        for first in range(0, heads, 2):
            here = slice(first * head_dim, first * head_dim + pair)
            cut = slice(g * cols + here.start, g * cols + here.stop)
            act = conv_act(x[:, cut].astype(F32), before(cut.start, cut.stop), taps_x[:, cut])
            lane = lax.broadcasted_iota(jnp.int32, act.shape, 1)
            full = act.astype(F32)
            blocks = jnp.concatenate(
                [jnp.where(lane < head_dim, full, 0.0), jnp.where(lane < head_dim, 0.0, full)],
                axis=0,
            ).astype(BF16)
            weights = []
            for h in (g * heads + first, g * heads + first + 1):
                gap = jnp.minimum(cum_t[:, h : h + 1] - cum[h : h + 1, :], 0.0)
                weights.append((jnp.exp(gap) * dt[h : h + 1, :] * inner).astype(BF16))
            y = jnp.dot(jnp.concatenate(weights, axis=1), blocks, preferred_element_type=F32)
            gate = silu(z[:, cut].astype(F32))
            y_part[:, cut] = (y + skip[:, cut] * full) * gate
            lead[:, cut] = wide[:, here] * gate


def gated_slice(low, which, c, y_part, lead, arrived):
    tokens, width = y_part.shape
    state_dim = arrived[-1].shape[0]
    size = arrived[-1].shape[1]
    state = jnp.zeros((state_dim, size), BF16)
    for i, came in enumerate(arrived):
        state = jnp.where(which[0] == i, came[...][:state_dim], state)
    pieces = []
    for group, begin, stop in by_group(low, low + size, width * state_dim // c.shape[1]):
        from_state = jnp.dot(
            c[:, group * state_dim : (group + 1) * state_dim],
            state[:, begin - low : stop - low],
            preferred_element_type=F32,
        )
        pieces.append(y_part[:, begin:stop] + lead[:, begin:stop] * from_state)
    return pieces


def gated_kernel(low, which, c, y_part, lead, *refs):
    at = 0
    for piece in gated_slice(low, which, c, y_part, lead, refs[:-1]):
        refs[-1][:, at : at + piece.shape[1]] = piece
        at += piece.shape[1]


def output_kernel(begin, ready, low, which, c, y_part, lead, gain, *refs):
    out, made, sems = refs[-3:]
    tokens, cols = made.shape
    pieces = [refs[i][:, a:b] for i, (a, b) in enumerate(ready)]
    if low is not None:
        arrived = refs[len(ready) : len(refs) - 3]
        if begin > 0:
            arrived = arrived[:-1]
        pieces += gated_slice(low, which, c, y_part, lead, arrived)
    total = jnp.zeros((tokens, 1), F32)
    for piece in pieces:
        total = total + jnp.sum(piece * piece, axis=1, keepdims=True)
    factor = lax.rsqrt(total / cols + EPS)
    copies = []
    at = 0
    for i, piece in enumerate(pieces):
        span = slice(at, at + piece.shape[1])
        made[:, span] = (piece * factor * gain[:, begin + at : begin + span.stop]).astype(BF16)
        copies.append(
            pltpu.make_async_copy(
                made.at[:, span], out.at[:, pl.ds(begin + at, piece.shape[1])], sems.at[i]
            )
        )
        copies[-1].start()
        at = span.stop
    for copy in copies:
        copy.wait()


def params(mib):
    return pltpu.CompilerParams(vmem_limit_bytes=mib * 1024 * 1024)


def doubling(state, decay, devices):
    def moved(value, distance):
        return lax.ppermute(value, "seq", [(i, i + distance) for i in range(devices - distance)])

    total, decay = moved(state.astype(BF16), 1), moved(decay, 1)
    distance = 1
    while distance < devices - 1:
        came = moved(total, distance)
        total = (decay * came.astype(F32) + total.astype(F32)).astype(BF16)
        decay = decay * moved(decay, distance)
        distance *= 2
    return total


def shards(x_in, bc_in, z_in, dt_raw, conv_x, conv_bc, a_log, d_skip, norm_gain):
    tokens, width = x_in.shape
    groups, both = bc_in.shape[1:]
    state_dim = both // 2
    heads = dt_raw.shape[1]
    head_dim = width // heads
    cols = width // groups
    devices = lax.axis_size("seq")
    place = lax.axis_index("seq")
    edges = [width * sum(PARTS[:i]) // sum(PARTS) for i in range(len(PARTS) + 1)]
    cuts = list(zip(edges[:-1], edges[1:]))

    taps = conv_x.shape[0]
    dt_t = dt_raw.T
    a_row = a_log.reshape(1, heads)
    d_row = d_skip.reshape(1, heads)
    gain = norm_gain.reshape(1, width)
    sources = [x_in, bc_in, conv_x, conv_bc]
    operands = sources + [dt_t, a_row]
    pinned = [pltpu.with_memory_space_constraint(v, pltpu.HBM) for v in operands]
    landed = [pltpu.VMEM(v.shape, v.dtype) for v in operands]
    scale_shape = jax.ShapeDtypeStruct((tokens, width), F32)
    scalar = pl.BlockSpec(memory_space=pltpu.SMEM)
    in_vmem = pl.BlockSpec(memory_space=pltpu.VMEM)
    anywhere = pl.BlockSpec(memory_space=pl.ANY)
    in_hbm = [pl.BlockSpec(memory_space=pltpu.HBM)] * len(operands)

    def here(condition):
        return condition.astype(jnp.int32).reshape(1)

    def shifted(value, route):
        return lax.ppermute(value, "seq", route)

    def first_states(low, high):
        blocks = -(-(width + groups * both) // (high - low))
        extra = -(-(taps - 1) * blocks // (2 * RIM)) * 2 * RIM
        return pl.pallas_call(
            functools.partial(first_kernel, low, high),
            out_shape=[jax.ShapeDtypeStruct((state_dim + extra, high - low), BF16), scale_shape],
            in_specs=[scalar] + in_hbm,
            scratch_shapes=landed + [pltpu.SemaphoreType.DMA((len(operands),))],
            compiler_params=params(16),
            name="first_states",
        )(here(place == 0), *pinned)

    def next_states(token, scale, low, high):
        return pl.pallas_call(
            functools.partial(next_kernel, low, high),
            out_shape=jax.ShapeDtypeStruct((state_dim, high - low), BF16),
            in_specs=[scalar, anywhere] + [in_vmem] * (len(sources) + 1),
            compiler_params=params(16),
            name="next_states",
        )(here(place == 0), token, *sources, scale)

    def prepared(token):
        return pl.pallas_call(
            functools.partial(prepare_kernel, cuts),
            out_shape=[
                jax.ShapeDtypeStruct((RIM, width + groups * both), BF16),
                jax.ShapeDtypeStruct((1, width), F32),
                scale_shape,
            ]
            + [jax.ShapeDtypeStruct((1, high - low), F32) for low, high in cuts],
            in_specs=[anywhere] + [in_vmem] * 5,
            compiler_params=params(16),
            name="prepared",
        )(token, x_in, bc_in, dt_t, a_row, gain)

    def later_states(condition, rows, token, scale, low, high, at_hand=()):
        return pl.pallas_call(
            functools.partial(later_kernel, low, high),
            out_shape=jax.ShapeDtypeStruct((state_dim, high - low), F32),
            in_specs=[scalar, in_vmem, anywhere] + [in_vmem] * (len(sources) + 1 + len(at_hand)),
            compiler_params=params(16),
            name="later_states",
        )(here(condition), rows, token, *sources, scale, *at_hand)

    along = [(i, i + 1) for i in range(devices - 1)]
    def intra(token, befores):
        return pl.pallas_call(
            functools.partial(intra_kernel, len(befores)),
            out_shape=[
                scale_shape, scale_shape, jax.ShapeDtypeStruct((tokens, groups * state_dim), BF16)
            ],
            in_specs=[anywhere] + [in_vmem] * (len(befores) + 8),
            scratch_shapes=[pltpu.VMEM((tokens, cols), F32)],
            compiler_params=params(24),
            cost_estimate=pl.CostEstimate(
                flops=4 * tokens * tokens * width,
                bytes_accessed=12 * tokens * width,
                transcendentals=tokens * tokens * heads,
            ),
            name="intra",
        )(token, *befores, x_in, bc_in, z_in, conv_x, conv_bc, dt_t, a_row, d_row)

    if devices <= CHAIN_MOST:
        first, scale = first_states(*cuts[0])
        sent = [first, next_states(first, scale, *cuts[1])]
        last, gain, scale_own, *decays = prepared(sent[-1])
        token = last
        for cut in cuts[2:]:
            sent.append(next_states(token, scale, *cut))
            token = sent[-1]
        soon = along[1 : max(devices - 2, 1)]
        late = along[max(devices - 2, 1) :]
        befores = [shifted(last, soon)] if soon else []
        arrived = [[shifted(v, along[:1])] for v in sent]
        befores.append(arrived[0][0])
        rows, token = arrived[0][0], last
        for hop in range(1, devices - 1):
            runs = place == 1 if hop == 1 else (place >= 2) & (place < devices - 1)
            after = token
            for i, cut in enumerate(cuts):
                if hop <= 2:
                    made = later_states(
                        runs, rows, after, scale_own, *cut, at_hand=() if hop == 1 else (d_row,)
                    )
                    states = [made] if i == 0 else states + [made]
                early = ()
                if hop == devices - 2 and hop > 1 and i == len(cuts) - 1:
                    early = (arrived[0][-1], befores[-1])
                before, *_ = lax.optimization_barrier((arrived[i][-1], token) + early)
                joined = decays[i] * before[:state_dim].astype(F32) + states[i]
                token = joined.astype(BF16)
                after = token if hop == 1 else after
                arrived[i].append(shifted(token, along[hop : hop + 1]))
            if hop == 1 and late:
                moved, _ = lax.optimization_barrier((last, token))
                befores.append(shifted(moved, late))
            rows = befores[0]
        which = place - 1
    else:
        last, gain, scale, *decays = prepared(a_row)
        befores = [shifted(last, along)]
        arrived = []
        for decay, cut in zip(decays, cuts):
            state = later_states(place >= 0, befores[0], a_row, scale, *cut)
            arrived.append([doubling(state, decay, devices)])
        which = jnp.zeros_like(place)
    which = which.astype(jnp.int32).reshape(1)
    y_part, lead, c_act = intra(a_row, befores)

    common = [which, c_act, y_part, lead]
    common_specs = [scalar] + [in_vmem] * 3
    last_low, last_high = cuts[-1]
    ready = []
    for (low, high), seen in zip(cuts[:-1], arrived):
        ready.append(
            pl.pallas_call(
                functools.partial(gated_kernel, low),
                out_shape=jax.ShapeDtypeStruct((tokens, high - low), F32),
                in_specs=common_specs + [in_vmem] * len(seen),
                compiler_params=params(16),
                name="gated",
            )(*common, *seen)
        )
    out = None
    for g in range(groups):
        begin, stop = g * cols, (g + 1) * cols
        taken, spans = [], []
        for (low, high), v in zip(cuts[:-1], ready):
            if low < stop and high > begin:
                taken.append(v)
                spans.append((max(low, begin) - low, min(high, stop) - low))
        inputs = taken
        unready = None
        if last_low < stop:
            unready = last_low
            inputs = taken + arrived[-1]
        aliases = {}
        specs = common_specs + [in_vmem] * (1 + len(inputs))
        if out is not None:
            aliases = {len(common) + 1 + len(inputs): 0}
            inputs = inputs + [out]
            specs = specs + [anywhere]
        out = pl.pallas_call(
            functools.partial(output_kernel, begin, spans, unready),
            out_shape=jax.ShapeDtypeStruct((tokens, width), BF16),
            in_specs=specs,
            out_specs=anywhere,
            scratch_shapes=[
                pltpu.VMEM((tokens, cols), BF16),
                pltpu.SemaphoreType.DMA((len(cuts) + groups,)),
            ],
            input_output_aliases=aliases,
            compiler_params=params(16),
            name="outputs",
        )(*common, gain, *inputs)
    return out


def solution(mesh):
    return jax.shard_map(
        shards,
        mesh=mesh,
        in_specs=(
            P(("groups", "seq"), "head"),
            P(("groups", "seq"), "head", None),
            P(("groups", "seq"), "head"),
            P(("groups", "seq"), "head"),
            P(None, "head"),
            P(None, "head", None),
            P("head"),
            P("head"),
            P("head"),
        ),
        out_specs=P(("groups", "seq"), "head"),
        check_vma=False,
    )
```

```python
import functools

import jax
import jax.numpy as jnp
from jax import lax
from jax.experimental import pallas as pl
from jax.experimental.pallas import tpu as pltpu
from jax.sharding import PartitionSpec as P

EPS = 1e-05
F32 = jnp.float32
BF16 = jnp.bfloat16
CHAIN_MOST = 4
PARTS = (1, 1, 1, 1)
CHUNK = 128
RIM = 8


def silu(u):
    return 0.5 * u * (1.0 + jnp.tanh(0.5 * u))


def softplus(v):
    return jnp.maximum(v, 0.0) + jnp.log1p(jnp.exp(-jnp.abs(v)))


def halves(v, count, axis):
    parts = []
    for _ in range(count - 1):
        part = v.astype(BF16)
        parts.append(part)
        v = v - part.astype(F32)
    parts.append(v.astype(BF16))
    return jnp.concatenate(parts, axis=axis)


def spread(per_head, head_dim, count):
    heads = per_head.shape[0]
    rows = lax.broadcasted_iota(jnp.int32, (heads * count, heads * head_dim), 0)
    cols = lax.broadcasted_iota(jnp.int32, (heads * count, heads * head_dim), 1)
    pick = (rows % heads == cols // head_dim).astype(F32).astype(BF16)
    return lax.dot_general(
        halves(per_head, count, 0), pick, (((0,), (0,)), ((), ())), preferred_element_type=F32
    )


def spread_row(column, head_dim):
    heads = column.shape[0]
    rows = lax.broadcasted_iota(jnp.int32, (heads, heads * head_dim), 0)
    cols = lax.broadcasted_iota(jnp.int32, (heads, heads * head_dim), 1)
    return jnp.sum(jnp.where(rows == cols // head_dim, column, 0.0), axis=0, keepdims=True)


def as_column(row, start, heads):
    every = row.shape[1]
    rows = lax.broadcasted_iota(jnp.int32, (heads, every), 0)
    cols = lax.broadcasted_iota(jnp.int32, (heads, every), 1)
    return jnp.sum(jnp.where(cols == rows + start, row, 0.0), axis=1, keepdims=True)


def conv_act(series, tail, taps):
    count = taps.shape[0]
    above = tail.shape[0]
    padded = jnp.concatenate([tail, series], axis=0)
    total = taps[count - 1 : count] * series
    for back in range(1, count):
        total = total + taps[count - 1 - back : count - back] * pltpu.roll(padded, back, 0)[above:]
    return silu(total).astype(BF16)


def rates(dt_raw, a_log_row, start):
    heads, tokens = dt_raw.shape
    dt = softplus(dt_raw)
    rate = -jnp.exp(as_column(a_log_row, start, heads)) * dt
    earlier = lax.broadcasted_iota(jnp.int32, (tokens, tokens), 0)
    later = lax.broadcasted_iota(jnp.int32, (tokens, tokens), 1)
    upto = (earlier <= later).astype(F32).astype(BF16)
    cum = jnp.dot(
        halves(rate, 3, 1), jnp.concatenate([upto] * 3, axis=0), preferred_element_type=F32
    )
    return dt, cum


def scales(groups, head_dim, dt_raw, a_log, scale):
    dt, cum = rates(dt_raw[...], a_log[...], 0)
    end = cum[:, -1:]
    tail_decay = jnp.exp(end - cum) * dt
    heads = dt.shape[0] // groups
    for g in range(groups):
        scale[:, g * heads * head_dim : (g + 1) * heads * head_dim] = spread(
            tail_decay[g * heads : (g + 1) * heads], head_dim, 2
        )
    return spread_row(jnp.exp(end), head_dim)


def by_group(low, high, cols):
    found = []
    while low < high:
        stop = min(high, (low // cols + 1) * cols)
        found.append((low // cols, low, stop))
        low = stop
    return found


def emit_states(low, high, x, tail_x, bc, tail_bc, taps_x, taps_bc, scale, emit):
    groups, both = bc.shape[1:]
    state_dim = both // 2
    for group, begin, stop in by_group(low, high, x.shape[1] // groups):
        b = conv_act(
            bc[:, :, :state_dim].astype(F32)[:, group],
            tail_bc(group),
            taps_bc[:, :, :state_dim][:, group],
        )
        b_t = b.astype(F32).T.astype(BF16)
        for at in range(begin, stop, CHUNK):
            cut = slice(at, at + CHUNK)
            act = conv_act(x[:, cut].astype(F32), tail_x(cut), taps_x[:, cut])
            scaled = (scale[:, cut] * act.astype(F32)).astype(BF16)
            here = slice(at - low, at - low + CHUNK)
            emit(here, jnp.dot(b_t, scaled, preferred_element_type=F32))


def head_rows(low, high, x, bc, taps_x, taps_bc, scale, out):
    state_dim = bc.shape[2] // 2

    def emit(here, total):
        out[:state_dim, here] = total.astype(BF16)

    emit_states(
        low, high, x, lambda cut: jnp.zeros((RIM, CHUNK), F32),
        bc, lambda group: jnp.zeros((RIM, state_dim), F32), taps_x, taps_bc, scale, emit,
    )


def first_kernel(
    low, high, active, x_hbm, bc_hbm, taps_x_hbm, taps_bc_hbm, dt_hbm, a_hbm,
    out, scale, x, bc, taps_x, taps_bc, dt_raw, a_log, sems,
):
    tokens, width = x.shape
    groups, both = bc.shape[1:]

    @pl.when(active[0] == 1)
    def _():
        pairs = [
            (dt_hbm, dt_raw), (a_hbm, a_log), (x_hbm, x), (bc_hbm, bc),
            (taps_x_hbm, taps_x), (taps_bc_hbm, taps_bc),
        ]
        copies = [pltpu.make_async_copy(*pair, sems.at[i]) for i, pair in enumerate(pairs)]
        for copy in copies:
            copy.start()
        for copy in copies[:2]:
            copy.wait()
        scales(groups, width // dt_raw.shape[0], dt_raw, a_log, scale)
        for copy in copies[2:]:
            copy.wait()
        state_dim, step = both // 2, high - low
        keep = taps_x.shape[0] - 1
        extra = out.shape[0] - state_dim
        last_bc = bc[tokens - 2 * RIM :].astype(F32)[-RIM:]
        last = [x[tokens - 2 * RIM :, :].astype(F32)[-RIM:]] + [last_bc[:, g] for g in range(groups)]
        length = width + groups * both
        last.append(jnp.zeros((RIM, -length % step + step), F32))
        last = jnp.concatenate(last, axis=1)
        at = lax.broadcasted_iota(jnp.int32, (extra, step), 0)
        below = jnp.zeros((extra, step), F32)
        fill = jnp.zeros((extra - RIM, step), F32)
        for k in range(-(-length // step)):
            block = jnp.concatenate([last[:, k * step : (k + 1) * step], fill], axis=0)
            block = pltpu.roll(block, (keep * (k + 1) - RIM) % extra, 0)
            below = jnp.where((at >= keep * k) & (at < keep * (k + 1)), block, below)
        out[state_dim:, :] = below.astype(BF16)
        head_rows(low, high, x, bc, taps_x, taps_bc, scale, out)


def next_kernel(low, high, active, _, x, bc, taps_x, taps_bc, scale, out):
    @pl.when(active[0] == 1)
    def _():
        head_rows(low, high, x, bc, taps_x, taps_bc, scale, out)


def prepare_kernel(cuts, _, x, bc, dt_raw, a_log, gain, pack, gain_out, scale, *decays):
    tokens, width = x.shape
    groups, both = bc.shape[1:]
    pack[:, :width] = x[tokens - 2 * RIM :, :].astype(F32)[-RIM:].astype(BF16)
    last_bc = bc[tokens - 2 * RIM :].astype(F32)[-RIM:]
    for g in range(groups):
        pack[:, width + g * both : width + (g + 1) * both] = last_bc[:, g].astype(BF16)
    gain_out[...] = gain[...]
    row = scales(groups, width // dt_raw.shape[0], dt_raw, a_log, scale)
    for decay, (low, high) in zip(decays, cuts):
        decay[...] = row[:, low:high]


def rows_before(rows, begin, stop, keep, state_dim):
    if rows.shape[0] == RIM:
        return rows[:, begin:stop].astype(F32)
    step = rows.shape[1]
    below = rows[state_dim:, begin % step : begin % step + stop - begin].astype(F32)
    return pltpu.roll(below, (RIM - keep * (begin // step + 1)) % below.shape[0], 0)[:RIM]


def later_kernel(low, high, active, rows, _, x, bc, taps_x, taps_bc, scale, *refs):
    state = refs[-1]
    both = bc.shape[2]
    state_dim = both // 2
    keep = taps_x.shape[0] - 1

    def before(begin, stop):
        return rows_before(rows, begin, stop, keep, state_dim)

    def tail_bc(group):
        at = x.shape[1] + group * both
        return before(at, at + state_dim)

    @pl.when(active[0] == 1)
    def _():
        def emit(here, total):
            state[:, here] = total

        emit_states(
            low, high, x, lambda cut: before(cut.start, cut.stop), bc, tail_bc,
            taps_x, taps_bc, scale, emit,
        )


def intra_kernel(count, _, *refs):
    sources, refs = refs[:count], refs[count:]
    x, bc, z_hbm, taps_x, taps_bc, dt_raw, a_log, d_skip, y_part, lead, c_act, wide, z, sem = refs
    z_copy = pltpu.make_async_copy(z_hbm, z, sem.at[0])
    z_copy.start()
    tokens, width = x.shape
    groups, both = bc.shape[1:]
    state_dim = both // 2
    keep = taps_x.shape[0] - 1
    cols = width // groups
    heads = dt_raw.shape[0] // groups
    head_dim = cols // heads
    dt, cum = rates(dt_raw[...], a_log[...], 0)
    cum_t = cum.T
    leading = jnp.exp(cum)
    skip = spread_row(as_column(d_skip[...], 0, groups * heads), head_dim)
    t_at = lax.broadcasted_iota(jnp.int32, (tokens, tokens), 0)
    s_at = lax.broadcasted_iota(jnp.int32, (tokens, tokens), 1)
    pair = 2 * head_dim

    def before(begin, stop):
        found = [rows_before(rows, begin, stop, keep, state_dim) for rows in sources]
        return sum(found[1:], found[0])

    for g in range(groups):
        at = width + g * both
        tail_bc = jnp.concatenate(
            [before(at, at + state_dim), before(at + state_dim, at + both)], axis=1
        )
        bc_act = conv_act(bc[...].astype(F32)[:, g], tail_bc, taps_bc[...][:, g])
        b, c = bc_act[:, :state_dim], bc_act[:, state_dim:]
        c_act[:, g * state_dim : (g + 1) * state_dim] = c
        inner = lax.dot_general(c, b, (((1,), (1,)), ((), ())), preferred_element_type=F32)
        inner = jnp.where(t_at >= s_at, inner, 0.0)
        wide[...] = spread(leading[g * heads : (g + 1) * heads], head_dim, 2)
        if g == 0:
            z_copy.wait()
        for first in range(0, heads, 2):
            here = slice(first * head_dim, first * head_dim + pair)
            cut = slice(g * cols + here.start, g * cols + here.stop)
            act = conv_act(x[:, cut].astype(F32), before(cut.start, cut.stop), taps_x[:, cut])
            lane = lax.broadcasted_iota(jnp.int32, act.shape, 1)
            full = act.astype(F32)
            blocks = jnp.concatenate(
                [jnp.where(lane < head_dim, full, 0.0), jnp.where(lane < head_dim, 0.0, full)],
                axis=0,
            ).astype(BF16)
            weights = []
            for h in (g * heads + first, g * heads + first + 1):
                gap = jnp.minimum(cum_t[:, h : h + 1] - cum[h : h + 1, :], 0.0)
                weights.append((jnp.exp(gap) * dt[h : h + 1, :] * inner).astype(BF16))
            y = jnp.dot(jnp.concatenate(weights, axis=1), blocks, preferred_element_type=F32)
            gate = silu(z[:, cut].astype(F32))
            y_part[:, cut] = (y + skip[:, cut] * full) * gate
            lead[:, cut] = wide[:, here] * gate


def gated_slice(low, which, c, y_part, lead, arrived):
    tokens, width = y_part.shape
    state_dim = arrived[-1].shape[0]
    size = arrived[-1].shape[1]
    state = jnp.zeros((state_dim, size), BF16)
    for i, came in enumerate(arrived):
        state = jnp.where(which[0] == i, came[...][:state_dim], state)
    pieces = []
    for group, begin, stop in by_group(low, low + size, width * state_dim // c.shape[1]):
        from_state = jnp.dot(
            c[:, group * state_dim : (group + 1) * state_dim],
            state[:, begin - low : stop - low],
            preferred_element_type=F32,
        )
        pieces.append(y_part[:, begin:stop] + lead[:, begin:stop] * from_state)
    return pieces


def gated_kernel(low, which, c, y_part, lead, *refs):
    at = 0
    for piece in gated_slice(low, which, c, y_part, lead, refs[:-1]):
        refs[-1][:, at : at + piece.shape[1]] = piece
        at += piece.shape[1]


def output_kernel(begin, ready, low, which, c, y_part, lead, gain, *refs):
    out, made, sems = refs[-3:]
    tokens, cols = made.shape
    pieces = [refs[i][:, a:b] for i, (a, b) in enumerate(ready)]
    if low is not None:
        arrived = refs[len(ready) : len(refs) - 3]
        if begin > 0:
            arrived = arrived[:-1]
        pieces += gated_slice(low, which, c, y_part, lead, arrived)
    total = jnp.zeros((tokens, 1), F32)
    for piece in pieces:
        total = total + jnp.sum(piece * piece, axis=1, keepdims=True)
    factor = lax.rsqrt(total / cols + EPS)
    copies = []
    at = 0
    for i, piece in enumerate(pieces):
        span = slice(at, at + piece.shape[1])
        made[:, span] = (piece * factor * gain[:, begin + at : begin + span.stop]).astype(BF16)
        copies.append(
            pltpu.make_async_copy(
                made.at[:, span], out.at[:, pl.ds(begin + at, piece.shape[1])], sems.at[i]
            )
        )
        copies[-1].start()
        at = span.stop
    for copy in copies:
        copy.wait()


def params(mib):
    return pltpu.CompilerParams(vmem_limit_bytes=mib * 1024 * 1024)


def doubling(state, decay, devices):
    def moved(value, distance):
        return lax.ppermute(value, "seq", [(i, i + distance) for i in range(devices - distance)])

    total, decay = moved(state.astype(BF16), 1), moved(decay, 1)
    distance = 1
    while distance < devices - 1:
        came = moved(total, distance)
        total = (decay * came.astype(F32) + total.astype(F32)).astype(BF16)
        decay = decay * moved(decay, distance)
        distance *= 2
    return total


def shards(x_in, bc_in, z_in, dt_raw, conv_x, conv_bc, a_log, d_skip, norm_gain):
    tokens, width = x_in.shape
    groups, both = bc_in.shape[1:]
    state_dim = both // 2
    heads = dt_raw.shape[1]
    head_dim = width // heads
    cols = width // groups
    devices = lax.axis_size("seq")
    place = lax.axis_index("seq")
    edges = [width * sum(PARTS[:i]) // sum(PARTS) for i in range(len(PARTS) + 1)]
    cuts = list(zip(edges[:-1], edges[1:]))

    taps = conv_x.shape[0]
    dt_t = dt_raw.T
    a_row = a_log.reshape(1, heads)
    d_row = d_skip.reshape(1, heads)
    gain = norm_gain.reshape(1, width)
    sources = [x_in, bc_in, conv_x, conv_bc]
    operands = sources + [dt_t, a_row]
    pinned = [pltpu.with_memory_space_constraint(v, pltpu.HBM) for v in operands]
    z_pinned = pltpu.with_memory_space_constraint(z_in, pltpu.HBM)
    landed = [pltpu.VMEM(v.shape, v.dtype) for v in operands]
    scale_shape = jax.ShapeDtypeStruct((tokens, width), F32)
    scalar = pl.BlockSpec(memory_space=pltpu.SMEM)
    in_vmem = pl.BlockSpec(memory_space=pltpu.VMEM)
    anywhere = pl.BlockSpec(memory_space=pl.ANY)
    in_hbm = [pl.BlockSpec(memory_space=pltpu.HBM)] * len(operands)

    def here(condition):
        return condition.astype(jnp.int32).reshape(1)

    def shifted(value, route):
        return lax.ppermute(value, "seq", route)

    def first_states(low, high):
        blocks = -(-(width + groups * both) // (high - low))
        extra = -(-(taps - 1) * blocks // (2 * RIM)) * 2 * RIM
        return pl.pallas_call(
            functools.partial(first_kernel, low, high),
            out_shape=[jax.ShapeDtypeStruct((state_dim + extra, high - low), BF16), scale_shape],
            in_specs=[scalar] + in_hbm,
            scratch_shapes=landed + [pltpu.SemaphoreType.DMA((len(operands),))],
            compiler_params=params(16),
            name="first_states",
        )(here(place == 0), *pinned)

    def next_states(token, scale, low, high):
        return pl.pallas_call(
            functools.partial(next_kernel, low, high),
            out_shape=jax.ShapeDtypeStruct((state_dim, high - low), BF16),
            in_specs=[scalar, anywhere] + [in_vmem] * (len(sources) + 1),
            compiler_params=params(16),
            name="next_states",
        )(here(place == 0), token, *sources, scale)

    def prepared(token):
        return pl.pallas_call(
            functools.partial(prepare_kernel, cuts),
            out_shape=[
                jax.ShapeDtypeStruct((RIM, width + groups * both), BF16),
                jax.ShapeDtypeStruct((1, width), F32),
                scale_shape,
            ]
            + [jax.ShapeDtypeStruct((1, high - low), F32) for low, high in cuts],
            in_specs=[anywhere] + [in_vmem] * 5,
            compiler_params=params(16),
            name="prepared",
        )(token, x_in, bc_in, dt_t, a_row, gain)

    def later_states(condition, rows, token, scale, low, high, at_hand=()):
        return pl.pallas_call(
            functools.partial(later_kernel, low, high),
            out_shape=jax.ShapeDtypeStruct((state_dim, high - low), F32),
            in_specs=[scalar, in_vmem, anywhere] + [in_vmem] * (len(sources) + 1 + len(at_hand)),
            compiler_params=params(16),
            name="later_states",
        )(here(condition), rows, token, *sources, scale, *at_hand)

    along = [(i, i + 1) for i in range(devices - 1)]
    def intra(token, befores):
        return pl.pallas_call(
            functools.partial(intra_kernel, len(befores)),
            out_shape=[
                scale_shape, scale_shape, jax.ShapeDtypeStruct((tokens, groups * state_dim), BF16)
            ],
            in_specs=[anywhere]
            + [in_vmem] * (len(befores) + 2)
            + [pl.BlockSpec(memory_space=pltpu.HBM)]
            + [in_vmem] * 5,
            scratch_shapes=[
                pltpu.VMEM((tokens, cols), F32),
                pltpu.VMEM(z_in.shape, z_in.dtype),
                pltpu.SemaphoreType.DMA((1,)),
            ],
            compiler_params=params(24),
            cost_estimate=pl.CostEstimate(
                flops=4 * tokens * tokens * width,
                bytes_accessed=12 * tokens * width,
                transcendentals=tokens * tokens * heads,
            ),
            name="intra",
        )(token, *befores, x_in, bc_in, z_pinned, conv_x, conv_bc, dt_t, a_row, d_row)

    if devices <= CHAIN_MOST:
        first, scale = first_states(*cuts[0])
        sent = [first, next_states(first, scale, *cuts[1])]
        last, gain, scale_own, *decays = prepared(sent[-1])
        token = last
        for cut in cuts[2:]:
            sent.append(next_states(token, scale, *cut))
            token = sent[-1]
        soon = along[1 : max(devices - 2, 1)]
        late = along[max(devices - 2, 1) :]
        befores = [shifted(last, soon)] if soon else []
        arrived = [[shifted(v, along[:1])] for v in sent]
        befores.append(arrived[0][0])
        rows, token = arrived[0][0], last
        for hop in range(1, devices - 1):
            runs = place == 1 if hop == 1 else (place >= 2) & (place < devices - 1)
            after = token
            for i, cut in enumerate(cuts):
                if hop <= 2:
                    made = later_states(
                        runs, rows, after, scale_own, *cut, at_hand=() if hop == 1 else (d_row,)
                    )
                    states = [made] if i == 0 else states + [made]
                early = ()
                if hop == devices - 2 and hop > 1 and i == len(cuts) - 1:
                    early = (befores[-1],)
                before, *_ = lax.optimization_barrier((arrived[i][-1], token) + early)
                joined = decays[i] * before[:state_dim].astype(F32) + states[i]
                token = joined.astype(BF16)
                after = token if hop == 1 else after
                arrived[i].append(shifted(token, along[hop : hop + 1]))
            if hop == 1 and late:
                moved, _ = lax.optimization_barrier((last, token))
                befores.append(shifted(moved, late))
            rows = befores[0]
        which = place - 1
    else:
        last, gain, scale, *decays = prepared(a_row)
        befores = [shifted(last, along)]
        arrived = []
        for decay, cut in zip(decays, cuts):
            state = later_states(place >= 0, befores[0], a_row, scale, *cut)
            arrived.append([doubling(state, decay, devices)])
        which = jnp.zeros_like(place)
    which = which.astype(jnp.int32).reshape(1)
    y_part, lead, c_act = intra(a_row, befores)

    common = [which, c_act, y_part, lead]
    common_specs = [scalar] + [in_vmem] * 3
    last_low, last_high = cuts[-1]
    ready = []
    for (low, high), seen in zip(cuts[:-1], arrived):
        ready.append(
            pl.pallas_call(
                functools.partial(gated_kernel, low),
                out_shape=jax.ShapeDtypeStruct((tokens, high - low), F32),
                in_specs=common_specs + [in_vmem] * len(seen),
                compiler_params=params(16),
                name="gated",
            )(*common, *seen)
        )
    out = None
    for g in range(groups):
        begin, stop = g * cols, (g + 1) * cols
        taken, spans = [], []
        for (low, high), v in zip(cuts[:-1], ready):
            if low < stop and high > begin:
                taken.append(v)
                spans.append((max(low, begin) - low, min(high, stop) - low))
        inputs = taken
        unready = None
        if last_low < stop:
            unready = last_low
            inputs = taken + arrived[-1]
        aliases = {}
        specs = common_specs + [in_vmem] * (1 + len(inputs))
        if out is not None:
            aliases = {len(common) + 1 + len(inputs): 0}
            inputs = inputs + [out]
            specs = specs + [anywhere]
        out = pl.pallas_call(
            functools.partial(output_kernel, begin, spans, unready),
            out_shape=jax.ShapeDtypeStruct((tokens, width), BF16),
            in_specs=specs,
            out_specs=anywhere,
            scratch_shapes=[
                pltpu.VMEM((tokens, cols), BF16),
                pltpu.SemaphoreType.DMA((len(cuts) + groups,)),
            ],
            input_output_aliases=aliases,
            compiler_params=params(16),
            name="outputs",
        )(*common, gain, *inputs)
    return out


def solution(mesh):
    return jax.shard_map(
        shards,
        mesh=mesh,
        in_specs=(
            P(("groups", "seq"), "head"),
            P(("groups", "seq"), "head", None),
            P(("groups", "seq"), "head"),
            P(("groups", "seq"), "head"),
            P(None, "head"),
            P(None, "head", None),
            P("head"),
            P("head"),
            P("head"),
        ),
        out_specs=P(("groups", "seq"), "head"),
        check_vma=False,
    )
```

```python
import functools

import jax
import jax.numpy as jnp
from jax import lax
from jax.experimental import pallas as pl
from jax.experimental.pallas import tpu as pltpu
from jax.sharding import PartitionSpec as P

EPS = 1e-05
F32 = jnp.float32
BF16 = jnp.bfloat16
CHAIN_MOST = 4
PARTS = (1, 1, 1, 1)
CHUNK = 128
RIM = 8


def silu(u):
    return 0.5 * u * (1.0 + jnp.tanh(0.5 * u))


def softplus(v):
    return jnp.maximum(v, 0.0) + jnp.log1p(jnp.exp(-jnp.abs(v)))


def halves(v, count, axis):
    parts = []
    for _ in range(count - 1):
        part = v.astype(BF16)
        parts.append(part)
        v = v - part.astype(F32)
    parts.append(v.astype(BF16))
    return jnp.concatenate(parts, axis=axis)


def spread(per_head, head_dim, count):
    heads = per_head.shape[0]
    rows = lax.broadcasted_iota(jnp.int32, (heads * count, heads * head_dim), 0)
    cols = lax.broadcasted_iota(jnp.int32, (heads * count, heads * head_dim), 1)
    pick = (rows % heads == cols // head_dim).astype(F32).astype(BF16)
    return lax.dot_general(
        halves(per_head, count, 0), pick, (((0,), (0,)), ((), ())), preferred_element_type=F32
    )


def spread_row(column, head_dim):
    heads = column.shape[0]
    rows = lax.broadcasted_iota(jnp.int32, (heads, heads * head_dim), 0)
    cols = lax.broadcasted_iota(jnp.int32, (heads, heads * head_dim), 1)
    return jnp.sum(jnp.where(rows == cols // head_dim, column, 0.0), axis=0, keepdims=True)


def as_column(row, start, heads):
    every = row.shape[1]
    rows = lax.broadcasted_iota(jnp.int32, (heads, every), 0)
    cols = lax.broadcasted_iota(jnp.int32, (heads, every), 1)
    return jnp.sum(jnp.where(cols == rows + start, row, 0.0), axis=1, keepdims=True)


def conv_act(series, tail, taps):
    count = taps.shape[0]
    above = tail.shape[0]
    padded = jnp.concatenate([tail, series], axis=0)
    total = taps[count - 1 : count] * series
    for back in range(1, count):
        total = total + taps[count - 1 - back : count - back] * pltpu.roll(padded, back, 0)[above:]
    return silu(total).astype(BF16)


def rates(dt_raw, a_log_row, start):
    heads, tokens = dt_raw.shape
    dt = softplus(dt_raw)
    rate = -jnp.exp(as_column(a_log_row, start, heads)) * dt
    earlier = lax.broadcasted_iota(jnp.int32, (tokens, tokens), 0)
    later = lax.broadcasted_iota(jnp.int32, (tokens, tokens), 1)
    upto = (earlier <= later).astype(F32).astype(BF16)
    cum = jnp.dot(
        halves(rate, 3, 1), jnp.concatenate([upto] * 3, axis=0), preferred_element_type=F32
    )
    return dt, cum


def scales(groups, head_dim, dt_raw, a_log, scale):
    dt, cum = rates(dt_raw[...], a_log[...], 0)
    end = cum[:, -1:]
    tail_decay = jnp.exp(end - cum) * dt
    heads = dt.shape[0] // groups
    for g in range(groups):
        scale[:, g * heads * head_dim : (g + 1) * heads * head_dim] = spread(
            tail_decay[g * heads : (g + 1) * heads], head_dim, 2
        )
    return spread_row(jnp.exp(end), head_dim)


def by_group(low, high, cols):
    found = []
    while low < high:
        stop = min(high, (low // cols + 1) * cols)
        found.append((low // cols, low, stop))
        low = stop
    return found


def emit_states(low, high, x, tail_x, bc, tail_bc, taps_x, taps_bc, scale, emit):
    groups, both = bc.shape[1:]
    state_dim = both // 2
    for group, begin, stop in by_group(low, high, x.shape[1] // groups):
        b = conv_act(
            bc[:, :, :state_dim].astype(F32)[:, group],
            tail_bc(group),
            taps_bc[:, :, :state_dim][:, group],
        )
        b_t = b.astype(F32).T.astype(BF16)
        for at in range(begin, stop, CHUNK):
            cut = slice(at, at + CHUNK)
            act = conv_act(x[:, cut].astype(F32), tail_x(cut), taps_x[:, cut])
            scaled = (scale[:, cut] * act.astype(F32)).astype(BF16)
            here = slice(at - low, at - low + CHUNK)
            emit(here, jnp.dot(b_t, scaled, preferred_element_type=F32))


def head_rows(low, high, x, bc, taps_x, taps_bc, scale, out):
    state_dim = bc.shape[2] // 2

    def emit(here, total):
        out[:state_dim, here] = total.astype(BF16)

    emit_states(
        low, high, x, lambda cut: jnp.zeros((RIM, CHUNK), F32),
        bc, lambda group: jnp.zeros((RIM, state_dim), F32), taps_x, taps_bc, scale, emit,
    )


def first_kernel(
    low, high, active, x_hbm, bc_hbm, taps_x_hbm, taps_bc_hbm, dt_hbm, a_hbm,
    out, scale, x, bc, taps_x, taps_bc, dt_raw, a_log, sems,
):
    tokens, width = x.shape
    groups, both = bc.shape[1:]

    @pl.when(active[0] == 1)
    def _():
        pairs = [
            (dt_hbm, dt_raw), (a_hbm, a_log), (x_hbm, x), (bc_hbm, bc),
            (taps_x_hbm, taps_x), (taps_bc_hbm, taps_bc),
        ]
        copies = [pltpu.make_async_copy(*pair, sems.at[i]) for i, pair in enumerate(pairs)]
        for copy in copies:
            copy.start()
        for copy in copies[:2]:
            copy.wait()
        scales(groups, width // dt_raw.shape[0], dt_raw, a_log, scale)
        for copy in copies[2:]:
            copy.wait()
        state_dim, step = both // 2, high - low
        keep = taps_x.shape[0] - 1
        extra = out.shape[0] - state_dim
        last_bc = bc[tokens - 2 * RIM :].astype(F32)[-RIM:]
        last = [x[tokens - 2 * RIM :, :].astype(F32)[-RIM:]] + [last_bc[:, g] for g in range(groups)]
        length = width + groups * both
        last.append(jnp.zeros((RIM, -length % step + step), F32))
        last = jnp.concatenate(last, axis=1)
        at = lax.broadcasted_iota(jnp.int32, (extra, step), 0)
        below = jnp.zeros((extra, step), F32)
        fill = jnp.zeros((extra - RIM, step), F32)
        for k in range(-(-length // step)):
            block = jnp.concatenate([last[:, k * step : (k + 1) * step], fill], axis=0)
            block = pltpu.roll(block, (keep * (k + 1) - RIM) % extra, 0)
            below = jnp.where((at >= keep * k) & (at < keep * (k + 1)), block, below)
        out[state_dim:, :] = below.astype(BF16)
        head_rows(low, high, x, bc, taps_x, taps_bc, scale, out)


def next_kernel(low, high, active, _, x, bc, taps_x, taps_bc, scale, out):
    @pl.when(active[0] == 1)
    def _():
        head_rows(low, high, x, bc, taps_x, taps_bc, scale, out)


def prepare_kernel(cuts, _, x, bc, dt_raw, a_log, gain, pack, gain_out, scale, *decays):
    tokens, width = x.shape
    groups, both = bc.shape[1:]
    pack[:, :width] = x[tokens - 2 * RIM :, :].astype(F32)[-RIM:].astype(BF16)
    last_bc = bc[tokens - 2 * RIM :].astype(F32)[-RIM:]
    for g in range(groups):
        pack[:, width + g * both : width + (g + 1) * both] = last_bc[:, g].astype(BF16)
    gain_out[...] = gain[...]
    row = scales(groups, width // dt_raw.shape[0], dt_raw, a_log, scale)
    for decay, (low, high) in zip(decays, cuts):
        decay[...] = row[:, low:high]


def rows_before(rows, begin, stop, keep, state_dim):
    if rows.shape[0] == RIM:
        return rows[:, begin:stop].astype(F32)
    step = rows.shape[1]
    below = rows[state_dim:, begin % step : begin % step + stop - begin].astype(F32)
    return pltpu.roll(below, (RIM - keep * (begin // step + 1)) % below.shape[0], 0)[:RIM]


def later_kernel(low, high, active, rows, _, x, bc, taps_x, taps_bc, scale, *refs):
    state = refs[-1]
    both = bc.shape[2]
    state_dim = both // 2
    keep = taps_x.shape[0] - 1

    def before(begin, stop):
        return rows_before(rows, begin, stop, keep, state_dim)

    def tail_bc(group):
        at = x.shape[1] + group * both
        return before(at, at + state_dim)

    @pl.when(active[0] == 1)
    def _():
        def emit(here, total):
            state[:, here] = total

        emit_states(
            low, high, x, lambda cut: before(cut.start, cut.stop), bc, tail_bc,
            taps_x, taps_bc, scale, emit,
        )


def intra_kernel(count, _, *refs):
    sources, refs = refs[:count], refs[count:]
    x, bc, z, taps_x, taps_bc, dt_raw, a_log, d_skip, y_part, lead, c_act, wide = refs
    tokens, width = x.shape
    groups, both = bc.shape[1:]
    state_dim = both // 2
    keep = taps_x.shape[0] - 1
    cols = width // groups
    heads = dt_raw.shape[0] // groups
    head_dim = cols // heads
    dt, cum = rates(dt_raw[...], a_log[...], 0)
    cum_t = cum.T
    leading = jnp.exp(cum)
    skip = spread_row(as_column(d_skip[...], 0, groups * heads), head_dim)
    t_at = lax.broadcasted_iota(jnp.int32, (tokens, tokens), 0)
    s_at = lax.broadcasted_iota(jnp.int32, (tokens, tokens), 1)
    pair = 2 * head_dim

    def before(begin, stop):
        found = [rows_before(rows, begin, stop, keep, state_dim) for rows in sources]
        return sum(found[1:], found[0])

    for g in range(groups):
        at = width + g * both
        tail_bc = jnp.concatenate(
            [before(at, at + state_dim), before(at + state_dim, at + both)], axis=1
        )
        bc_act = conv_act(bc[...].astype(F32)[:, g], tail_bc, taps_bc[...][:, g])
        b, c = bc_act[:, :state_dim], bc_act[:, state_dim:]
        c_act[:, g * state_dim : (g + 1) * state_dim] = c
        inner = lax.dot_general(c, b, (((1,), (1,)), ((), ())), preferred_element_type=F32)
        inner = jnp.where(t_at >= s_at, inner, 0.0)
        wide[...] = spread(leading[g * heads : (g + 1) * heads], head_dim, 2)
        for first in range(0, heads, 2):
            here = slice(first * head_dim, first * head_dim + pair)
            cut = slice(g * cols + here.start, g * cols + here.stop)
            act = conv_act(x[:, cut].astype(F32), before(cut.start, cut.stop), taps_x[:, cut])
            lane = lax.broadcasted_iota(jnp.int32, act.shape, 1)
            full = act.astype(F32)
            blocks = jnp.concatenate(
                [jnp.where(lane < head_dim, full, 0.0), jnp.where(lane < head_dim, 0.0, full)],
                axis=0,
            ).astype(BF16)
            weights = []
            for h in (g * heads + first, g * heads + first + 1):
                gap = jnp.minimum(cum_t[:, h : h + 1] - cum[h : h + 1, :], 0.0)
                weights.append((jnp.exp(gap) * dt[h : h + 1, :] * inner).astype(BF16))
            y = jnp.dot(jnp.concatenate(weights, axis=1), blocks, preferred_element_type=F32)
            gate = silu(z[:, cut].astype(F32))
            y_part[:, cut] = (y + skip[:, cut] * full) * gate
            lead[:, cut] = wide[:, here] * gate


def gated_slice(low, which, c, y_part, lead, arrived):
    tokens, width = y_part.shape
    state_dim = arrived[-1].shape[0]
    size = arrived[-1].shape[1]
    state = jnp.zeros((state_dim, size), BF16)
    for i, came in enumerate(arrived):
        state = jnp.where(which[0] == i, came[...][:state_dim], state)
    pieces = []
    for group, begin, stop in by_group(low, low + size, width * state_dim // c.shape[1]):
        from_state = jnp.dot(
            c[:, group * state_dim : (group + 1) * state_dim],
            state[:, begin - low : stop - low],
            preferred_element_type=F32,
        )
        pieces.append(y_part[:, begin:stop] + lead[:, begin:stop] * from_state)
    return pieces


def gated_kernel(low, which, c, y_part, lead, *refs):
    at = 0
    for piece in gated_slice(low, which, c, y_part, lead, refs[:-1]):
        refs[-1][:, at : at + piece.shape[1]] = piece
        at += piece.shape[1]


def output_kernel(begin, ready, low, which, c, y_part, lead, gain, *refs):
    out, made, sems = refs[-3:]
    tokens, cols = made.shape
    pieces = [refs[i][:, a:b] for i, (a, b) in enumerate(ready)]
    if low is not None:
        arrived = refs[len(ready) : len(refs) - 3]
        if begin > 0:
            arrived = arrived[:-1]
        pieces += gated_slice(low, which, c, y_part, lead, arrived)
    total = jnp.zeros((tokens, 1), F32)
    for piece in pieces:
        total = total + jnp.sum(piece * piece, axis=1, keepdims=True)
    factor = lax.rsqrt(total / cols + EPS)
    copies = []
    at = 0
    for i, piece in enumerate(pieces):
        span = slice(at, at + piece.shape[1])
        made[:, span] = (piece * factor * gain[:, begin + at : begin + span.stop]).astype(BF16)
        copies.append(
            pltpu.make_async_copy(
                made.at[:, span], out.at[:, pl.ds(begin + at, piece.shape[1])], sems.at[i]
            )
        )
        copies[-1].start()
        at = span.stop
    for copy in copies:
        copy.wait()


def params(mib):
    return pltpu.CompilerParams(vmem_limit_bytes=mib * 1024 * 1024)


def doubling(state, decay, devices):
    def moved(value, distance):
        return lax.ppermute(value, "seq", [(i, i + distance) for i in range(devices - distance)])

    total, decay = moved(state.astype(BF16), 1), moved(decay, 1)
    distance = 1
    while distance < devices - 1:
        came = moved(total, distance)
        total = (decay * came.astype(F32) + total.astype(F32)).astype(BF16)
        decay = decay * moved(decay, distance)
        distance *= 2
    return total


def shards(x_in, bc_in, z_in, dt_raw, conv_x, conv_bc, a_log, d_skip, norm_gain):
    tokens, width = x_in.shape
    groups, both = bc_in.shape[1:]
    state_dim = both // 2
    heads = dt_raw.shape[1]
    head_dim = width // heads
    cols = width // groups
    devices = lax.axis_size("seq")
    place = lax.axis_index("seq")
    edges = [width * sum(PARTS[:i]) // sum(PARTS) for i in range(len(PARTS) + 1)]
    cuts = list(zip(edges[:-1], edges[1:]))

    taps = conv_x.shape[0]
    dt_t = dt_raw.T
    a_row = a_log.reshape(1, heads)
    d_row = d_skip.reshape(1, heads)
    gain = norm_gain.reshape(1, width)
    sources = [x_in, bc_in, conv_x, conv_bc]
    operands = sources + [dt_t, a_row]
    pinned = [pltpu.with_memory_space_constraint(v, pltpu.HBM) for v in operands]
    landed = [pltpu.VMEM(v.shape, v.dtype) for v in operands]
    scale_shape = jax.ShapeDtypeStruct((tokens, width), F32)
    scalar = pl.BlockSpec(memory_space=pltpu.SMEM)
    in_vmem = pl.BlockSpec(memory_space=pltpu.VMEM)
    anywhere = pl.BlockSpec(memory_space=pl.ANY)
    in_hbm = [pl.BlockSpec(memory_space=pltpu.HBM)] * len(operands)

    def here(condition):
        return condition.astype(jnp.int32).reshape(1)

    def shifted(value, route):
        return lax.ppermute(value, "seq", route)

    def first_states(low, high):
        blocks = -(-(width + groups * both) // (high - low))
        extra = -(-(taps - 1) * blocks // (2 * RIM)) * 2 * RIM
        return pl.pallas_call(
            functools.partial(first_kernel, low, high),
            out_shape=[jax.ShapeDtypeStruct((state_dim + extra, high - low), BF16), scale_shape],
            in_specs=[scalar] + in_hbm,
            scratch_shapes=landed + [pltpu.SemaphoreType.DMA((len(operands),))],
            compiler_params=params(16),
            name="first_states",
        )(here(place == 0), *pinned)

    def next_states(token, scale, low, high):
        return pl.pallas_call(
            functools.partial(next_kernel, low, high),
            out_shape=jax.ShapeDtypeStruct((state_dim, high - low), BF16),
            in_specs=[scalar, anywhere] + [in_vmem] * (len(sources) + 1),
            compiler_params=params(16),
            name="next_states",
        )(here(place == 0), token, *sources, scale)

    def prepared(token):
        return pl.pallas_call(
            functools.partial(prepare_kernel, cuts),
            out_shape=[
                jax.ShapeDtypeStruct((RIM, width + groups * both), BF16),
                jax.ShapeDtypeStruct((1, width), F32),
                scale_shape,
            ]
            + [jax.ShapeDtypeStruct((1, high - low), F32) for low, high in cuts],
            in_specs=[anywhere] + [in_vmem] * 5,
            compiler_params=params(16),
            name="prepared",
        )(token, x_in, bc_in, dt_t, a_row, gain)

    def later_states(condition, rows, token, scale, low, high, at_hand=()):
        return pl.pallas_call(
            functools.partial(later_kernel, low, high),
            out_shape=jax.ShapeDtypeStruct((state_dim, high - low), F32),
            in_specs=[scalar, in_vmem, anywhere] + [in_vmem] * (len(sources) + 1 + len(at_hand)),
            compiler_params=params(16),
            name="later_states",
        )(here(condition), rows, token, *sources, scale, *at_hand)

    along = [(i, i + 1) for i in range(devices - 1)]
    def intra(token, befores):
        return pl.pallas_call(
            functools.partial(intra_kernel, len(befores)),
            out_shape=[
                scale_shape, scale_shape, jax.ShapeDtypeStruct((tokens, groups * state_dim), BF16)
            ],
            in_specs=[anywhere] + [in_vmem] * (len(befores) + 8),
            scratch_shapes=[pltpu.VMEM((tokens, cols), F32)],
            compiler_params=params(24),
            cost_estimate=pl.CostEstimate(
                flops=4 * tokens * tokens * width,
                bytes_accessed=12 * tokens * width,
                transcendentals=tokens * tokens * heads,
            ),
            name="intra",
        )(token, *befores, x_in, bc_in, z_in, conv_x, conv_bc, dt_t, a_row, d_row)

    if devices <= CHAIN_MOST:
        first, scale = first_states(*cuts[0])
        last, gain, scale_own, *decays = prepared(first)
        sent, token = [first], last
        for cut in cuts[1:]:
            sent.append(next_states(token, scale, *cut))
            token = sent[-1]
        soon = along[1 : max(devices - 2, 1)]
        late = along[max(devices - 2, 1) :]
        rows, _ = lax.optimization_barrier((last, sent[1]))
        befores = [shifted(rows, soon)] if soon else []
        arrived = [[shifted(v, along[:1])] for v in sent]
        befores.append(arrived[0][0])
        rows, token = arrived[0][0], last
        for hop in range(1, devices - 1):
            runs = place == 1 if hop == 1 else (place >= 2) & (place < devices - 1)
            after = token
            for i, cut in enumerate(cuts):
                if hop <= 2:
                    made = later_states(
                        runs, rows, after, scale_own, *cut, at_hand=() if hop == 1 else (d_row,)
                    )
                    states = [made] if i == 0 else states + [made]
                early = ()
                if hop == devices - 2 and hop > 1 and i == len(cuts) - 1:
                    early = (arrived[0][-1], befores[-1])
                before, *_ = lax.optimization_barrier((arrived[i][-1], token) + early)
                joined = decays[i] * before[:state_dim].astype(F32) + states[i]
                token = joined.astype(BF16)
                after = token if hop == 1 else after
                arrived[i].append(shifted(token, along[hop : hop + 1]))
            if hop == 1 and late:
                moved, _ = lax.optimization_barrier((last, token))
                befores.append(shifted(moved, late))
            rows = befores[0]
        which = place - 1
    else:
        last, gain, scale, *decays = prepared(a_row)
        befores = [shifted(last, along)]
        arrived = []
        for decay, cut in zip(decays, cuts):
            state = later_states(place >= 0, befores[0], a_row, scale, *cut)
            arrived.append([doubling(state, decay, devices)])
        which = jnp.zeros_like(place)
    which = which.astype(jnp.int32).reshape(1)
    y_part, lead, c_act = intra(a_row, befores)

    common = [which, c_act, y_part, lead]
    common_specs = [scalar] + [in_vmem] * 3
    last_low, last_high = cuts[-1]
    ready = []
    for (low, high), seen in zip(cuts[:-1], arrived):
        ready.append(
            pl.pallas_call(
                functools.partial(gated_kernel, low),
                out_shape=jax.ShapeDtypeStruct((tokens, high - low), F32),
                in_specs=common_specs + [in_vmem] * len(seen),
                compiler_params=params(16),
                name="gated",
            )(*common, *seen)
        )
    out = None
    for g in range(groups):
        begin, stop = g * cols, (g + 1) * cols
        taken, spans = [], []
        for (low, high), v in zip(cuts[:-1], ready):
            if low < stop and high > begin:
                taken.append(v)
                spans.append((max(low, begin) - low, min(high, stop) - low))
        inputs = taken
        unready = None
        if last_low < stop:
            unready = last_low
            inputs = taken + arrived[-1]
        aliases = {}
        specs = common_specs + [in_vmem] * (1 + len(inputs))
        if out is not None:
            aliases = {len(common) + 1 + len(inputs): 0}
            inputs = inputs + [out]
            specs = specs + [anywhere]
        out = pl.pallas_call(
            functools.partial(output_kernel, begin, spans, unready),
            out_shape=jax.ShapeDtypeStruct((tokens, width), BF16),
            in_specs=specs,
            out_specs=anywhere,
            scratch_shapes=[
                pltpu.VMEM((tokens, cols), BF16),
                pltpu.SemaphoreType.DMA((len(cuts) + groups,)),
            ],
            input_output_aliases=aliases,
            compiler_params=params(16),
            name="outputs",
        )(*common, gain, *inputs)
    return out


def solution(mesh):
    return jax.shard_map(
        shards,
        mesh=mesh,
        in_specs=(
            P(("groups", "seq"), "head"),
            P(("groups", "seq"), "head", None),
            P(("groups", "seq"), "head"),
            P(("groups", "seq"), "head"),
            P(None, "head"),
            P(None, "head", None),
            P("head"),
            P("head"),
            P("head"),
        ),
        out_specs=P(("groups", "seq"), "head"),
        check_vma=False,
    )
```

```python
import functools

import jax
import jax.numpy as jnp
from jax import lax
from jax.experimental import pallas as pl
from jax.experimental.pallas import tpu as pltpu
from jax.sharding import PartitionSpec as P

EPS = 1e-05
F32 = jnp.float32
BF16 = jnp.bfloat16
CHAIN_MOST = 4
PARTS = (1, 1, 1, 1)
CHUNK = 128
RIM = 8


def silu(u):
    return 0.5 * u * (1.0 + jnp.tanh(0.5 * u))


def softplus(v):
    return jnp.maximum(v, 0.0) + jnp.log1p(jnp.exp(-jnp.abs(v)))


def halves(v, count, axis):
    parts = []
    for _ in range(count - 1):
        part = v.astype(BF16)
        parts.append(part)
        v = v - part.astype(F32)
    parts.append(v.astype(BF16))
    return jnp.concatenate(parts, axis=axis)


def spread(per_head, head_dim, count):
    heads = per_head.shape[0]
    rows = lax.broadcasted_iota(jnp.int32, (heads * count, heads * head_dim), 0)
    cols = lax.broadcasted_iota(jnp.int32, (heads * count, heads * head_dim), 1)
    pick = (rows % heads == cols // head_dim).astype(F32).astype(BF16)
    return lax.dot_general(
        halves(per_head, count, 0), pick, (((0,), (0,)), ((), ())), preferred_element_type=F32
    )


def spread_row(column, head_dim):
    heads = column.shape[0]
    rows = lax.broadcasted_iota(jnp.int32, (heads, heads * head_dim), 0)
    cols = lax.broadcasted_iota(jnp.int32, (heads, heads * head_dim), 1)
    return jnp.sum(jnp.where(rows == cols // head_dim, column, 0.0), axis=0, keepdims=True)


def as_column(row, start, heads):
    every = row.shape[1]
    rows = lax.broadcasted_iota(jnp.int32, (heads, every), 0)
    cols = lax.broadcasted_iota(jnp.int32, (heads, every), 1)
    return jnp.sum(jnp.where(cols == rows + start, row, 0.0), axis=1, keepdims=True)


def conv_act(series, tail, taps):
    count = taps.shape[0]
    above = tail.shape[0]
    padded = jnp.concatenate([tail, series], axis=0)
    total = taps[count - 1 : count] * series
    for back in range(1, count):
        total = total + taps[count - 1 - back : count - back] * pltpu.roll(padded, back, 0)[above:]
    return silu(total).astype(BF16)


def rates(dt_raw, a_log_row, start):
    heads, tokens = dt_raw.shape
    dt = softplus(dt_raw)
    rate = -jnp.exp(as_column(a_log_row, start, heads)) * dt
    earlier = lax.broadcasted_iota(jnp.int32, (tokens, tokens), 0)
    later = lax.broadcasted_iota(jnp.int32, (tokens, tokens), 1)
    upto = (earlier <= later).astype(F32).astype(BF16)
    cum = jnp.dot(
        halves(rate, 3, 1), jnp.concatenate([upto] * 3, axis=0), preferred_element_type=F32
    )
    return dt, cum


def scales(groups, head_dim, dt_raw, a_log, scale):
    dt, cum = rates(dt_raw[...], a_log[...], 0)
    end = cum[:, -1:]
    tail_decay = jnp.exp(end - cum) * dt
    heads = dt.shape[0] // groups
    for g in range(groups):
        scale[:, g * heads * head_dim : (g + 1) * heads * head_dim] = spread(
            tail_decay[g * heads : (g + 1) * heads], head_dim, 2
        )
    return spread_row(jnp.exp(end), head_dim)


def by_group(low, high, cols):
    found = []
    while low < high:
        stop = min(high, (low // cols + 1) * cols)
        found.append((low // cols, low, stop))
        low = stop
    return found


def emit_states(low, high, x, tail_x, bc, tail_bc, taps_x, taps_bc, scale, emit):
    groups, both = bc.shape[1:]
    state_dim = both // 2
    for group, begin, stop in by_group(low, high, x.shape[1] // groups):
        b = conv_act(
            bc[:, :, :state_dim].astype(F32)[:, group],
            tail_bc(group),
            taps_bc[:, :, :state_dim][:, group],
        )
        b_t = b.astype(F32).T.astype(BF16)
        for at in range(begin, stop, CHUNK):
            cut = slice(at, at + CHUNK)
            act = conv_act(x[:, cut].astype(F32), tail_x(cut), taps_x[:, cut])
            scaled = (scale[:, cut] * act.astype(F32)).astype(BF16)
            here = slice(at - low, at - low + CHUNK)
            emit(here, jnp.dot(b_t, scaled, preferred_element_type=F32))


def head_rows(low, high, x, bc, taps_x, taps_bc, scale, out):
    state_dim = bc.shape[2] // 2

    def emit(here, total):
        out[:state_dim, here] = total.astype(BF16)

    emit_states(
        low, high, x, lambda cut: jnp.zeros((RIM, CHUNK), F32),
        bc, lambda group: jnp.zeros((RIM, state_dim), F32), taps_x, taps_bc, scale, emit,
    )


def first_kernel(
    low, high, active, x_hbm, bc_hbm, taps_x_hbm, taps_bc_hbm, dt_hbm, a_hbm,
    out, scale, x, bc, taps_x, taps_bc, dt_raw, a_log, sems,
):
    tokens, width = x.shape
    groups, both = bc.shape[1:]

    @pl.when(active[0] == 1)
    def _():
        pairs = [
            (dt_hbm, dt_raw), (a_hbm, a_log), (x_hbm, x), (bc_hbm, bc),
            (taps_x_hbm, taps_x), (taps_bc_hbm, taps_bc),
        ]
        copies = [pltpu.make_async_copy(*pair, sems.at[i]) for i, pair in enumerate(pairs)]
        for copy in copies:
            copy.start()
        for copy in copies[:2]:
            copy.wait()
        scales(groups, width // dt_raw.shape[0], dt_raw, a_log, scale)
        for copy in copies[2:]:
            copy.wait()
        state_dim, step = both // 2, high - low
        keep = taps_x.shape[0] - 1
        extra = out.shape[0] - state_dim
        last_bc = bc[tokens - 2 * RIM :].astype(F32)[-RIM:]
        last = [x[tokens - 2 * RIM :, :].astype(F32)[-RIM:]] + [last_bc[:, g] for g in range(groups)]
        length = width + groups * both
        last.append(jnp.zeros((RIM, -length % step + step), F32))
        last = jnp.concatenate(last, axis=1)
        at = lax.broadcasted_iota(jnp.int32, (extra, step), 0)
        below = jnp.zeros((extra, step), F32)
        fill = jnp.zeros((extra - RIM, step), F32)
        for k in range(-(-length // step)):
            block = jnp.concatenate([last[:, k * step : (k + 1) * step], fill], axis=0)
            block = pltpu.roll(block, (keep * (k + 1) - RIM) % extra, 0)
            below = jnp.where((at >= keep * k) & (at < keep * (k + 1)), block, below)
        out[state_dim:, :] = below.astype(BF16)
        head_rows(low, high, x, bc, taps_x, taps_bc, scale, out)


def next_kernel(low, high, active, _, x, bc, taps_x, taps_bc, scale, out):
    @pl.when(active[0] == 1)
    def _():
        head_rows(low, high, x, bc, taps_x, taps_bc, scale, out)


def prepare_kernel(cuts, _, x, bc, dt_raw, a_log, gain, pack, gain_out, scale, *decays):
    tokens, width = x.shape
    groups, both = bc.shape[1:]
    pack[:, :width] = x[tokens - 2 * RIM :, :].astype(F32)[-RIM:].astype(BF16)
    last_bc = bc[tokens - 2 * RIM :].astype(F32)[-RIM:]
    for g in range(groups):
        pack[:, width + g * both : width + (g + 1) * both] = last_bc[:, g].astype(BF16)
    gain_out[...] = gain[...]
    row = scales(groups, width // dt_raw.shape[0], dt_raw, a_log, scale)
    for decay, (low, high) in zip(decays, cuts):
        decay[...] = row[:, low:high]


def rows_before(rows, begin, stop, keep, state_dim):
    if rows.shape[0] == RIM:
        return rows[:, begin:stop].astype(F32)
    step = rows.shape[1]
    below = rows[state_dim:, begin % step : begin % step + stop - begin].astype(F32)
    return pltpu.roll(below, (RIM - keep * (begin // step + 1)) % below.shape[0], 0)[:RIM]


def later_kernel(low, high, active, rows, _, x, bc, taps_x, taps_bc, scale, *refs):
    state = refs[-1]
    both = bc.shape[2]
    state_dim = both // 2
    keep = taps_x.shape[0] - 1

    def before(begin, stop):
        return rows_before(rows, begin, stop, keep, state_dim)

    def tail_bc(group):
        at = x.shape[1] + group * both
        return before(at, at + state_dim)

    @pl.when(active[0] == 1)
    def _():
        def emit(here, total):
            state[:, here] = total

        emit_states(
            low, high, x, lambda cut: before(cut.start, cut.stop), bc, tail_bc,
            taps_x, taps_bc, scale, emit,
        )


def intra_kernel(count, _, *refs):
    sources, refs = refs[:count], refs[count:]
    x, bc, z_hbm, taps_x, taps_bc, dt_raw, a_log, d_skip, y_part, lead, c_act, z, sem = refs
    z_copy = pltpu.make_async_copy(z_hbm, z, sem.at[0])
    z_copy.start()
    tokens, width = x.shape
    groups, both = bc.shape[1:]
    state_dim = both // 2
    keep = taps_x.shape[0] - 1
    cols = width // groups
    heads = dt_raw.shape[0] // groups
    head_dim = cols // heads
    dt, cum = rates(dt_raw[...], a_log[...], 0)
    cum_t = cum.T
    leading = jnp.exp(cum)
    skip = spread_row(as_column(d_skip[...], 0, groups * heads), head_dim)
    t_at = lax.broadcasted_iota(jnp.int32, (tokens, tokens), 0)
    s_at = lax.broadcasted_iota(jnp.int32, (tokens, tokens), 1)
    pair = 2 * head_dim

    def before(begin, stop):
        found = [rows_before(rows, begin, stop, keep, state_dim) for rows in sources]
        return sum(found[1:], found[0])

    for g in range(groups):
        at = width + g * both
        tail_bc = jnp.concatenate(
            [before(at, at + state_dim), before(at + state_dim, at + both)], axis=1
        )
        bc_act = conv_act(bc[...].astype(F32)[:, g], tail_bc, taps_bc[...][:, g])
        b, c = bc_act[:, :state_dim], bc_act[:, state_dim:]
        c_act[:, g * state_dim : (g + 1) * state_dim] = c
        inner = lax.dot_general(c, b, (((1,), (1,)), ((), ())), preferred_element_type=F32)
        inner = jnp.where(t_at >= s_at, inner, 0.0)
        lead[:, g * cols : (g + 1) * cols] = spread(
            leading[g * heads : (g + 1) * heads], head_dim, 2
        )
        for first in range(0, heads, 2):
            here = slice(first * head_dim, first * head_dim + pair)
            cut = slice(g * cols + here.start, g * cols + here.stop)
            act = conv_act(x[:, cut].astype(F32), before(cut.start, cut.stop), taps_x[:, cut])
            lane = lax.broadcasted_iota(jnp.int32, act.shape, 1)
            full = act.astype(F32)
            blocks = jnp.concatenate(
                [jnp.where(lane < head_dim, full, 0.0), jnp.where(lane < head_dim, 0.0, full)],
                axis=0,
            ).astype(BF16)
            weights = []
            for h in (g * heads + first, g * heads + first + 1):
                gap = jnp.minimum(cum_t[:, h : h + 1] - cum[h : h + 1, :], 0.0)
                weights.append((jnp.exp(gap) * dt[h : h + 1, :] * inner).astype(BF16))
            y = jnp.dot(jnp.concatenate(weights, axis=1), blocks, preferred_element_type=F32)
            y_part[:, cut] = y + skip[:, cut] * full
    z_copy.wait()
    for at in range(0, width, CHUNK):
        cut = slice(at, at + CHUNK)
        gate = silu(z[:, cut].astype(F32))
        y_part[:, cut] = y_part[:, cut] * gate
        lead[:, cut] = lead[:, cut] * gate


def gated_slice(low, which, c, y_part, lead, arrived):
    tokens, width = y_part.shape
    state_dim = arrived[-1].shape[0]
    size = arrived[-1].shape[1]
    state = jnp.zeros((state_dim, size), BF16)
    for i, came in enumerate(arrived):
        state = jnp.where(which[0] == i, came[...][:state_dim], state)
    pieces = []
    for group, begin, stop in by_group(low, low + size, width * state_dim // c.shape[1]):
        from_state = jnp.dot(
            c[:, group * state_dim : (group + 1) * state_dim],
            state[:, begin - low : stop - low],
            preferred_element_type=F32,
        )
        pieces.append(y_part[:, begin:stop] + lead[:, begin:stop] * from_state)
    return pieces


def gated_kernel(low, which, c, y_part, lead, *refs):
    at = 0
    for piece in gated_slice(low, which, c, y_part, lead, refs[:-1]):
        refs[-1][:, at : at + piece.shape[1]] = piece
        at += piece.shape[1]


def output_kernel(begin, ready, low, which, c, y_part, lead, gain, *refs):
    out, made, sems = refs[-3:]
    tokens, cols = made.shape
    pieces = [refs[i][:, a:b] for i, (a, b) in enumerate(ready)]
    if low is not None:
        arrived = refs[len(ready) : len(refs) - 3]
        if begin > 0:
            arrived = arrived[:-1]
        pieces += gated_slice(low, which, c, y_part, lead, arrived)
    total = jnp.zeros((tokens, 1), F32)
    for piece in pieces:
        total = total + jnp.sum(piece * piece, axis=1, keepdims=True)
    factor = lax.rsqrt(total / cols + EPS)
    copies = []
    at = 0
    for i, piece in enumerate(pieces):
        span = slice(at, at + piece.shape[1])
        made[:, span] = (piece * factor * gain[:, begin + at : begin + span.stop]).astype(BF16)
        copies.append(
            pltpu.make_async_copy(
                made.at[:, span], out.at[:, pl.ds(begin + at, piece.shape[1])], sems.at[i]
            )
        )
        copies[-1].start()
        at = span.stop
    for copy in copies:
        copy.wait()


def params(mib):
    return pltpu.CompilerParams(vmem_limit_bytes=mib * 1024 * 1024)


def doubling(state, decay, devices):
    def moved(value, distance):
        return lax.ppermute(value, "seq", [(i, i + distance) for i in range(devices - distance)])

    total, decay = moved(state.astype(BF16), 1), moved(decay, 1)
    distance = 1
    while distance < devices - 1:
        came = moved(total, distance)
        total = (decay * came.astype(F32) + total.astype(F32)).astype(BF16)
        decay = decay * moved(decay, distance)
        distance *= 2
    return total


def shards(x_in, bc_in, z_in, dt_raw, conv_x, conv_bc, a_log, d_skip, norm_gain):
    tokens, width = x_in.shape
    groups, both = bc_in.shape[1:]
    state_dim = both // 2
    heads = dt_raw.shape[1]
    head_dim = width // heads
    cols = width // groups
    devices = lax.axis_size("seq")
    place = lax.axis_index("seq")
    edges = [width * sum(PARTS[:i]) // sum(PARTS) for i in range(len(PARTS) + 1)]
    cuts = list(zip(edges[:-1], edges[1:]))

    taps = conv_x.shape[0]
    dt_t = dt_raw.T
    a_row = a_log.reshape(1, heads)
    d_row = d_skip.reshape(1, heads)
    gain = norm_gain.reshape(1, width)
    sources = [x_in, bc_in, conv_x, conv_bc]
    operands = sources + [dt_t, a_row]
    pinned = [pltpu.with_memory_space_constraint(v, pltpu.HBM) for v in operands]
    z_pinned = pltpu.with_memory_space_constraint(z_in, pltpu.HBM)
    landed = [pltpu.VMEM(v.shape, v.dtype) for v in operands]
    scale_shape = jax.ShapeDtypeStruct((tokens, width), F32)
    scalar = pl.BlockSpec(memory_space=pltpu.SMEM)
    in_vmem = pl.BlockSpec(memory_space=pltpu.VMEM)
    anywhere = pl.BlockSpec(memory_space=pl.ANY)
    in_hbm = [pl.BlockSpec(memory_space=pltpu.HBM)] * len(operands)

    def here(condition):
        return condition.astype(jnp.int32).reshape(1)

    def shifted(value, route):
        return lax.ppermute(value, "seq", route)

    def first_states(low, high):
        blocks = -(-(width + groups * both) // (high - low))
        extra = -(-(taps - 1) * blocks // (2 * RIM)) * 2 * RIM
        return pl.pallas_call(
            functools.partial(first_kernel, low, high),
            out_shape=[jax.ShapeDtypeStruct((state_dim + extra, high - low), BF16), scale_shape],
            in_specs=[scalar] + in_hbm,
            scratch_shapes=landed + [pltpu.SemaphoreType.DMA((len(operands),))],
            compiler_params=params(16),
            name="first_states",
        )(here(place == 0), *pinned)

    def next_states(token, scale, low, high):
        return pl.pallas_call(
            functools.partial(next_kernel, low, high),
            out_shape=jax.ShapeDtypeStruct((state_dim, high - low), BF16),
            in_specs=[scalar, anywhere] + [in_vmem] * (len(sources) + 1),
            compiler_params=params(16),
            name="next_states",
        )(here(place == 0), token, *sources, scale)

    def prepared(token):
        return pl.pallas_call(
            functools.partial(prepare_kernel, cuts),
            out_shape=[
                jax.ShapeDtypeStruct((RIM, width + groups * both), BF16),
                jax.ShapeDtypeStruct((1, width), F32),
                scale_shape,
            ]
            + [jax.ShapeDtypeStruct((1, high - low), F32) for low, high in cuts],
            in_specs=[anywhere] + [in_vmem] * 5,
            compiler_params=params(16),
            name="prepared",
        )(token, x_in, bc_in, dt_t, a_row, gain)

    def later_states(condition, rows, token, scale, low, high, at_hand=()):
        return pl.pallas_call(
            functools.partial(later_kernel, low, high),
            out_shape=jax.ShapeDtypeStruct((state_dim, high - low), F32),
            in_specs=[scalar, in_vmem, anywhere] + [in_vmem] * (len(sources) + 1 + len(at_hand)),
            compiler_params=params(16),
            name="later_states",
        )(here(condition), rows, token, *sources, scale, *at_hand)

    along = [(i, i + 1) for i in range(devices - 1)]
    def intra(token, befores):
        return pl.pallas_call(
            functools.partial(intra_kernel, len(befores)),
            out_shape=[
                scale_shape, scale_shape, jax.ShapeDtypeStruct((tokens, groups * state_dim), BF16)
            ],
            in_specs=[anywhere]
            + [in_vmem] * (len(befores) + 2)
            + [pl.BlockSpec(memory_space=pltpu.HBM)]
            + [in_vmem] * 5,
            scratch_shapes=[
                pltpu.VMEM(z_in.shape, z_in.dtype),
                pltpu.SemaphoreType.DMA((1,)),
            ],
            compiler_params=params(24),
            cost_estimate=pl.CostEstimate(
                flops=4 * tokens * tokens * width,
                bytes_accessed=12 * tokens * width,
                transcendentals=tokens * tokens * heads,
            ),
            name="intra",
        )(token, *befores, x_in, bc_in, z_pinned, conv_x, conv_bc, dt_t, a_row, d_row)

    if devices <= CHAIN_MOST:
        first, scale = first_states(*cuts[0])
        last, gain, scale_own, *decays = prepared(first)
        sent, token = [first], last
        for cut in cuts[1:]:
            sent.append(next_states(token, scale, *cut))
            token = sent[-1]
        soon = along[1 : max(devices - 2, 1)]
        late = along[max(devices - 2, 1) :]
        rows, _ = lax.optimization_barrier((last, sent[1]))
        befores = [shifted(rows, soon)] if soon else []
        arrived = [[shifted(v, along[:1])] for v in sent]
        befores.append(arrived[0][0])
        rows, token = arrived[0][0], last
        for hop in range(1, devices - 1):
            runs = place == 1 if hop == 1 else (place >= 2) & (place < devices - 1)
            after = token
            for i, cut in enumerate(cuts):
                if hop <= 2:
                    made = later_states(
                        runs, rows, after, scale_own, *cut, at_hand=() if hop == 1 else (d_row,)
                    )
                    states = [made] if i == 0 else states + [made]
                early = ()
                if hop == devices - 2 and hop > 1 and i == len(cuts) - 1:
                    early = (befores[-1],)
                before, *_ = lax.optimization_barrier((arrived[i][-1], token) + early)
                joined = decays[i] * before[:state_dim].astype(F32) + states[i]
                token = joined.astype(BF16)
                after = token if hop == 1 else after
                arrived[i].append(shifted(token, along[hop : hop + 1]))
            if hop == 1 and late:
                moved, _ = lax.optimization_barrier((last, token))
                befores.append(shifted(moved, late))
            rows = befores[0]
        which = place - 1
    else:
        last, gain, scale, *decays = prepared(a_row)
        befores = [shifted(last, along)]
        arrived = []
        for decay, cut in zip(decays, cuts):
            state = later_states(place >= 0, befores[0], a_row, scale, *cut)
            arrived.append([doubling(state, decay, devices)])
        which = jnp.zeros_like(place)
    which = which.astype(jnp.int32).reshape(1)
    y_part, lead, c_act = intra(a_row, befores)

    common = [which, c_act, y_part, lead]
    common_specs = [scalar] + [in_vmem] * 3
    last_low, last_high = cuts[-1]
    ready = []
    for (low, high), seen in zip(cuts[:-1], arrived):
        ready.append(
            pl.pallas_call(
                functools.partial(gated_kernel, low),
                out_shape=jax.ShapeDtypeStruct((tokens, high - low), F32),
                in_specs=common_specs + [in_vmem] * len(seen),
                compiler_params=params(16),
                name="gated",
            )(*common, *seen)
        )
    out = None
    for g in range(groups):
        begin, stop = g * cols, (g + 1) * cols
        taken, spans = [], []
        for (low, high), v in zip(cuts[:-1], ready):
            if low < stop and high > begin:
                taken.append(v)
                spans.append((max(low, begin) - low, min(high, stop) - low))
        inputs = taken
        unready = None
        if last_low < stop:
            unready = last_low
            inputs = taken + arrived[-1]
        aliases = {}
        specs = common_specs + [in_vmem] * (1 + len(inputs))
        if out is not None:
            aliases = {len(common) + 1 + len(inputs): 0}
            inputs = inputs + [out]
            specs = specs + [anywhere]
        out = pl.pallas_call(
            functools.partial(output_kernel, begin, spans, unready),
            out_shape=jax.ShapeDtypeStruct((tokens, width), BF16),
            in_specs=specs,
            out_specs=anywhere,
            scratch_shapes=[
                pltpu.VMEM((tokens, cols), BF16),
                pltpu.SemaphoreType.DMA((len(cuts) + groups,)),
            ],
            input_output_aliases=aliases,
            compiler_params=params(16),
            name="outputs",
        )(*common, gain, *inputs)
    return out


def solution(mesh):
    return jax.shard_map(
        shards,
        mesh=mesh,
        in_specs=(
            P(("groups", "seq"), "head"),
            P(("groups", "seq"), "head", None),
            P(("groups", "seq"), "head"),
            P(("groups", "seq"), "head"),
            P(None, "head"),
            P(None, "head", None),
            P("head"),
            P("head"),
            P("head"),
        ),
        out_specs=P(("groups", "seq"), "head"),
        check_vma=False,
    )
```

```python
import functools

import jax
import jax.numpy as jnp
from jax import lax
from jax.experimental import pallas as pl
from jax.experimental.pallas import tpu as pltpu
from jax.sharding import PartitionSpec as P

EPS = 1e-05
F32 = jnp.float32
BF16 = jnp.bfloat16
CHAIN_MOST = 4
PARTS = (1, 1, 1, 1)
CHUNK = 256
RIM = 8


def silu(u):
    return 0.5 * u * (1.0 + jnp.tanh(0.5 * u))


def softplus(v):
    return jnp.maximum(v, 0.0) + jnp.log1p(jnp.exp(-jnp.abs(v)))


def halves(v, count, axis):
    parts = []
    for _ in range(count - 1):
        part = v.astype(BF16)
        parts.append(part)
        v = v - part.astype(F32)
    parts.append(v.astype(BF16))
    return jnp.concatenate(parts, axis=axis)


def spread(per_head, head_dim, count):
    heads = per_head.shape[0]
    rows = lax.broadcasted_iota(jnp.int32, (heads * count, heads * head_dim), 0)
    cols = lax.broadcasted_iota(jnp.int32, (heads * count, heads * head_dim), 1)
    pick = (rows % heads == cols // head_dim).astype(F32).astype(BF16)
    return lax.dot_general(
        halves(per_head, count, 0), pick, (((0,), (0,)), ((), ())), preferred_element_type=F32
    )


def spread_row(column, head_dim):
    heads = column.shape[0]
    rows = lax.broadcasted_iota(jnp.int32, (heads, heads * head_dim), 0)
    cols = lax.broadcasted_iota(jnp.int32, (heads, heads * head_dim), 1)
    return jnp.sum(jnp.where(rows == cols // head_dim, column, 0.0), axis=0, keepdims=True)


def as_column(row, start, heads):
    every = row.shape[1]
    rows = lax.broadcasted_iota(jnp.int32, (heads, every), 0)
    cols = lax.broadcasted_iota(jnp.int32, (heads, every), 1)
    return jnp.sum(jnp.where(cols == rows + start, row, 0.0), axis=1, keepdims=True)


def conv_act(series, tail, taps):
    count = taps.shape[0]
    above = tail.shape[0]
    padded = jnp.concatenate([tail, series], axis=0)
    total = taps[count - 1 : count] * series
    for back in range(1, count):
        total = total + taps[count - 1 - back : count - back] * pltpu.roll(padded, back, 0)[above:]
    return silu(total).astype(BF16)


def rates(dt_raw, a_log_row, start):
    heads, tokens = dt_raw.shape
    dt = softplus(dt_raw)
    rate = -jnp.exp(as_column(a_log_row, start, heads)) * dt
    earlier = lax.broadcasted_iota(jnp.int32, (tokens, tokens), 0)
    later = lax.broadcasted_iota(jnp.int32, (tokens, tokens), 1)
    upto = (earlier <= later).astype(F32).astype(BF16)
    cum = jnp.dot(
        halves(rate, 3, 1), jnp.concatenate([upto] * 3, axis=0), preferred_element_type=F32
    )
    return dt, cum


def scales(groups, head_dim, dt_raw, a_log, scale):
    dt, cum = rates(dt_raw[...], a_log[...], 0)
    end = cum[:, -1:]
    tail_decay = jnp.exp(end - cum) * dt
    heads = dt.shape[0] // groups
    for g in range(groups):
        scale[:, g * heads * head_dim : (g + 1) * heads * head_dim] = spread(
            tail_decay[g * heads : (g + 1) * heads], head_dim, 2
        )
    return spread_row(jnp.exp(end), head_dim)


def by_group(low, high, cols):
    found = []
    while low < high:
        stop = min(high, (low // cols + 1) * cols)
        found.append((low // cols, low, stop))
        low = stop
    return found


def emit_states(low, high, x, tail_x, bc, tail_bc, taps_x, taps_bc, scale, emit):
    groups, both = bc.shape[1:]
    state_dim = both // 2
    for group, begin, stop in by_group(low, high, x.shape[1] // groups):
        b = conv_act(
            bc[:, :, :state_dim].astype(F32)[:, group],
            tail_bc(group),
            taps_bc[:, :, :state_dim][:, group],
        )
        b_t = b.astype(F32).T.astype(BF16)
        for at in range(begin, stop, CHUNK):
            cut = slice(at, at + CHUNK)
            act = conv_act(x[:, cut].astype(F32), tail_x(cut), taps_x[:, cut])
            scaled = (scale[:, cut] * act.astype(F32)).astype(BF16)
            here = slice(at - low, at - low + CHUNK)
            emit(here, jnp.dot(b_t, scaled, preferred_element_type=F32))


def head_rows(low, high, x, bc, taps_x, taps_bc, scale, out):
    state_dim = bc.shape[2] // 2

    def emit(here, total):
        out[:state_dim, here] = total.astype(BF16)

    emit_states(
        low, high, x, lambda cut: jnp.zeros((RIM, CHUNK), F32),
        bc, lambda group: jnp.zeros((RIM, state_dim), F32), taps_x, taps_bc, scale, emit,
    )


def first_kernel(
    low, high, active, x_hbm, bc_hbm, taps_x_hbm, taps_bc_hbm, dt_hbm, a_hbm,
    out, scale, x, bc, taps_x, taps_bc, dt_raw, a_log, sems,
):
    tokens, width = x.shape
    groups, both = bc.shape[1:]

    @pl.when(active[0] == 1)
    def _():
        pairs = [
            (dt_hbm, dt_raw), (a_hbm, a_log), (x_hbm, x), (bc_hbm, bc),
            (taps_x_hbm, taps_x), (taps_bc_hbm, taps_bc),
        ]
        copies = [pltpu.make_async_copy(*pair, sems.at[i]) for i, pair in enumerate(pairs)]
        for copy in copies:
            copy.start()
        for copy in copies[:2]:
            copy.wait()
        scales(groups, width // dt_raw.shape[0], dt_raw, a_log, scale)
        for copy in copies[2:]:
            copy.wait()
        state_dim, step = both // 2, high - low
        keep = taps_x.shape[0] - 1
        extra = out.shape[0] - state_dim
        last_bc = bc[tokens - 2 * RIM :].astype(F32)[-RIM:]
        last = [x[tokens - 2 * RIM :, :].astype(F32)[-RIM:]] + [last_bc[:, g] for g in range(groups)]
        length = width + groups * both
        last.append(jnp.zeros((RIM, -length % step + step), F32))
        last = jnp.concatenate(last, axis=1)
        at = lax.broadcasted_iota(jnp.int32, (extra, step), 0)
        below = jnp.zeros((extra, step), F32)
        fill = jnp.zeros((extra - RIM, step), F32)
        for k in range(-(-length // step)):
            block = jnp.concatenate([last[:, k * step : (k + 1) * step], fill], axis=0)
            block = pltpu.roll(block, (keep * (k + 1) - RIM) % extra, 0)
            below = jnp.where((at >= keep * k) & (at < keep * (k + 1)), block, below)
        out[state_dim:, :] = below.astype(BF16)
        head_rows(low, high, x, bc, taps_x, taps_bc, scale, out)


def next_kernel(low, high, active, _, x, bc, taps_x, taps_bc, scale, out):
    @pl.when(active[0] == 1)
    def _():
        head_rows(low, high, x, bc, taps_x, taps_bc, scale, out)


def prepare_kernel(cuts, _, x, bc, dt_raw, a_log, gain, pack, gain_out, scale, *decays):
    tokens, width = x.shape
    groups, both = bc.shape[1:]
    pack[:, :width] = x[tokens - 2 * RIM :, :].astype(F32)[-RIM:].astype(BF16)
    last_bc = bc[tokens - 2 * RIM :].astype(F32)[-RIM:]
    for g in range(groups):
        pack[:, width + g * both : width + (g + 1) * both] = last_bc[:, g].astype(BF16)
    gain_out[...] = gain[...]
    row = scales(groups, width // dt_raw.shape[0], dt_raw, a_log, scale)
    for decay, (low, high) in zip(decays, cuts):
        decay[...] = row[:, low:high]


def rows_before(rows, begin, stop, keep, state_dim):
    if rows.shape[0] == RIM:
        return rows[:, begin:stop].astype(F32)
    step = rows.shape[1]
    below = rows[state_dim:, begin % step : begin % step + stop - begin].astype(F32)
    return pltpu.roll(below, (RIM - keep * (begin // step + 1)) % below.shape[0], 0)[:RIM]


def later_kernel(low, high, active, rows, _, x, bc, taps_x, taps_bc, scale, *refs):
    state = refs[-1]
    both = bc.shape[2]
    state_dim = both // 2
    keep = taps_x.shape[0] - 1

    def before(begin, stop):
        return rows_before(rows, begin, stop, keep, state_dim)

    def tail_bc(group):
        at = x.shape[1] + group * both
        return before(at, at + state_dim)

    @pl.when(active[0] == 1)
    def _():
        def emit(here, total):
            state[:, here] = total

        emit_states(
            low, high, x, lambda cut: before(cut.start, cut.stop), bc, tail_bc,
            taps_x, taps_bc, scale, emit,
        )


def intra_kernel(count, _, *refs):
    sources, refs = refs[:count], refs[count:]
    x, bc, z, taps_x, taps_bc, dt_raw, a_log, d_skip, y_part, lead, c_act, wide = refs
    tokens, width = x.shape
    groups, both = bc.shape[1:]
    state_dim = both // 2
    keep = taps_x.shape[0] - 1
    cols = width // groups
    heads = dt_raw.shape[0] // groups
    head_dim = cols // heads
    dt, cum = rates(dt_raw[...], a_log[...], 0)
    cum_t = cum.T
    leading = jnp.exp(cum)
    skip = spread_row(as_column(d_skip[...], 0, groups * heads), head_dim)
    t_at = lax.broadcasted_iota(jnp.int32, (tokens, tokens), 0)
    s_at = lax.broadcasted_iota(jnp.int32, (tokens, tokens), 1)
    pair = 2 * head_dim

    def before(begin, stop):
        found = [rows_before(rows, begin, stop, keep, state_dim) for rows in sources]
        return sum(found[1:], found[0])

    for g in range(groups):
        at = width + g * both
        tail_bc = jnp.concatenate(
            [before(at, at + state_dim), before(at + state_dim, at + both)], axis=1
        )
        bc_act = conv_act(bc[...].astype(F32)[:, g], tail_bc, taps_bc[...][:, g])
        b, c = bc_act[:, :state_dim], bc_act[:, state_dim:]
        c_act[:, g * state_dim : (g + 1) * state_dim] = c
        inner = lax.dot_general(c, b, (((1,), (1,)), ((), ())), preferred_element_type=F32)
        inner = jnp.where(t_at >= s_at, inner, 0.0)
        wide[...] = spread(leading[g * heads : (g + 1) * heads], head_dim, 2)
        for first in range(0, heads, 2):
            here = slice(first * head_dim, first * head_dim + pair)
            cut = slice(g * cols + here.start, g * cols + here.stop)
            act = conv_act(x[:, cut].astype(F32), before(cut.start, cut.stop), taps_x[:, cut])
            lane = lax.broadcasted_iota(jnp.int32, act.shape, 1)
            full = act.astype(F32)
            blocks = jnp.concatenate(
                [jnp.where(lane < head_dim, full, 0.0), jnp.where(lane < head_dim, 0.0, full)],
                axis=0,
            ).astype(BF16)
            weights = []
            for h in (g * heads + first, g * heads + first + 1):
                gap = jnp.minimum(cum_t[:, h : h + 1] - cum[h : h + 1, :], 0.0)
                weights.append((jnp.exp(gap) * dt[h : h + 1, :] * inner).astype(BF16))
            y = jnp.dot(jnp.concatenate(weights, axis=1), blocks, preferred_element_type=F32)
            gate = silu(z[:, cut].astype(F32))
            y_part[:, cut] = (y + skip[:, cut] * full) * gate
            lead[:, cut] = wide[:, here] * gate


def gated_slice(low, which, c, y_part, lead, arrived):
    tokens, width = y_part.shape
    state_dim = arrived[-1].shape[0]
    size = arrived[-1].shape[1]
    state = jnp.zeros((state_dim, size), BF16)
    for i, came in enumerate(arrived):
        state = jnp.where(which[0] == i, came[...][:state_dim], state)
    pieces = []
    for group, begin, stop in by_group(low, low + size, width * state_dim // c.shape[1]):
        from_state = jnp.dot(
            c[:, group * state_dim : (group + 1) * state_dim],
            state[:, begin - low : stop - low],
            preferred_element_type=F32,
        )
        pieces.append(y_part[:, begin:stop] + lead[:, begin:stop] * from_state)
    return pieces


def gated_kernel(low, which, c, y_part, lead, *refs):
    at = 0
    for piece in gated_slice(low, which, c, y_part, lead, refs[:-1]):
        refs[-1][:, at : at + piece.shape[1]] = piece
        at += piece.shape[1]


def output_kernel(begin, ready, low, which, c, y_part, lead, gain, *refs):
    out, made, sems = refs[-3:]
    tokens, cols = made.shape
    pieces = [refs[i][:, a:b] for i, (a, b) in enumerate(ready)]
    if low is not None:
        arrived = refs[len(ready) : len(refs) - 3]
        if begin > 0:
            arrived = arrived[:-1]
        pieces += gated_slice(low, which, c, y_part, lead, arrived)
    total = jnp.zeros((tokens, 1), F32)
    for piece in pieces:
        total = total + jnp.sum(piece * piece, axis=1, keepdims=True)
    factor = lax.rsqrt(total / cols + EPS)
    copies = []
    at = 0
    for i, piece in enumerate(pieces):
        span = slice(at, at + piece.shape[1])
        made[:, span] = (piece * factor * gain[:, begin + at : begin + span.stop]).astype(BF16)
        copies.append(
            pltpu.make_async_copy(
                made.at[:, span], out.at[:, pl.ds(begin + at, piece.shape[1])], sems.at[i]
            )
        )
        copies[-1].start()
        at = span.stop
    for copy in copies:
        copy.wait()


def params(mib):
    return pltpu.CompilerParams(vmem_limit_bytes=mib * 1024 * 1024)


def doubling(state, decay, devices):
    def moved(value, distance):
        return lax.ppermute(value, "seq", [(i, i + distance) for i in range(devices - distance)])

    total, decay = moved(state.astype(BF16), 1), moved(decay, 1)
    distance = 1
    while distance < devices - 1:
        came = moved(total, distance)
        total = (decay * came.astype(F32) + total.astype(F32)).astype(BF16)
        decay = decay * moved(decay, distance)
        distance *= 2
    return total


def shards(x_in, bc_in, z_in, dt_raw, conv_x, conv_bc, a_log, d_skip, norm_gain):
    tokens, width = x_in.shape
    groups, both = bc_in.shape[1:]
    state_dim = both // 2
    heads = dt_raw.shape[1]
    head_dim = width // heads
    cols = width // groups
    devices = lax.axis_size("seq")
    place = lax.axis_index("seq")
    edges = [width * sum(PARTS[:i]) // sum(PARTS) for i in range(len(PARTS) + 1)]
    cuts = list(zip(edges[:-1], edges[1:]))

    taps = conv_x.shape[0]
    dt_t = dt_raw.T
    a_row = a_log.reshape(1, heads)
    d_row = d_skip.reshape(1, heads)
    gain = norm_gain.reshape(1, width)
    sources = [x_in, bc_in, conv_x, conv_bc]
    operands = sources + [dt_t, a_row]
    pinned = [pltpu.with_memory_space_constraint(v, pltpu.HBM) for v in operands]
    landed = [pltpu.VMEM(v.shape, v.dtype) for v in operands]
    scale_shape = jax.ShapeDtypeStruct((tokens, width), F32)
    scalar = pl.BlockSpec(memory_space=pltpu.SMEM)
    in_vmem = pl.BlockSpec(memory_space=pltpu.VMEM)
    anywhere = pl.BlockSpec(memory_space=pl.ANY)
    in_hbm = [pl.BlockSpec(memory_space=pltpu.HBM)] * len(operands)

    def here(condition):
        return condition.astype(jnp.int32).reshape(1)

    def shifted(value, route):
        return lax.ppermute(value, "seq", route)

    def first_states(low, high):
        blocks = -(-(width + groups * both) // (high - low))
        extra = -(-(taps - 1) * blocks // (2 * RIM)) * 2 * RIM
        return pl.pallas_call(
            functools.partial(first_kernel, low, high),
            out_shape=[jax.ShapeDtypeStruct((state_dim + extra, high - low), BF16), scale_shape],
            in_specs=[scalar] + in_hbm,
            scratch_shapes=landed + [pltpu.SemaphoreType.DMA((len(operands),))],
            compiler_params=params(16),
            name="first_states",
        )(here(place == 0), *pinned)

    def next_states(token, scale, low, high):
        return pl.pallas_call(
            functools.partial(next_kernel, low, high),
            out_shape=jax.ShapeDtypeStruct((state_dim, high - low), BF16),
            in_specs=[scalar, anywhere] + [in_vmem] * (len(sources) + 1),
            compiler_params=params(16),
            name="next_states",
        )(here(place == 0), token, *sources, scale)

    def prepared(token):
        return pl.pallas_call(
            functools.partial(prepare_kernel, cuts),
            out_shape=[
                jax.ShapeDtypeStruct((RIM, width + groups * both), BF16),
                jax.ShapeDtypeStruct((1, width), F32),
                scale_shape,
            ]
            + [jax.ShapeDtypeStruct((1, high - low), F32) for low, high in cuts],
            in_specs=[anywhere] + [in_vmem] * 5,
            compiler_params=params(16),
            name="prepared",
        )(token, x_in, bc_in, dt_t, a_row, gain)

    def later_states(condition, rows, token, scale, low, high, at_hand=()):
        return pl.pallas_call(
            functools.partial(later_kernel, low, high),
            out_shape=jax.ShapeDtypeStruct((state_dim, high - low), F32),
            in_specs=[scalar, in_vmem, anywhere] + [in_vmem] * (len(sources) + 1 + len(at_hand)),
            compiler_params=params(16),
            name="later_states",
        )(here(condition), rows, token, *sources, scale, *at_hand)

    along = [(i, i + 1) for i in range(devices - 1)]
    def intra(token, befores):
        return pl.pallas_call(
            functools.partial(intra_kernel, len(befores)),
            out_shape=[
                scale_shape, scale_shape, jax.ShapeDtypeStruct((tokens, groups * state_dim), BF16)
            ],
            in_specs=[anywhere] + [in_vmem] * (len(befores) + 8),
            scratch_shapes=[pltpu.VMEM((tokens, cols), F32)],
            compiler_params=params(24),
            cost_estimate=pl.CostEstimate(
                flops=4 * tokens * tokens * width,
                bytes_accessed=12 * tokens * width,
                transcendentals=tokens * tokens * heads,
            ),
            name="intra",
        )(token, *befores, x_in, bc_in, z_in, conv_x, conv_bc, dt_t, a_row, d_row)

    if devices <= CHAIN_MOST:
        first, scale = first_states(*cuts[0])
        last, gain, scale_own, *decays = prepared(first)
        sent, token = [first], last
        for cut in cuts[1:]:
            sent.append(next_states(token, scale, *cut))
            token = sent[-1]
        soon = along[1 : max(devices - 2, 1)]
        late = along[max(devices - 2, 1) :]
        rows, _ = lax.optimization_barrier((last, sent[1]))
        befores = [shifted(rows, soon)] if soon else []
        arrived = [[shifted(v, along[:1])] for v in sent]
        befores.append(arrived[0][0])
        rows, token = arrived[0][0], last
        for hop in range(1, devices - 1):
            runs = place == 1 if hop == 1 else (place >= 2) & (place < devices - 1)
            after = token
            for i, cut in enumerate(cuts):
                if hop <= 2:
                    made = later_states(
                        runs, rows, after, scale_own, *cut, at_hand=() if hop == 1 else (d_row,)
                    )
                    states = [made] if i == 0 else states + [made]
                early = ()
                if hop == devices - 2 and hop > 1 and i == len(cuts) - 1:
                    early = (arrived[0][-1], befores[-1])
                before, *_ = lax.optimization_barrier((arrived[i][-1], token) + early)
                joined = decays[i] * before[:state_dim].astype(F32) + states[i]
                token = joined.astype(BF16)
                after = token if hop == 1 else after
                arrived[i].append(shifted(token, along[hop : hop + 1]))
            if hop == 1 and late:
                moved, _ = lax.optimization_barrier((last, token))
                befores.append(shifted(moved, late))
            rows = befores[0]
        which = place - 1
    else:
        last, gain, scale, *decays = prepared(a_row)
        befores = [shifted(last, along)]
        arrived = []
        for decay, cut in zip(decays, cuts):
            state = later_states(place >= 0, befores[0], a_row, scale, *cut)
            arrived.append([doubling(state, decay, devices)])
        which = jnp.zeros_like(place)
    which = which.astype(jnp.int32).reshape(1)
    y_part, lead, c_act = intra(a_row, befores)

    common = [which, c_act, y_part, lead]
    common_specs = [scalar] + [in_vmem] * 3
    last_low, last_high = cuts[-1]
    ready = []
    for (low, high), seen in zip(cuts[:-1], arrived):
        ready.append(
            pl.pallas_call(
                functools.partial(gated_kernel, low),
                out_shape=jax.ShapeDtypeStruct((tokens, high - low), F32),
                in_specs=common_specs + [in_vmem] * len(seen),
                compiler_params=params(16),
                name="gated",
            )(*common, *seen)
        )
    out = None
    for g in range(groups):
        begin, stop = g * cols, (g + 1) * cols
        taken, spans = [], []
        for (low, high), v in zip(cuts[:-1], ready):
            if low < stop and high > begin:
                taken.append(v)
                spans.append((max(low, begin) - low, min(high, stop) - low))
        inputs = taken
        unready = None
        if last_low < stop:
            unready = last_low
            inputs = taken + arrived[-1]
        aliases = {}
        specs = common_specs + [in_vmem] * (1 + len(inputs))
        if out is not None:
            aliases = {len(common) + 1 + len(inputs): 0}
            inputs = inputs + [out]
            specs = specs + [anywhere]
        out = pl.pallas_call(
            functools.partial(output_kernel, begin, spans, unready),
            out_shape=jax.ShapeDtypeStruct((tokens, width), BF16),
            in_specs=specs,
            out_specs=anywhere,
            scratch_shapes=[
                pltpu.VMEM((tokens, cols), BF16),
                pltpu.SemaphoreType.DMA((len(cuts) + groups,)),
            ],
            input_output_aliases=aliases,
            compiler_params=params(16),
            name="outputs",
        )(*common, gain, *inputs)
    return out


def solution(mesh):
    return jax.shard_map(
        shards,
        mesh=mesh,
        in_specs=(
            P(("groups", "seq"), "head"),
            P(("groups", "seq"), "head", None),
            P(("groups", "seq"), "head"),
            P(("groups", "seq"), "head"),
            P(None, "head"),
            P(None, "head", None),
            P("head"),
            P("head"),
            P("head"),
        ),
        out_specs=P(("groups", "seq"), "head"),
        check_vma=False,
    )
```
